32 devices in a mesh: slab: 2 (over x), iface: 4 (over y, core), mech: 4 (over z).
Axes of the slice: x: 2, y: 2, z: 4, core: 2. Of those that a mesh axis runs over, the one named last changes fastest.
Arguments:
- temp_start: float32 [16, 4, 8, 512], P(('slab', 'mech'), 'iface'), may hold values from 0.5 to 3
- conductivity: float32 [16, 4, 8, 512], P(('slab', 'mech'), 'iface'), may hold values from 0.3 to 2.8
- gap_conductance: float32 [16, 4, 8], P(('slab', 'mech'), 'iface'), may hold values from 10 to 20
- partner: int32 [32], P('iface'), may hold values from 0 to 31, each once
- row_order: int32 [4, 8], P('iface'), may hold values from 0 to 7, each once within a row
- active_layers: int32 [4, 8], P('iface', ('slab', 'mech')), may hold values from 1 to 2, as said below
- trial_stress: float32 [16, 4, 8, 512], P(None, 'iface', ('slab', 'mech')), may hold values from 0.5 to 2
Outputs:
- stress: float32 [16, 4, 8, 512], P(None, 'iface', ('slab', 'mech'))
- element_strain: float32 [2, 4, 8, 512], P(None, 'iface', ('slab', 'mech'))
The draws below stay inside these ranges and needn't reach their ends.
Inputs may be any that keep to these rules, and one draw needn't show every extreme that they name: `active_layers`: element layers that creep in one element row; some row has all 2.
All inputs are finite; a program needn't handle non-finite values.
Results may differ from the reference program's by a relative error of at most 0.00005.
Values sent between devices are 32-bit elements; how exact they have to be, the bound alone decides.
No kernel may reach another device: no remote copies, remote signals or barrier semaphores. Data moves between devices by JAX's collectives and lax.ppermute only.
A program may use at most 64 MiB of HBM per device.

```python
import math
import jax
import jax.numpy as jnp

NR = 512
SWEEPS = 2
NEWTON = 4
SECTIONS = 4
CA = 8
NA = 32
NZ = 16


def draw_temp_start(key, part):
    first, second = jax.random.split(key)
    shape = (NZ, SECTIONS, CA, NR)
    coin = jax.random.uniform(first, shape, jnp.float32)
    jitter = jax.random.uniform(second, shape, jnp.float32)
    hot = coin < 0.5
    spread = 0.1 * jitter
    return jnp.where(hot, 3.0 - spread, 0.5 + spread).astype(jnp.float32)


def draw_conductivity(key, part):
    shape = (NZ, SECTIONS, CA, NR)
    unit = jax.random.uniform(key, shape, jnp.float32)
    radial = jnp.arange(NR, dtype=jnp.int32)
    middle = NR // 2
    near_face = ((radial >= middle - 2) & (radial <= middle + 1))[None, None, None, :]
    wide = 0.3 * jnp.exp(unit * math.log(2.8 / 0.3))
    close = 1.5 * jnp.exp(unit * math.log(2.0 / 1.5))
    return jnp.where(near_face, close, wide).astype(jnp.float32)


def draw_active_layers(key, part):
    first, second, third = jax.random.split(key, 3)
    top = NZ // 8
    draw_one = jax.random.randint(first, (SECTIONS, CA), 1, top + 1)
    draw_two = jax.random.randint(second, (SECTIONS, CA), 1, top + 1)
    upper = jnp.maximum(draw_one, draw_two).reshape(-1)
    chosen = jax.random.randint(third, (), 0, SECTIONS * CA)
    upper = jnp.where(jnp.arange(SECTIONS * CA) == chosen, top, upper)
    return upper.reshape(SECTIONS, CA).astype(jnp.int32)


def block_levels(rng, extent, cuts, least, largest):
    loudness = 1.0
    for axis_at, parts in cuts:
        heights = jax.random.uniform(jax.random.fold_in(jax.random.fold_in(rng, 6), axis_at), (parts,), jnp.float32, least / len(cuts), largest / len(cuts))
        loudness = loudness * jnp.repeat(jnp.exp(heights), extent[axis_at] // parts).reshape((-1,) + (1,) * (len(extent) - 1 - axis_at))
    return loudness


def setup_inputs(seed: int = 0) -> dict:
    keys = jax.random.split(jax.random.key(seed), 8)
    return {
        "temp_start": draw_temp_start(jax.random.fold_in(keys[7], 71), 0),
        "conductivity": draw_conductivity(jax.random.fold_in(keys[7], 71), 0),
        "gap_conductance": jnp.clip(jnp.exp(math.log(20.0) - 0.6931472 * jax.random.uniform(keys[2], (NZ, SECTIONS, CA), jnp.float32) ** block_levels(keys[2], (NZ, SECTIONS, CA), ((0, 8), (1, 4)), -0.2, 0.2)), 10.0, 20.0),
        "partner": jax.random.permutation(keys[3], NA).astype(jnp.int32),
        "row_order": jax.vmap(lambda own: jax.random.permutation(own, CA))(jax.random.split(keys[4], SECTIONS)).reshape((SECTIONS, CA)).astype(jnp.int32),
        "active_layers": draw_active_layers(jax.random.fold_in(keys[7], 71), 0),
        "trial_stress": jnp.clip(jnp.exp(math.log(2.0) - 1.3862944 * jax.random.uniform(keys[6], (NZ, SECTIONS, CA, NR), jnp.float32) ** block_levels(keys[6], (NZ, SECTIONS, CA, NR), ((1, 4), (2, 8)), -0.2, 0.2)), 0.5, 2.0),
    }


FLUX_STEP = 0.03
CREEP_RATE = 200.0
ACTIVATION = 12.0
REFERENCE_TEMP = 1.0


def neighbour_weight(shift_z, shift_a, shift_r):
    reach = abs(shift_z) + abs(shift_a) + abs(shift_r)
    return [0.0, 1.0, 0.5, 0.25][reach]


def conduction(padded_temp, padded_cond):
    center_temp = padded_temp[1:-1, 1:-1, 1:-1]
    center_cond = padded_cond[1:-1, 1:-1, 1:-1]
    depth, across, radial = center_temp.shape
    radial_index = jnp.arange(radial, dtype=jnp.int32)
    gap_row = radial // 2
    outward_open = (radial_index != gap_row - 1).astype(jnp.float32)
    inward_open = (radial_index != gap_row).astype(jnp.float32)
    total = jnp.zeros(center_temp.shape, jnp.float32)
    for shift_z in (-1, 0, 1):
        for shift_a in (-1, 0, 1):
            for shift_r in (-1, 0, 1):
                if shift_z == 0 and shift_a == 0 and shift_r == 0:
                    continue
                near_temp = padded_temp[1 + shift_z:1 + shift_z + depth, 1 + shift_a:1 + shift_a + across, 1 + shift_r:1 + shift_r + radial]
                near_cond = padded_cond[1 + shift_z:1 + shift_z + depth, 1 + shift_a:1 + shift_a + across, 1 + shift_r:1 + shift_r + radial]
                face = neighbour_weight(shift_z, shift_a, shift_r) * 0.5 * (center_cond + near_cond)
                if shift_r == 1:
                    face = face * outward_open
                elif shift_r == -1:
                    face = face * inward_open
                total = total + face * (near_temp - center_temp)
    return FLUX_STEP * total


def creep_return(mech_temp, trial, active_layers):
    rate = CREEP_RATE * jnp.exp(-ACTIVATION / (mech_temp + REFERENCE_TEMP))
    slip = jnp.zeros(trial.shape, jnp.float32)
    for newton_step in range(NEWTON):
        left = trial - slip
        residue = slip - rate * left ** 3
        slope = 1.0 + 3.0 * rate * left ** 2
        slip = slip - residue / slope
    depth = trial.shape[0]
    layer = jnp.arange(depth, dtype=jnp.int32) // 8
    live = (layer[:, None, None] < active_layers[None, :, :]).astype(jnp.float32)[..., None]
    creep = live * slip
    stress = trial - creep
    strain = jnp.sum(creep.reshape((depth // 8, 8) + trial.shape[1:]), axis=1) * 0.125
    return stress, strain


def reference(temp_start, conductivity, gap_conductance, partner, row_order, active_layers, trial_stress):
    depth, sections, rows, radial = temp_start.shape
    temp = temp_start.reshape(depth, sections * rows, radial)
    cond = conductivity.reshape(depth, sections * rows, radial)
    gap = gap_conductance.reshape(depth, sections * rows)
    padded_cond = jnp.pad(cond, 1)
    gap_row = radial // 2
    for sweep in range(SWEEPS):
        compact = temp[:, :, gap_row - 1]
        canister = temp[:, :, gap_row]
        flux = gap * (compact[:, partner] - canister)
        returned = jnp.zeros(flux.shape, jnp.float32).at[:, partner].add(flux)
        fresh = temp + conduction(jnp.pad(temp, 1), padded_cond)
        temp = fresh.at[:, :, gap_row].add(FLUX_STEP * flux).at[:, :, gap_row - 1].add(-FLUX_STEP * returned)
    grouped = temp.reshape(depth, sections, rows, radial)
    order = jnp.broadcast_to(row_order[None, :, :, None], grouped.shape).astype(jnp.int32)
    mech_temp = jnp.take_along_axis(grouped, order, axis=2)
    return creep_return(mech_temp, trial_stress, active_layers)
```

```python
import jax
import jax.numpy as jnp
from jax import lax
from jax.experimental import pallas as pl
from jax.experimental.pallas import tpu as pltpu
from jax.sharding import PartitionSpec as P

SWEEPS = 2
NEWTON = 4


FLUX_STEP = 0.03
CREEP_RATE = 200.0
ACTIVATION = 12.0
REFERENCE_TEMP = 1.0


def padded(block, sides, width):
    for axis, dim in sides:
        count = lax.axis_size(axis)
        forward = [(i, i + 1) for i in range(count - 1)]
        backward = [(target, source) for source, target in forward]
        low = lax.ppermute(
            lax.slice_in_dim(block, block.shape[dim] - width, None, axis=dim), axis, forward
        )
        high = lax.ppermute(lax.slice_in_dim(block, 0, width, axis=dim), axis, backward)
        block = jnp.concatenate([low, block, high], axis=dim)
    return block


def neighbour_weight(shift_z, shift_a, shift_r):
    reach = abs(shift_z) + abs(shift_a) + abs(shift_r)
    return [0.0, 1.0, 0.5, 0.25][reach]


def conduction(padded_temp, padded_cond):
    center_temp = padded_temp[1:-1, 1:-1, 1:-1]
    center_cond = padded_cond[1:-1, 1:-1, 1:-1]
    depth, across, radial = center_temp.shape
    radial_index = jnp.arange(radial, dtype=jnp.int32)
    gap_row = radial // 2
    outward_open = (radial_index != gap_row - 1).astype(jnp.float32)
    inward_open = (radial_index != gap_row).astype(jnp.float32)
    total = jnp.zeros(center_temp.shape, jnp.float32)
    for shift_z in (-1, 0, 1):
        for shift_a in (-1, 0, 1):
            for shift_r in (-1, 0, 1):
                if shift_z == 0 and shift_a == 0 and (shift_r == 0):
                    continue
                near_temp = padded_temp[
                    1 + shift_z : 1 + shift_z + depth,
                    1 + shift_a : 1 + shift_a + across,
                    1 + shift_r : 1 + shift_r + radial,
                ]
                near_cond = padded_cond[
                    1 + shift_z : 1 + shift_z + depth,
                    1 + shift_a : 1 + shift_a + across,
                    1 + shift_r : 1 + shift_r + radial,
                ]
                face = neighbour_weight(shift_z, shift_a, shift_r) * 0.5 * (center_cond + near_cond)
                if shift_r == 1:
                    face = face * outward_open
                elif shift_r == -1:
                    face = face * inward_open
                total = total + face * (near_temp - center_temp)
    return FLUX_STEP * total


def creep_return(mech_temp, trial, active_layers):
    rate = CREEP_RATE * jnp.exp(-ACTIVATION / (mech_temp + REFERENCE_TEMP))
    slip = jnp.zeros(trial.shape, jnp.float32)
    for newton_step in range(NEWTON):
        left = trial - slip
        residue = slip - rate * left**3
        slope = 1.0 + 3.0 * rate * left**2
        slip = slip - residue / slope
    depth = trial.shape[0]
    layer = jnp.arange(depth, dtype=jnp.int32) // 8
    live = (layer[:, None, None] < active_layers[None, :, :]).astype(jnp.float32)[..., None]
    creep = live * slip
    stress = trial - creep
    strain = jnp.sum(creep.reshape((depth // 8, 8) + trial.shape[1:]), axis=1) * 0.125
    return (stress, strain)


def stepwise(
    temp_start, conductivity, gap_conductance, partner, row_order, active_layers, trial_stress
):
    depth = temp_start.shape[0]
    rows = temp_start.shape[2]
    radial = temp_start.shape[3]
    temp = temp_start.reshape(depth, rows, radial)
    cond = conductivity.reshape(depth, rows, radial)
    gap = gap_conductance.reshape(depth, rows)
    gap_row = radial // 2
    sections = lax.axis_size("iface")
    across = rows * sections
    all_cols = jnp.arange(across, dtype=jnp.int32)
    cond_rim = padded(cond, ((("slab", "mech"), 0), ("iface", 1)), 1)
    padded_cond = jnp.pad(cond_rim, ((0, 0), (0, 0), (1, 1)))
    spread_table = (partner[:, None] == all_cols[None, :]).astype(jnp.float32)
    for sweep in range(SWEEPS):
        temp_rim = padded(temp, ((("slab", "mech"), 0), ("iface", 1)), 1)
        padded_temp = jnp.pad(temp_rim, ((0, 0), (0, 0), (1, 1)))
        compact = temp[:, :, gap_row - 1]
        canister = temp[:, :, gap_row]
        compact_all = lax.all_gather(compact, "iface", axis=1, tiled=True)
        facing = jnp.take(compact_all, partner, axis=1)
        flux = gap * (facing - canister)
        spread = jnp.dot(
            flux, spread_table, precision=lax.Precision.HIGHEST, preferred_element_type=jnp.float32
        )
        returned = lax.psum_scatter(spread, "iface", scatter_dimension=1, tiled=True)
        fresh = temp + conduction(padded_temp, padded_cond)
        temp = (
            fresh.at[:, :, gap_row]
            .add(FLUX_STEP * flux)
            .at[:, :, gap_row - 1]
            .add(-FLUX_STEP * returned)
        )
    permuted = jnp.take(temp, row_order[0], axis=1)
    mech_temp = lax.all_to_all(permuted, ("slab", "mech"), split_axis=1, concat_axis=0, tiled=True)
    mech_temp = mech_temp.reshape(mech_temp.shape[0], 1, mech_temp.shape[1], radial)
    return creep_return(mech_temp, trial_stress, active_layers)


LANES = 128
GATHER_LIMIT = 4 * 1024 * 1024


def lane_index(like):
    return lax.broadcasted_iota(jnp.int32, like.shape, 1)


def axial_sum(field):
    depth = field.shape[0]
    row = lax.broadcasted_iota(jnp.int32, field.shape, 0)
    below = jnp.where(row == 0, 0.0, pltpu.roll(field, 1, 0))
    above = jnp.where(row == depth - 1, 0.0, pltpu.roll(field, depth - 1, 0))
    return field + 0.5 * (below + above)


def radial_sum(tiles):
    middle = len(tiles) // 2
    lane = lane_index(tiles[0])
    inward = [pltpu.roll(tile, 1, 1) for tile in tiles]
    outward = [pltpu.roll(tile, LANES - 1, 1) for tile in tiles]
    result = []
    for index, tile in enumerate(tiles):
        left = 0.0 if index in (0, middle) else inward[index - 1]
        right = 0.0 if index in (middle - 1, len(tiles) - 1) else outward[index + 1]
        left = jnp.where(lane == 0, left, inward[index])
        right = jnp.where(lane == LANES - 1, right, outward[index])
        result.append(tile + 0.5 * (left + right))
    return result


def across_sum(near, center, far):
    return [c + 0.5 * (n + f) for n, c, f in zip(near, center, far)]


def box_sum(near, center, far):
    return radial_sum([axial_sum(tile) for tile in across_sum(near, center, far)])


def increments(temp, cond, box_temp, box_cond, box_heat, weights):
    return [
        FLUX_STEP * (k * (bt - w * t) + bh - t * bk)
        for t, k, bt, bk, bh, w in zip(temp, cond, box_temp, box_cond, box_heat, weights)
    ]


def product(left, right):
    return [a * b for a, b in zip(left, right)]


def column_step(
    sections,
    depth,
    rows,
    radial,
    axes,
    partner_ref,
    order_ref,
    active_ref,
    temp_ref,
    cond_ref,
    gap_ref,
    trial_ref,
    stress_ref,
    strain_ref,
):
    count = radial // LANES
    middle = count // 2
    across = sections * rows
    section = lax.axis_index("iface")
    member = lax.axis_index(axes[0]) * lax.axis_size(axes[1]) + lax.axis_index(axes[1])
    own = section * rows + order_ref[0, member]

    def inverse(column):
        found = jnp.int32(0)
        for segment in range(across):
            found = jnp.where(partner_ref[segment] == column, jnp.int32(segment), found)
        return found

    def inside(column):
        return jnp.where((column >= 0) & (column < across), 1.0, 0.0).astype(jnp.float32)

    def clipped(column):
        return jnp.minimum(jnp.maximum(column, 0), across - 1)

    def load(ref, column, tile):
        base = (column // rows) * (depth * rows * count) + tile * rows + column % rows
        return ref[pl.ds(base, depth, stride=rows * count), :]

    def load_column(ref, column):
        scale = inside(column)
        at = clipped(column)
        return [scale * load(ref, at, tile) for tile in range(count)]

    def load_gap(column):
        block = gap_ref[column // rows]
        lane = lane_index(block)
        chosen = jnp.where(lane == column % rows, block, 0.0)
        return jnp.sum(chosen, axis=1, keepdims=True)

    compact = middle - 1
    canister = middle
    temps = {d: load_column(temp_ref, own + d) for d in range(-2, 3)}
    conds = {d: load_column(cond_ref, own + d) for d in range(-2, 3)}
    heats = {d: product(temps[d], conds[d]) for d in range(-2, 3)}
    lane = lane_index(temps[0][0])
    at_compact = lane == LANES - 1
    at_canister = lane == 0

    def crossing(gap, compact_tile, canister_tile):
        return gap * (pltpu.roll(compact_tile, 1, 1) - canister_tile)

    weights = [8.0] * count
    weights[compact] = jnp.where(at_compact, 6.0, 8.0)
    weights[canister] = jnp.where(at_canister, 6.0, 8.0)

    def with_flux(tiles, flux, returned):
        tiles = list(tiles)
        tiles[canister] = tiles[canister] + jnp.where(at_canister, FLUX_STEP * flux, 0.0)
        back = pltpu.roll(FLUX_STEP * returned, LANES - 1, 1)
        tiles[compact] = tiles[compact] - jnp.where(at_compact, back, 0.0)
        return tiles

    first = {}
    box_cond_own = None
    own_flux = None
    own_returned = None
    for d in (-1, 0, 1):
        at = clipped(own + d)
        facing = partner_ref[at]
        source = inverse(at)
        flux = crossing(load_gap(at), load(temp_ref, facing, compact), temps[d][canister])
        returned = crossing(load_gap(source), temps[d][compact], load(temp_ref, source, canister))
        box_temp = box_sum(temps[d - 1], temps[d], temps[d + 1])
        box_cond = box_sum(conds[d - 1], conds[d], conds[d + 1])
        box_heat = box_sum(heats[d - 1], heats[d], heats[d + 1])
        change = increments(temps[d], conds[d], box_temp, box_cond, box_heat, weights)
        tiles = with_flux([t + c for t, c in zip(temps[d], change)], flux, returned)
        scale = inside(own + d)
        first[d] = [scale * tile for tile in tiles] if d else tiles
        if d == 0:
            box_cond_own = box_cond
            own_flux = flux
            own_returned = returned

    def face_after(column, tile, shift):
        def summed(fields):
            total = axial_sum(fields[1] + 0.5 * (fields[0] + fields[2]))
            return total + 0.5 * pltpu.roll(total, shift, 1)

        near = [inside(column + d) for d in (-1, 0, 1)]
        spots = [clipped(column + d) for d in (-1, 0, 1)]
        temp = [s * load(temp_ref, c, tile) for s, c in zip(near, spots)]
        cond = [s * load(cond_ref, c, tile) for s, c in zip(near, spots)]
        heat = product(temp, cond)
        change = cond[1] * (summed(temp) - 6.0 * temp[1]) + summed(heat) - temp[1] * summed(cond)
        return temp[1] + FLUX_STEP * change

    facing = partner_ref[own]
    source = inverse(own)
    facing_tile = face_after(facing, compact, 1)
    facing_tile = facing_tile - pltpu.roll(FLUX_STEP * own_flux, LANES - 1, 1)
    source_tile = face_after(source, canister, LANES - 1) + FLUX_STEP * own_returned
    flux = crossing(load_gap(own), facing_tile, first[0][canister])
    returned = crossing(load_gap(source), first[0][compact], source_tile)
    first_heat = {d: product(first[d], conds[d]) for d in (-1, 0, 1)}
    change = increments(
        first[0],
        conds[0],
        box_sum(first[-1], first[0], first[1]),
        box_cond_own,
        box_sum(first_heat[-1], first_heat[0], first_heat[1]),
        weights,
    )
    final = with_flux([t + c for t, c in zip(first[0], change)], flux, returned)

    active = active_ref[0, 0]
    for tile in range(count):
        for element in range(depth // 8):
            spot = pl.ds(element * 8 * count + tile, 8, stride=count)
            trial = trial_ref[spot, :]
            mech_temp = final[tile][element * 8 : element * 8 + 8]
            rate = CREEP_RATE * jnp.exp(-ACTIVATION / (mech_temp + REFERENCE_TEMP))
            slip = jnp.zeros(trial.shape, jnp.float32)
            for newton_step in range(NEWTON):
                left = trial - slip
                pull = rate * left * left
                slip = slip - (slip - pull * left) / (1.0 + 3.0 * pull)
            live = jnp.where(element < active, 1.0, 0.0).astype(jnp.float32)
            creep = live * slip
            stress_ref[spot, :] = trial - creep
            strain_ref[pl.ds(element * count + tile, 1), :] = 0.125 * jnp.sum(
                creep, axis=0, keepdims=True
            )


def column_call(sections, depth, rows, radial, axes, operands):
    count = radial // LANES
    smem = pl.BlockSpec(memory_space=pltpu.SMEM)
    vmem = pl.BlockSpec(memory_space=pltpu.VMEM)
    return pl.pallas_call(
        lambda *refs: column_step(sections, depth, rows, radial, axes, *refs),
        out_shape=(
            jax.ShapeDtypeStruct((depth * count, LANES), jnp.float32),
            jax.ShapeDtypeStruct((depth // 8 * count, LANES), jnp.float32),
        ),
        in_specs=[smem, smem, smem, vmem, vmem, vmem, vmem],
        out_specs=(vmem, vmem),
        compiler_params=pltpu.CompilerParams(vmem_limit_bytes=32 * 1024 * 1024),
    )(*operands)


def on_device(
    temp_start, conductivity, gap_conductance, partner, row_order, active_layers, trial_stress
):
    layers, _, rows, radial = temp_start.shape
    sections = lax.axis_size("iface")
    axes = ("slab", "mech")
    members = lax.axis_size(axes[0]) * lax.axis_size(axes[1])
    depth = layers * members
    total = 2 * 4 * depth * sections * rows * radial
    if total > GATHER_LIMIT or rows != members or radial % (2 * LANES) or depth % 8:
        return stepwise(
            temp_start,
            conductivity,
            gap_conductance,
            partner,
            row_order,
            active_layers,
            trial_stress,
        )
    everyone = ("iface",) + axes
    count = radial // LANES

    def by_lanes(block):
        split = block.reshape(layers, rows, count, LANES)
        return split.transpose(0, 2, 1, 3)

    temp_all = lax.all_gather(by_lanes(temp_start), everyone, axis=0, tiled=False)
    cond_all = lax.all_gather(by_lanes(conductivity), everyone, axis=0, tiled=False)
    gap_all = lax.all_gather(gap_conductance, everyone, axis=0, tiled=False)
    partner_all = lax.all_gather(partner, everyone, axis=0, tiled=False)
    partner_all = partner_all.reshape(sections, members, rows)[:, 0].reshape(sections * rows)
    grid = sections * depth * rows * count
    stress, strain = column_call(
        sections,
        depth,
        rows,
        radial,
        axes,
        (
            partner_all,
            row_order,
            active_layers,
            temp_all.reshape(grid, LANES),
            cond_all.reshape(grid, LANES),
            gap_all.reshape(sections, depth, rows),
            trial_stress.reshape(depth * count, LANES),
        ),
    )
    return (
        stress.reshape(depth, 1, 1, radial),
        strain.reshape(depth // 8, 1, 1, radial),
    )


def solution(mesh):
    placed = (
        P(("slab", "mech"), "iface", None, None),
        P(("slab", "mech"), "iface", None, None),
        P(("slab", "mech"), "iface", None),
        P("iface"),
        P("iface", None),
        P("iface", ("slab", "mech")),
        P(None, "iface", ("slab", "mech"), None),
    )
    return jax.shard_map(
        on_device,
        mesh=mesh,
        in_specs=placed,
        out_specs=(
            P(None, "iface", ("slab", "mech"), None),
            P(None, "iface", ("slab", "mech"), None),
        ),
        check_vma=False,
    )
```

```python
import functools
import jax
import jax.numpy as jnp
from jax import lax
from jax.experimental import pallas as pl
from jax.experimental.pallas import tpu as pltpu
from jax.sharding import PartitionSpec as P

SWEEPS = 2
NEWTON = 4


FLUX_STEP = 0.03
CREEP_RATE = 200.0
ACTIVATION = 12.0
REFERENCE_TEMP = 1.0


def padded(block, sides, width):
    for axis, dim in sides:
        count = lax.axis_size(axis)
        forward = [(i, i + 1) for i in range(count - 1)]
        backward = [(target, source) for source, target in forward]
        low = lax.ppermute(
            lax.slice_in_dim(block, block.shape[dim] - width, None, axis=dim), axis, forward
        )
        high = lax.ppermute(lax.slice_in_dim(block, 0, width, axis=dim), axis, backward)
        block = jnp.concatenate([low, block, high], axis=dim)
    return block


def neighbour_weight(shift_z, shift_a, shift_r):
    reach = abs(shift_z) + abs(shift_a) + abs(shift_r)
    return [0.0, 1.0, 0.5, 0.25][reach]


def conduction(padded_temp, padded_cond):
    center_temp = padded_temp[1:-1, 1:-1, 1:-1]
    center_cond = padded_cond[1:-1, 1:-1, 1:-1]
    depth, across, radial = center_temp.shape
    radial_index = jnp.arange(radial, dtype=jnp.int32)
    gap_row = radial // 2
    outward_open = (radial_index != gap_row - 1).astype(jnp.float32)
    inward_open = (radial_index != gap_row).astype(jnp.float32)
    total = jnp.zeros(center_temp.shape, jnp.float32)
    for shift_z in (-1, 0, 1):
        for shift_a in (-1, 0, 1):
            for shift_r in (-1, 0, 1):
                if shift_z == 0 and shift_a == 0 and (shift_r == 0):
                    continue
                near_temp = padded_temp[
                    1 + shift_z : 1 + shift_z + depth,
                    1 + shift_a : 1 + shift_a + across,
                    1 + shift_r : 1 + shift_r + radial,
                ]
                near_cond = padded_cond[
                    1 + shift_z : 1 + shift_z + depth,
                    1 + shift_a : 1 + shift_a + across,
                    1 + shift_r : 1 + shift_r + radial,
                ]
                face = neighbour_weight(shift_z, shift_a, shift_r) * 0.5 * (center_cond + near_cond)
                if shift_r == 1:
                    face = face * outward_open
                elif shift_r == -1:
                    face = face * inward_open
                total = total + face * (near_temp - center_temp)
    return FLUX_STEP * total


def creep_return(mech_temp, trial, active_layers):
    rate = CREEP_RATE * jnp.exp(-ACTIVATION / (mech_temp + REFERENCE_TEMP))
    slip = jnp.zeros(trial.shape, jnp.float32)
    for newton_step in range(NEWTON):
        left = trial - slip
        residue = slip - rate * left**3
        slope = 1.0 + 3.0 * rate * left**2
        slip = slip - residue / slope
    depth = trial.shape[0]
    layer = jnp.arange(depth, dtype=jnp.int32) // 8
    live = (layer[:, None, None] < active_layers[None, :, :]).astype(jnp.float32)[..., None]
    creep = live * slip
    stress = trial - creep
    strain = jnp.sum(creep.reshape((depth // 8, 8) + trial.shape[1:]), axis=1) * 0.125
    return (stress, strain)


def stepwise(
    temp_start, conductivity, gap_conductance, partner, row_order, active_layers, trial_stress
):
    depth = temp_start.shape[0]
    rows = temp_start.shape[2]
    radial = temp_start.shape[3]
    temp = temp_start.reshape(depth, rows, radial)
    cond = conductivity.reshape(depth, rows, radial)
    gap = gap_conductance.reshape(depth, rows)
    gap_row = radial // 2
    sections = lax.axis_size("iface")
    across = rows * sections
    all_cols = jnp.arange(across, dtype=jnp.int32)
    cond_rim = padded(cond, ((("slab", "mech"), 0), ("iface", 1)), 1)
    padded_cond = jnp.pad(cond_rim, ((0, 0), (0, 0), (1, 1)))
    spread_table = (partner[:, None] == all_cols[None, :]).astype(jnp.float32)
    for sweep in range(SWEEPS):
        temp_rim = padded(temp, ((("slab", "mech"), 0), ("iface", 1)), 1)
        padded_temp = jnp.pad(temp_rim, ((0, 0), (0, 0), (1, 1)))
        compact = temp[:, :, gap_row - 1]
        canister = temp[:, :, gap_row]
        compact_all = lax.all_gather(compact, "iface", axis=1, tiled=True)
        facing = jnp.take(compact_all, partner, axis=1)
        flux = gap * (facing - canister)
        spread = jnp.dot(
            flux, spread_table, precision=lax.Precision.HIGHEST, preferred_element_type=jnp.float32
        )
        returned = lax.psum_scatter(spread, "iface", scatter_dimension=1, tiled=True)
        fresh = temp + conduction(padded_temp, padded_cond)
        temp = (
            fresh.at[:, :, gap_row]
            .add(FLUX_STEP * flux)
            .at[:, :, gap_row - 1]
            .add(-FLUX_STEP * returned)
        )
    permuted = jnp.take(temp, row_order[0], axis=1)
    mech_temp = lax.all_to_all(permuted, ("slab", "mech"), split_axis=1, concat_axis=0, tiled=True)
    mech_temp = mech_temp.reshape(mech_temp.shape[0], 1, mech_temp.shape[1], radial)
    return creep_return(mech_temp, trial_stress, active_layers)


LANES = 128
FACES = 4
REACH = 2
WINDOW = 2 * REACH + 1


def iota(shape, axis):
    return lax.broadcasted_iota(jnp.int32, shape, axis)


def axial_sum(field):
    depth = field.shape[0]
    row = iota(field.shape, 0)
    below = jnp.where(row == 0, 0.0, pltpu.roll(field, 1, 0))
    above = jnp.where(row == depth - 1, 0.0, pltpu.roll(field, depth - 1, 0))
    return field + 0.5 * (below + above)


def radial_sum(tiles):
    middle = len(tiles) // 2
    lane = iota(tiles[0].shape, 1)
    inward = [pltpu.roll(tile, 1, 1) for tile in tiles]
    outward = [pltpu.roll(tile, LANES - 1, 1) for tile in tiles]
    result = []
    for index, tile in enumerate(tiles):
        left = 0.0 if index in (0, middle) else inward[index - 1]
        right = 0.0 if index in (middle - 1, len(tiles) - 1) else outward[index + 1]
        left = jnp.where(lane == 0, left, inward[index])
        right = jnp.where(lane == LANES - 1, right, outward[index])
        result.append(tile + 0.5 * (left + right))
    return result


def box_sum(near, center, far):
    return radial_sum([axial_sum(c + 0.5 * (n + f)) for n, c, f in zip(near, center, far)])


def product(left, right):
    return [a * b for a, b in zip(left, right)]


class Sizes:
    def __init__(self, layers, rows, radial):
        self.layers = layers
        self.rows = rows
        self.radial = radial
        self.tiles = radial // LANES
        self.sections = lax.axis_size("iface")
        self.members = lax.axis_size("slab") * lax.axis_size("mech")
        self.depth = layers * self.members
        self.across = self.sections * rows
        self.window_rows = WINDOW * self.tiles
        self.edge_rows = REACH * self.tiles
        self.extra_at = 2 * self.window_rows
        self.layer_rows = self.extra_at + 8
        self.edge_extra_at = 2 * layers * self.edge_rows
        self.message_rows = self.edge_extra_at + 8 * layers


def spread_rows(sizes, block_ref, layer, put):
    for tile in range(sizes.tiles):
        put(tile, block_ref[layer, 0, :, pl.ds(tile * LANES, LANES)])


def edge_kernel(sizes, partner_ref, gap_ref, temp_ref, cond_ref, out_ref, rows_ref):
    section = lax.axis_index("iface")
    lane = iota((8, LANES), 1)
    sub = iota((8, LANES), 0)
    group = lane // sizes.across
    mine = lane % sizes.across == section * sizes.rows + sub
    middle = sizes.tiles // 2
    slot = 0
    strips = []
    for layer in range(sizes.layers):
        for ref in (temp_ref, cond_ref):
            base = slot * sizes.rows * sizes.tiles

            def put(tile, value, base=base):
                rows_ref[pl.ds(base + tile, sizes.rows, stride=sizes.tiles), :] = value

            spread_rows(sizes, ref, layer, put)
            inner = ref[layer, 0, :, pl.ds((middle - 1) * LANES, LANES)]
            outer = ref[layer, 0, :, pl.ds(middle * LANES, LANES)]
            picked = [
                inner[:, LANES - 2 : LANES - 1],
                inner[:, LANES - 1 : LANES],
                outer[:, 0:1],
                outer[:, 1:2],
            ]
            strip = jnp.zeros((8, LANES), jnp.float32)
            for face, column in enumerate(picked):
                strip = jnp.where(group == face, jnp.broadcast_to(column, (8, LANES)), strip)
            strip = jnp.where(mine, strip, 0.0)
            strips.append(jnp.sum(strip, axis=0, keepdims=True))
            slot += 1
    row = iota((1, LANES), 1)
    table = jnp.zeros((1, LANES), jnp.float32)
    gaps = [jnp.zeros((1, LANES), jnp.float32) for _ in range(sizes.layers)]
    for index in range(sizes.rows):
        compact_lane = sizes.across + partner_ref[index]
        canister_lane = 2 * sizes.across + section * sizes.rows + index
        at_compact = row == compact_lane
        at_canister = row == canister_lane
        table = jnp.where(at_canister, compact_lane.astype(jnp.float32), table)
        table = jnp.where(at_compact, canister_lane.astype(jnp.float32), table)
        for layer in range(sizes.layers):
            gaps[layer] = jnp.where(at_compact | at_canister, gap_ref[layer, 0, index], gaps[layer])
    extras = []
    for layer in range(sizes.layers):
        extra = jnp.zeros((8, LANES), jnp.float32)
        for place, value in enumerate(
            (strips[2 * layer], strips[2 * layer + 1], gaps[layer], table)
        ):
            extra = jnp.where(sub == place, jnp.broadcast_to(value, (8, LANES)), extra)
        extras.append(extra)
    for target in range(sizes.sections):
        start = jnp.where(target > section, (sizes.rows - REACH) * sizes.tiles, 0)
        for slot in range(2 * sizes.layers):
            base = slot * sizes.rows * sizes.tiles
            out_ref[target, pl.ds(slot * sizes.edge_rows, sizes.edge_rows), :] = rows_ref[
                pl.ds(pl.multiple_of(base + start, 8), sizes.edge_rows), :
            ]
        for layer in range(sizes.layers):
            out_ref[target, pl.ds(sizes.edge_extra_at + 8 * layer, 8), :] = extras[layer]


def window_kernel(sizes, order_ref, temp_ref, cond_ref, edge_ref, out_ref, rows_ref):
    section = lax.axis_index("iface")
    before = jnp.maximum(section - 1, 0)
    after = jnp.minimum(section + 1, sizes.sections - 1)
    has_before = jnp.where(section > 0, 1.0, 0.0).astype(jnp.float32)
    has_after = jnp.where(section < sizes.sections - 1, 1.0, 0.0).astype(jnp.float32)
    own_rows = sizes.rows * sizes.tiles
    slot_rows = own_rows + 2 * sizes.edge_rows
    slot = 0
    for layer in range(sizes.layers):
        for ref in (temp_ref, cond_ref):
            base = slot * slot_rows
            edge = pl.ds(slot * sizes.edge_rows, sizes.edge_rows)
            rows_ref[pl.ds(base, sizes.edge_rows), :] = has_before * edge_ref[before, edge, :]
            rows_ref[pl.ds(base + sizes.edge_rows + own_rows, sizes.edge_rows), :] = (
                has_after * edge_ref[after, edge, :]
            )

            def put(tile, value, base=base):
                first = base + sizes.edge_rows + tile
                rows_ref[pl.ds(first, sizes.rows, stride=sizes.tiles), :] = value

            spread_rows(sizes, ref, layer, put)
            slot += 1
    extras = []
    for layer in range(sizes.layers):
        spot = pl.ds(sizes.edge_extra_at + 8 * layer, 8)
        extra = edge_ref[0, spot, :]
        for source in range(1, sizes.sections):
            extra = extra + edge_ref[source, spot, :]
        extras.append(extra)
    for member in range(sizes.members):
        start = order_ref[0, member] * sizes.tiles
        for layer in range(sizes.layers):
            for kind in range(2):
                base = (2 * layer + kind) * slot_rows
                out_ref[
                    member, layer, pl.ds(kind * sizes.window_rows, sizes.window_rows), :
                ] = rows_ref[pl.ds(base + start, sizes.window_rows), :]
            out_ref[member, layer, pl.ds(sizes.extra_at, 8), :] = extras[layer]


def column_kernel(sizes, order_ref, active_ref, parts_ref, trial_ref, stress_ref, strain_ref):
    depth, tiles, across = sizes.depth, sizes.tiles, sizes.across
    member = lax.axis_index("slab") * lax.axis_size("mech") + lax.axis_index("mech")
    own = lax.axis_index("iface") * sizes.rows + order_ref[0, member]

    def load(index):
        return parts_ref[pl.ds(index, depth, stride=sizes.layer_rows), :]

    def load_column(kind, shift):
        base = kind * sizes.window_rows + (shift + REACH) * tiles
        return [load(base + tile) for tile in range(tiles)]

    def inside(column):
        return jnp.where((column >= 0) & (column < across), 1.0, 0.0).astype(jnp.float32)

    compact = tiles // 2 - 1
    canister = tiles // 2
    lane = iota((depth, LANES), 1)

    strip_temp = load(sizes.extra_at)
    strip_cond = load(sizes.extra_at + 1)
    strip_gap = load(sizes.extra_at + 2)
    table = parts_ref[pl.ds(sizes.extra_at + 3, 1), :].astype(jnp.int32)
    table = jnp.broadcast_to(table, (depth, LANES))
    place = lane % across
    face = lane // across
    is_face = (face == 1) | (face == 2)

    def across_sum(field):
        before = jnp.where(place == 0, 0.0, pltpu.roll(field, 1, 1))
        after = jnp.where(place == across - 1, 0.0, pltpu.roll(field, LANES - 1, 1))
        return field + 0.5 * (before + after)

    def strip_sum(field):
        total = axial_sum(across_sum(field))
        inner = pltpu.roll(total, across, 1)
        outer = pltpu.roll(total, LANES - across, 1)
        return total + 0.5 * jnp.where(face == 1, inner, outer)

    def exchange(strip):
        met = jnp.take_along_axis(strip, table, axis=1)
        return FLUX_STEP * strip_gap * (met - strip)

    first_gain = exchange(strip_temp)
    strip_change = strip_cond * (strip_sum(strip_temp) - 6.0 * strip_temp)
    strip_change = strip_change + strip_sum(strip_temp * strip_cond)
    strip_change = strip_change - strip_temp * strip_sum(strip_cond)
    strip_first = strip_temp + FLUX_STEP * strip_change + first_gain
    second_gain = exchange(strip_first)

    weights = [8.0] * tiles
    weights[compact] = jnp.where(lane == LANES - 1, 6.0, 8.0)
    weights[canister] = jnp.where(lane == 0, 6.0, 8.0)

    def with_gain(columns, gain, column):
        to_compact = (2 * LANES - 1 - across - column) % LANES
        to_canister = (2 * LANES - 2 * across - column) % LANES
        columns = list(columns)
        moved = pltpu.roll(gain, to_compact, 1)
        columns[compact] = columns[compact] + jnp.where(lane == LANES - 1, moved, 0.0)
        moved = pltpu.roll(gain, to_canister, 1)
        columns[canister] = columns[canister] + jnp.where(lane == 0, moved, 0.0)
        return columns

    def swept(temp, cond, box_temp, box_cond, box_heat):
        return [
            t + FLUX_STEP * (k * (bt - w * t) + bh - t * bk)
            for t, k, bt, bk, bh, w in zip(temp, cond, box_temp, box_cond, box_heat, weights)
        ]

    span = range(-REACH, REACH + 1)
    temps = {d: load_column(0, d) for d in span}
    conds = {d: load_column(1, d) for d in span}
    heats = {d: product(temps[d], conds[d]) for d in span}
    first = {}
    box_conds = {}
    for d in (-1, 0, 1):
        box_conds[d] = box_sum(conds[d - 1], conds[d], conds[d + 1])
        columns = swept(
            temps[d],
            conds[d],
            box_sum(temps[d - 1], temps[d], temps[d + 1]),
            box_conds[d],
            box_sum(heats[d - 1], heats[d], heats[d + 1]),
        )
        columns = with_gain(columns, first_gain, own + d)
        first[d] = [inside(own + d) * tile for tile in columns] if d else columns
    heats = {d: product(first[d], conds[d]) for d in (-1, 0, 1)}
    columns = swept(
        first[0],
        conds[0],
        box_sum(first[-1], first[0], first[1]),
        box_conds[0],
        box_sum(heats[-1], heats[0], heats[1]),
    )
    final = with_gain(columns, second_gain, own)

    active = active_ref[0, 0]
    for tile in range(tiles):
        for element in range(depth // 8):
            spot = pl.ds(element * 8 * tiles + tile, 8, stride=tiles)
            trial = trial_ref[spot, :]
            mech_temp = final[tile][element * 8 : element * 8 + 8]
            rate = CREEP_RATE * jnp.exp(-ACTIVATION / (mech_temp + REFERENCE_TEMP))
            slip = jnp.zeros(trial.shape, jnp.float32)
            for newton_step in range(NEWTON):
                left = trial - slip
                pull = rate * left * left
                slip = slip - (slip - pull * left) / (1.0 + 3.0 * pull)
            live = jnp.where(element < active, 1.0, 0.0).astype(jnp.float32)
            creep = live * slip
            stress_ref[spot, :] = trial - creep
            strain_ref[pl.ds(element * tiles + tile, 1), :] = 0.125 * jnp.sum(
                creep, axis=0, keepdims=True
            )


def kernel_call(body, sizes, out_shape, memories, scratch, operands):
    spaces = {"smem": pltpu.SMEM, "vmem": pltpu.VMEM}
    out_spec = pl.BlockSpec(memory_space=pltpu.VMEM)
    return pl.pallas_call(
        functools.partial(body, sizes),
        out_shape=out_shape,
        in_specs=[pl.BlockSpec(memory_space=spaces[memory]) for memory in memories],
        out_specs=jax.tree.map(lambda _: out_spec, out_shape),
        scratch_shapes=scratch,
        compiler_params=pltpu.CompilerParams(vmem_limit_bytes=16 * 1024 * 1024),
    )(*operands)


def fits_columns(sizes):
    return (
        sizes.rows == 8
        and sizes.members == sizes.rows
        and sizes.across * FACES == LANES
        and sizes.radial == 4 * LANES
        and sizes.layers == 2
    )


def on_device(
    temp_start, conductivity, gap_conductance, partner, row_order, active_layers, trial_stress
):
    layers, _, rows, radial = temp_start.shape
    sizes = Sizes(layers, rows, radial)
    if not fits_columns(sizes):
        return stepwise(
            temp_start,
            conductivity,
            gap_conductance,
            partner,
            row_order,
            active_layers,
            trial_stress,
        )

    def floats(*shape):
        return jax.ShapeDtypeStruct(shape, jnp.float32)

    edges = kernel_call(
        edge_kernel,
        sizes,
        floats(sizes.sections, sizes.message_rows, LANES),
        ["smem", "smem", "vmem", "vmem"],
        [pltpu.VMEM((2 * layers * rows * sizes.tiles, LANES), jnp.float32)],
        (partner, gap_conductance, temp_start, conductivity),
    )
    edges = lax.all_to_all(edges, "iface", split_axis=0, concat_axis=0, tiled=True)
    slot_rows = rows * sizes.tiles + 2 * sizes.edge_rows
    parts = kernel_call(
        window_kernel,
        sizes,
        floats(sizes.members, layers, sizes.layer_rows, LANES),
        ["smem", "vmem", "vmem", "vmem"],
        [pltpu.VMEM((2 * layers * slot_rows, LANES), jnp.float32)],
        (row_order, temp_start, conductivity, edges),
    )
    parts = parts.reshape(sizes.members, layers * sizes.layer_rows, LANES)
    parts = lax.all_to_all(parts, ("slab", "mech"), split_axis=0, concat_axis=0, tiled=True)
    stress, strain = kernel_call(
        column_kernel,
        sizes,
        (
            floats(sizes.depth * sizes.tiles, LANES),
            floats(sizes.depth // 8 * sizes.tiles, LANES),
        ),
        ["smem", "smem", "vmem", "vmem"],
        [],
        (
            row_order,
            active_layers,
            parts.reshape(sizes.depth * sizes.layer_rows, LANES),
            trial_stress.reshape(sizes.depth * sizes.tiles, LANES),
        ),
    )
    return (
        stress.reshape(sizes.depth, 1, 1, radial),
        strain.reshape(sizes.depth // 8, 1, 1, radial),
    )


def solution(mesh):
    placed = (
        P(("slab", "mech"), "iface", None, None),
        P(("slab", "mech"), "iface", None, None),
        P(("slab", "mech"), "iface", None),
        P("iface"),
        P("iface", None),
        P("iface", ("slab", "mech")),
        P(None, "iface", ("slab", "mech"), None),
    )
    return jax.shard_map(
        on_device,
        mesh=mesh,
        in_specs=placed,
        out_specs=(
            P(None, "iface", ("slab", "mech"), None),
            P(None, "iface", ("slab", "mech"), None),
        ),
        check_vma=False,
    )
```

```python
import functools
import jax
import jax.numpy as jnp
from jax import lax
from jax.experimental import pallas as pl
from jax.experimental.pallas import tpu as pltpu
from jax.sharding import PartitionSpec as P

SWEEPS = 2
NEWTON = 4


FLUX_STEP = 0.03
CREEP_RATE = 200.0
ACTIVATION = 12.0
REFERENCE_TEMP = 1.0


def padded(block, sides, width):
    for axis, dim in sides:
        count = lax.axis_size(axis)
        forward = [(i, i + 1) for i in range(count - 1)]
        backward = [(target, source) for source, target in forward]
        low = lax.ppermute(
            lax.slice_in_dim(block, block.shape[dim] - width, None, axis=dim), axis, forward
        )
        high = lax.ppermute(lax.slice_in_dim(block, 0, width, axis=dim), axis, backward)
        block = jnp.concatenate([low, block, high], axis=dim)
    return block


def neighbour_weight(shift_z, shift_a, shift_r):
    reach = abs(shift_z) + abs(shift_a) + abs(shift_r)
    return [0.0, 1.0, 0.5, 0.25][reach]


def conduction(padded_temp, padded_cond):
    center_temp = padded_temp[1:-1, 1:-1, 1:-1]
    center_cond = padded_cond[1:-1, 1:-1, 1:-1]
    depth, across, radial = center_temp.shape
    radial_index = jnp.arange(radial, dtype=jnp.int32)
    gap_row = radial // 2
    outward_open = (radial_index != gap_row - 1).astype(jnp.float32)
    inward_open = (radial_index != gap_row).astype(jnp.float32)
    total = jnp.zeros(center_temp.shape, jnp.float32)
    for shift_z in (-1, 0, 1):
        for shift_a in (-1, 0, 1):
            for shift_r in (-1, 0, 1):
                if shift_z == 0 and shift_a == 0 and (shift_r == 0):
                    continue
                near_temp = padded_temp[
                    1 + shift_z : 1 + shift_z + depth,
                    1 + shift_a : 1 + shift_a + across,
                    1 + shift_r : 1 + shift_r + radial,
                ]
                near_cond = padded_cond[
                    1 + shift_z : 1 + shift_z + depth,
                    1 + shift_a : 1 + shift_a + across,
                    1 + shift_r : 1 + shift_r + radial,
                ]
                face = neighbour_weight(shift_z, shift_a, shift_r) * 0.5 * (center_cond + near_cond)
                if shift_r == 1:
                    face = face * outward_open
                elif shift_r == -1:
                    face = face * inward_open
                total = total + face * (near_temp - center_temp)
    return FLUX_STEP * total


def creep_return(mech_temp, trial, active_layers):
    rate = CREEP_RATE * jnp.exp(-ACTIVATION / (mech_temp + REFERENCE_TEMP))
    slip = jnp.zeros(trial.shape, jnp.float32)
    for newton_step in range(NEWTON):
        left = trial - slip
        residue = slip - rate * left**3
        slope = 1.0 + 3.0 * rate * left**2
        slip = slip - residue / slope
    depth = trial.shape[0]
    layer = jnp.arange(depth, dtype=jnp.int32) // 8
    live = (layer[:, None, None] < active_layers[None, :, :]).astype(jnp.float32)[..., None]
    creep = live * slip
    stress = trial - creep
    strain = jnp.sum(creep.reshape((depth // 8, 8) + trial.shape[1:]), axis=1) * 0.125
    return (stress, strain)


def stepwise(
    temp_start, conductivity, gap_conductance, partner, row_order, active_layers, trial_stress
):
    depth = temp_start.shape[0]
    rows = temp_start.shape[2]
    radial = temp_start.shape[3]
    temp = temp_start.reshape(depth, rows, radial)
    cond = conductivity.reshape(depth, rows, radial)
    gap = gap_conductance.reshape(depth, rows)
    gap_row = radial // 2
    sections = lax.axis_size("iface")
    across = rows * sections
    all_cols = jnp.arange(across, dtype=jnp.int32)
    cond_rim = padded(cond, ((("slab", "mech"), 0), ("iface", 1)), 1)
    padded_cond = jnp.pad(cond_rim, ((0, 0), (0, 0), (1, 1)))
    spread_table = (partner[:, None] == all_cols[None, :]).astype(jnp.float32)
    for sweep in range(SWEEPS):
        temp_rim = padded(temp, ((("slab", "mech"), 0), ("iface", 1)), 1)
        padded_temp = jnp.pad(temp_rim, ((0, 0), (0, 0), (1, 1)))
        compact = temp[:, :, gap_row - 1]
        canister = temp[:, :, gap_row]
        compact_all = lax.all_gather(compact, "iface", axis=1, tiled=True)
        facing = jnp.take(compact_all, partner, axis=1)
        flux = gap * (facing - canister)
        spread = jnp.dot(
            flux, spread_table, precision=lax.Precision.HIGHEST, preferred_element_type=jnp.float32
        )
        returned = lax.psum_scatter(spread, "iface", scatter_dimension=1, tiled=True)
        fresh = temp + conduction(padded_temp, padded_cond)
        temp = (
            fresh.at[:, :, gap_row]
            .add(FLUX_STEP * flux)
            .at[:, :, gap_row - 1]
            .add(-FLUX_STEP * returned)
        )
    permuted = jnp.take(temp, row_order[0], axis=1)
    mech_temp = lax.all_to_all(permuted, ("slab", "mech"), split_axis=1, concat_axis=0, tiled=True)
    mech_temp = mech_temp.reshape(mech_temp.shape[0], 1, mech_temp.shape[1], radial)
    return creep_return(mech_temp, trial_stress, active_layers)


LANES = 128
HALO = 2
EVERYONE = ("iface", "slab", "mech")


def iota(shape, axis):
    return lax.broadcasted_iota(jnp.int32, shape, axis)


class Sizes:
    def __init__(self, layers, rows, radial):
        self.layers = layers
        self.rows = rows
        self.radial = radial
        self.tiles = radial // LANES
        self.sections = lax.axis_size("iface")
        self.members = lax.axis_size("slab") * lax.axis_size("mech")
        self.devices = self.sections * self.members
        self.depth = layers * self.members
        self.chunk = radial // self.devices
        self.width = self.chunk + 2 * HALO
        self.field = layers * self.width
        self.gap_row = radial // 2


def fits_tiles(sizes):
    return (
        sizes.rows == 8
        and sizes.members == sizes.rows
        and sizes.layers == 2
        and sizes.sections * sizes.rows <= LANES
        and sizes.radial % sizes.devices == 0
        and sizes.chunk * 8 == LANES
        and sizes.radial % (2 * LANES) == 0
    )


def deal_kernel(
    sizes,
    partner_hbm,
    order_hbm,
    gap_hbm,
    temp_hbm,
    cond_hbm,
    out_ref,
    partner_ref,
    order_ref,
    gap_ref,
    temp_ref,
    cond_ref,
    sems,
):
    pairs = (
        (temp_hbm, temp_ref),
        (cond_hbm, cond_ref),
        (gap_hbm, gap_ref),
        (partner_hbm, partner_ref),
        (order_hbm, order_ref),
    )
    copies = [
        pltpu.make_async_copy(source, target, sems.at[index])
        for index, (source, target) in enumerate(pairs)
    ]
    for copy in copies:
        copy.start()
    for copy in copies:
        copy.wait()
    shape = (sizes.rows, LANES)
    lane = iota(shape, 1)
    sub = iota(shape, 0)
    extra_at = 2 * sizes.field
    extra = jnp.zeros(shape, jnp.float32)
    for row in range(sizes.rows):
        for layer in range(sizes.layers):
            spot = (sub == row) & (lane == extra_at + layer * sizes.width)
            extra = jnp.where(spot, gap_ref[layer, 0, row], extra)
        spot = (sub == row) & (lane == extra_at + 1)
        extra = jnp.where(spot, partner_ref[row].astype(jnp.float32), extra)
        spot = (sub == row) & (lane == extra_at + 2)
        extra = jnp.where(spot, order_ref[0, row].astype(jnp.float32), extra)
    blocks = [
        [ref[layer, 0, :, pl.ds(tile * LANES, LANES)] for tile in range(sizes.tiles)]
        for ref in (temp_ref, cond_ref)
        for layer in range(sizes.layers)
    ]
    for device in range(sizes.devices):
        first = device * sizes.chunk - HALO
        packed = extra
        for index, block in enumerate(blocks):
            base = index * sizes.width
            for tile in range(sizes.tiles):
                low = max(first, tile * LANES)
                high = min(first + sizes.width, (tile + 1) * LANES)
                if low >= high:
                    continue
                moved = pltpu.roll(block[tile], (base - first + tile * LANES) % LANES, 1)
                spot = (lane >= base + low - first) & (lane < base + high - first)
                packed = jnp.where(spot, moved, packed)
        out_ref[device] = packed


def sweep_kernel(sizes, dealt_ref, out_ref):
    rows, width, field = sizes.rows, sizes.width, sizes.field
    sections, members = sizes.sections, sizes.members
    shape = (rows, LANES)
    lane = iota(shape, 1)
    sub = iota(shape, 0)
    place = lax.axis_index("iface") * members
    place = place + lax.axis_index("slab") * lax.axis_size("mech") + lax.axis_index("mech")
    first = place * sizes.chunk - HALO
    segment = lane // width
    radius = first + lane % width
    lower_layer = segment % 2 == 0
    at_compact = radius == sizes.gap_row - 1
    at_canister = radius == sizes.gap_row
    in_grid = (radius >= 0) & (radius < sizes.radial)
    weight = jnp.where(at_compact | at_canister, 6.0, 8.0)
    is_temp = lane < field
    at_face = is_temp & (at_compact | at_canister)
    keep_temp = jnp.where(is_temp & in_grid, 1.0, 0.0)
    face_lane = sizes.gap_row - 1 - first

    def turn(value, shift):
        return pltpu.roll(value, shift % LANES, 1)

    dealt = [[dealt_ref[s * members + k] for k in range(members)] for s in range(sections)]

    strip_lane = (lane < 2 * members) | ((lane >= width) & (lane < width + 2 * members))
    odd = (lane % width) % 2 == 1

    def strip_of(values, start):
        strips = []
        for s in range(sections):
            strip = jnp.zeros(shape, jnp.float32)
            for k in range(members):
                moved = pltpu.roll(values[s][k], (start + 2 * k + LANES) % LANES, 1)
                spot = ((lane % width) // 2 == k) & (lane < 2 * width)
                strip = jnp.where(spot, moved, strip)
            strips.append(strip)
        return jnp.concatenate(strips, axis=0)

    total = sections * rows
    meets = jnp.concatenate(
        [
            jnp.where(
                lane == dealt[s][0][:, 2 * field + 1 : 2 * field + 2].astype(jnp.int32), 1.0, 0.0
            )
            for s in range(sections)
        ]
        + [jnp.zeros((LANES - total, LANES), jnp.float32)],
        axis=0,
    )
    met_by = meets.T[:total, :total]
    meets = meets[:total, :total]
    both = jnp.concatenate([meets, met_by], axis=0)

    def pick(table, strip):
        return jnp.dot(
            table, strip, precision=lax.Precision.HIGHEST, preferred_element_type=jnp.float32
        )

    wide_odd = jnp.concatenate([odd] * sections, axis=0)
    gap = strip_of(dealt, 1 - 2 * field)
    gap = jnp.where(wide_odd, gap, turn(pick(met_by, gap), -1))

    def gains(values):
        strip = strip_of(values, LANES - face_lane)
        met = pick(both, strip)
        met = jnp.where(wide_odd, turn(met[:total], 1), turn(met[total:], -1))
        gain = FLUX_STEP * gap * (met - strip)
        return [gain[s * rows : (s + 1) * rows] for s in range(sections)]

    def with_product(value):
        conds = turn(value, -field)
        return jnp.where(lane < 2 * field, value, turn(value * conds, 2 * field))

    def box_sum(values):
        summed = []
        for s in range(sections):
            less = [turn(value, -width) for value in values[s]]
            more = [turn(value, width) for value in values[s]]
            line = []
            for k in range(members):
                low = less[k] + (less[k - 1] if k else 0.0)
                high = more[k] + (more[k + 1] if k < members - 1 else 0.0)
                line.append(values[s][k] + 0.5 * jnp.where(lower_layer, low, high))
            summed.append(line)
        result = []
        up = [[pltpu.roll(value, 1, 0) for value in line] for line in summed]
        down = [[pltpu.roll(value, rows - 1, 0) for value in line] for line in summed]
        for s in range(sections):
            line = []
            for k in range(members):
                before = jnp.where(sub == 0, up[s - 1][k] if s else 0.0, up[s][k])
                after = jnp.where(
                    sub == rows - 1, down[s + 1][k] if s < sections - 1 else 0.0, down[s][k]
                )
                value = summed[s][k] + 0.5 * (before + after)
                inward = jnp.where(at_canister, 0.0, turn(value, 1))
                outward = jnp.where(at_compact, 0.0, turn(value, -1))
                line.append(value + 0.5 * (inward + outward))
            result.append(line)
        return result

    values = dealt
    for sweep in range(SWEEPS):
        gain = gains(values)
        packed = [[with_product(value) for value in line] for line in values]
        sums = box_sum(packed)
        fresh = []
        for s in range(sections):
            line = []
            for k in range(members):
                value = values[s][k]
                total_sum = sums[s][k]
                conds = turn(value, -field)
                change = conds * (total_sum - weight * value)
                change = change + turn(total_sum, -2 * field) - value * turn(total_sum, -field)
                back = pltpu.roll(gain[s], (face_lane - 2 * k + LANES) % LANES, 1)
                temp = value + FLUX_STEP * change + jnp.where(at_face, back, 0.0)
                line.append(jnp.where(is_temp, keep_temp * temp, value))
            fresh.append(line)
        values = fresh

    per_row = 8 // sizes.layers
    for s in range(sections):
        order = dealt[s][0][:, 2 * field + 2 : 2 * field + 3].astype(jnp.int32)
        order = jnp.broadcast_to(order, shape)
        for half in range(sizes.depth // 8):
            merged = jnp.zeros(shape, jnp.float32)
            for k in range(per_row):
                for layer in range(sizes.layers):
                    spot = (k * sizes.layers + layer) * sizes.chunk
                    moved = turn(values[s][half * per_row + k], spot - layer * width - HALO)
                    merged = jnp.where(lane // sizes.chunk == spot // sizes.chunk, moved, merged)
            chosen = jnp.take_along_axis(merged, order, axis=0)
            start = s * rows * (sizes.depth // 8) + half
            out_ref[pl.ds(start, rows, stride=sizes.depth // 8), :] = chosen


def swap_blocks(tile, block):
    sub = iota(tile.shape, 0)
    spot = iota(tile.shape, 1) // block
    for bit in (4, 2, 1):
        up = pltpu.roll(pltpu.roll(tile, 8 - bit, 0), bit * block, 1)
        down = pltpu.roll(pltpu.roll(tile, bit, 0), LANES - bit * block, 1)
        moved = jnp.where(sub & bit == 0, up, down)
        tile = jnp.where((sub & bit) == (spot & bit), tile, moved)
    return tile


def creep_kernel(sizes, active_ref, temps_ref, trial_ref, stress_ref, strain_ref):
    tiles = sizes.tiles
    halves = sizes.depth // 8
    active = active_ref[0, 0]
    for tile in range(tiles):
        for element in range(halves):
            source = pl.ds(tile * 8 * halves + element, 8, stride=halves)
            mech_temp = swap_blocks(temps_ref[source, :], sizes.chunk)
            spot = pl.ds(element * 8 * tiles + tile, 8, stride=tiles)
            trial = trial_ref[spot, :]
            rate = CREEP_RATE * jnp.exp(-ACTIVATION / (mech_temp + REFERENCE_TEMP))
            slip = jnp.zeros(trial.shape, jnp.float32)
            for newton_step in range(NEWTON):
                left = trial - slip
                pull = rate * left * left
                slip = slip - (slip - pull * left) / (1.0 + 3.0 * pull)
            live = jnp.where(element < active, 1.0, 0.0).astype(jnp.float32)
            creep = live * slip
            stress_ref[spot, :] = trial - creep
            strain_ref[pl.ds(element * tiles + tile, 1), :] = 0.125 * jnp.sum(
                creep, axis=0, keepdims=True
            )


def kernel_call(body, sizes, out_shape, memories, scratch, operands):
    out_spec = pl.BlockSpec(memory_space=pltpu.VMEM)
    return pl.pallas_call(
        functools.partial(body, sizes),
        out_shape=out_shape,
        in_specs=[pl.BlockSpec(memory_space=memory) for memory in memories],
        out_specs=jax.tree.map(lambda _: out_spec, out_shape),
        scratch_shapes=scratch,
        compiler_params=pltpu.CompilerParams(vmem_limit_bytes=16 * 1024 * 1024),
    )(*operands)


def on_device(
    temp_start, conductivity, gap_conductance, partner, row_order, active_layers, trial_stress
):
    layers, _, rows, radial = temp_start.shape
    sizes = Sizes(layers, rows, radial)
    if not fits_tiles(sizes):
        return stepwise(
            temp_start,
            conductivity,
            gap_conductance,
            partner,
            row_order,
            active_layers,
            trial_stress,
        )

    def floats(*shape):
        return jax.ShapeDtypeStruct(shape, jnp.float32)

    dealt = kernel_call(
        deal_kernel,
        sizes,
        floats(sizes.devices, rows, LANES),
        [pltpu.HBM] * 5,
        [
            pltpu.SMEM(partner.shape, jnp.int32),
            pltpu.SMEM(row_order.shape, jnp.int32),
            pltpu.SMEM(gap_conductance.shape, jnp.float32),
            pltpu.VMEM(temp_start.shape, jnp.float32),
            pltpu.VMEM(conductivity.shape, jnp.float32),
            pltpu.SemaphoreType.DMA((5,)),
        ],
        (partner, row_order, gap_conductance, temp_start, conductivity),
    )
    dealt = lax.all_to_all(dealt, EVERYONE, split_axis=0, concat_axis=0, tiled=True)
    halves = sizes.depth // 8
    temps = kernel_call(
        sweep_kernel,
        sizes,
        floats(sizes.devices * halves, LANES),
        [pltpu.VMEM],
        [],
        (dealt,),
    )
    temps = temps.reshape(sizes.devices, halves, LANES)
    temps = lax.all_to_all(temps, EVERYONE, split_axis=0, concat_axis=0, tiled=True)
    stress, strain = kernel_call(
        creep_kernel,
        sizes,
        (floats(sizes.depth * sizes.tiles, LANES), floats(halves * sizes.tiles, LANES)),
        [pltpu.SMEM, pltpu.VMEM, pltpu.VMEM],
        [],
        (
            active_layers,
            temps.reshape(sizes.devices * halves, LANES),
            trial_stress.reshape(sizes.depth * sizes.tiles, LANES),
        ),
    )
    return (
        stress.reshape(sizes.depth, 1, 1, radial),
        strain.reshape(halves, 1, 1, radial),
    )


def solution(mesh):
    placed = (
        P(("slab", "mech"), "iface", None, None),
        P(("slab", "mech"), "iface", None, None),
        P(("slab", "mech"), "iface", None),
        P("iface"),
        P("iface", None),
        P("iface", ("slab", "mech")),
        P(None, "iface", ("slab", "mech"), None),
    )
    return jax.shard_map(
        on_device,
        mesh=mesh,
        in_specs=placed,
        out_specs=(
            P(None, "iface", ("slab", "mech"), None),
            P(None, "iface", ("slab", "mech"), None),
        ),
        check_vma=False,
    )
```

```python
import functools
import jax
import jax.numpy as jnp
from jax import lax
from jax.experimental import pallas as pl
from jax.experimental.pallas import tpu as pltpu
from jax.sharding import PartitionSpec as P

SWEEPS = 2
NEWTON = 4


FLUX_STEP = 0.03
CREEP_RATE = 200.0
ACTIVATION = 12.0
REFERENCE_TEMP = 1.0


def padded(block, sides, width):
    for axis, dim in sides:
        count = lax.axis_size(axis)
        forward = [(i, i + 1) for i in range(count - 1)]
        backward = [(target, source) for source, target in forward]
        low = lax.ppermute(
            lax.slice_in_dim(block, block.shape[dim] - width, None, axis=dim), axis, forward
        )
        high = lax.ppermute(lax.slice_in_dim(block, 0, width, axis=dim), axis, backward)
        block = jnp.concatenate([low, block, high], axis=dim)
    return block


def neighbour_weight(shift_z, shift_a, shift_r):
    reach = abs(shift_z) + abs(shift_a) + abs(shift_r)
    return [0.0, 1.0, 0.5, 0.25][reach]


def conduction(padded_temp, padded_cond):
    center_temp = padded_temp[1:-1, 1:-1, 1:-1]
    center_cond = padded_cond[1:-1, 1:-1, 1:-1]
    depth, across, radial = center_temp.shape
    radial_index = jnp.arange(radial, dtype=jnp.int32)
    gap_row = radial // 2
    outward_open = (radial_index != gap_row - 1).astype(jnp.float32)
    inward_open = (radial_index != gap_row).astype(jnp.float32)
    total = jnp.zeros(center_temp.shape, jnp.float32)
    for shift_z in (-1, 0, 1):
        for shift_a in (-1, 0, 1):
            for shift_r in (-1, 0, 1):
                if shift_z == 0 and shift_a == 0 and (shift_r == 0):
                    continue
                near_temp = padded_temp[
                    1 + shift_z : 1 + shift_z + depth,
                    1 + shift_a : 1 + shift_a + across,
                    1 + shift_r : 1 + shift_r + radial,
                ]
                near_cond = padded_cond[
                    1 + shift_z : 1 + shift_z + depth,
                    1 + shift_a : 1 + shift_a + across,
                    1 + shift_r : 1 + shift_r + radial,
                ]
                face = neighbour_weight(shift_z, shift_a, shift_r) * 0.5 * (center_cond + near_cond)
                if shift_r == 1:
                    face = face * outward_open
                elif shift_r == -1:
                    face = face * inward_open
                total = total + face * (near_temp - center_temp)
    return FLUX_STEP * total


def creep_return(mech_temp, trial, active_layers):
    rate = CREEP_RATE * jnp.exp(-ACTIVATION / (mech_temp + REFERENCE_TEMP))
    slip = jnp.zeros(trial.shape, jnp.float32)
    for newton_step in range(NEWTON):
        left = trial - slip
        residue = slip - rate * left**3
        slope = 1.0 + 3.0 * rate * left**2
        slip = slip - residue / slope
    depth = trial.shape[0]
    layer = jnp.arange(depth, dtype=jnp.int32) // 8
    live = (layer[:, None, None] < active_layers[None, :, :]).astype(jnp.float32)[..., None]
    creep = live * slip
    stress = trial - creep
    strain = jnp.sum(creep.reshape((depth // 8, 8) + trial.shape[1:]), axis=1) * 0.125
    return (stress, strain)


def stepwise(
    temp_start, conductivity, gap_conductance, partner, row_order, active_layers, trial_stress
):
    depth = temp_start.shape[0]
    rows = temp_start.shape[2]
    radial = temp_start.shape[3]
    temp = temp_start.reshape(depth, rows, radial)
    cond = conductivity.reshape(depth, rows, radial)
    gap = gap_conductance.reshape(depth, rows)
    gap_row = radial // 2
    sections = lax.axis_size("iface")
    across = rows * sections
    all_cols = jnp.arange(across, dtype=jnp.int32)
    cond_rim = padded(cond, ((("slab", "mech"), 0), ("iface", 1)), 1)
    padded_cond = jnp.pad(cond_rim, ((0, 0), (0, 0), (1, 1)))
    spread_table = (partner[:, None] == all_cols[None, :]).astype(jnp.float32)
    for sweep in range(SWEEPS):
        temp_rim = padded(temp, ((("slab", "mech"), 0), ("iface", 1)), 1)
        padded_temp = jnp.pad(temp_rim, ((0, 0), (0, 0), (1, 1)))
        compact = temp[:, :, gap_row - 1]
        canister = temp[:, :, gap_row]
        compact_all = lax.all_gather(compact, "iface", axis=1, tiled=True)
        facing = jnp.take(compact_all, partner, axis=1)
        flux = gap * (facing - canister)
        spread = jnp.dot(
            flux, spread_table, precision=lax.Precision.HIGHEST, preferred_element_type=jnp.float32
        )
        returned = lax.psum_scatter(spread, "iface", scatter_dimension=1, tiled=True)
        fresh = temp + conduction(padded_temp, padded_cond)
        temp = (
            fresh.at[:, :, gap_row]
            .add(FLUX_STEP * flux)
            .at[:, :, gap_row - 1]
            .add(-FLUX_STEP * returned)
        )
    permuted = jnp.take(temp, row_order[0], axis=1)
    mech_temp = lax.all_to_all(permuted, ("slab", "mech"), split_axis=1, concat_axis=0, tiled=True)
    mech_temp = mech_temp.reshape(mech_temp.shape[0], 1, mech_temp.shape[1], radial)
    return creep_return(mech_temp, trial_stress, active_layers)


LANES = 128
HALO = 2
EVERYONE = ("iface", "slab", "mech")


def iota(shape, axis):
    return lax.broadcasted_iota(jnp.int32, shape, axis)


class Sizes:
    def __init__(self, layers, rows, radial):
        self.layers = layers
        self.rows = rows
        self.radial = radial
        self.tiles = radial // LANES
        self.sections = lax.axis_size("iface")
        self.members = lax.axis_size("slab") * lax.axis_size("mech")
        self.devices = self.sections * self.members
        self.depth = layers * self.members
        self.chunk = radial // self.devices
        self.width = self.chunk + 2 * HALO
        self.field = layers * self.width
        self.gap_row = radial // 2


def fits_tiles(sizes):
    return (
        sizes.rows == 8
        and sizes.members == sizes.rows
        and sizes.layers == 2
        and sizes.sections * sizes.rows <= LANES
        and sizes.radial % sizes.devices == 0
        and sizes.chunk * 8 == LANES
        and sizes.radial % (2 * LANES) == 0
    )


def deal_kernel(
    sizes,
    partner_hbm,
    order_hbm,
    gap_hbm,
    temp_hbm,
    cond_hbm,
    out_ref,
    partner_ref,
    order_ref,
    gap_ref,
    temp_ref,
    cond_ref,
    sems,
):
    pairs = (
        (temp_hbm, temp_ref),
        (cond_hbm, cond_ref),
        (gap_hbm, gap_ref),
        (partner_hbm, partner_ref),
        (order_hbm, order_ref),
    )
    copies = [
        pltpu.make_async_copy(source, target, sems.at[index])
        for index, (source, target) in enumerate(pairs)
    ]
    for copy in copies:
        copy.start()
    for copy in copies:
        copy.wait()
    shape = (sizes.rows, LANES)
    lane = iota(shape, 1)
    sub = iota(shape, 0)
    extra_at = 2 * sizes.field
    extra = jnp.zeros(shape, jnp.float32)
    for row in range(sizes.rows):
        for layer in range(sizes.layers):
            spot = (sub == row) & (lane == extra_at + layer * sizes.width)
            extra = jnp.where(spot, gap_ref[layer, 0, row], extra)
        spot = (sub == row) & (lane == extra_at + 1)
        extra = jnp.where(spot, partner_ref[row].astype(jnp.float32), extra)
        spot = (sub == row) & (lane == extra_at + 2)
        extra = jnp.where(spot, order_ref[0, row].astype(jnp.float32), extra)
    blocks = [
        [ref[layer, 0, :, pl.ds(tile * LANES, LANES)] for tile in range(sizes.tiles)]
        for ref in (temp_ref, cond_ref)
        for layer in range(sizes.layers)
    ]
    for device in range(sizes.devices):
        first = device * sizes.chunk - HALO
        packed = extra
        for index, block in enumerate(blocks):
            base = index * sizes.width
            for tile in range(sizes.tiles):
                low = max(first, tile * LANES)
                high = min(first + sizes.width, (tile + 1) * LANES)
                if low >= high:
                    continue
                moved = pltpu.roll(block[tile], (base - first + tile * LANES) % LANES, 1)
                spot = (lane >= base + low - first) & (lane < base + high - first)
                packed = jnp.where(spot, moved, packed)
        out_ref[device] = packed


def sweep_kernel(sizes, dealt_ref, out_ref):
    rows, width, field = sizes.rows, sizes.width, sizes.field
    sections, members = sizes.sections, sizes.members
    shape = (rows, LANES)
    lane = iota(shape, 1)
    sub = iota(shape, 0)
    place = lax.axis_index("iface") * members
    place = place + lax.axis_index("slab") * lax.axis_size("mech") + lax.axis_index("mech")
    first = place * sizes.chunk - HALO
    segment = lane // width
    radius = first + lane % width
    lower_layer = segment % 2 == 0
    at_compact = radius == sizes.gap_row - 1
    at_canister = radius == sizes.gap_row
    in_grid = (radius >= 0) & (radius < sizes.radial)
    weight = jnp.where(at_compact | at_canister, 6.0, 8.0)
    is_temp = lane < field
    at_face = is_temp & (at_compact | at_canister)
    keep_temp = jnp.where(is_temp & in_grid, 1.0, 0.0)
    face_lane = sizes.gap_row - 1 - first

    def turn(value, shift):
        return pltpu.roll(value, shift % LANES, 1)

    dealt = [[dealt_ref[s * members + k] for k in range(members)] for s in range(sections)]

    strip_lane = (lane < 2 * members) | ((lane >= width) & (lane < width + 2 * members))
    odd = (lane % width) % 2 == 1

    def strip_of(values, start):
        strips = []
        for s in range(sections):
            strip = jnp.zeros(shape, jnp.float32)
            for k in range(members):
                moved = pltpu.roll(values[s][k], (start + 2 * k + LANES) % LANES, 1)
                spot = ((lane % width) // 2 == k) & (lane < 2 * width)
                strip = jnp.where(spot, moved, strip)
            strips.append(strip)
        return jnp.concatenate(strips, axis=0)

    total = sections * rows
    meets = jnp.concatenate(
        [
            jnp.where(
                lane == dealt[s][0][:, 2 * field + 1 : 2 * field + 2].astype(jnp.int32), 1.0, 0.0
            )
            for s in range(sections)
        ]
        + [jnp.zeros((LANES - total, LANES), jnp.float32)],
        axis=0,
    )
    met_by = meets.T[:total, :total]
    meets = meets[:total, :total]
    both = jnp.concatenate([meets, met_by], axis=0)

    def pick(table, strip):
        return jnp.dot(
            table, strip, precision=lax.Precision.HIGHEST, preferred_element_type=jnp.float32
        )

    wide_odd = jnp.concatenate([odd] * sections, axis=0)
    gap = strip_of(dealt, 1 - 2 * field)
    gap = jnp.where(wide_odd, gap, turn(pick(met_by, gap), -1))

    def gains(values):
        strip = strip_of(values, LANES - face_lane)
        met = pick(both, strip)
        met = jnp.where(wide_odd, turn(met[:total], 1), turn(met[total:], -1))
        gain = FLUX_STEP * gap * (met - strip)
        return [gain[s * rows : (s + 1) * rows] for s in range(sections)]

    def with_product(value):
        conds = turn(value, -field)
        return jnp.where(lane < 2 * field, value, turn(value * conds, 2 * field))

    def box_sum(values):
        summed = []
        for s in range(sections):
            less = [turn(value, -width) for value in values[s]]
            more = [turn(value, width) for value in values[s]]
            line = []
            for k in range(members):
                low = less[k] + (less[k - 1] if k else 0.0)
                high = more[k] + (more[k + 1] if k < members - 1 else 0.0)
                line.append(values[s][k] + 0.5 * jnp.where(lower_layer, low, high))
            summed.append(line)
        result = []
        up = [[pltpu.roll(value, 1, 0) for value in line] for line in summed]
        down = [[pltpu.roll(value, rows - 1, 0) for value in line] for line in summed]
        for s in range(sections):
            line = []
            for k in range(members):
                before = jnp.where(sub == 0, up[s - 1][k] if s else 0.0, up[s][k])
                after = jnp.where(
                    sub == rows - 1, down[s + 1][k] if s < sections - 1 else 0.0, down[s][k]
                )
                value = summed[s][k] + 0.5 * (before + after)
                inward = jnp.where(at_canister, 0.0, turn(value, 1))
                outward = jnp.where(at_compact, 0.0, turn(value, -1))
                line.append(value + 0.5 * (inward + outward))
            result.append(line)
        return result

    values = dealt
    for sweep in range(SWEEPS):
        gain = gains(values)
        packed = [[with_product(value) for value in line] for line in values]
        sums = box_sum(packed)
        fresh = []
        for s in range(sections):
            line = []
            for k in range(members):
                value = values[s][k]
                total_sum = sums[s][k]
                conds = turn(value, -field)
                change = conds * (total_sum - weight * value)
                change = change + turn(total_sum, -2 * field) - value * turn(total_sum, -field)
                back = pltpu.roll(gain[s], (face_lane - 2 * k + LANES) % LANES, 1)
                temp = value + FLUX_STEP * change + jnp.where(at_face, back, 0.0)
                line.append(jnp.where(is_temp, keep_temp * temp, value))
            fresh.append(line)
        values = fresh

    per_row = 8 // sizes.layers
    for s in range(sections):
        order = dealt[s][0][:, 2 * field + 2 : 2 * field + 3].astype(jnp.int32)
        order = jnp.broadcast_to(order, shape)
        for half in range(sizes.depth // 8):
            merged = jnp.zeros(shape, jnp.float32)
            for k in range(per_row):
                for layer in range(sizes.layers):
                    spot = (k * sizes.layers + layer) * sizes.chunk
                    moved = turn(values[s][half * per_row + k], spot - layer * width - HALO)
                    merged = jnp.where(lane // sizes.chunk == spot // sizes.chunk, moved, merged)
            chosen = jnp.take_along_axis(merged, order, axis=0)
            start = s * rows * (sizes.depth // 8) + half
            out_ref[pl.ds(start, rows, stride=sizes.depth // 8), :] = chosen


def swap_blocks(tile, block):
    sub = iota(tile.shape, 0)
    spot = iota(tile.shape, 1) // block
    for bit in (4, 2, 1):
        up = pltpu.roll(pltpu.roll(tile, 8 - bit, 0), bit * block, 1)
        down = pltpu.roll(pltpu.roll(tile, bit, 0), LANES - bit * block, 1)
        moved = jnp.where(sub & bit == 0, up, down)
        tile = jnp.where((sub & bit) == (spot & bit), tile, moved)
    return tile


def creep_kernel(sizes, active_ref, temps_ref, trial_ref, stress_ref, strain_ref):
    tiles = sizes.tiles
    halves = sizes.depth // 8
    active = active_ref[0, 0]
    for tile in range(tiles):
        for element in range(halves):
            source = pl.ds(tile * 8 * halves + element, 8, stride=halves)
            mech_temp = swap_blocks(temps_ref[source, :], sizes.chunk)
            spot = pl.ds(element * 8 * tiles + tile, 8, stride=tiles)
            trial = trial_ref[spot, :]
            rate = CREEP_RATE * jnp.exp(-ACTIVATION / (mech_temp + REFERENCE_TEMP))
            slip = jnp.zeros(trial.shape, jnp.float32)
            for newton_step in range(NEWTON):
                left = trial - slip
                pull = rate * left * left
                slip = slip - (slip - pull * left) / (1.0 + 3.0 * pull)
            live = jnp.where(element < active, 1.0, 0.0).astype(jnp.float32)
            creep = live * slip
            stress_ref[spot, :] = trial - creep
            strain_ref[pl.ds(element * tiles + tile, 1), :] = 0.125 * jnp.sum(
                creep, axis=0, keepdims=True
            )


def kernel_call(body, sizes, out_shape, memories, scratch, operands, grant=16 * 1024 * 1024):
    out_spec = pl.BlockSpec(memory_space=pltpu.VMEM)
    return pl.pallas_call(
        functools.partial(body, sizes),
        out_shape=out_shape,
        in_specs=[pl.BlockSpec(memory_space=memory) for memory in memories],
        out_specs=jax.tree.map(lambda _: out_spec, out_shape),
        scratch_shapes=scratch,
        compiler_params=pltpu.CompilerParams(vmem_limit_bytes=grant),
    )(*operands)


def on_device(
    temp_start, conductivity, gap_conductance, partner, row_order, active_layers, trial_stress
):
    layers, _, rows, radial = temp_start.shape
    sizes = Sizes(layers, rows, radial)
    if not fits_tiles(sizes):
        return stepwise(
            temp_start,
            conductivity,
            gap_conductance,
            partner,
            row_order,
            active_layers,
            trial_stress,
        )

    def floats(*shape):
        return jax.ShapeDtypeStruct(shape, jnp.float32)

    dealt = kernel_call(
        deal_kernel,
        sizes,
        floats(sizes.devices, rows, LANES),
        [pltpu.HBM] * 5,
        [
            pltpu.SMEM(partner.shape, jnp.int32),
            pltpu.SMEM(row_order.shape, jnp.int32),
            pltpu.SMEM(gap_conductance.shape, jnp.float32),
            pltpu.VMEM(temp_start.shape, jnp.float32),
            pltpu.VMEM(conductivity.shape, jnp.float32),
            pltpu.SemaphoreType.DMA((5,)),
        ],
        (partner, row_order, gap_conductance, temp_start, conductivity),
        grant=60 * 1024 * 1024,
    )
    dealt = lax.all_to_all(dealt, EVERYONE, split_axis=0, concat_axis=0, tiled=True)
    halves = sizes.depth // 8
    temps = kernel_call(
        sweep_kernel,
        sizes,
        floats(sizes.devices * halves, LANES),
        [pltpu.VMEM],
        [],
        (dealt,),
    )
    temps = temps.reshape(sizes.devices, halves, LANES)
    temps = lax.all_to_all(temps, EVERYONE, split_axis=0, concat_axis=0, tiled=True)
    stress, strain = kernel_call(
        creep_kernel,
        sizes,
        (floats(sizes.depth * sizes.tiles, LANES), floats(halves * sizes.tiles, LANES)),
        [pltpu.SMEM, pltpu.VMEM, pltpu.VMEM],
        [],
        (
            active_layers,
            temps.reshape(sizes.devices * halves, LANES),
            trial_stress.reshape(sizes.depth * sizes.tiles, LANES),
        ),
    )
    return (
        stress.reshape(sizes.depth, 1, 1, radial),
        strain.reshape(halves, 1, 1, radial),
    )


def solution(mesh):
    placed = (
        P(("slab", "mech"), "iface", None, None),
        P(("slab", "mech"), "iface", None, None),
        P(("slab", "mech"), "iface", None),
        P("iface"),
        P("iface", None),
        P("iface", ("slab", "mech")),
        P(None, "iface", ("slab", "mech"), None),
    )
    return jax.shard_map(
        on_device,
        mesh=mesh,
        in_specs=placed,
        out_specs=(
            P(None, "iface", ("slab", "mech"), None),
            P(None, "iface", ("slab", "mech"), None),
        ),
        check_vma=False,
    )
```

```python
import functools
import jax
import jax.numpy as jnp
from jax import lax
from jax.experimental import pallas as pl
from jax.experimental.pallas import tpu as pltpu
from jax.sharding import PartitionSpec as P

SWEEPS = 2
NEWTON = 4


FLUX_STEP = 0.03
CREEP_RATE = 200.0
ACTIVATION = 12.0
REFERENCE_TEMP = 1.0


def padded(block, sides, width):
    for axis, dim in sides:
        count = lax.axis_size(axis)
        forward = [(i, i + 1) for i in range(count - 1)]
        backward = [(target, source) for source, target in forward]
        low = lax.ppermute(
            lax.slice_in_dim(block, block.shape[dim] - width, None, axis=dim), axis, forward
        )
        high = lax.ppermute(lax.slice_in_dim(block, 0, width, axis=dim), axis, backward)
        block = jnp.concatenate([low, block, high], axis=dim)
    return block


def neighbour_weight(shift_z, shift_a, shift_r):
    reach = abs(shift_z) + abs(shift_a) + abs(shift_r)
    return [0.0, 1.0, 0.5, 0.25][reach]


def conduction(padded_temp, padded_cond):
    center_temp = padded_temp[1:-1, 1:-1, 1:-1]
    center_cond = padded_cond[1:-1, 1:-1, 1:-1]
    depth, across, radial = center_temp.shape
    radial_index = jnp.arange(radial, dtype=jnp.int32)
    gap_row = radial // 2
    outward_open = (radial_index != gap_row - 1).astype(jnp.float32)
    inward_open = (radial_index != gap_row).astype(jnp.float32)
    total = jnp.zeros(center_temp.shape, jnp.float32)
    for shift_z in (-1, 0, 1):
        for shift_a in (-1, 0, 1):
            for shift_r in (-1, 0, 1):
                if shift_z == 0 and shift_a == 0 and (shift_r == 0):
                    continue
                near_temp = padded_temp[
                    1 + shift_z : 1 + shift_z + depth,
                    1 + shift_a : 1 + shift_a + across,
                    1 + shift_r : 1 + shift_r + radial,
                ]
                near_cond = padded_cond[
                    1 + shift_z : 1 + shift_z + depth,
                    1 + shift_a : 1 + shift_a + across,
                    1 + shift_r : 1 + shift_r + radial,
                ]
                face = neighbour_weight(shift_z, shift_a, shift_r) * 0.5 * (center_cond + near_cond)
                if shift_r == 1:
                    face = face * outward_open
                elif shift_r == -1:
                    face = face * inward_open
                total = total + face * (near_temp - center_temp)
    return FLUX_STEP * total


def creep_return(mech_temp, trial, active_layers):
    rate = CREEP_RATE * jnp.exp(-ACTIVATION / (mech_temp + REFERENCE_TEMP))
    slip = jnp.zeros(trial.shape, jnp.float32)
    for newton_step in range(NEWTON):
        left = trial - slip
        residue = slip - rate * left**3
        slope = 1.0 + 3.0 * rate * left**2
        slip = slip - residue / slope
    depth = trial.shape[0]
    layer = jnp.arange(depth, dtype=jnp.int32) // 8
    live = (layer[:, None, None] < active_layers[None, :, :]).astype(jnp.float32)[..., None]
    creep = live * slip
    stress = trial - creep
    strain = jnp.sum(creep.reshape((depth // 8, 8) + trial.shape[1:]), axis=1) * 0.125
    return (stress, strain)


def stepwise(
    temp_start, conductivity, gap_conductance, partner, row_order, active_layers, trial_stress
):
    depth = temp_start.shape[0]
    rows = temp_start.shape[2]
    radial = temp_start.shape[3]
    temp = temp_start.reshape(depth, rows, radial)
    cond = conductivity.reshape(depth, rows, radial)
    gap = gap_conductance.reshape(depth, rows)
    gap_row = radial // 2
    sections = lax.axis_size("iface")
    across = rows * sections
    all_cols = jnp.arange(across, dtype=jnp.int32)
    cond_rim = padded(cond, ((("slab", "mech"), 0), ("iface", 1)), 1)
    padded_cond = jnp.pad(cond_rim, ((0, 0), (0, 0), (1, 1)))
    spread_table = (partner[:, None] == all_cols[None, :]).astype(jnp.float32)
    for sweep in range(SWEEPS):
        temp_rim = padded(temp, ((("slab", "mech"), 0), ("iface", 1)), 1)
        padded_temp = jnp.pad(temp_rim, ((0, 0), (0, 0), (1, 1)))
        compact = temp[:, :, gap_row - 1]
        canister = temp[:, :, gap_row]
        compact_all = lax.all_gather(compact, "iface", axis=1, tiled=True)
        facing = jnp.take(compact_all, partner, axis=1)
        flux = gap * (facing - canister)
        spread = jnp.dot(
            flux, spread_table, precision=lax.Precision.HIGHEST, preferred_element_type=jnp.float32
        )
        returned = lax.psum_scatter(spread, "iface", scatter_dimension=1, tiled=True)
        fresh = temp + conduction(padded_temp, padded_cond)
        temp = (
            fresh.at[:, :, gap_row]
            .add(FLUX_STEP * flux)
            .at[:, :, gap_row - 1]
            .add(-FLUX_STEP * returned)
        )
    permuted = jnp.take(temp, row_order[0], axis=1)
    mech_temp = lax.all_to_all(permuted, ("slab", "mech"), split_axis=1, concat_axis=0, tiled=True)
    mech_temp = mech_temp.reshape(mech_temp.shape[0], 1, mech_temp.shape[1], radial)
    return creep_return(mech_temp, trial_stress, active_layers)


LANES = 128
HALO = 2
EVERYONE = ("iface", "slab", "mech")


def iota(shape, axis):
    return lax.broadcasted_iota(jnp.int32, shape, axis)


class Sizes:
    def __init__(self, layers, rows, radial):
        self.layers = layers
        self.rows = rows
        self.radial = radial
        self.tiles = radial // LANES
        self.sections = lax.axis_size("iface")
        self.members = lax.axis_size("slab") * lax.axis_size("mech")
        self.devices = self.sections * self.members
        self.depth = layers * self.members
        self.chunk = radial // self.devices
        self.width = self.chunk + 2 * HALO
        self.field = layers * self.width
        self.gap_row = radial // 2


def fits_tiles(sizes):
    return (
        sizes.rows == 8
        and sizes.members == sizes.rows
        and sizes.layers == 2
        and sizes.sections * sizes.rows <= LANES
        and sizes.radial % sizes.devices == 0
        and sizes.chunk * 8 == LANES
        and sizes.radial % (2 * LANES) == 0
    )


def deal_kernel(
    sizes,
    partner_hbm,
    order_hbm,
    gap_hbm,
    temp_hbm,
    cond_hbm,
    out_ref,
    partner_ref,
    order_ref,
    gap_ref,
    temp_ref,
    cond_ref,
    sems,
):
    pairs = (
        (gap_hbm, gap_ref),
        (partner_hbm, partner_ref),
        (order_hbm, order_ref),
        (temp_hbm, temp_ref),
        (cond_hbm, cond_ref),
    )
    copies = [
        pltpu.make_async_copy(source, target, sems.at[index])
        for index, (source, target) in enumerate(pairs)
    ]
    for copy in copies:
        copy.start()
    for copy in copies[:3]:
        copy.wait()
    shape = (sizes.rows, LANES)
    lane = iota(shape, 1)
    sub = iota(shape, 0)
    extra_at = 2 * sizes.field
    extra = jnp.zeros(shape, jnp.float32)
    for row in range(sizes.rows):
        for layer in range(sizes.layers):
            spot = (sub == row) & (lane == extra_at + layer * sizes.width)
            extra = jnp.where(spot, gap_ref[layer, 0, row], extra)
        spot = (sub == row) & (lane == extra_at + 1)
        extra = jnp.where(spot, partner_ref[row].astype(jnp.float32), extra)
        spot = (sub == row) & (lane == extra_at + 2)
        extra = jnp.where(spot, order_ref[0, row].astype(jnp.float32), extra)
    for copy in copies[3:]:
        copy.wait()
    blocks = [
        [ref[layer, 0, :, pl.ds(tile * LANES, LANES)] for tile in range(sizes.tiles)]
        for ref in (temp_ref, cond_ref)
        for layer in range(sizes.layers)
    ]
    for device in range(sizes.devices):
        first = device * sizes.chunk - HALO
        packed = extra
        for index, block in enumerate(blocks):
            base = index * sizes.width
            for tile in range(sizes.tiles):
                low = max(first, tile * LANES)
                high = min(first + sizes.width, (tile + 1) * LANES)
                if low >= high:
                    continue
                moved = pltpu.roll(block[tile], (base - first + tile * LANES) % LANES, 1)
                spot = (lane >= base + low - first) & (lane < base + high - first)
                packed = jnp.where(spot, moved, packed)
        out_ref[device] = packed


def sweep_kernel(sizes, dealt_ref, out_ref):
    rows, width, field = sizes.rows, sizes.width, sizes.field
    sections, members = sizes.sections, sizes.members
    shape = (rows, LANES)
    lane = iota(shape, 1)
    sub = iota(shape, 0)
    place = lax.axis_index("iface") * members
    place = place + lax.axis_index("slab") * lax.axis_size("mech") + lax.axis_index("mech")
    first = place * sizes.chunk - HALO
    segment = lane // width
    radius = first + lane % width
    lower_layer = segment % 2 == 0
    at_compact = radius == sizes.gap_row - 1
    at_canister = radius == sizes.gap_row
    in_grid = (radius >= 0) & (radius < sizes.radial)
    weight = jnp.where(at_compact | at_canister, 6.0, 8.0)
    is_temp = lane < field
    at_face = is_temp & (at_compact | at_canister)
    keep_temp = jnp.where(is_temp & in_grid, 1.0, 0.0)
    face_lane = sizes.gap_row - 1 - first

    def turn(value, shift):
        return pltpu.roll(value, shift % LANES, 1)

    dealt = [[dealt_ref[s * members + k] for k in range(members)] for s in range(sections)]

    strip_lane = (lane < 2 * members) | ((lane >= width) & (lane < width + 2 * members))
    odd = (lane % width) % 2 == 1

    def strip_of(values, start):
        strips = []
        for s in range(sections):
            strip = jnp.zeros(shape, jnp.float32)
            for k in range(members):
                moved = pltpu.roll(values[s][k], (start + 2 * k + LANES) % LANES, 1)
                spot = ((lane % width) // 2 == k) & (lane < 2 * width)
                strip = jnp.where(spot, moved, strip)
            strips.append(strip)
        return jnp.concatenate(strips, axis=0)

    total = sections * rows
    meets = jnp.concatenate(
        [
            jnp.where(
                lane == dealt[s][0][:, 2 * field + 1 : 2 * field + 2].astype(jnp.int32), 1.0, 0.0
            )
            for s in range(sections)
        ]
        + [jnp.zeros((LANES - total, LANES), jnp.float32)],
        axis=0,
    )
    met_by = meets.T[:total, :total]
    meets = meets[:total, :total]
    both = jnp.concatenate([meets, met_by], axis=0)

    def pick(table, strip):
        return jnp.dot(
            table, strip, precision=lax.Precision.HIGHEST, preferred_element_type=jnp.float32
        )

    wide_odd = jnp.concatenate([odd] * sections, axis=0)
    gap = strip_of(dealt, 1 - 2 * field)
    gap = jnp.where(wide_odd, gap, turn(pick(met_by, gap), -1))

    def gains(values):
        strip = strip_of(values, LANES - face_lane)
        met = pick(both, strip)
        met = jnp.where(wide_odd, turn(met[:total], 1), turn(met[total:], -1))
        gain = FLUX_STEP * gap * (met - strip)
        return [gain[s * rows : (s + 1) * rows] for s in range(sections)]

    conds = [[turn(value, -field) for value in line] for line in dealt]

    def with_product(value, cond):
        return jnp.where(lane < 2 * field, value, turn(value * cond, 2 * field))

    def box_sum(values):
        summed = []
        for s in range(sections):
            less = [turn(value, -width) for value in values[s]]
            more = [turn(value, width) for value in values[s]]
            line = []
            for k in range(members):
                low = less[k] + (less[k - 1] if k else 0.0)
                high = more[k] + (more[k + 1] if k < members - 1 else 0.0)
                line.append(values[s][k] + 0.5 * jnp.where(lower_layer, low, high))
            summed.append(line)
        result = []
        up = [[pltpu.roll(value, 1, 0) for value in line] for line in summed]
        down = [[pltpu.roll(value, rows - 1, 0) for value in line] for line in summed]
        for s in range(sections):
            line = []
            for k in range(members):
                before = jnp.where(sub == 0, up[s - 1][k] if s else 0.0, up[s][k])
                after = jnp.where(
                    sub == rows - 1, down[s + 1][k] if s < sections - 1 else 0.0, down[s][k]
                )
                value = summed[s][k] + 0.5 * (before + after)
                inward = jnp.where(at_canister, 0.0, turn(value, 1))
                outward = jnp.where(at_compact, 0.0, turn(value, -1))
                line.append(value + 0.5 * (inward + outward))
            result.append(line)
        return result

    values = dealt
    cond_sums = None
    for sweep in range(SWEEPS):
        gain = gains(values)
        packed = [
            [with_product(value, cond) for value, cond in zip(*lines)]
            for lines in zip(values, conds)
        ]
        sums = box_sum(packed)
        if cond_sums is None:
            cond_sums = [[turn(total_sum, -field) for total_sum in line] for line in sums]
        fresh = []
        for s in range(sections):
            line = []
            for k in range(members):
                value = values[s][k]
                total_sum = sums[s][k]
                change = conds[s][k] * (total_sum - weight * value)
                change = change + turn(total_sum, -2 * field) - value * cond_sums[s][k]
                back = pltpu.roll(gain[s], (face_lane - 2 * k + LANES) % LANES, 1)
                temp = value + FLUX_STEP * change + jnp.where(at_face, back, 0.0)
                line.append(jnp.where(is_temp, keep_temp * temp, value))
            fresh.append(line)
        values = fresh

    per_row = 8 // sizes.layers
    for s in range(sections):
        order = dealt[s][0][:, 2 * field + 2 : 2 * field + 3].astype(jnp.int32)
        order = jnp.broadcast_to(order, shape)
        for half in range(sizes.depth // 8):
            merged = jnp.zeros(shape, jnp.float32)
            for k in range(per_row):
                for layer in range(sizes.layers):
                    spot = (k * sizes.layers + layer) * sizes.chunk
                    moved = turn(values[s][half * per_row + k], spot - layer * width - HALO)
                    merged = jnp.where(lane // sizes.chunk == spot // sizes.chunk, moved, merged)
            chosen = jnp.take_along_axis(merged, order, axis=0)
            start = s * rows * (sizes.depth // 8) + half
            out_ref[pl.ds(start, rows, stride=sizes.depth // 8), :] = chosen


def swap_blocks(tile, block):
    sub = iota(tile.shape, 0)
    spot = iota(tile.shape, 1) // block
    for bit in (4, 2, 1):
        up = pltpu.roll(pltpu.roll(tile, 8 - bit, 0), bit * block, 1)
        down = pltpu.roll(pltpu.roll(tile, bit, 0), LANES - bit * block, 1)
        moved = jnp.where(sub & bit == 0, up, down)
        tile = jnp.where((sub & bit) == (spot & bit), tile, moved)
    return tile


def creep_kernel(sizes, active_ref, temps_ref, trial_ref, stress_ref, strain_ref):
    tiles = sizes.tiles
    halves = sizes.depth // 8
    active = active_ref[0, 0]
    for tile in range(tiles):
        for element in range(halves):
            source = pl.ds(tile * 8 * halves + element, 8, stride=halves)
            mech_temp = swap_blocks(temps_ref[source, :], sizes.chunk)
            spot = pl.ds(element * 8 * tiles + tile, 8, stride=tiles)
            trial = trial_ref[spot, :]
            rate = CREEP_RATE * jnp.exp(-ACTIVATION / (mech_temp + REFERENCE_TEMP))
            slip = jnp.zeros(trial.shape, jnp.float32)
            for newton_step in range(NEWTON):
                left = trial - slip
                pull = rate * left * left
                slip = slip - (slip - pull * left) / (1.0 + 3.0 * pull)
            creep = jnp.where(element < active, slip, 0.0)
            stress_ref[spot, :] = trial - creep
            strain_ref[pl.ds(element * tiles + tile, 1), :] = 0.125 * jnp.sum(
                creep, axis=0, keepdims=True
            )


def kernel_call(body, sizes, out_shape, memories, scratch, operands):
    out_spec = pl.BlockSpec(memory_space=pltpu.VMEM)
    pinned = [
        pltpu.with_memory_space_constraint(operand, memory) if memory is pltpu.HBM else operand
        for operand, memory in zip(operands, memories)
    ]
    return pl.pallas_call(
        functools.partial(body, sizes),
        out_shape=out_shape,
        in_specs=[pl.BlockSpec(memory_space=memory) for memory in memories],
        out_specs=[out_spec] * len(out_shape),
        scratch_shapes=scratch,
        compiler_params=pltpu.CompilerParams(vmem_limit_bytes=16 * 1024 * 1024),
    )(*pinned)


def on_device(
    temp_start, conductivity, gap_conductance, partner, row_order, active_layers, trial_stress
):
    layers, _, rows, radial = temp_start.shape
    sizes = Sizes(layers, rows, radial)
    if not fits_tiles(sizes):
        return stepwise(
            temp_start,
            conductivity,
            gap_conductance,
            partner,
            row_order,
            active_layers,
            trial_stress,
        )

    def floats(*shape):
        return jax.ShapeDtypeStruct(shape, jnp.float32)

    def near(*shape):
        return pltpu.VMEM(shape, jnp.float32)

    (dealt,) = kernel_call(
        deal_kernel,
        sizes,
        (near(sizes.devices, rows, LANES),),
        [pltpu.HBM] * 5,
        [
            pltpu.SMEM(partner.shape, jnp.int32),
            pltpu.SMEM(row_order.shape, jnp.int32),
            pltpu.SMEM(gap_conductance.shape, jnp.float32),
            pltpu.VMEM(temp_start.shape, jnp.float32),
            pltpu.VMEM(conductivity.shape, jnp.float32),
            pltpu.SemaphoreType.DMA((5,)),
        ],
        (partner, row_order, gap_conductance, temp_start, conductivity),
    )
    dealt = lax.all_to_all(dealt, EVERYONE, split_axis=0, concat_axis=0, tiled=True)
    halves = sizes.depth // 8
    (temps,) = kernel_call(
        sweep_kernel,
        sizes,
        (near(sizes.devices * halves, LANES),),
        [pltpu.VMEM],
        [],
        (dealt,),
    )
    temps = temps.reshape(sizes.devices, halves, LANES)
    temps = lax.all_to_all(temps, EVERYONE, split_axis=0, concat_axis=0, tiled=True)
    stress, strain = kernel_call(
        creep_kernel,
        sizes,
        (floats(sizes.depth * sizes.tiles, LANES), floats(halves * sizes.tiles, LANES)),
        [pltpu.SMEM, pltpu.VMEM, pltpu.VMEM],
        [],
        (
            active_layers,
            temps.reshape(sizes.devices * halves, LANES),
            trial_stress.reshape(sizes.depth * sizes.tiles, LANES),
        ),
    )
    return (
        stress.reshape(sizes.depth, 1, 1, radial),
        strain.reshape(halves, 1, 1, radial),
    )


def solution(mesh):
    placed = (
        P(("slab", "mech"), "iface", None, None),
        P(("slab", "mech"), "iface", None, None),
        P(("slab", "mech"), "iface", None),
        P("iface"),
        P("iface", None),
        P("iface", ("slab", "mech")),
        P(None, "iface", ("slab", "mech"), None),
    )
    return jax.shard_map(
        on_device,
        mesh=mesh,
        in_specs=placed,
        out_specs=(
            P(None, "iface", ("slab", "mech"), None),
            P(None, "iface", ("slab", "mech"), None),
        ),
        check_vma=False,
    )
```

```python
import functools
import jax
import jax.numpy as jnp
from jax import lax
from jax.experimental import pallas as pl
from jax.experimental.pallas import tpu as pltpu
from jax.sharding import PartitionSpec as P

SWEEPS = 2
NEWTON = 4


FLUX_STEP = 0.03
CREEP_RATE = 200.0
ACTIVATION = 12.0
REFERENCE_TEMP = 1.0


def padded(block, sides, width):
    for axis, dim in sides:
        count = lax.axis_size(axis)
        forward = [(i, i + 1) for i in range(count - 1)]
        backward = [(target, source) for source, target in forward]
        low = lax.ppermute(
            lax.slice_in_dim(block, block.shape[dim] - width, None, axis=dim), axis, forward
        )
        high = lax.ppermute(lax.slice_in_dim(block, 0, width, axis=dim), axis, backward)
        block = jnp.concatenate([low, block, high], axis=dim)
    return block


def neighbour_weight(shift_z, shift_a, shift_r):
    reach = abs(shift_z) + abs(shift_a) + abs(shift_r)
    return [0.0, 1.0, 0.5, 0.25][reach]


def conduction(padded_temp, padded_cond):
    center_temp = padded_temp[1:-1, 1:-1, 1:-1]
    center_cond = padded_cond[1:-1, 1:-1, 1:-1]
    depth, across, radial = center_temp.shape
    radial_index = jnp.arange(radial, dtype=jnp.int32)
    gap_row = radial // 2
    outward_open = (radial_index != gap_row - 1).astype(jnp.float32)
    inward_open = (radial_index != gap_row).astype(jnp.float32)
    total = jnp.zeros(center_temp.shape, jnp.float32)
    for shift_z in (-1, 0, 1):
        for shift_a in (-1, 0, 1):
            for shift_r in (-1, 0, 1):
                if shift_z == 0 and shift_a == 0 and (shift_r == 0):
                    continue
                near_temp = padded_temp[
                    1 + shift_z : 1 + shift_z + depth,
                    1 + shift_a : 1 + shift_a + across,
                    1 + shift_r : 1 + shift_r + radial,
                ]
                near_cond = padded_cond[
                    1 + shift_z : 1 + shift_z + depth,
                    1 + shift_a : 1 + shift_a + across,
                    1 + shift_r : 1 + shift_r + radial,
                ]
                face = neighbour_weight(shift_z, shift_a, shift_r) * 0.5 * (center_cond + near_cond)
                if shift_r == 1:
                    face = face * outward_open
                elif shift_r == -1:
                    face = face * inward_open
                total = total + face * (near_temp - center_temp)
    return FLUX_STEP * total


def creep_return(mech_temp, trial, active_layers):
    rate = CREEP_RATE * jnp.exp(-ACTIVATION / (mech_temp + REFERENCE_TEMP))
    slip = jnp.zeros(trial.shape, jnp.float32)
    for newton_step in range(NEWTON):
        left = trial - slip
        residue = slip - rate * left**3
        slope = 1.0 + 3.0 * rate * left**2
        slip = slip - residue / slope
    depth = trial.shape[0]
    layer = jnp.arange(depth, dtype=jnp.int32) // 8
    live = (layer[:, None, None] < active_layers[None, :, :]).astype(jnp.float32)[..., None]
    creep = live * slip
    stress = trial - creep
    strain = jnp.sum(creep.reshape((depth // 8, 8) + trial.shape[1:]), axis=1) * 0.125
    return (stress, strain)


def stepwise(
    temp_start, conductivity, gap_conductance, partner, row_order, active_layers, trial_stress
):
    depth = temp_start.shape[0]
    rows = temp_start.shape[2]
    radial = temp_start.shape[3]
    temp = temp_start.reshape(depth, rows, radial)
    cond = conductivity.reshape(depth, rows, radial)
    gap = gap_conductance.reshape(depth, rows)
    gap_row = radial // 2
    sections = lax.axis_size("iface")
    across = rows * sections
    all_cols = jnp.arange(across, dtype=jnp.int32)
    cond_rim = padded(cond, ((("slab", "mech"), 0), ("iface", 1)), 1)
    padded_cond = jnp.pad(cond_rim, ((0, 0), (0, 0), (1, 1)))
    spread_table = (partner[:, None] == all_cols[None, :]).astype(jnp.float32)
    for sweep in range(SWEEPS):
        temp_rim = padded(temp, ((("slab", "mech"), 0), ("iface", 1)), 1)
        padded_temp = jnp.pad(temp_rim, ((0, 0), (0, 0), (1, 1)))
        compact = temp[:, :, gap_row - 1]
        canister = temp[:, :, gap_row]
        compact_all = lax.all_gather(compact, "iface", axis=1, tiled=True)
        facing = jnp.take(compact_all, partner, axis=1)
        flux = gap * (facing - canister)
        spread = jnp.dot(
            flux, spread_table, precision=lax.Precision.HIGHEST, preferred_element_type=jnp.float32
        )
        returned = lax.psum_scatter(spread, "iface", scatter_dimension=1, tiled=True)
        fresh = temp + conduction(padded_temp, padded_cond)
        temp = (
            fresh.at[:, :, gap_row]
            .add(FLUX_STEP * flux)
            .at[:, :, gap_row - 1]
            .add(-FLUX_STEP * returned)
        )
    permuted = jnp.take(temp, row_order[0], axis=1)
    mech_temp = lax.all_to_all(permuted, ("slab", "mech"), split_axis=1, concat_axis=0, tiled=True)
    mech_temp = mech_temp.reshape(mech_temp.shape[0], 1, mech_temp.shape[1], radial)
    return creep_return(mech_temp, trial_stress, active_layers)


LANES = 128
HALO = 2
EVERYONE = ("iface", "slab", "mech")


def iota(shape, axis):
    return lax.broadcasted_iota(jnp.int32, shape, axis)


class Sizes:
    def __init__(self, layers, rows, radial):
        self.layers = layers
        self.rows = rows
        self.radial = radial
        self.tiles = radial // LANES
        self.sections = lax.axis_size("iface")
        self.members = lax.axis_size("slab") * lax.axis_size("mech")
        self.devices = self.sections * self.members
        self.depth = layers * self.members
        self.chunk = radial // self.devices
        self.width = self.chunk + 2 * HALO
        self.field = layers * self.width
        self.gap_row = radial // 2


def fits_tiles(sizes):
    return (
        sizes.rows == 8
        and sizes.members == sizes.rows
        and sizes.layers == 2
        and sizes.sections * sizes.rows <= LANES
        and sizes.radial % sizes.devices == 0
        and sizes.chunk * 8 == LANES
        and sizes.radial % (2 * LANES) == 0
    )


def deal_kernel(
    sizes,
    partner_hbm,
    order_hbm,
    gap_hbm,
    temp_hbm,
    cond_hbm,
    out_ref,
    partner_ref,
    order_ref,
    gap_ref,
    temp_ref,
    cond_ref,
    sems,
):
    pairs = (
        (gap_hbm, gap_ref),
        (partner_hbm, partner_ref),
        (order_hbm, order_ref),
        (temp_hbm, temp_ref),
        (cond_hbm, cond_ref),
    )
    copies = [
        pltpu.make_async_copy(source, target, sems.at[index])
        for index, (source, target) in enumerate(pairs)
    ]
    for copy in copies:
        copy.start()
    for copy in copies[:3]:
        copy.wait()
    shape = (sizes.rows, LANES)
    lane = iota(shape, 1)
    sub = iota(shape, 0)
    extra_at = 2 * sizes.field
    extra = jnp.zeros(shape, jnp.float32)
    for row in range(sizes.rows):
        for layer in range(sizes.layers):
            spot = (sub == row) & (lane == extra_at + layer * sizes.width)
            extra = jnp.where(spot, gap_ref[layer, 0, row], extra)
        spot = (sub == row) & (lane == extra_at + 1)
        extra = jnp.where(spot, partner_ref[row].astype(jnp.float32), extra)
        extra = jnp.where(
            lane == extra_at + sizes.rows + row, partner_ref[row].astype(jnp.float32), extra
        )
        spot = (sub == row) & (lane == extra_at + 2)
        extra = jnp.where(spot, order_ref[0, row].astype(jnp.float32), extra)
    for copy in copies[3:]:
        copy.wait()
    blocks = [
        [ref[layer, 0, :, pl.ds(tile * LANES, LANES)] for tile in range(sizes.tiles)]
        for ref in (temp_ref, cond_ref)
        for layer in range(sizes.layers)
    ]
    for device in range(sizes.devices):
        first = device * sizes.chunk - HALO
        packed = extra
        for index, block in enumerate(blocks):
            base = index * sizes.width
            for tile in range(sizes.tiles):
                low = max(first, tile * LANES)
                high = min(first + sizes.width, (tile + 1) * LANES)
                if low >= high:
                    continue
                moved = pltpu.roll(block[tile], (base - first + tile * LANES) % LANES, 1)
                spot = (lane >= base + low - first) & (lane < base + high - first)
                packed = jnp.where(spot, moved, packed)
        out_ref[device] = packed


def sweep_kernel(sizes, dealt_ref, out_ref):
    rows, width, field = sizes.rows, sizes.width, sizes.field
    sections, members = sizes.sections, sizes.members
    shape = (rows, LANES)
    lane = iota(shape, 1)
    sub = iota(shape, 0)
    place = lax.axis_index("iface") * members
    place = place + lax.axis_index("slab") * lax.axis_size("mech") + lax.axis_index("mech")
    first = place * sizes.chunk - HALO
    segment = lane // width
    radius = first + lane % width
    lower_layer = segment % 2 == 0
    at_compact = radius == sizes.gap_row - 1
    at_canister = radius == sizes.gap_row
    in_grid = (radius >= 0) & (radius < sizes.radial)
    weight = jnp.where(at_compact | at_canister, 6.0, 8.0)
    is_temp = lane < field
    at_face = is_temp & (at_compact | at_canister)
    keep_temp = jnp.where(is_temp & in_grid, 1.0, 0.0)
    face_lane = sizes.gap_row - 1 - first

    def turn(value, shift):
        return pltpu.roll(value, shift % LANES, 1)

    dealt = [[dealt_ref[s * members + k] for k in range(members)] for s in range(sections)]

    odd = (lane % width) % 2 == 1

    def strip_of(values, start):
        strips = []
        for s in range(sections):
            strip = jnp.zeros(shape, jnp.float32)
            for k in range(members):
                moved = pltpu.roll(values[s][k], (start + 2 * k) % LANES, 1)
                spot = ((lane % width) // 2 == k) & (lane < 2 * width)
                strip = jnp.where(spot, moved, strip)
            strips.append(strip)
        return strips

    name_at = 2 * field + rows
    named = (lane >= name_at) & (lane < name_at + rows)
    blocks = []
    places = []
    for s in range(sections):
        partner = dealt[s][0][:, 2 * field + 1 : 2 * field + 2]
        names = jnp.zeros(shape, jnp.float32)
        target = (s * rows + sub).astype(jnp.float32)
        for t in range(sections):
            hit = named & (dealt[t][0] == target)
            names = jnp.where(hit, (t * rows + lane - name_at).astype(jnp.float32), names)
        inverse = jnp.sum(names, axis=1, keepdims=True)
        index = jnp.where(
            odd, jnp.broadcast_to(partner, shape), jnp.broadcast_to(inverse, shape)
        ).astype(jnp.int32)
        blocks.append(index // rows)
        places.append(index % rows)

    def met_by(strips):
        swapped = [jnp.where(odd, turn(strip, 1), turn(strip, -1)) for strip in strips]
        result = []
        for s in range(sections):
            met = jnp.take_along_axis(swapped[0], places[s], axis=0)
            for t in range(1, sections):
                other = jnp.take_along_axis(swapped[t], places[s], axis=0)
                met = jnp.where(blocks[s] == t, other, met)
            result.append(met)
        return result

    gap = strip_of(dealt, LANES + 1 - 2 * field)
    gap = [jnp.where(odd, own, met) for own, met in zip(gap, met_by(gap))]

    def gains(values):
        strips = strip_of(values, LANES - face_lane)
        met = met_by(strips)
        return [FLUX_STEP * g * (m - own) for g, m, own in zip(gap, met, strips)]

    conds = [[turn(value, -field) for value in line] for line in dealt]

    def with_product(value, cond):
        return jnp.where(lane < 2 * field, value, turn(value * cond, 2 * field))

    def box_sum(values):
        summed = []
        for s in range(sections):
            less = [turn(value, -width) for value in values[s]]
            more = [turn(value, width) for value in values[s]]
            line = []
            for k in range(members):
                low = less[k] + (less[k - 1] if k else 0.0)
                high = more[k] + (more[k + 1] if k < members - 1 else 0.0)
                line.append(values[s][k] + 0.5 * jnp.where(lower_layer, low, high))
            summed.append(line)
        result = []
        up = [[pltpu.roll(value, 1, 0) for value in line] for line in summed]
        down = [[pltpu.roll(value, rows - 1, 0) for value in line] for line in summed]
        for s in range(sections):
            line = []
            for k in range(members):
                before = jnp.where(sub == 0, up[s - 1][k] if s else 0.0, up[s][k])
                after = jnp.where(
                    sub == rows - 1, down[s + 1][k] if s < sections - 1 else 0.0, down[s][k]
                )
                value = summed[s][k] + 0.5 * (before + after)
                inward = jnp.where(at_canister, 0.0, turn(value, 1))
                outward = jnp.where(at_compact, 0.0, turn(value, -1))
                line.append(value + 0.5 * (inward + outward))
            result.append(line)
        return result

    values = dealt
    cond_sums = None
    for sweep in range(SWEEPS):
        gain = gains(values)
        packed = [
            [with_product(value, cond) for value, cond in zip(*lines)]
            for lines in zip(values, conds)
        ]
        sums = box_sum(packed)
        if cond_sums is None:
            cond_sums = [[turn(total_sum, -field) for total_sum in line] for line in sums]
        fresh = []
        for s in range(sections):
            line = []
            for k in range(members):
                value = values[s][k]
                total_sum = sums[s][k]
                change = conds[s][k] * (total_sum - weight * value)
                change = change + turn(total_sum, -2 * field) - value * cond_sums[s][k]
                back = pltpu.roll(gain[s], (face_lane - 2 * k + LANES) % LANES, 1)
                temp = value + FLUX_STEP * change + jnp.where(at_face, back, 0.0)
                line.append(jnp.where(is_temp, keep_temp * temp, value))
            fresh.append(line)
        values = fresh

    per_row = 8 // sizes.layers
    for s in range(sections):
        order = dealt[s][0][:, 2 * field + 2 : 2 * field + 3].astype(jnp.int32)
        order = jnp.broadcast_to(order, shape)
        for half in range(sizes.depth // 8):
            merged = jnp.zeros(shape, jnp.float32)
            for k in range(per_row):
                for layer in range(sizes.layers):
                    spot = (k * sizes.layers + layer) * sizes.chunk
                    moved = turn(values[s][half * per_row + k], spot - layer * width - HALO)
                    merged = jnp.where(lane // sizes.chunk == spot // sizes.chunk, moved, merged)
            chosen = jnp.take_along_axis(merged, order, axis=0)
            start = s * rows * (sizes.depth // 8) + half
            out_ref[pl.ds(start, rows, stride=sizes.depth // 8), :] = chosen


def swap_blocks(tile, block):
    sub = iota(tile.shape, 0)
    spot = iota(tile.shape, 1) // block
    for bit in (4, 2, 1):
        up = pltpu.roll(pltpu.roll(tile, 8 - bit, 0), bit * block, 1)
        down = pltpu.roll(pltpu.roll(tile, bit, 0), LANES - bit * block, 1)
        moved = jnp.where(sub & bit == 0, up, down)
        tile = jnp.where((sub & bit) == (spot & bit), tile, moved)
    return tile


def creep_kernel(sizes, active_ref, temps_ref, trial_ref, stress_ref, strain_ref):
    tiles = sizes.tiles
    halves = sizes.depth // 8
    active = active_ref[0, 0]
    for tile in range(tiles):
        for element in range(halves):
            source = pl.ds(tile * 8 * halves + element, 8, stride=halves)
            mech_temp = swap_blocks(temps_ref[source, :], sizes.chunk)
            spot = pl.ds(element * 8 * tiles + tile, 8, stride=tiles)
            trial = trial_ref[spot, :]
            rate = CREEP_RATE * jnp.exp(-ACTIVATION / (mech_temp + REFERENCE_TEMP))
            slip = jnp.zeros(trial.shape, jnp.float32)
            for newton_step in range(NEWTON):
                left = trial - slip
                pull = rate * left * left
                slip = slip - (slip - pull * left) / (1.0 + 3.0 * pull)
            creep = jnp.where(element < active, slip, 0.0)
            stress_ref[spot, :] = trial - creep
            strain_ref[pl.ds(element * tiles + tile, 1), :] = 0.125 * jnp.sum(
                creep, axis=0, keepdims=True
            )


def kernel_call(body, sizes, out_shape, memories, scratch, operands):
    out_spec = pl.BlockSpec(memory_space=pltpu.VMEM)
    pinned = [
        pltpu.with_memory_space_constraint(operand, memory) if memory is pltpu.HBM else operand
        for operand, memory in zip(operands, memories)
    ]
    return pl.pallas_call(
        functools.partial(body, sizes),
        out_shape=out_shape,
        in_specs=[pl.BlockSpec(memory_space=memory) for memory in memories],
        out_specs=[out_spec] * len(out_shape),
        scratch_shapes=scratch,
        compiler_params=pltpu.CompilerParams(vmem_limit_bytes=16 * 1024 * 1024),
    )(*pinned)


def on_device(
    temp_start, conductivity, gap_conductance, partner, row_order, active_layers, trial_stress
):
    layers, _, rows, radial = temp_start.shape
    sizes = Sizes(layers, rows, radial)
    if not fits_tiles(sizes):
        return stepwise(
            temp_start,
            conductivity,
            gap_conductance,
            partner,
            row_order,
            active_layers,
            trial_stress,
        )

    def floats(*shape):
        return jax.ShapeDtypeStruct(shape, jnp.float32)

    def near(*shape):
        return pltpu.VMEM(shape, jnp.float32)

    (dealt,) = kernel_call(
        deal_kernel,
        sizes,
        (near(sizes.devices, rows, LANES),),
        [pltpu.HBM] * 5,
        [
            pltpu.SMEM(partner.shape, jnp.int32),
            pltpu.SMEM(row_order.shape, jnp.int32),
            pltpu.SMEM(gap_conductance.shape, jnp.float32),
            pltpu.VMEM(temp_start.shape, jnp.float32),
            pltpu.VMEM(conductivity.shape, jnp.float32),
            pltpu.SemaphoreType.DMA((5,)),
        ],
        (partner, row_order, gap_conductance, temp_start, conductivity),
    )
    dealt = lax.all_to_all(dealt, EVERYONE, split_axis=0, concat_axis=0, tiled=True)
    halves = sizes.depth // 8
    (temps,) = kernel_call(
        sweep_kernel,
        sizes,
        (near(sizes.devices * halves, LANES),),
        [pltpu.VMEM],
        [],
        (dealt,),
    )
    temps = temps.reshape(sizes.devices, halves, LANES)
    temps = lax.all_to_all(temps, EVERYONE, split_axis=0, concat_axis=0, tiled=True)
    stress, strain = kernel_call(
        creep_kernel,
        sizes,
        (floats(sizes.depth * sizes.tiles, LANES), floats(halves * sizes.tiles, LANES)),
        [pltpu.SMEM, pltpu.VMEM, pltpu.VMEM],
        [],
        (
            active_layers,
            temps.reshape(sizes.devices * halves, LANES),
            trial_stress.reshape(sizes.depth * sizes.tiles, LANES),
        ),
    )
    return (
        stress.reshape(sizes.depth, 1, 1, radial),
        strain.reshape(halves, 1, 1, radial),
    )


def solution(mesh):
    placed = (
        P(("slab", "mech"), "iface", None, None),
        P(("slab", "mech"), "iface", None, None),
        P(("slab", "mech"), "iface", None),
        P("iface"),
        P("iface", None),
        P("iface", ("slab", "mech")),
        P(None, "iface", ("slab", "mech"), None),
    )
    return jax.shard_map(
        on_device,
        mesh=mesh,
        in_specs=placed,
        out_specs=(
            P(None, "iface", ("slab", "mech"), None),
            P(None, "iface", ("slab", "mech"), None),
        ),
        check_vma=False,
    )
```

```python
import functools
import jax
import jax.numpy as jnp
from jax import lax
from jax.experimental import pallas as pl
from jax.experimental.pallas import tpu as pltpu
from jax.sharding import PartitionSpec as P

SWEEPS = 2
NEWTON = 4


FLUX_STEP = 0.03
CREEP_RATE = 200.0
ACTIVATION = 12.0
REFERENCE_TEMP = 1.0


def padded(block, sides, width):
    for axis, dim in sides:
        count = lax.axis_size(axis)
        forward = [(i, i + 1) for i in range(count - 1)]
        backward = [(target, source) for source, target in forward]
        low = lax.ppermute(
            lax.slice_in_dim(block, block.shape[dim] - width, None, axis=dim), axis, forward
        )
        high = lax.ppermute(lax.slice_in_dim(block, 0, width, axis=dim), axis, backward)
        block = jnp.concatenate([low, block, high], axis=dim)
    return block


def neighbour_weight(shift_z, shift_a, shift_r):
    reach = abs(shift_z) + abs(shift_a) + abs(shift_r)
    return [0.0, 1.0, 0.5, 0.25][reach]


def conduction(padded_temp, padded_cond):
    center_temp = padded_temp[1:-1, 1:-1, 1:-1]
    center_cond = padded_cond[1:-1, 1:-1, 1:-1]
    depth, across, radial = center_temp.shape
    radial_index = jnp.arange(radial, dtype=jnp.int32)
    gap_row = radial // 2
    outward_open = (radial_index != gap_row - 1).astype(jnp.float32)
    inward_open = (radial_index != gap_row).astype(jnp.float32)
    total = jnp.zeros(center_temp.shape, jnp.float32)
    for shift_z in (-1, 0, 1):
        for shift_a in (-1, 0, 1):
            for shift_r in (-1, 0, 1):
                if shift_z == 0 and shift_a == 0 and (shift_r == 0):
                    continue
                near_temp = padded_temp[
                    1 + shift_z : 1 + shift_z + depth,
                    1 + shift_a : 1 + shift_a + across,
                    1 + shift_r : 1 + shift_r + radial,
                ]
                near_cond = padded_cond[
                    1 + shift_z : 1 + shift_z + depth,
                    1 + shift_a : 1 + shift_a + across,
                    1 + shift_r : 1 + shift_r + radial,
                ]
                face = neighbour_weight(shift_z, shift_a, shift_r) * 0.5 * (center_cond + near_cond)
                if shift_r == 1:
                    face = face * outward_open
                elif shift_r == -1:
                    face = face * inward_open
                total = total + face * (near_temp - center_temp)
    return FLUX_STEP * total


def creep_return(mech_temp, trial, active_layers):
    rate = CREEP_RATE * jnp.exp(-ACTIVATION / (mech_temp + REFERENCE_TEMP))
    slip = jnp.zeros(trial.shape, jnp.float32)
    for newton_step in range(NEWTON):
        left = trial - slip
        residue = slip - rate * left**3
        slope = 1.0 + 3.0 * rate * left**2
        slip = slip - residue / slope
    depth = trial.shape[0]
    layer = jnp.arange(depth, dtype=jnp.int32) // 8
    live = (layer[:, None, None] < active_layers[None, :, :]).astype(jnp.float32)[..., None]
    creep = live * slip
    stress = trial - creep
    strain = jnp.sum(creep.reshape((depth // 8, 8) + trial.shape[1:]), axis=1) * 0.125
    return (stress, strain)


def stepwise(
    temp_start, conductivity, gap_conductance, partner, row_order, active_layers, trial_stress
):
    depth = temp_start.shape[0]
    rows = temp_start.shape[2]
    radial = temp_start.shape[3]
    temp = temp_start.reshape(depth, rows, radial)
    cond = conductivity.reshape(depth, rows, radial)
    gap = gap_conductance.reshape(depth, rows)
    gap_row = radial // 2
    sections = lax.axis_size("iface")
    across = rows * sections
    all_cols = jnp.arange(across, dtype=jnp.int32)
    cond_rim = padded(cond, ((("slab", "mech"), 0), ("iface", 1)), 1)
    padded_cond = jnp.pad(cond_rim, ((0, 0), (0, 0), (1, 1)))
    spread_table = (partner[:, None] == all_cols[None, :]).astype(jnp.float32)
    for sweep in range(SWEEPS):
        temp_rim = padded(temp, ((("slab", "mech"), 0), ("iface", 1)), 1)
        padded_temp = jnp.pad(temp_rim, ((0, 0), (0, 0), (1, 1)))
        compact = temp[:, :, gap_row - 1]
        canister = temp[:, :, gap_row]
        compact_all = lax.all_gather(compact, "iface", axis=1, tiled=True)
        facing = jnp.take(compact_all, partner, axis=1)
        flux = gap * (facing - canister)
        spread = jnp.dot(
            flux, spread_table, precision=lax.Precision.HIGHEST, preferred_element_type=jnp.float32
        )
        returned = lax.psum_scatter(spread, "iface", scatter_dimension=1, tiled=True)
        fresh = temp + conduction(padded_temp, padded_cond)
        temp = (
            fresh.at[:, :, gap_row]
            .add(FLUX_STEP * flux)
            .at[:, :, gap_row - 1]
            .add(-FLUX_STEP * returned)
        )
    permuted = jnp.take(temp, row_order[0], axis=1)
    mech_temp = lax.all_to_all(permuted, ("slab", "mech"), split_axis=1, concat_axis=0, tiled=True)
    mech_temp = mech_temp.reshape(mech_temp.shape[0], 1, mech_temp.shape[1], radial)
    return creep_return(mech_temp, trial_stress, active_layers)


LANES = 128
HALO = 2
EVERYONE = ("iface", "slab", "mech")


def iota(shape, axis):
    return lax.broadcasted_iota(jnp.int32, shape, axis)


class Sizes:
    def __init__(self, layers, rows, radial):
        self.layers = layers
        self.rows = rows
        self.radial = radial
        self.tiles = radial // LANES
        self.sections = lax.axis_size("iface")
        self.members = lax.axis_size("slab") * lax.axis_size("mech")
        self.devices = self.sections * self.members
        self.depth = layers * self.members
        self.chunk = radial // self.devices
        self.width = self.chunk + 2 * HALO
        self.layer_lanes = LANES // layers
        self.extra_at = 3 * self.width
        self.gap_row = radial // 2


def fits_tiles(sizes):
    return (
        sizes.rows == 8
        and sizes.members == sizes.rows
        and sizes.layers == 2
        and sizes.sections * sizes.rows <= LANES
        and sizes.radial % sizes.devices == 0
        and sizes.chunk * 8 == LANES
        and sizes.radial % (2 * LANES) == 0
        and sizes.extra_at + 3 <= sizes.layer_lanes
    )


def deal_kernel(
    sizes,
    partner_hbm,
    order_hbm,
    gap_hbm,
    temp_hbm,
    cond_hbm,
    out_ref,
    partner_ref,
    order_ref,
    gap_ref,
    temp_ref,
    cond_ref,
    sems,
):
    pairs = (
        (gap_hbm, gap_ref),
        (partner_hbm, partner_ref),
        (order_hbm, order_ref),
        (temp_hbm, temp_ref),
        (cond_hbm, cond_ref),
    )
    copies = [
        pltpu.make_async_copy(source, target, sems.at[index])
        for index, (source, target) in enumerate(pairs)
    ]
    for copy in copies:
        copy.start()
    for copy in copies[:3]:
        copy.wait()
    shape = (sizes.rows, LANES)
    lane = iota(shape, 1)
    sub = iota(shape, 0)
    extra_at = sizes.extra_at
    extra = jnp.zeros(shape, jnp.float32)
    for row in range(sizes.rows):
        for layer in range(sizes.layers):
            spot = (sub == row) & (lane == extra_at + layer * sizes.layer_lanes)
            extra = jnp.where(spot, gap_ref[layer, 0, row], extra)
        spot = (sub == row) & (lane == extra_at + 1)
        extra = jnp.where(spot, partner_ref[row].astype(jnp.float32), extra)
        spot = (sub == row) & (lane == extra_at + 2)
        extra = jnp.where(spot, order_ref[0, row].astype(jnp.float32), extra)
    for copy in copies[3:]:
        copy.wait()
    blocks = [
        (
            layer * sizes.layer_lanes + field * sizes.width,
            [ref[layer, 0, :, pl.ds(tile * LANES, LANES)] for tile in range(sizes.tiles)],
        )
        for field, ref in enumerate((temp_ref, cond_ref))
        for layer in range(sizes.layers)
    ]
    for device in range(sizes.devices):
        first = device * sizes.chunk - HALO
        packed = extra
        for base, block in blocks:
            for tile in range(sizes.tiles):
                low = max(first, tile * LANES)
                high = min(first + sizes.width, (tile + 1) * LANES)
                if low >= high:
                    continue
                moved = pltpu.roll(block[tile], (base - first + tile * LANES) % LANES, 1)
                spot = (lane >= base + low - first) & (lane < base + high - first)
                packed = jnp.where(spot, moved, packed)
        out_ref[device] = packed


def sweep_kernel(sizes, dealt_ref, out_ref, line_ref):
    rows, width, half_lanes = sizes.rows, sizes.width, sizes.layer_lanes
    sections, members = sizes.sections, sizes.members
    shape = (rows, LANES)
    lane = iota(shape, 1)
    sub = iota(shape, 0)
    place = lax.axis_index("iface") * members
    place = place + lax.axis_index("slab") * lax.axis_size("mech") + lax.axis_index("mech")
    first = place * sizes.chunk - HALO
    spot_in_layer = lane % half_lanes
    radius = first + spot_in_layer % width
    lower_layer = lane < half_lanes
    at_compact = radius == sizes.gap_row - 1
    at_canister = radius == sizes.gap_row
    in_grid = (radius >= 0) & (radius < sizes.radial)
    weight = jnp.where(at_compact | at_canister, 6.0, 8.0)
    is_temp = spot_in_layer < width
    at_face = is_temp & (at_compact | at_canister)
    keep_temp = jnp.where(is_temp & in_grid, 1.0, 0.0)
    face_lane = sizes.gap_row - 1 - first

    def turn(value, shift):
        return pltpu.roll(value, shift % LANES, 1)

    dealt = [[dealt_ref[s * members + k] for k in range(members)] for s in range(sections)]

    odd = lane % 2 == 1

    def strip_of(values, start):
        strips = []
        for s in range(sections):
            strip = jnp.zeros(shape, jnp.float32)
            for k in range(members):
                moved = pltpu.roll(values[s][k], (start + 2 * k) % LANES, 1)
                spot = spot_in_layer // 2 == k
                strip = jnp.where(spot, moved, strip)
            strips.append(strip)
        return jnp.concatenate(strips, axis=0)

    total = sections * rows
    meets = jnp.concatenate(
        [
            jnp.where(
                lane == dealt[s][0][:, sizes.extra_at + 1 : sizes.extra_at + 2].astype(jnp.int32), 1.0, 0.0
            )
            for s in range(sections)
        ]
        + [jnp.zeros((LANES - total, LANES), jnp.float32)],
        axis=0,
    )
    met_by = meets.T[:total, :total]
    meets = meets[:total, :total]
    both = jnp.concatenate([meets, met_by], axis=0)

    def pick(table, strip):
        return jnp.dot(
            table, strip, precision=lax.Precision.HIGHEST, preferred_element_type=jnp.float32
        )

    wide_odd = jnp.concatenate([odd] * sections, axis=0)
    gap = strip_of(dealt, LANES + 1 - sizes.extra_at)
    gap = jnp.where(wide_odd, gap, turn(pick(met_by, gap), -1))

    def gains(values):
        strip = strip_of(values, LANES - face_lane)
        met = pick(both, strip)
        met = jnp.where(wide_odd, turn(met[:total], 1), turn(met[total:], -1))
        gain = FLUX_STEP * gap * (met - strip)
        return [gain[s * rows : (s + 1) * rows] for s in range(sections)]

    conds = [[turn(value, -width) for value in line] for line in dealt]
    edge = jnp.zeros(shape, jnp.float32)
    for k in range(members):
        line_ref[k, pl.ds(0, rows), :] = edge
        line_ref[k, pl.ds(rows + total, rows), :] = edge

    def with_product(value, cond):
        return jnp.where(spot_in_layer < 2 * width, value, turn(value * cond, 2 * width))

    def box_sum(values):
        for s in range(sections):
            other = [turn(value, half_lanes) for value in values[s]]
            for k in range(members):
                before = other[k - 1] if k else 0.0
                after = other[k + 1] if k < members - 1 else 0.0
                near = other[k] + jnp.where(lower_layer, before, after)
                line_ref[k, pl.ds(rows + s * rows, rows), :] = values[s][k] + 0.5 * near
        result = []
        for s in range(sections):
            line = []
            for k in range(members):
                start = rows + s * rows
                near = line_ref[k, pl.ds(start - 1, rows), :] + line_ref[k, pl.ds(start + 1, rows), :]
                value = line_ref[k, pl.ds(start, rows), :] + 0.5 * near
                inward = jnp.where(at_canister, 0.0, turn(value, 1))
                outward = jnp.where(at_compact, 0.0, turn(value, -1))
                line.append(value + 0.5 * (inward + outward))
            result.append(line)
        return result

    values = dealt
    cond_sums = None
    for sweep in range(SWEEPS):
        gain = gains(values)
        packed = [
            [with_product(value, cond) for value, cond in zip(*lines)]
            for lines in zip(values, conds)
        ]
        sums = box_sum(packed)
        if cond_sums is None:
            cond_sums = [[turn(total_sum, -width) for total_sum in line] for line in sums]
        fresh = []
        for s in range(sections):
            line = []
            for k in range(members):
                value = values[s][k]
                total_sum = sums[s][k]
                change = conds[s][k] * (total_sum - weight * value)
                change = change + turn(total_sum, -2 * width) - value * cond_sums[s][k]
                back = pltpu.roll(gain[s], (face_lane - 2 * k + LANES) % LANES, 1)
                temp = value + FLUX_STEP * change + jnp.where(at_face, back, 0.0)
                line.append(jnp.where(is_temp, keep_temp * temp, value))
            fresh.append(line)
        values = fresh

    per_row = 8 // sizes.layers
    for s in range(sections):
        order = dealt[s][0][:, sizes.extra_at + 2 : sizes.extra_at + 3].astype(jnp.int32)
        order = jnp.broadcast_to(order, shape)
        for half in range(sizes.depth // 8):
            merged = jnp.zeros(shape, jnp.float32)
            for k in range(per_row):
                moved = turn(values[s][half * per_row + k], k * sizes.chunk - HALO)
                merged = jnp.where(spot_in_layer // sizes.chunk == k, moved, merged)
            chosen = jnp.take_along_axis(merged, order, axis=0)
            start = s * rows * (sizes.depth // 8) + half
            out_ref[pl.ds(start, rows, stride=sizes.depth // 8), :] = chosen


def swap_blocks(tile, block):
    sub = iota(tile.shape, 0)
    spot = iota(tile.shape, 1) // block
    for bit in (4, 2, 1):
        up = pltpu.roll(pltpu.roll(tile, 8 - bit, 0), bit * block, 1)
        down = pltpu.roll(pltpu.roll(tile, bit, 0), LANES - bit * block, 1)
        moved = jnp.where(sub & bit == 0, up, down)
        tile = jnp.where((sub & bit) == (spot & bit), tile, moved)
    return tile


def creep_kernel(sizes, active_ref, temps_ref, trial_ref, stress_ref, strain_ref):
    tiles = sizes.tiles
    halves = sizes.depth // 8
    active = active_ref[0, 0]
    sub = iota((8, LANES), 0)
    natural = sub % sizes.layers * (8 // sizes.layers) + sub // sizes.layers
    for tile in range(tiles):
        for element in range(halves):
            source = pl.ds(tile * 8 * halves + element, 8, stride=halves)
            mech_temp = swap_blocks(temps_ref[source, :], sizes.chunk)
            mech_temp = jnp.take_along_axis(mech_temp, natural, axis=0)
            spot = pl.ds(element * 8 * tiles + tile, 8, stride=tiles)
            trial = trial_ref[spot, :]
            rate = CREEP_RATE * jnp.exp(-ACTIVATION / (mech_temp + REFERENCE_TEMP))
            slip = jnp.zeros(trial.shape, jnp.float32)
            for newton_step in range(NEWTON):
                left = trial - slip
                pull = rate * left * left
                slip = slip - (slip - pull * left) / (1.0 + 3.0 * pull)
            creep = jnp.where(element < active, slip, 0.0)
            stress_ref[spot, :] = trial - creep
            strain_ref[pl.ds(element * tiles + tile, 1), :] = 0.125 * jnp.sum(
                creep, axis=0, keepdims=True
            )


def kernel_call(body, sizes, out_shape, memories, scratch, operands):
    out_spec = pl.BlockSpec(memory_space=pltpu.VMEM)
    pinned = [
        pltpu.with_memory_space_constraint(operand, memory) if memory is pltpu.HBM else operand
        for operand, memory in zip(operands, memories)
    ]
    return pl.pallas_call(
        functools.partial(body, sizes),
        out_shape=out_shape,
        in_specs=[pl.BlockSpec(memory_space=memory) for memory in memories],
        out_specs=[out_spec] * len(out_shape),
        scratch_shapes=scratch,
        compiler_params=pltpu.CompilerParams(vmem_limit_bytes=16 * 1024 * 1024),
    )(*pinned)


def on_device(
    temp_start, conductivity, gap_conductance, partner, row_order, active_layers, trial_stress
):
    layers, _, rows, radial = temp_start.shape
    sizes = Sizes(layers, rows, radial)
    if not fits_tiles(sizes):
        return stepwise(
            temp_start,
            conductivity,
            gap_conductance,
            partner,
            row_order,
            active_layers,
            trial_stress,
        )

    def floats(*shape):
        return jax.ShapeDtypeStruct(shape, jnp.float32)

    def near(*shape):
        return pltpu.VMEM(shape, jnp.float32)

    (dealt,) = kernel_call(
        deal_kernel,
        sizes,
        (near(sizes.devices, rows, LANES),),
        [pltpu.HBM] * 5,
        [
            pltpu.SMEM(partner.shape, jnp.int32),
            pltpu.SMEM(row_order.shape, jnp.int32),
            pltpu.SMEM(gap_conductance.shape, jnp.float32),
            pltpu.VMEM(temp_start.shape, jnp.float32),
            pltpu.VMEM(conductivity.shape, jnp.float32),
            pltpu.SemaphoreType.DMA((5,)),
        ],
        (partner, row_order, gap_conductance, temp_start, conductivity),
    )
    dealt = lax.all_to_all(dealt, EVERYONE, split_axis=0, concat_axis=0, tiled=True)
    halves = sizes.depth // 8
    (temps,) = kernel_call(
        sweep_kernel,
        sizes,
        (near(sizes.devices * halves, LANES),),
        [pltpu.VMEM],
        [pltpu.VMEM((sizes.members, rows * (sizes.sections + 2), LANES), jnp.float32)],
        (dealt,),
    )
    temps = temps.reshape(sizes.devices, halves, LANES)
    temps = lax.all_to_all(temps, EVERYONE, split_axis=0, concat_axis=0, tiled=True)
    stress, strain = kernel_call(
        creep_kernel,
        sizes,
        (floats(sizes.depth * sizes.tiles, LANES), floats(halves * sizes.tiles, LANES)),
        [pltpu.SMEM, pltpu.VMEM, pltpu.VMEM],
        [],
        (
            active_layers,
            temps.reshape(sizes.devices * halves, LANES),
            trial_stress.reshape(sizes.depth * sizes.tiles, LANES),
        ),
    )
    return (
        stress.reshape(sizes.depth, 1, 1, radial),
        strain.reshape(halves, 1, 1, radial),
    )


def solution(mesh):
    placed = (
        P(("slab", "mech"), "iface", None, None),
        P(("slab", "mech"), "iface", None, None),
        P(("slab", "mech"), "iface", None),
        P("iface"),
        P("iface", None),
        P("iface", ("slab", "mech")),
        P(None, "iface", ("slab", "mech"), None),
    )
    return jax.shard_map(
        on_device,
        mesh=mesh,
        in_specs=placed,
        out_specs=(
            P(None, "iface", ("slab", "mech"), None),
            P(None, "iface", ("slab", "mech"), None),
        ),
        check_vma=False,
    )
```

```python
import functools
import jax
import jax.numpy as jnp
from jax import lax
from jax.experimental import pallas as pl
from jax.experimental.pallas import tpu as pltpu
from jax.sharding import PartitionSpec as P

SWEEPS = 2
NEWTON = 4


FLUX_STEP = 0.03
CREEP_RATE = 200.0
ACTIVATION = 12.0
REFERENCE_TEMP = 1.0


def padded(block, sides, width):
    for axis, dim in sides:
        count = lax.axis_size(axis)
        forward = [(i, i + 1) for i in range(count - 1)]
        backward = [(target, source) for source, target in forward]
        low = lax.ppermute(
            lax.slice_in_dim(block, block.shape[dim] - width, None, axis=dim), axis, forward
        )
        high = lax.ppermute(lax.slice_in_dim(block, 0, width, axis=dim), axis, backward)
        block = jnp.concatenate([low, block, high], axis=dim)
    return block


def neighbour_weight(shift_z, shift_a, shift_r):
    reach = abs(shift_z) + abs(shift_a) + abs(shift_r)
    return [0.0, 1.0, 0.5, 0.25][reach]


def conduction(padded_temp, padded_cond):
    center_temp = padded_temp[1:-1, 1:-1, 1:-1]
    center_cond = padded_cond[1:-1, 1:-1, 1:-1]
    depth, across, radial = center_temp.shape
    radial_index = jnp.arange(radial, dtype=jnp.int32)
    gap_row = radial // 2
    outward_open = (radial_index != gap_row - 1).astype(jnp.float32)
    inward_open = (radial_index != gap_row).astype(jnp.float32)
    total = jnp.zeros(center_temp.shape, jnp.float32)
    for shift_z in (-1, 0, 1):
        for shift_a in (-1, 0, 1):
            for shift_r in (-1, 0, 1):
                if shift_z == 0 and shift_a == 0 and (shift_r == 0):
                    continue
                near_temp = padded_temp[
                    1 + shift_z : 1 + shift_z + depth,
                    1 + shift_a : 1 + shift_a + across,
                    1 + shift_r : 1 + shift_r + radial,
                ]
                near_cond = padded_cond[
                    1 + shift_z : 1 + shift_z + depth,
                    1 + shift_a : 1 + shift_a + across,
                    1 + shift_r : 1 + shift_r + radial,
                ]
                face = neighbour_weight(shift_z, shift_a, shift_r) * 0.5 * (center_cond + near_cond)
                if shift_r == 1:
                    face = face * outward_open
                elif shift_r == -1:
                    face = face * inward_open
                total = total + face * (near_temp - center_temp)
    return FLUX_STEP * total


def creep_return(mech_temp, trial, active_layers):
    rate = CREEP_RATE * jnp.exp(-ACTIVATION / (mech_temp + REFERENCE_TEMP))
    slip = jnp.zeros(trial.shape, jnp.float32)
    for newton_step in range(NEWTON):
        left = trial - slip
        residue = slip - rate * left**3
        slope = 1.0 + 3.0 * rate * left**2
        slip = slip - residue / slope
    depth = trial.shape[0]
    layer = jnp.arange(depth, dtype=jnp.int32) // 8
    live = (layer[:, None, None] < active_layers[None, :, :]).astype(jnp.float32)[..., None]
    creep = live * slip
    stress = trial - creep
    strain = jnp.sum(creep.reshape((depth // 8, 8) + trial.shape[1:]), axis=1) * 0.125
    return (stress, strain)


def stepwise(
    temp_start, conductivity, gap_conductance, partner, row_order, active_layers, trial_stress
):
    depth = temp_start.shape[0]
    rows = temp_start.shape[2]
    radial = temp_start.shape[3]
    temp = temp_start.reshape(depth, rows, radial)
    cond = conductivity.reshape(depth, rows, radial)
    gap = gap_conductance.reshape(depth, rows)
    gap_row = radial // 2
    sections = lax.axis_size("iface")
    across = rows * sections
    all_cols = jnp.arange(across, dtype=jnp.int32)
    cond_rim = padded(cond, ((("slab", "mech"), 0), ("iface", 1)), 1)
    padded_cond = jnp.pad(cond_rim, ((0, 0), (0, 0), (1, 1)))
    spread_table = (partner[:, None] == all_cols[None, :]).astype(jnp.float32)
    for sweep in range(SWEEPS):
        temp_rim = padded(temp, ((("slab", "mech"), 0), ("iface", 1)), 1)
        padded_temp = jnp.pad(temp_rim, ((0, 0), (0, 0), (1, 1)))
        compact = temp[:, :, gap_row - 1]
        canister = temp[:, :, gap_row]
        compact_all = lax.all_gather(compact, "iface", axis=1, tiled=True)
        facing = jnp.take(compact_all, partner, axis=1)
        flux = gap * (facing - canister)
        spread = jnp.dot(
            flux, spread_table, precision=lax.Precision.HIGHEST, preferred_element_type=jnp.float32
        )
        returned = lax.psum_scatter(spread, "iface", scatter_dimension=1, tiled=True)
        fresh = temp + conduction(padded_temp, padded_cond)
        temp = (
            fresh.at[:, :, gap_row]
            .add(FLUX_STEP * flux)
            .at[:, :, gap_row - 1]
            .add(-FLUX_STEP * returned)
        )
    permuted = jnp.take(temp, row_order[0], axis=1)
    mech_temp = lax.all_to_all(permuted, ("slab", "mech"), split_axis=1, concat_axis=0, tiled=True)
    mech_temp = mech_temp.reshape(mech_temp.shape[0], 1, mech_temp.shape[1], radial)
    return creep_return(mech_temp, trial_stress, active_layers)


LANES = 128
HALO = 2
EVERYONE = ("iface", "slab", "mech")


def iota(shape, axis):
    return lax.broadcasted_iota(jnp.int32, shape, axis)


class Sizes:
    def __init__(self, layers, rows, radial):
        self.layers = layers
        self.rows = rows
        self.radial = radial
        self.tiles = radial // LANES
        self.sections = lax.axis_size("iface")
        self.members = lax.axis_size("slab") * lax.axis_size("mech")
        self.devices = self.sections * self.members
        self.depth = layers * self.members
        self.chunk = radial // self.devices
        self.width = self.chunk + 2 * HALO
        self.layer_lanes = LANES // layers
        self.extra_at = 3 * self.width
        self.gap_row = radial // 2


def fits_tiles(sizes):
    return (
        sizes.rows == 8
        and sizes.members == sizes.rows
        and sizes.layers == 2
        and sizes.sections * sizes.rows <= LANES
        and sizes.radial % sizes.devices == 0
        and sizes.chunk * 8 == LANES
        and sizes.radial % (2 * LANES) == 0
        and sizes.extra_at + 3 <= sizes.layer_lanes
    )


def deal_kernel(
    sizes,
    partner_hbm,
    order_hbm,
    gap_hbm,
    temp_hbm,
    cond_hbm,
    out_ref,
    partner_ref,
    order_ref,
    gap_ref,
    temp_ref,
    cond_ref,
    sems,
):
    pairs = (
        (gap_hbm, gap_ref),
        (partner_hbm, partner_ref),
        (order_hbm, order_ref),
        (temp_hbm, temp_ref),
        (cond_hbm, cond_ref),
    )
    copies = [
        pltpu.make_async_copy(source, target, sems.at[index])
        for index, (source, target) in enumerate(pairs)
    ]
    for copy in copies:
        copy.start()
    for copy in copies[:3]:
        copy.wait()
    shape = (sizes.rows, LANES)
    lane = iota(shape, 1)
    sub = iota(shape, 0)
    extra_at = sizes.extra_at
    extra = jnp.zeros(shape, jnp.float32)
    for row in range(sizes.rows):
        for layer in range(sizes.layers):
            spot = (sub == row) & (lane == extra_at + layer * sizes.layer_lanes)
            extra = jnp.where(spot, gap_ref[layer, 0, row], extra)
        spot = (sub == row) & (lane == extra_at + 1)
        extra = jnp.where(spot, partner_ref[row].astype(jnp.float32), extra)
        spot = (sub == row) & (lane == extra_at + 2)
        extra = jnp.where(spot, order_ref[0, row].astype(jnp.float32), extra)
    for copy in copies[3:]:
        copy.wait()
    blocks = [
        (
            layer * sizes.layer_lanes + field * sizes.width,
            [scale * ref[layer, 0, :, pl.ds(tile * LANES, LANES)] for tile in range(sizes.tiles)],
        )
        for field, (ref, scale) in enumerate(((temp_ref, 1.0), (cond_ref, FLUX_STEP)))
        for layer in range(sizes.layers)
    ]
    for device in range(sizes.devices):
        first = device * sizes.chunk - HALO
        packed = extra
        for base, block in blocks:
            for tile in range(sizes.tiles):
                low = max(first, tile * LANES)
                high = min(first + sizes.width, (tile + 1) * LANES)
                if low >= high:
                    continue
                moved = pltpu.roll(block[tile], (base - first + tile * LANES) % LANES, 1)
                spot = (lane >= base + low - first) & (lane < base + high - first)
                packed = jnp.where(spot, moved, packed)
        out_ref[device] = packed


def sweep_kernel(sizes, dealt_ref, out_ref, line_ref):
    rows, width, half_lanes = sizes.rows, sizes.width, sizes.layer_lanes
    sections, members = sizes.sections, sizes.members
    shape = (rows, LANES)
    lane = iota(shape, 1)
    sub = iota(shape, 0)
    place = lax.axis_index("iface") * members
    place = place + lax.axis_index("slab") * lax.axis_size("mech") + lax.axis_index("mech")
    first = place * sizes.chunk - HALO
    spot_in_layer = lane % half_lanes
    radius = first + spot_in_layer % width
    lower_layer = lane < half_lanes
    at_compact = radius == sizes.gap_row - 1
    at_canister = radius == sizes.gap_row
    weight = jnp.where(at_compact | at_canister, 6.0, 8.0)
    is_temp = spot_in_layer < width
    at_face = jnp.where(is_temp & (at_compact | at_canister), 1.0, 0.0)
    from_inward = jnp.where(at_canister | (radius == 0), 0.0, 0.5)
    from_outward = jnp.where(at_compact | (radius == sizes.radial - 1), 0.0, 0.5)
    face_lane = sizes.gap_row - 1 - first

    def turn(value, shift):
        return pltpu.roll(value, shift % LANES, 1)

    dealt = [[dealt_ref[s * members + k] for k in range(members)] for s in range(sections)]

    odd = lane % 2 == 1

    def strip_of(values, start):
        strips = []
        for s in range(sections):
            strip = jnp.zeros(shape, jnp.float32)
            for k in range(members):
                moved = pltpu.roll(values[s][k], (start + 2 * k) % LANES, 1)
                spot = spot_in_layer // 2 == k
                strip = jnp.where(spot, moved, strip)
            strips.append(strip)
        return jnp.concatenate(strips, axis=0)

    total = sections * rows
    meets = jnp.concatenate(
        [
            jnp.where(
                lane == dealt[s][0][:, sizes.extra_at + 1 : sizes.extra_at + 2].astype(jnp.int32), 1.0, 0.0
            )
            for s in range(sections)
        ]
        + [jnp.zeros((LANES - total, LANES), jnp.float32)],
        axis=0,
    )
    met_by = meets.T[:total, :total]
    meets = meets[:total, :total]
    both = jnp.concatenate([meets, met_by], axis=0).astype(jnp.bfloat16)
    third = 2 * members

    def pick(table, strip):
        rest = strip
        parts = jnp.zeros(strip.shape, jnp.float32)
        for index in range(3):
            part = rest.astype(jnp.bfloat16).astype(jnp.float32)
            rest = rest - part
            parts = parts + (turn(part, index * third) if index else part)
        picked = jnp.dot(
            table, parts.astype(jnp.bfloat16), preferred_element_type=jnp.float32
        )
        return picked + turn(picked, -third) + turn(picked, -2 * third)

    wide_odd = jnp.concatenate([odd] * sections, axis=0)
    gap = strip_of(dealt, LANES + 1 - sizes.extra_at)
    gap = FLUX_STEP * jnp.where(wide_odd, gap, turn(pick(both[total:], gap), -1))

    def gains(values):
        strip = strip_of(values, LANES - face_lane)
        met = pick(both, strip)
        met = jnp.where(wide_odd, turn(met[:total], 1), turn(met[total:], -1))
        gain = gap * (met - strip)
        return [gain[s * rows : (s + 1) * rows] for s in range(sections)]

    conds = [[turn(value, -width) for value in line] for line in dealt]
    edge = jnp.zeros(shape, jnp.float32)
    for k in range(members):
        line_ref[k, pl.ds(0, rows), :] = edge
        line_ref[k, pl.ds(rows + total, rows), :] = edge

    def with_product(value, cond):
        return jnp.where(spot_in_layer < 2 * width, value, turn(value * cond, 2 * width))

    def box_sum(values):
        for s in range(sections):
            other = [turn(value, half_lanes) for value in values[s]]
            for k in range(members):
                before = other[k - 1] if k else 0.0
                after = other[k + 1] if k < members - 1 else 0.0
                near = other[k] + jnp.where(lower_layer, before, after)
                line_ref[k, pl.ds(rows + s * rows, rows), :] = values[s][k] + 0.5 * near
        result = []
        for s in range(sections):
            line = []
            for k in range(members):
                start = rows + s * rows
                near = line_ref[k, pl.ds(start - 1, rows), :] + line_ref[k, pl.ds(start + 1, rows), :]
                value = line_ref[k, pl.ds(start, rows), :] + 0.5 * near
                line.append(value + from_inward * turn(value, 1) + from_outward * turn(value, -1))
            result.append(line)
        return result

    values = dealt
    keeps = None
    for sweep in range(SWEEPS):
        gain = gains(values)
        packed = [
            [with_product(value, cond) for value, cond in zip(*lines)]
            for lines in zip(values, conds)
        ]
        sums = box_sum(packed)
        if keeps is None:
            keeps = [
                [1.0 - weight * cond - turn(total_sum, -width) for cond, total_sum in zip(*lines)]
                for lines in zip(conds, sums)
            ]
        fresh = []
        for s in range(sections):
            line = []
            for k in range(members):
                temp = values[s][k] * keeps[s][k] + conds[s][k] * sums[s][k]
                temp = temp + turn(sums[s][k], -2 * width)
                back = pltpu.roll(gain[s], (face_lane - 2 * k + LANES) % LANES, 1)
                line.append(temp + at_face * back)
            fresh.append(line)
        values = fresh

    per_row = 8 // sizes.layers
    for s in range(sections):
        order = dealt[s][0][:, sizes.extra_at + 2 : sizes.extra_at + 3].astype(jnp.int32)
        order = jnp.broadcast_to(order, shape)
        for half in range(sizes.depth // 8):
            merged = jnp.zeros(shape, jnp.float32)
            for k in range(per_row):
                moved = turn(values[s][half * per_row + k], k * sizes.chunk - HALO)
                merged = jnp.where(spot_in_layer // sizes.chunk == k, moved, merged)
            chosen = jnp.take_along_axis(merged, order, axis=0)
            start = s * rows * (sizes.depth // 8) + half
            out_ref[pl.ds(start, rows, stride=sizes.depth // 8), :] = chosen


def swap_blocks(tile, block):
    sub = iota(tile.shape, 0)
    spot = iota(tile.shape, 1) // block
    for bit in (4, 2, 1):
        up = pltpu.roll(pltpu.roll(tile, 8 - bit, 0), bit * block, 1)
        down = pltpu.roll(pltpu.roll(tile, bit, 0), LANES - bit * block, 1)
        moved = jnp.where(sub & bit == 0, up, down)
        tile = jnp.where((sub & bit) == (spot & bit), tile, moved)
    return tile


def creep_kernel(sizes, active_ref, temps_ref, trial_ref, stress_ref, strain_ref):
    tiles = sizes.tiles
    halves = sizes.depth // 8
    active = active_ref[0, 0]
    sub = iota((8, LANES), 0)
    natural = sub % sizes.layers * (8 // sizes.layers) + sub // sizes.layers
    for tile in range(tiles):
        for element in range(halves):
            source = pl.ds(tile * 8 * halves + element, 8, stride=halves)
            mech_temp = swap_blocks(temps_ref[source, :], sizes.chunk)
            mech_temp = jnp.take_along_axis(mech_temp, natural, axis=0)
            spot = pl.ds(element * 8 * tiles + tile, 8, stride=tiles)
            trial = trial_ref[spot, :]
            rate = CREEP_RATE * jnp.exp(-ACTIVATION / (mech_temp + REFERENCE_TEMP))
            slip = jnp.zeros(trial.shape, jnp.float32)
            for newton_step in range(NEWTON):
                left = trial - slip
                pull = rate * left * left
                slip = slip - (slip - pull * left) / (1.0 + 3.0 * pull)
            creep = jnp.where(element < active, slip, 0.0)
            stress_ref[spot, :] = trial - creep
            strain_ref[pl.ds(element * tiles + tile, 1), :] = 0.125 * jnp.sum(
                creep, axis=0, keepdims=True
            )


def kernel_call(body, sizes, out_shape, memories, scratch, operands):
    out_spec = pl.BlockSpec(memory_space=pltpu.VMEM)
    pinned = [
        pltpu.with_memory_space_constraint(operand, memory) if memory is pltpu.HBM else operand
        for operand, memory in zip(operands, memories)
    ]
    return pl.pallas_call(
        functools.partial(body, sizes),
        out_shape=out_shape,
        in_specs=[pl.BlockSpec(memory_space=memory) for memory in memories],
        out_specs=[out_spec] * len(out_shape),
        scratch_shapes=scratch,
        compiler_params=pltpu.CompilerParams(vmem_limit_bytes=16 * 1024 * 1024),
    )(*pinned)


def on_device(
    temp_start, conductivity, gap_conductance, partner, row_order, active_layers, trial_stress
):
    layers, _, rows, radial = temp_start.shape
    sizes = Sizes(layers, rows, radial)
    if not fits_tiles(sizes):
        return stepwise(
            temp_start,
            conductivity,
            gap_conductance,
            partner,
            row_order,
            active_layers,
            trial_stress,
        )

    def floats(*shape):
        return jax.ShapeDtypeStruct(shape, jnp.float32)

    def near(*shape):
        return pltpu.VMEM(shape, jnp.float32)

    (dealt,) = kernel_call(
        deal_kernel,
        sizes,
        (near(sizes.devices, rows, LANES),),
        [pltpu.HBM] * 5,
        [
            pltpu.SMEM(partner.shape, jnp.int32),
            pltpu.SMEM(row_order.shape, jnp.int32),
            pltpu.SMEM(gap_conductance.shape, jnp.float32),
            pltpu.VMEM(temp_start.shape, jnp.float32),
            pltpu.VMEM(conductivity.shape, jnp.float32),
            pltpu.SemaphoreType.DMA((5,)),
        ],
        (partner, row_order, gap_conductance, temp_start, conductivity),
    )
    dealt = lax.all_to_all(dealt, EVERYONE, split_axis=0, concat_axis=0, tiled=True)
    halves = sizes.depth // 8
    (temps,) = kernel_call(
        sweep_kernel,
        sizes,
        (near(sizes.devices * halves, LANES),),
        [pltpu.VMEM],
        [pltpu.VMEM((sizes.members, rows * (sizes.sections + 2), LANES), jnp.float32)],
        (dealt,),
    )
    temps = temps.reshape(sizes.devices, halves, LANES)
    temps = lax.all_to_all(temps, EVERYONE, split_axis=0, concat_axis=0, tiled=True)
    stress, strain = kernel_call(
        creep_kernel,
        sizes,
        (floats(sizes.depth * sizes.tiles, LANES), floats(halves * sizes.tiles, LANES)),
        [pltpu.SMEM, pltpu.VMEM, pltpu.VMEM],
        [],
        (
            active_layers,
            temps.reshape(sizes.devices * halves, LANES),
            trial_stress.reshape(sizes.depth * sizes.tiles, LANES),
        ),
    )
    return (
        stress.reshape(sizes.depth, 1, 1, radial),
        strain.reshape(halves, 1, 1, radial),
    )


def solution(mesh):
    placed = (
        P(("slab", "mech"), "iface", None, None),
        P(("slab", "mech"), "iface", None, None),
        P(("slab", "mech"), "iface", None),
        P("iface"),
        P("iface", None),
        P("iface", ("slab", "mech")),
        P(None, "iface", ("slab", "mech"), None),
    )
    return jax.shard_map(
        on_device,
        mesh=mesh,
        in_specs=placed,
        out_specs=(
            P(None, "iface", ("slab", "mech"), None),
            P(None, "iface", ("slab", "mech"), None),
        ),
        check_vma=False,
    )
```

```python
import functools
import jax
import jax.numpy as jnp
from jax import lax
from jax.experimental import pallas as pl
from jax.experimental.pallas import tpu as pltpu
from jax.sharding import PartitionSpec as P

SWEEPS = 2
NEWTON = 4


FLUX_STEP = 0.03
CREEP_RATE = 200.0
ACTIVATION = 12.0
REFERENCE_TEMP = 1.0


def padded(block, sides, width):
    for axis, dim in sides:
        count = lax.axis_size(axis)
        forward = [(i, i + 1) for i in range(count - 1)]
        backward = [(target, source) for source, target in forward]
        low = lax.ppermute(
            lax.slice_in_dim(block, block.shape[dim] - width, None, axis=dim), axis, forward
        )
        high = lax.ppermute(lax.slice_in_dim(block, 0, width, axis=dim), axis, backward)
        block = jnp.concatenate([low, block, high], axis=dim)
    return block


def neighbour_weight(shift_z, shift_a, shift_r):
    reach = abs(shift_z) + abs(shift_a) + abs(shift_r)
    return [0.0, 1.0, 0.5, 0.25][reach]


def conduction(padded_temp, padded_cond):
    center_temp = padded_temp[1:-1, 1:-1, 1:-1]
    center_cond = padded_cond[1:-1, 1:-1, 1:-1]
    depth, across, radial = center_temp.shape
    radial_index = jnp.arange(radial, dtype=jnp.int32)
    gap_row = radial // 2
    outward_open = (radial_index != gap_row - 1).astype(jnp.float32)
    inward_open = (radial_index != gap_row).astype(jnp.float32)
    total = jnp.zeros(center_temp.shape, jnp.float32)
    for shift_z in (-1, 0, 1):
        for shift_a in (-1, 0, 1):
            for shift_r in (-1, 0, 1):
                if shift_z == 0 and shift_a == 0 and (shift_r == 0):
                    continue
                near_temp = padded_temp[
                    1 + shift_z : 1 + shift_z + depth,
                    1 + shift_a : 1 + shift_a + across,
                    1 + shift_r : 1 + shift_r + radial,
                ]
                near_cond = padded_cond[
                    1 + shift_z : 1 + shift_z + depth,
                    1 + shift_a : 1 + shift_a + across,
                    1 + shift_r : 1 + shift_r + radial,
                ]
                face = neighbour_weight(shift_z, shift_a, shift_r) * 0.5 * (center_cond + near_cond)
                if shift_r == 1:
                    face = face * outward_open
                elif shift_r == -1:
                    face = face * inward_open
                total = total + face * (near_temp - center_temp)
    return FLUX_STEP * total


def creep_return(mech_temp, trial, active_layers):
    rate = CREEP_RATE * jnp.exp(-ACTIVATION / (mech_temp + REFERENCE_TEMP))
    slip = jnp.zeros(trial.shape, jnp.float32)
    for newton_step in range(NEWTON):
        left = trial - slip
        residue = slip - rate * left**3
        slope = 1.0 + 3.0 * rate * left**2
        slip = slip - residue / slope
    depth = trial.shape[0]
    layer = jnp.arange(depth, dtype=jnp.int32) // 8
    live = (layer[:, None, None] < active_layers[None, :, :]).astype(jnp.float32)[..., None]
    creep = live * slip
    stress = trial - creep
    strain = jnp.sum(creep.reshape((depth // 8, 8) + trial.shape[1:]), axis=1) * 0.125
    return (stress, strain)


def stepwise(
    temp_start, conductivity, gap_conductance, partner, row_order, active_layers, trial_stress
):
    depth = temp_start.shape[0]
    rows = temp_start.shape[2]
    radial = temp_start.shape[3]
    temp = temp_start.reshape(depth, rows, radial)
    cond = conductivity.reshape(depth, rows, radial)
    gap = gap_conductance.reshape(depth, rows)
    gap_row = radial // 2
    sections = lax.axis_size("iface")
    across = rows * sections
    all_cols = jnp.arange(across, dtype=jnp.int32)
    cond_rim = padded(cond, ((("slab", "mech"), 0), ("iface", 1)), 1)
    padded_cond = jnp.pad(cond_rim, ((0, 0), (0, 0), (1, 1)))
    spread_table = (partner[:, None] == all_cols[None, :]).astype(jnp.float32)
    for sweep in range(SWEEPS):
        temp_rim = padded(temp, ((("slab", "mech"), 0), ("iface", 1)), 1)
        padded_temp = jnp.pad(temp_rim, ((0, 0), (0, 0), (1, 1)))
        compact = temp[:, :, gap_row - 1]
        canister = temp[:, :, gap_row]
        compact_all = lax.all_gather(compact, "iface", axis=1, tiled=True)
        facing = jnp.take(compact_all, partner, axis=1)
        flux = gap * (facing - canister)
        spread = jnp.dot(
            flux, spread_table, precision=lax.Precision.HIGHEST, preferred_element_type=jnp.float32
        )
        returned = lax.psum_scatter(spread, "iface", scatter_dimension=1, tiled=True)
        fresh = temp + conduction(padded_temp, padded_cond)
        temp = (
            fresh.at[:, :, gap_row]
            .add(FLUX_STEP * flux)
            .at[:, :, gap_row - 1]
            .add(-FLUX_STEP * returned)
        )
    permuted = jnp.take(temp, row_order[0], axis=1)
    mech_temp = lax.all_to_all(permuted, ("slab", "mech"), split_axis=1, concat_axis=0, tiled=True)
    mech_temp = mech_temp.reshape(mech_temp.shape[0], 1, mech_temp.shape[1], radial)
    return creep_return(mech_temp, trial_stress, active_layers)


LANES = 128
HALO = 2
EVERYONE = ("slab", "mech", "iface")


def iota(shape, axis):
    return lax.broadcasted_iota(jnp.int32, shape, axis)


class Sizes:
    def __init__(self, layers, rows, radial):
        self.layers = layers
        self.rows = rows
        self.radial = radial
        self.tiles = radial // LANES
        self.sections = lax.axis_size("iface")
        self.members = lax.axis_size("slab") * lax.axis_size("mech")
        self.devices = self.sections * self.members
        self.depth = layers * self.members
        self.chunk = radial // self.devices
        self.width = self.chunk + 2 * HALO
        self.field = layers * self.width
        self.gap_row = radial // 2


def fits_tiles(sizes):
    return (
        sizes.rows == 8
        and sizes.members == sizes.rows
        and sizes.layers == 2
        and sizes.sections * sizes.rows <= LANES
        and sizes.radial % sizes.devices == 0
        and sizes.chunk * 8 == LANES
        and sizes.radial % (2 * LANES) == 0
    )


def deal_kernel(
    sizes,
    partner_hbm,
    order_hbm,
    gap_hbm,
    temp_hbm,
    cond_hbm,
    out_ref,
    partner_ref,
    order_ref,
    gap_ref,
    temp_ref,
    cond_ref,
    sems,
):
    pairs = (
        (gap_hbm, gap_ref),
        (partner_hbm, partner_ref),
        (order_hbm, order_ref),
        (temp_hbm, temp_ref),
        (cond_hbm, cond_ref),
    )
    copies = [
        pltpu.make_async_copy(source, target, sems.at[index])
        for index, (source, target) in enumerate(pairs)
    ]
    for copy in copies:
        copy.start()
    for copy in copies[:3]:
        copy.wait()
    shape = (sizes.rows, LANES)
    lane = iota(shape, 1)
    sub = iota(shape, 0)
    extra_at = 2 * sizes.field
    extra = jnp.zeros(shape, jnp.float32)
    for row in range(sizes.rows):
        for layer in range(sizes.layers):
            spot = (sub == row) & (lane == extra_at + layer * sizes.width)
            extra = jnp.where(spot, gap_ref[layer, 0, row], extra)
        spot = (sub == row) & (lane == extra_at + 1)
        extra = jnp.where(spot, partner_ref[row].astype(jnp.float32), extra)
        spot = (sub == row) & (lane == extra_at + 2)
        extra = jnp.where(spot, order_ref[0, row].astype(jnp.float32), extra)
    for copy in copies[3:]:
        copy.wait()
    blocks = [
        [ref[layer, 0, :, pl.ds(tile * LANES, LANES)] for tile in range(sizes.tiles)]
        for ref in (temp_ref, cond_ref)
        for layer in range(sizes.layers)
    ]
    for device in range(sizes.devices):
        first = device * sizes.chunk - HALO
        packed = extra
        for index, block in enumerate(blocks):
            base = index * sizes.width
            for tile in range(sizes.tiles):
                low = max(first, tile * LANES)
                high = min(first + sizes.width, (tile + 1) * LANES)
                if low >= high:
                    continue
                moved = pltpu.roll(block[tile], (base - first + tile * LANES) % LANES, 1)
                spot = (lane >= base + low - first) & (lane < base + high - first)
                packed = jnp.where(spot, moved, packed)
        out_ref[device] = packed


def sweep_kernel(sizes, dealt_ref, out_ref):
    rows, width, field = sizes.rows, sizes.width, sizes.field
    sections, members = sizes.sections, sizes.members
    shape = (rows, LANES)
    lane = iota(shape, 1)
    sub = iota(shape, 0)
    place = lax.axis_index("slab") * lax.axis_size("mech") + lax.axis_index("mech")
    place = place * sections + lax.axis_index("iface")
    first = place * sizes.chunk - HALO
    segment = lane // width
    radius = first + lane % width
    lower_layer = segment % 2 == 0
    at_compact = radius == sizes.gap_row - 1
    at_canister = radius == sizes.gap_row
    in_grid = (radius >= 0) & (radius < sizes.radial)
    weight = jnp.where(at_compact | at_canister, 6.0, 8.0)
    is_temp = lane < field
    at_face = is_temp & (at_compact | at_canister)
    keep_temp = jnp.where(is_temp & in_grid, 1.0, 0.0)
    face_lane = sizes.gap_row - 1 - first

    def turn(value, shift):
        return pltpu.roll(value, shift % LANES, 1)

    dealt = [[dealt_ref[k * sections + s] for k in range(members)] for s in range(sections)]

    strip_lane = (lane < 2 * members) | ((lane >= width) & (lane < width + 2 * members))
    odd = (lane % width) % 2 == 1

    def strip_of(values, start):
        strips = []
        for s in range(sections):
            strip = jnp.zeros(shape, jnp.float32)
            for k in range(members):
                moved = pltpu.roll(values[s][k], (start + 2 * k + LANES) % LANES, 1)
                spot = ((lane % width) // 2 == k) & (lane < 2 * width)
                strip = jnp.where(spot, moved, strip)
            strips.append(strip)
        return jnp.concatenate(strips, axis=0)

    total = sections * rows
    meets = jnp.concatenate(
        [
            jnp.where(
                lane == dealt[s][0][:, 2 * field + 1 : 2 * field + 2].astype(jnp.int32), 1.0, 0.0
            )
            for s in range(sections)
        ]
        + [jnp.zeros((LANES - total, LANES), jnp.float32)],
        axis=0,
    )
    met_by = meets.T[:total, :total]
    meets = meets[:total, :total]
    both = jnp.concatenate([meets, met_by], axis=0)

    def pick(table, strip):
        return jnp.dot(
            table, strip, precision=lax.Precision.HIGHEST, preferred_element_type=jnp.float32
        )

    wide_odd = jnp.concatenate([odd] * sections, axis=0)
    gap = strip_of(dealt, 1 - 2 * field)
    gap = jnp.where(wide_odd, gap, turn(pick(met_by, gap), -1))

    def gains(values):
        strip = strip_of(values, LANES - face_lane)
        met = pick(both, strip)
        met = jnp.where(wide_odd, turn(met[:total], 1), turn(met[total:], -1))
        gain = FLUX_STEP * gap * (met - strip)
        return [gain[s * rows : (s + 1) * rows] for s in range(sections)]

    conds = [[turn(value, -field) for value in line] for line in dealt]

    def with_product(value, cond):
        return jnp.where(lane < 2 * field, value, turn(value * cond, 2 * field))

    def box_sum(values):
        summed = []
        for s in range(sections):
            less = [turn(value, -width) for value in values[s]]
            more = [turn(value, width) for value in values[s]]
            line = []
            for k in range(members):
                low = less[k] + (less[k - 1] if k else 0.0)
                high = more[k] + (more[k + 1] if k < members - 1 else 0.0)
                line.append(values[s][k] + 0.5 * jnp.where(lower_layer, low, high))
            summed.append(line)
        result = []
        up = [[pltpu.roll(value, 1, 0) for value in line] for line in summed]
        down = [[pltpu.roll(value, rows - 1, 0) for value in line] for line in summed]
        for s in range(sections):
            line = []
            for k in range(members):
                before = jnp.where(sub == 0, up[s - 1][k] if s else 0.0, up[s][k])
                after = jnp.where(
                    sub == rows - 1, down[s + 1][k] if s < sections - 1 else 0.0, down[s][k]
                )
                value = summed[s][k] + 0.5 * (before + after)
                inward = jnp.where(at_canister, 0.0, turn(value, 1))
                outward = jnp.where(at_compact, 0.0, turn(value, -1))
                line.append(value + 0.5 * (inward + outward))
            result.append(line)
        return result

    values = dealt
    cond_sums = None
    for sweep in range(SWEEPS):
        gain = gains(values)
        packed = [
            [with_product(value, cond) for value, cond in zip(*lines)]
            for lines in zip(values, conds)
        ]
        sums = box_sum(packed)
        if cond_sums is None:
            cond_sums = [[turn(total_sum, -field) for total_sum in line] for line in sums]
        fresh = []
        for s in range(sections):
            line = []
            for k in range(members):
                value = values[s][k]
                total_sum = sums[s][k]
                change = conds[s][k] * (total_sum - weight * value)
                change = change + turn(total_sum, -2 * field) - value * cond_sums[s][k]
                back = pltpu.roll(gain[s], (face_lane - 2 * k + LANES) % LANES, 1)
                temp = value + FLUX_STEP * change + jnp.where(at_face, back, 0.0)
                line.append(jnp.where(is_temp, keep_temp * temp, value))
            fresh.append(line)
        values = fresh

    per_row = 8 // sizes.layers
    for s in range(sections):
        order = dealt[s][0][:, 2 * field + 2 : 2 * field + 3].astype(jnp.int32)
        order = jnp.broadcast_to(order, shape)
        for half in range(sizes.depth // 8):
            merged = jnp.zeros(shape, jnp.float32)
            for k in range(per_row):
                for layer in range(sizes.layers):
                    spot = (k * sizes.layers + layer) * sizes.chunk
                    moved = turn(values[s][half * per_row + k], spot - layer * width - HALO)
                    merged = jnp.where(lane // sizes.chunk == spot // sizes.chunk, moved, merged)
            chosen = jnp.take_along_axis(merged, order, axis=0)
            start = s * (sizes.depth // 8) + half
            out_ref[pl.ds(start, rows, stride=sections * (sizes.depth // 8)), :] = chosen


def swap_blocks(tile, block):
    sub = iota(tile.shape, 0)
    spot = iota(tile.shape, 1) // block
    for bit in (4, 2, 1):
        up = pltpu.roll(pltpu.roll(tile, 8 - bit, 0), bit * block, 1)
        down = pltpu.roll(pltpu.roll(tile, bit, 0), LANES - bit * block, 1)
        moved = jnp.where(sub & bit == 0, up, down)
        tile = jnp.where((sub & bit) == (spot & bit), tile, moved)
    return tile


def creep_kernel(sizes, active_ref, temps_ref, trial_ref, stress_ref, strain_ref):
    tiles = sizes.tiles
    halves = sizes.depth // 8
    active = active_ref[0, 0]
    for tile in range(tiles):
        for element in range(halves):
            source = pl.ds(tile * 8 * halves + element, 8, stride=halves)
            mech_temp = swap_blocks(temps_ref[source, :], sizes.chunk)
            spot = pl.ds(element * 8 * tiles + tile, 8, stride=tiles)
            trial = trial_ref[spot, :]
            rate = CREEP_RATE * jnp.exp(-ACTIVATION / (mech_temp + REFERENCE_TEMP))
            slip = jnp.zeros(trial.shape, jnp.float32)
            for newton_step in range(NEWTON):
                left = trial - slip
                pull = rate * left * left
                slip = slip - (slip - pull * left) / (1.0 + 3.0 * pull)
            creep = jnp.where(element < active, slip, 0.0)
            stress_ref[spot, :] = trial - creep
            strain_ref[pl.ds(element * tiles + tile, 1), :] = 0.125 * jnp.sum(
                creep, axis=0, keepdims=True
            )


def kernel_call(body, sizes, out_shape, memories, scratch, operands):
    out_spec = pl.BlockSpec(memory_space=pltpu.VMEM)
    pinned = [
        pltpu.with_memory_space_constraint(operand, memory) if memory is pltpu.HBM else operand
        for operand, memory in zip(operands, memories)
    ]
    return pl.pallas_call(
        functools.partial(body, sizes),
        out_shape=out_shape,
        in_specs=[pl.BlockSpec(memory_space=memory) for memory in memories],
        out_specs=[out_spec] * len(out_shape),
        scratch_shapes=scratch,
        compiler_params=pltpu.CompilerParams(vmem_limit_bytes=16 * 1024 * 1024),
    )(*pinned)


def on_device(
    temp_start, conductivity, gap_conductance, partner, row_order, active_layers, trial_stress
):
    layers, _, rows, radial = temp_start.shape
    sizes = Sizes(layers, rows, radial)
    if not fits_tiles(sizes):
        return stepwise(
            temp_start,
            conductivity,
            gap_conductance,
            partner,
            row_order,
            active_layers,
            trial_stress,
        )

    def floats(*shape):
        return jax.ShapeDtypeStruct(shape, jnp.float32)

    def near(*shape):
        return pltpu.VMEM(shape, jnp.float32)

    (dealt,) = kernel_call(
        deal_kernel,
        sizes,
        (near(sizes.devices, rows, LANES),),
        [pltpu.HBM] * 5,
        [
            pltpu.SMEM(partner.shape, jnp.int32),
            pltpu.SMEM(row_order.shape, jnp.int32),
            pltpu.SMEM(gap_conductance.shape, jnp.float32),
            pltpu.VMEM(temp_start.shape, jnp.float32),
            pltpu.VMEM(conductivity.shape, jnp.float32),
            pltpu.SemaphoreType.DMA((5,)),
        ],
        (partner, row_order, gap_conductance, temp_start, conductivity),
    )
    dealt = lax.all_to_all(dealt, EVERYONE, split_axis=0, concat_axis=0, tiled=True)
    halves = sizes.depth // 8
    (temps,) = kernel_call(
        sweep_kernel,
        sizes,
        (near(sizes.devices * halves, LANES),),
        [pltpu.VMEM],
        [],
        (dealt,),
    )
    temps = temps.reshape(sizes.devices, halves, LANES)
    temps = lax.all_to_all(temps, EVERYONE, split_axis=0, concat_axis=0, tiled=True)
    stress, strain = kernel_call(
        creep_kernel,
        sizes,
        (floats(sizes.depth * sizes.tiles, LANES), floats(halves * sizes.tiles, LANES)),
        [pltpu.SMEM, pltpu.VMEM, pltpu.VMEM],
        [],
        (
            active_layers,
            temps.reshape(sizes.devices * halves, LANES),
            trial_stress.reshape(sizes.depth * sizes.tiles, LANES),
        ),
    )
    return (
        stress.reshape(sizes.depth, 1, 1, radial),
        strain.reshape(halves, 1, 1, radial),
    )


def solution(mesh):
    placed = (
        P(("slab", "mech"), "iface", None, None),
        P(("slab", "mech"), "iface", None, None),
        P(("slab", "mech"), "iface", None),
        P("iface"),
        P("iface", None),
        P("iface", ("slab", "mech")),
        P(None, "iface", ("slab", "mech"), None),
    )
    return jax.shard_map(
        on_device,
        mesh=mesh,
        in_specs=placed,
        out_specs=(
            P(None, "iface", ("slab", "mech"), None),
            P(None, "iface", ("slab", "mech"), None),
        ),
        check_vma=False,
    )
```

```python
import functools
import jax
import jax.numpy as jnp
from jax import lax
from jax.experimental import pallas as pl
from jax.experimental.pallas import tpu as pltpu
from jax.sharding import PartitionSpec as P

SWEEPS = 2
NEWTON = 4


FLUX_STEP = 0.03
CREEP_RATE = 200.0
ACTIVATION = 12.0
REFERENCE_TEMP = 1.0


def padded(block, sides, width):
    for axis, dim in sides:
        count = lax.axis_size(axis)
        forward = [(i, i + 1) for i in range(count - 1)]
        backward = [(target, source) for source, target in forward]
        low = lax.ppermute(
            lax.slice_in_dim(block, block.shape[dim] - width, None, axis=dim), axis, forward
        )
        high = lax.ppermute(lax.slice_in_dim(block, 0, width, axis=dim), axis, backward)
        block = jnp.concatenate([low, block, high], axis=dim)
    return block


def neighbour_weight(shift_z, shift_a, shift_r):
    reach = abs(shift_z) + abs(shift_a) + abs(shift_r)
    return [0.0, 1.0, 0.5, 0.25][reach]


def conduction(padded_temp, padded_cond):
    center_temp = padded_temp[1:-1, 1:-1, 1:-1]
    center_cond = padded_cond[1:-1, 1:-1, 1:-1]
    depth, across, radial = center_temp.shape
    radial_index = jnp.arange(radial, dtype=jnp.int32)
    gap_row = radial // 2
    outward_open = (radial_index != gap_row - 1).astype(jnp.float32)
    inward_open = (radial_index != gap_row).astype(jnp.float32)
    total = jnp.zeros(center_temp.shape, jnp.float32)
    for shift_z in (-1, 0, 1):
        for shift_a in (-1, 0, 1):
            for shift_r in (-1, 0, 1):
                if shift_z == 0 and shift_a == 0 and (shift_r == 0):
                    continue
                near_temp = padded_temp[
                    1 + shift_z : 1 + shift_z + depth,
                    1 + shift_a : 1 + shift_a + across,
                    1 + shift_r : 1 + shift_r + radial,
                ]
                near_cond = padded_cond[
                    1 + shift_z : 1 + shift_z + depth,
                    1 + shift_a : 1 + shift_a + across,
                    1 + shift_r : 1 + shift_r + radial,
                ]
                face = neighbour_weight(shift_z, shift_a, shift_r) * 0.5 * (center_cond + near_cond)
                if shift_r == 1:
                    face = face * outward_open
                elif shift_r == -1:
                    face = face * inward_open
                total = total + face * (near_temp - center_temp)
    return FLUX_STEP * total


def creep_return(mech_temp, trial, active_layers):
    rate = CREEP_RATE * jnp.exp(-ACTIVATION / (mech_temp + REFERENCE_TEMP))
    slip = jnp.zeros(trial.shape, jnp.float32)
    for newton_step in range(NEWTON):
        left = trial - slip
        residue = slip - rate * left**3
        slope = 1.0 + 3.0 * rate * left**2
        slip = slip - residue / slope
    depth = trial.shape[0]
    layer = jnp.arange(depth, dtype=jnp.int32) // 8
    live = (layer[:, None, None] < active_layers[None, :, :]).astype(jnp.float32)[..., None]
    creep = live * slip
    stress = trial - creep
    strain = jnp.sum(creep.reshape((depth // 8, 8) + trial.shape[1:]), axis=1) * 0.125
    return (stress, strain)


def stepwise(
    temp_start, conductivity, gap_conductance, partner, row_order, active_layers, trial_stress
):
    depth = temp_start.shape[0]
    rows = temp_start.shape[2]
    radial = temp_start.shape[3]
    temp = temp_start.reshape(depth, rows, radial)
    cond = conductivity.reshape(depth, rows, radial)
    gap = gap_conductance.reshape(depth, rows)
    gap_row = radial // 2
    sections = lax.axis_size("iface")
    across = rows * sections
    all_cols = jnp.arange(across, dtype=jnp.int32)
    cond_rim = padded(cond, ((("slab", "mech"), 0), ("iface", 1)), 1)
    padded_cond = jnp.pad(cond_rim, ((0, 0), (0, 0), (1, 1)))
    spread_table = (partner[:, None] == all_cols[None, :]).astype(jnp.float32)
    for sweep in range(SWEEPS):
        temp_rim = padded(temp, ((("slab", "mech"), 0), ("iface", 1)), 1)
        padded_temp = jnp.pad(temp_rim, ((0, 0), (0, 0), (1, 1)))
        compact = temp[:, :, gap_row - 1]
        canister = temp[:, :, gap_row]
        compact_all = lax.all_gather(compact, "iface", axis=1, tiled=True)
        facing = jnp.take(compact_all, partner, axis=1)
        flux = gap * (facing - canister)
        spread = jnp.dot(
            flux, spread_table, precision=lax.Precision.HIGHEST, preferred_element_type=jnp.float32
        )
        returned = lax.psum_scatter(spread, "iface", scatter_dimension=1, tiled=True)
        fresh = temp + conduction(padded_temp, padded_cond)
        temp = (
            fresh.at[:, :, gap_row]
            .add(FLUX_STEP * flux)
            .at[:, :, gap_row - 1]
            .add(-FLUX_STEP * returned)
        )
    permuted = jnp.take(temp, row_order[0], axis=1)
    mech_temp = lax.all_to_all(permuted, ("slab", "mech"), split_axis=1, concat_axis=0, tiled=True)
    mech_temp = mech_temp.reshape(mech_temp.shape[0], 1, mech_temp.shape[1], radial)
    return creep_return(mech_temp, trial_stress, active_layers)


LANES = 128
HALO = 2
EVERYONE = ("slab", "iface", "mech")


def iota(shape, axis):
    return lax.broadcasted_iota(jnp.int32, shape, axis)


class Sizes:
    def __init__(self, layers, rows, radial):
        self.layers = layers
        self.rows = rows
        self.radial = radial
        self.tiles = radial // LANES
        self.sections = lax.axis_size("iface")
        self.members = lax.axis_size("slab") * lax.axis_size("mech")
        self.devices = self.sections * self.members
        self.depth = layers * self.members
        self.chunk = radial // self.devices
        self.width = self.chunk + 2 * HALO
        self.field = layers * self.width
        self.gap_row = radial // 2


def fits_tiles(sizes):
    return (
        sizes.rows == 8
        and sizes.members == sizes.rows
        and sizes.layers == 2
        and sizes.sections * sizes.rows <= LANES
        and sizes.radial % sizes.devices == 0
        and sizes.chunk * 8 == LANES
        and sizes.radial % (2 * LANES) == 0
    )


def deal_kernel(
    sizes,
    partner_hbm,
    order_hbm,
    gap_hbm,
    temp_hbm,
    cond_hbm,
    out_ref,
    partner_ref,
    order_ref,
    gap_ref,
    temp_ref,
    cond_ref,
    sems,
):
    pairs = (
        (gap_hbm, gap_ref),
        (partner_hbm, partner_ref),
        (order_hbm, order_ref),
        (temp_hbm, temp_ref),
        (cond_hbm, cond_ref),
    )
    copies = [
        pltpu.make_async_copy(source, target, sems.at[index])
        for index, (source, target) in enumerate(pairs)
    ]
    for copy in copies:
        copy.start()
    for copy in copies[:3]:
        copy.wait()
    shape = (sizes.rows, LANES)
    lane = iota(shape, 1)
    sub = iota(shape, 0)
    extra_at = 2 * sizes.field
    extra = jnp.zeros(shape, jnp.float32)
    for row in range(sizes.rows):
        for layer in range(sizes.layers):
            spot = (sub == row) & (lane == extra_at + layer * sizes.width)
            extra = jnp.where(spot, gap_ref[layer, 0, row], extra)
        spot = (sub == row) & (lane == extra_at + 1)
        extra = jnp.where(spot, partner_ref[row].astype(jnp.float32), extra)
        spot = (sub == row) & (lane == extra_at + 2)
        extra = jnp.where(spot, order_ref[0, row].astype(jnp.float32), extra)
    for copy in copies[3:]:
        copy.wait()
    blocks = [
        [ref[layer, 0, :, pl.ds(tile * LANES, LANES)] for tile in range(sizes.tiles)]
        for ref in (temp_ref, cond_ref)
        for layer in range(sizes.layers)
    ]
    for device in range(sizes.devices):
        first = device * sizes.chunk - HALO
        packed = extra
        for index, block in enumerate(blocks):
            base = index * sizes.width
            for tile in range(sizes.tiles):
                low = max(first, tile * LANES)
                high = min(first + sizes.width, (tile + 1) * LANES)
                if low >= high:
                    continue
                moved = pltpu.roll(block[tile], (base - first + tile * LANES) % LANES, 1)
                spot = (lane >= base + low - first) & (lane < base + high - first)
                packed = jnp.where(spot, moved, packed)
        out_ref[device] = packed


def sweep_kernel(sizes, dealt_ref, out_ref):
    rows, width, field = sizes.rows, sizes.width, sizes.field
    sections, members = sizes.sections, sizes.members
    shape = (rows, LANES)
    lane = iota(shape, 1)
    sub = iota(shape, 0)
    per_slab = lax.axis_size("mech")

    def number(section, member):
        return (member // per_slab * sections + section) * per_slab + member % per_slab

    place = lax.axis_index("slab") * sections + lax.axis_index("iface")
    place = place * per_slab + lax.axis_index("mech")
    first = place * sizes.chunk - HALO
    segment = lane // width
    radius = first + lane % width
    lower_layer = segment % 2 == 0
    at_compact = radius == sizes.gap_row - 1
    at_canister = radius == sizes.gap_row
    in_grid = (radius >= 0) & (radius < sizes.radial)
    weight = jnp.where(at_compact | at_canister, 6.0, 8.0)
    is_temp = lane < field
    at_face = is_temp & (at_compact | at_canister)
    keep_temp = jnp.where(is_temp & in_grid, 1.0, 0.0)
    face_lane = sizes.gap_row - 1 - first

    def turn(value, shift):
        return pltpu.roll(value, shift % LANES, 1)

    dealt = [[dealt_ref[number(s, k)] for k in range(members)] for s in range(sections)]

    strip_lane = (lane < 2 * members) | ((lane >= width) & (lane < width + 2 * members))
    odd = (lane % width) % 2 == 1

    def strip_of(values, start):
        strips = []
        for s in range(sections):
            strip = jnp.zeros(shape, jnp.float32)
            for k in range(members):
                moved = pltpu.roll(values[s][k], (start + 2 * k + LANES) % LANES, 1)
                spot = ((lane % width) // 2 == k) & (lane < 2 * width)
                strip = jnp.where(spot, moved, strip)
            strips.append(strip)
        return jnp.concatenate(strips, axis=0)

    total = sections * rows
    meets = jnp.concatenate(
        [
            jnp.where(
                lane == dealt[s][0][:, 2 * field + 1 : 2 * field + 2].astype(jnp.int32), 1.0, 0.0
            )
            for s in range(sections)
        ]
        + [jnp.zeros((LANES - total, LANES), jnp.float32)],
        axis=0,
    )
    met_by = meets.T[:total, :total]
    meets = meets[:total, :total]
    both = jnp.concatenate([meets, met_by], axis=0)

    def pick(table, strip):
        return jnp.dot(
            table, strip, precision=lax.Precision.HIGHEST, preferred_element_type=jnp.float32
        )

    wide_odd = jnp.concatenate([odd] * sections, axis=0)
    gap = strip_of(dealt, 1 - 2 * field)
    gap = jnp.where(wide_odd, gap, turn(pick(met_by, gap), -1))

    def gains(values):
        strip = strip_of(values, LANES - face_lane)
        met = pick(both, strip)
        met = jnp.where(wide_odd, turn(met[:total], 1), turn(met[total:], -1))
        gain = FLUX_STEP * gap * (met - strip)
        return [gain[s * rows : (s + 1) * rows] for s in range(sections)]

    conds = [[turn(value, -field) for value in line] for line in dealt]

    def with_product(value, cond):
        return jnp.where(lane < 2 * field, value, turn(value * cond, 2 * field))

    def box_sum(values):
        summed = []
        for s in range(sections):
            less = [turn(value, -width) for value in values[s]]
            more = [turn(value, width) for value in values[s]]
            line = []
            for k in range(members):
                low = less[k] + (less[k - 1] if k else 0.0)
                high = more[k] + (more[k + 1] if k < members - 1 else 0.0)
                line.append(values[s][k] + 0.5 * jnp.where(lower_layer, low, high))
            summed.append(line)
        result = []
        up = [[pltpu.roll(value, 1, 0) for value in line] for line in summed]
        down = [[pltpu.roll(value, rows - 1, 0) for value in line] for line in summed]
        for s in range(sections):
            line = []
            for k in range(members):
                before = jnp.where(sub == 0, up[s - 1][k] if s else 0.0, up[s][k])
                after = jnp.where(
                    sub == rows - 1, down[s + 1][k] if s < sections - 1 else 0.0, down[s][k]
                )
                value = summed[s][k] + 0.5 * (before + after)
                inward = jnp.where(at_canister, 0.0, turn(value, 1))
                outward = jnp.where(at_compact, 0.0, turn(value, -1))
                line.append(value + 0.5 * (inward + outward))
            result.append(line)
        return result

    values = dealt
    cond_sums = None
    for sweep in range(SWEEPS):
        gain = gains(values)
        packed = [
            [with_product(value, cond) for value, cond in zip(*lines)]
            for lines in zip(values, conds)
        ]
        sums = box_sum(packed)
        if cond_sums is None:
            cond_sums = [[turn(total_sum, -field) for total_sum in line] for line in sums]
        fresh = []
        for s in range(sections):
            line = []
            for k in range(members):
                value = values[s][k]
                total_sum = sums[s][k]
                change = conds[s][k] * (total_sum - weight * value)
                change = change + turn(total_sum, -2 * field) - value * cond_sums[s][k]
                back = pltpu.roll(gain[s], (face_lane - 2 * k + LANES) % LANES, 1)
                temp = value + FLUX_STEP * change + jnp.where(at_face, back, 0.0)
                line.append(jnp.where(is_temp, keep_temp * temp, value))
            fresh.append(line)
        values = fresh

    per_row = 8 // sizes.layers
    for s in range(sections):
        order = dealt[s][0][:, 2 * field + 2 : 2 * field + 3].astype(jnp.int32)
        order = jnp.broadcast_to(order, shape)
        for half in range(sizes.depth // 8):
            merged = jnp.zeros(shape, jnp.float32)
            for k in range(per_row):
                for layer in range(sizes.layers):
                    spot = (k * sizes.layers + layer) * sizes.chunk
                    moved = turn(values[s][half * per_row + k], spot - layer * width - HALO)
                    merged = jnp.where(lane // sizes.chunk == spot // sizes.chunk, moved, merged)
            chosen = jnp.take_along_axis(merged, order, axis=0)
            halves = sizes.depth // 8
            for row in range(0, rows, per_slab):
                start = number(s, row) * halves + half
                out_ref[pl.ds(start, per_slab, stride=halves), :] = chosen[row : row + per_slab]


def swap_blocks(tile, block):
    sub = iota(tile.shape, 0)
    spot = iota(tile.shape, 1) // block
    for bit in (4, 2, 1):
        up = pltpu.roll(pltpu.roll(tile, 8 - bit, 0), bit * block, 1)
        down = pltpu.roll(pltpu.roll(tile, bit, 0), LANES - bit * block, 1)
        moved = jnp.where(sub & bit == 0, up, down)
        tile = jnp.where((sub & bit) == (spot & bit), tile, moved)
    return tile


def creep_kernel(sizes, active_ref, temps_ref, trial_ref, stress_ref, strain_ref):
    tiles = sizes.tiles
    halves = sizes.depth // 8
    active = active_ref[0, 0]
    for tile in range(tiles):
        for element in range(halves):
            source = pl.ds(tile * 8 * halves + element, 8, stride=halves)
            mech_temp = swap_blocks(temps_ref[source, :], sizes.chunk)
            spot = pl.ds(element * 8 * tiles + tile, 8, stride=tiles)
            trial = trial_ref[spot, :]
            rate = CREEP_RATE * jnp.exp(-ACTIVATION / (mech_temp + REFERENCE_TEMP))
            slip = jnp.zeros(trial.shape, jnp.float32)
            for newton_step in range(NEWTON):
                left = trial - slip
                pull = rate * left * left
                slip = slip - (slip - pull * left) / (1.0 + 3.0 * pull)
            creep = jnp.where(element < active, slip, 0.0)
            stress_ref[spot, :] = trial - creep
            strain_ref[pl.ds(element * tiles + tile, 1), :] = 0.125 * jnp.sum(
                creep, axis=0, keepdims=True
            )


def kernel_call(body, sizes, out_shape, memories, scratch, operands):
    out_spec = pl.BlockSpec(memory_space=pltpu.VMEM)
    pinned = [
        pltpu.with_memory_space_constraint(operand, memory) if memory is pltpu.HBM else operand
        for operand, memory in zip(operands, memories)
    ]
    return pl.pallas_call(
        functools.partial(body, sizes),
        out_shape=out_shape,
        in_specs=[pl.BlockSpec(memory_space=memory) for memory in memories],
        out_specs=[out_spec] * len(out_shape),
        scratch_shapes=scratch,
        compiler_params=pltpu.CompilerParams(vmem_limit_bytes=16 * 1024 * 1024),
    )(*pinned)


def on_device(
    temp_start, conductivity, gap_conductance, partner, row_order, active_layers, trial_stress
):
    layers, _, rows, radial = temp_start.shape
    sizes = Sizes(layers, rows, radial)
    if not fits_tiles(sizes):
        return stepwise(
            temp_start,
            conductivity,
            gap_conductance,
            partner,
            row_order,
            active_layers,
            trial_stress,
        )

    def floats(*shape):
        return jax.ShapeDtypeStruct(shape, jnp.float32)

    def near(*shape):
        return pltpu.VMEM(shape, jnp.float32)

    (dealt,) = kernel_call(
        deal_kernel,
        sizes,
        (near(sizes.devices, rows, LANES),),
        [pltpu.HBM] * 5,
        [
            pltpu.SMEM(partner.shape, jnp.int32),
            pltpu.SMEM(row_order.shape, jnp.int32),
            pltpu.SMEM(gap_conductance.shape, jnp.float32),
            pltpu.VMEM(temp_start.shape, jnp.float32),
            pltpu.VMEM(conductivity.shape, jnp.float32),
            pltpu.SemaphoreType.DMA((5,)),
        ],
        (partner, row_order, gap_conductance, temp_start, conductivity),
    )
    dealt = lax.all_to_all(dealt, EVERYONE, split_axis=0, concat_axis=0, tiled=True)
    halves = sizes.depth // 8
    (temps,) = kernel_call(
        sweep_kernel,
        sizes,
        (near(sizes.devices * halves, LANES),),
        [pltpu.VMEM],
        [],
        (dealt,),
    )
    temps = temps.reshape(sizes.devices, halves, LANES)
    temps = lax.all_to_all(temps, EVERYONE, split_axis=0, concat_axis=0, tiled=True)
    stress, strain = kernel_call(
        creep_kernel,
        sizes,
        (floats(sizes.depth * sizes.tiles, LANES), floats(halves * sizes.tiles, LANES)),
        [pltpu.SMEM, pltpu.VMEM, pltpu.VMEM],
        [],
        (
            active_layers,
            temps.reshape(sizes.devices * halves, LANES),
            trial_stress.reshape(sizes.depth * sizes.tiles, LANES),
        ),
    )
    return (
        stress.reshape(sizes.depth, 1, 1, radial),
        strain.reshape(halves, 1, 1, radial),
    )


def solution(mesh):
    placed = (
        P(("slab", "mech"), "iface", None, None),
        P(("slab", "mech"), "iface", None, None),
        P(("slab", "mech"), "iface", None),
        P("iface"),
        P("iface", None),
        P("iface", ("slab", "mech")),
        P(None, "iface", ("slab", "mech"), None),
    )
    return jax.shard_map(
        on_device,
        mesh=mesh,
        in_specs=placed,
        out_specs=(
            P(None, "iface", ("slab", "mech"), None),
            P(None, "iface", ("slab", "mech"), None),
        ),
        check_vma=False,
    )
```

```python
import functools
import jax
import jax.numpy as jnp
from jax import lax
from jax.experimental import pallas as pl
from jax.experimental.pallas import tpu as pltpu
from jax.sharding import PartitionSpec as P

SWEEPS = 2
NEWTON = 4


FLUX_STEP = 0.03
CREEP_RATE = 200.0
ACTIVATION = 12.0
REFERENCE_TEMP = 1.0


def padded(block, sides, width):
    for axis, dim in sides:
        count = lax.axis_size(axis)
        forward = [(i, i + 1) for i in range(count - 1)]
        backward = [(target, source) for source, target in forward]
        low = lax.ppermute(
            lax.slice_in_dim(block, block.shape[dim] - width, None, axis=dim), axis, forward
        )
        high = lax.ppermute(lax.slice_in_dim(block, 0, width, axis=dim), axis, backward)
        block = jnp.concatenate([low, block, high], axis=dim)
    return block


def neighbour_weight(shift_z, shift_a, shift_r):
    reach = abs(shift_z) + abs(shift_a) + abs(shift_r)
    return [0.0, 1.0, 0.5, 0.25][reach]


def conduction(padded_temp, padded_cond):
    center_temp = padded_temp[1:-1, 1:-1, 1:-1]
    center_cond = padded_cond[1:-1, 1:-1, 1:-1]
    depth, across, radial = center_temp.shape
    radial_index = jnp.arange(radial, dtype=jnp.int32)
    gap_row = radial // 2
    outward_open = (radial_index != gap_row - 1).astype(jnp.float32)
    inward_open = (radial_index != gap_row).astype(jnp.float32)
    total = jnp.zeros(center_temp.shape, jnp.float32)
    for shift_z in (-1, 0, 1):
        for shift_a in (-1, 0, 1):
            for shift_r in (-1, 0, 1):
                if shift_z == 0 and shift_a == 0 and (shift_r == 0):
                    continue
                near_temp = padded_temp[
                    1 + shift_z : 1 + shift_z + depth,
                    1 + shift_a : 1 + shift_a + across,
                    1 + shift_r : 1 + shift_r + radial,
                ]
                near_cond = padded_cond[
                    1 + shift_z : 1 + shift_z + depth,
                    1 + shift_a : 1 + shift_a + across,
                    1 + shift_r : 1 + shift_r + radial,
                ]
                face = neighbour_weight(shift_z, shift_a, shift_r) * 0.5 * (center_cond + near_cond)
                if shift_r == 1:
                    face = face * outward_open
                elif shift_r == -1:
                    face = face * inward_open
                total = total + face * (near_temp - center_temp)
    return FLUX_STEP * total


def creep_return(mech_temp, trial, active_layers):
    rate = CREEP_RATE * jnp.exp(-ACTIVATION / (mech_temp + REFERENCE_TEMP))
    slip = jnp.zeros(trial.shape, jnp.float32)
    for newton_step in range(NEWTON):
        left = trial - slip
        residue = slip - rate * left**3
        slope = 1.0 + 3.0 * rate * left**2
        slip = slip - residue / slope
    depth = trial.shape[0]
    layer = jnp.arange(depth, dtype=jnp.int32) // 8
    live = (layer[:, None, None] < active_layers[None, :, :]).astype(jnp.float32)[..., None]
    creep = live * slip
    stress = trial - creep
    strain = jnp.sum(creep.reshape((depth // 8, 8) + trial.shape[1:]), axis=1) * 0.125
    return (stress, strain)


def stepwise(
    temp_start, conductivity, gap_conductance, partner, row_order, active_layers, trial_stress
):
    depth = temp_start.shape[0]
    rows = temp_start.shape[2]
    radial = temp_start.shape[3]
    temp = temp_start.reshape(depth, rows, radial)
    cond = conductivity.reshape(depth, rows, radial)
    gap = gap_conductance.reshape(depth, rows)
    gap_row = radial // 2
    sections = lax.axis_size("iface")
    across = rows * sections
    all_cols = jnp.arange(across, dtype=jnp.int32)
    cond_rim = padded(cond, ((("slab", "mech"), 0), ("iface", 1)), 1)
    padded_cond = jnp.pad(cond_rim, ((0, 0), (0, 0), (1, 1)))
    spread_table = (partner[:, None] == all_cols[None, :]).astype(jnp.float32)
    for sweep in range(SWEEPS):
        temp_rim = padded(temp, ((("slab", "mech"), 0), ("iface", 1)), 1)
        padded_temp = jnp.pad(temp_rim, ((0, 0), (0, 0), (1, 1)))
        compact = temp[:, :, gap_row - 1]
        canister = temp[:, :, gap_row]
        compact_all = lax.all_gather(compact, "iface", axis=1, tiled=True)
        facing = jnp.take(compact_all, partner, axis=1)
        flux = gap * (facing - canister)
        spread = jnp.dot(
            flux, spread_table, precision=lax.Precision.HIGHEST, preferred_element_type=jnp.float32
        )
        returned = lax.psum_scatter(spread, "iface", scatter_dimension=1, tiled=True)
        fresh = temp + conduction(padded_temp, padded_cond)
        temp = (
            fresh.at[:, :, gap_row]
            .add(FLUX_STEP * flux)
            .at[:, :, gap_row - 1]
            .add(-FLUX_STEP * returned)
        )
    permuted = jnp.take(temp, row_order[0], axis=1)
    mech_temp = lax.all_to_all(permuted, ("slab", "mech"), split_axis=1, concat_axis=0, tiled=True)
    mech_temp = mech_temp.reshape(mech_temp.shape[0], 1, mech_temp.shape[1], radial)
    return creep_return(mech_temp, trial_stress, active_layers)


LANES = 128
HALO = 2
EVERYONE = ("iface", "slab", "mech")


def iota(shape, axis):
    return lax.broadcasted_iota(jnp.int32, shape, axis)


class Sizes:
    def __init__(self, layers, rows, radial):
        self.layers = layers
        self.rows = rows
        self.radial = radial
        self.tiles = radial // LANES
        self.sections = lax.axis_size("iface")
        self.members = lax.axis_size("slab") * lax.axis_size("mech")
        self.devices = self.sections * self.members
        self.depth = layers * self.members
        self.chunk = radial // self.devices
        self.width = self.chunk + 2 * HALO
        self.field = layers * self.width
        self.gap_row = radial // 2


def fits_tiles(sizes):
    return (
        sizes.rows == 8
        and sizes.members == sizes.rows
        and sizes.layers == 2
        and sizes.sections * sizes.rows <= LANES
        and sizes.radial % sizes.devices == 0
        and sizes.chunk * 8 == LANES
        and sizes.radial % (2 * LANES) == 0
    )


def deal_kernel(
    sizes,
    partner_hbm,
    order_hbm,
    gap_hbm,
    temp_hbm,
    cond_hbm,
    out_ref,
    partner_ref,
    order_ref,
    gap_ref,
    temp_ref,
    cond_ref,
    sems,
):
    pairs = (
        (gap_hbm, gap_ref),
        (partner_hbm, partner_ref),
        (order_hbm, order_ref),
        (temp_hbm, temp_ref),
        (cond_hbm, cond_ref),
    )
    copies = [
        pltpu.make_async_copy(source, target, sems.at[index])
        for index, (source, target) in enumerate(pairs)
    ]
    for copy in copies:
        copy.start()
    for copy in copies[:3]:
        copy.wait()
    shape = (sizes.rows, LANES)
    lane = iota(shape, 1)
    sub = iota(shape, 0)
    extra_at = 2 * sizes.field
    extra = jnp.zeros(shape, jnp.float32)
    for row in range(sizes.rows):
        for layer in range(sizes.layers):
            spot = (sub == row) & (lane == extra_at + layer * sizes.width)
            extra = jnp.where(spot, gap_ref[layer, 0, row], extra)
        spot = (sub == row) & (lane == extra_at + 1)
        extra = jnp.where(spot, partner_ref[row].astype(jnp.float32), extra)
        spot = (sub == row) & (lane == extra_at + 2)
        extra = jnp.where(spot, order_ref[0, sizes.rows - 1 - row].astype(jnp.float32), extra)
    for copy in copies[3:]:
        copy.wait()
    blocks = [
        [ref[layer, 0, :, pl.ds(tile * LANES, LANES)] for tile in range(sizes.tiles)]
        for ref in (temp_ref, cond_ref)
        for layer in range(sizes.layers)
    ]
    for device in range(sizes.devices):
        first = device * sizes.chunk - HALO
        packed = extra
        for index, block in enumerate(blocks):
            base = index * sizes.width
            for tile in range(sizes.tiles):
                low = max(first, tile * LANES)
                high = min(first + sizes.width, (tile + 1) * LANES)
                if low >= high:
                    continue
                moved = pltpu.roll(block[tile], (base - first + tile * LANES) % LANES, 1)
                spot = (lane >= base + low - first) & (lane < base + high - first)
                packed = jnp.where(spot, moved, packed)
        out_ref[device] = packed


def sweep_kernel(sizes, dealt_ref, out_ref):
    rows, width, field = sizes.rows, sizes.width, sizes.field
    sections, members = sizes.sections, sizes.members
    shape = (rows, LANES)
    lane = iota(shape, 1)
    sub = iota(shape, 0)
    place = lax.axis_index("iface") * members
    place = place + lax.axis_index("slab") * lax.axis_size("mech") + lax.axis_index("mech")
    place = sizes.devices - 1 - place
    first = place * sizes.chunk - HALO
    segment = lane // width
    radius = first + lane % width
    lower_layer = segment % 2 == 0
    at_compact = radius == sizes.gap_row - 1
    at_canister = radius == sizes.gap_row
    in_grid = (radius >= 0) & (radius < sizes.radial)
    weight = jnp.where(at_compact | at_canister, 6.0, 8.0)
    is_temp = lane < field
    at_face = is_temp & (at_compact | at_canister)
    keep_temp = jnp.where(is_temp & in_grid, 1.0, 0.0)
    face_lane = sizes.gap_row - 1 - first

    def turn(value, shift):
        return pltpu.roll(value, shift % LANES, 1)

    dealt = [[dealt_ref[sizes.devices - 1 - s * members - k] for k in range(members)] for s in range(sections)]

    strip_lane = (lane < 2 * members) | ((lane >= width) & (lane < width + 2 * members))
    odd = (lane % width) % 2 == 1

    def strip_of(values, start):
        strips = []
        for s in range(sections):
            strip = jnp.zeros(shape, jnp.float32)
            for k in range(members):
                moved = pltpu.roll(values[s][k], (start + 2 * k + LANES) % LANES, 1)
                spot = ((lane % width) // 2 == k) & (lane < 2 * width)
                strip = jnp.where(spot, moved, strip)
            strips.append(strip)
        return jnp.concatenate(strips, axis=0)

    total = sections * rows
    meets = jnp.concatenate(
        [
            jnp.where(
                lane == dealt[s][0][:, 2 * field + 1 : 2 * field + 2].astype(jnp.int32), 1.0, 0.0
            )
            for s in range(sections)
        ]
        + [jnp.zeros((LANES - total, LANES), jnp.float32)],
        axis=0,
    )
    met_by = meets.T[:total, :total]
    meets = meets[:total, :total]
    both = jnp.concatenate([meets, met_by], axis=0)

    def pick(table, strip):
        return jnp.dot(
            table, strip, precision=lax.Precision.HIGHEST, preferred_element_type=jnp.float32
        )

    wide_odd = jnp.concatenate([odd] * sections, axis=0)
    gap = strip_of(dealt, 1 - 2 * field)
    gap = jnp.where(wide_odd, gap, turn(pick(met_by, gap), -1))

    def gains(values):
        strip = strip_of(values, LANES - face_lane)
        met = pick(both, strip)
        met = jnp.where(wide_odd, turn(met[:total], 1), turn(met[total:], -1))
        gain = FLUX_STEP * gap * (met - strip)
        return [gain[s * rows : (s + 1) * rows] for s in range(sections)]

    conds = [[turn(value, -field) for value in line] for line in dealt]

    def with_product(value, cond):
        return jnp.where(lane < 2 * field, value, turn(value * cond, 2 * field))

    def box_sum(values):
        summed = []
        for s in range(sections):
            less = [turn(value, -width) for value in values[s]]
            more = [turn(value, width) for value in values[s]]
            line = []
            for k in range(members):
                low = less[k] + (less[k - 1] if k else 0.0)
                high = more[k] + (more[k + 1] if k < members - 1 else 0.0)
                line.append(values[s][k] + 0.5 * jnp.where(lower_layer, low, high))
            summed.append(line)
        result = []
        up = [[pltpu.roll(value, 1, 0) for value in line] for line in summed]
        down = [[pltpu.roll(value, rows - 1, 0) for value in line] for line in summed]
        for s in range(sections):
            line = []
            for k in range(members):
                before = jnp.where(sub == 0, up[s - 1][k] if s else 0.0, up[s][k])
                after = jnp.where(
                    sub == rows - 1, down[s + 1][k] if s < sections - 1 else 0.0, down[s][k]
                )
                value = summed[s][k] + 0.5 * (before + after)
                inward = jnp.where(at_canister, 0.0, turn(value, 1))
                outward = jnp.where(at_compact, 0.0, turn(value, -1))
                line.append(value + 0.5 * (inward + outward))
            result.append(line)
        return result

    values = dealt
    cond_sums = None
    for sweep in range(SWEEPS):
        gain = gains(values)
        packed = [
            [with_product(value, cond) for value, cond in zip(*lines)]
            for lines in zip(values, conds)
        ]
        sums = box_sum(packed)
        if cond_sums is None:
            cond_sums = [[turn(total_sum, -field) for total_sum in line] for line in sums]
        fresh = []
        for s in range(sections):
            line = []
            for k in range(members):
                value = values[s][k]
                total_sum = sums[s][k]
                change = conds[s][k] * (total_sum - weight * value)
                change = change + turn(total_sum, -2 * field) - value * cond_sums[s][k]
                back = pltpu.roll(gain[s], (face_lane - 2 * k + LANES) % LANES, 1)
                temp = value + FLUX_STEP * change + jnp.where(at_face, back, 0.0)
                line.append(jnp.where(is_temp, keep_temp * temp, value))
            fresh.append(line)
        values = fresh

    per_row = 8 // sizes.layers
    for s in range(sections):
        order = dealt[s][0][:, 2 * field + 2 : 2 * field + 3].astype(jnp.int32)
        order = jnp.broadcast_to(order, shape)
        for half in range(sizes.depth // 8):
            merged = jnp.zeros(shape, jnp.float32)
            for k in range(per_row):
                for layer in range(sizes.layers):
                    spot = (k * sizes.layers + layer) * sizes.chunk
                    moved = turn(values[s][half * per_row + k], spot - layer * width - HALO)
                    merged = jnp.where(lane // sizes.chunk == spot // sizes.chunk, moved, merged)
            chosen = jnp.take_along_axis(merged, order, axis=0)
            start = (sizes.devices - (s + 1) * rows) * (sizes.depth // 8) + half
            out_ref[pl.ds(start, rows, stride=sizes.depth // 8), :] = chosen


def swap_blocks(tile, block):
    sub = iota(tile.shape, 0)
    spot = iota(tile.shape, 1) // block
    for bit in (4, 2, 1):
        up = pltpu.roll(pltpu.roll(tile, 8 - bit, 0), bit * block, 1)
        down = pltpu.roll(pltpu.roll(tile, bit, 0), LANES - bit * block, 1)
        moved = jnp.where(sub & bit == 0, up, down)
        tile = jnp.where((sub & bit) == (spot & bit), tile, moved)
    return tile


def creep_kernel(sizes, active_ref, temps_ref, trial_ref, stress_ref, strain_ref):
    tiles = sizes.tiles
    halves = sizes.depth // 8
    active = active_ref[0, 0]
    for tile in range(tiles):
        for element in range(halves):
            source = pl.ds(tile * 8 * halves + element, 8, stride=halves)
            mech_temp = swap_blocks(temps_ref[source, :], sizes.chunk)
            spot = pl.ds(element * 8 * tiles + tile, 8, stride=tiles)
            trial = trial_ref[spot, :]
            rate = CREEP_RATE * jnp.exp(-ACTIVATION / (mech_temp + REFERENCE_TEMP))
            slip = jnp.zeros(trial.shape, jnp.float32)
            for newton_step in range(NEWTON):
                left = trial - slip
                pull = rate * left * left
                slip = slip - (slip - pull * left) / (1.0 + 3.0 * pull)
            creep = jnp.where(element < active, slip, 0.0)
            stress_ref[spot, :] = trial - creep
            strain_ref[pl.ds(element * tiles + tile, 1), :] = 0.125 * jnp.sum(
                creep, axis=0, keepdims=True
            )


def kernel_call(body, sizes, out_shape, memories, scratch, operands):
    out_spec = pl.BlockSpec(memory_space=pltpu.VMEM)
    pinned = [
        pltpu.with_memory_space_constraint(operand, memory) if memory is pltpu.HBM else operand
        for operand, memory in zip(operands, memories)
    ]
    return pl.pallas_call(
        functools.partial(body, sizes),
        out_shape=out_shape,
        in_specs=[pl.BlockSpec(memory_space=memory) for memory in memories],
        out_specs=[out_spec] * len(out_shape),
        scratch_shapes=scratch,
        compiler_params=pltpu.CompilerParams(vmem_limit_bytes=16 * 1024 * 1024),
    )(*pinned)


def exchanged(parts, sizes):
    return lax.all_to_all(
        parts,
        EVERYONE,
        split_axis=0,
        concat_axis=0,
        tiled=True,
        axis_index_groups=[list(range(sizes.devices - 1, -1, -1))],
    )


def on_device(
    temp_start, conductivity, gap_conductance, partner, row_order, active_layers, trial_stress
):
    layers, _, rows, radial = temp_start.shape
    sizes = Sizes(layers, rows, radial)
    if not fits_tiles(sizes):
        return stepwise(
            temp_start,
            conductivity,
            gap_conductance,
            partner,
            row_order,
            active_layers,
            trial_stress,
        )

    def floats(*shape):
        return jax.ShapeDtypeStruct(shape, jnp.float32)

    def near(*shape):
        return pltpu.VMEM(shape, jnp.float32)

    (dealt,) = kernel_call(
        deal_kernel,
        sizes,
        (near(sizes.devices, rows, LANES),),
        [pltpu.HBM] * 5,
        [
            pltpu.SMEM(partner.shape, jnp.int32),
            pltpu.SMEM(row_order.shape, jnp.int32),
            pltpu.SMEM(gap_conductance.shape, jnp.float32),
            pltpu.VMEM(temp_start.shape, jnp.float32),
            pltpu.VMEM(conductivity.shape, jnp.float32),
            pltpu.SemaphoreType.DMA((5,)),
        ],
        (partner, row_order, gap_conductance, temp_start, conductivity),
    )
    dealt = exchanged(dealt, sizes)
    halves = sizes.depth // 8
    (temps,) = kernel_call(
        sweep_kernel,
        sizes,
        (near(sizes.devices * halves, LANES),),
        [pltpu.VMEM],
        [],
        (dealt,),
    )
    temps = temps.reshape(sizes.devices, halves, LANES)
    temps = exchanged(temps, sizes)
    stress, strain = kernel_call(
        creep_kernel,
        sizes,
        (floats(sizes.depth * sizes.tiles, LANES), floats(halves * sizes.tiles, LANES)),
        [pltpu.SMEM, pltpu.VMEM, pltpu.VMEM],
        [],
        (
            active_layers,
            temps.reshape(sizes.devices * halves, LANES),
            trial_stress.reshape(sizes.depth * sizes.tiles, LANES),
        ),
    )
    return (
        stress.reshape(sizes.depth, 1, 1, radial),
        strain.reshape(halves, 1, 1, radial),
    )


def solution(mesh):
    placed = (
        P(("slab", "mech"), "iface", None, None),
        P(("slab", "mech"), "iface", None, None),
        P(("slab", "mech"), "iface", None),
        P("iface"),
        P("iface", None),
        P("iface", ("slab", "mech")),
        P(None, "iface", ("slab", "mech"), None),
    )
    return jax.shard_map(
        on_device,
        mesh=mesh,
        in_specs=placed,
        out_specs=(
            P(None, "iface", ("slab", "mech"), None),
            P(None, "iface", ("slab", "mech"), None),
        ),
        check_vma=False,
    )
```

```python
import functools
import jax
import jax.numpy as jnp
from jax import lax
from jax.experimental import pallas as pl
from jax.experimental.pallas import tpu as pltpu
from jax.sharding import PartitionSpec as P

SWEEPS = 2
NEWTON = 4


FLUX_STEP = 0.03
CREEP_RATE = 200.0
ACTIVATION = 12.0
REFERENCE_TEMP = 1.0


def padded(block, sides, width):
    for axis, dim in sides:
        count = lax.axis_size(axis)
        forward = [(i, i + 1) for i in range(count - 1)]
        backward = [(target, source) for source, target in forward]
        low = lax.ppermute(
            lax.slice_in_dim(block, block.shape[dim] - width, None, axis=dim), axis, forward
        )
        high = lax.ppermute(lax.slice_in_dim(block, 0, width, axis=dim), axis, backward)
        block = jnp.concatenate([low, block, high], axis=dim)
    return block


def neighbour_weight(shift_z, shift_a, shift_r):
    reach = abs(shift_z) + abs(shift_a) + abs(shift_r)
    return [0.0, 1.0, 0.5, 0.25][reach]


def conduction(padded_temp, padded_cond):
    center_temp = padded_temp[1:-1, 1:-1, 1:-1]
    center_cond = padded_cond[1:-1, 1:-1, 1:-1]
    depth, across, radial = center_temp.shape
    radial_index = jnp.arange(radial, dtype=jnp.int32)
    gap_row = radial // 2
    outward_open = (radial_index != gap_row - 1).astype(jnp.float32)
    inward_open = (radial_index != gap_row).astype(jnp.float32)
    total = jnp.zeros(center_temp.shape, jnp.float32)
    for shift_z in (-1, 0, 1):
        for shift_a in (-1, 0, 1):
            for shift_r in (-1, 0, 1):
                if shift_z == 0 and shift_a == 0 and (shift_r == 0):
                    continue
                near_temp = padded_temp[
                    1 + shift_z : 1 + shift_z + depth,
                    1 + shift_a : 1 + shift_a + across,
                    1 + shift_r : 1 + shift_r + radial,
                ]
                near_cond = padded_cond[
                    1 + shift_z : 1 + shift_z + depth,
                    1 + shift_a : 1 + shift_a + across,
                    1 + shift_r : 1 + shift_r + radial,
                ]
                face = neighbour_weight(shift_z, shift_a, shift_r) * 0.5 * (center_cond + near_cond)
                if shift_r == 1:
                    face = face * outward_open
                elif shift_r == -1:
                    face = face * inward_open
                total = total + face * (near_temp - center_temp)
    return FLUX_STEP * total


def creep_return(mech_temp, trial, active_layers):
    rate = CREEP_RATE * jnp.exp(-ACTIVATION / (mech_temp + REFERENCE_TEMP))
    slip = jnp.zeros(trial.shape, jnp.float32)
    for newton_step in range(NEWTON):
        left = trial - slip
        residue = slip - rate * left**3
        slope = 1.0 + 3.0 * rate * left**2
        slip = slip - residue / slope
    depth = trial.shape[0]
    layer = jnp.arange(depth, dtype=jnp.int32) // 8
    live = (layer[:, None, None] < active_layers[None, :, :]).astype(jnp.float32)[..., None]
    creep = live * slip
    stress = trial - creep
    strain = jnp.sum(creep.reshape((depth // 8, 8) + trial.shape[1:]), axis=1) * 0.125
    return (stress, strain)


def stepwise(
    temp_start, conductivity, gap_conductance, partner, row_order, active_layers, trial_stress
):
    depth = temp_start.shape[0]
    rows = temp_start.shape[2]
    radial = temp_start.shape[3]
    temp = temp_start.reshape(depth, rows, radial)
    cond = conductivity.reshape(depth, rows, radial)
    gap = gap_conductance.reshape(depth, rows)
    gap_row = radial // 2
    sections = lax.axis_size("iface")
    across = rows * sections
    all_cols = jnp.arange(across, dtype=jnp.int32)
    cond_rim = padded(cond, ((("slab", "mech"), 0), ("iface", 1)), 1)
    padded_cond = jnp.pad(cond_rim, ((0, 0), (0, 0), (1, 1)))
    spread_table = (partner[:, None] == all_cols[None, :]).astype(jnp.float32)
    for sweep in range(SWEEPS):
        temp_rim = padded(temp, ((("slab", "mech"), 0), ("iface", 1)), 1)
        padded_temp = jnp.pad(temp_rim, ((0, 0), (0, 0), (1, 1)))
        compact = temp[:, :, gap_row - 1]
        canister = temp[:, :, gap_row]
        compact_all = lax.all_gather(compact, "iface", axis=1, tiled=True)
        facing = jnp.take(compact_all, partner, axis=1)
        flux = gap * (facing - canister)
        spread = jnp.dot(
            flux, spread_table, precision=lax.Precision.HIGHEST, preferred_element_type=jnp.float32
        )
        returned = lax.psum_scatter(spread, "iface", scatter_dimension=1, tiled=True)
        fresh = temp + conduction(padded_temp, padded_cond)
        temp = (
            fresh.at[:, :, gap_row]
            .add(FLUX_STEP * flux)
            .at[:, :, gap_row - 1]
            .add(-FLUX_STEP * returned)
        )
    permuted = jnp.take(temp, row_order[0], axis=1)
    mech_temp = lax.all_to_all(permuted, ("slab", "mech"), split_axis=1, concat_axis=0, tiled=True)
    mech_temp = mech_temp.reshape(mech_temp.shape[0], 1, mech_temp.shape[1], radial)
    return creep_return(mech_temp, trial_stress, active_layers)


LANES = 128
HALO = 2
EVERYONE = ("mech", "slab", "iface")


def iota(shape, axis):
    return lax.broadcasted_iota(jnp.int32, shape, axis)


class Sizes:
    def __init__(self, layers, rows, radial):
        self.layers = layers
        self.rows = rows
        self.radial = radial
        self.tiles = radial // LANES
        self.sections = lax.axis_size("iface")
        self.members = lax.axis_size("slab") * lax.axis_size("mech")
        self.devices = self.sections * self.members
        self.depth = layers * self.members
        self.chunk = radial // self.devices
        self.width = self.chunk + 2 * HALO
        self.field = layers * self.width
        self.gap_row = radial // 2


def fits_tiles(sizes):
    return (
        sizes.rows == 8
        and sizes.members == sizes.rows
        and sizes.layers == 2
        and sizes.sections * sizes.rows <= LANES
        and sizes.radial % sizes.devices == 0
        and sizes.chunk * 8 == LANES
        and sizes.radial % (2 * LANES) == 0
    )


def deal_kernel(
    sizes,
    partner_hbm,
    order_hbm,
    gap_hbm,
    temp_hbm,
    cond_hbm,
    out_ref,
    partner_ref,
    order_ref,
    gap_ref,
    temp_ref,
    cond_ref,
    sems,
):
    pairs = (
        (gap_hbm, gap_ref),
        (partner_hbm, partner_ref),
        (order_hbm, order_ref),
        (temp_hbm, temp_ref),
        (cond_hbm, cond_ref),
    )
    copies = [
        pltpu.make_async_copy(source, target, sems.at[index])
        for index, (source, target) in enumerate(pairs)
    ]
    for copy in copies:
        copy.start()
    for copy in copies[:3]:
        copy.wait()
    shape = (sizes.rows, LANES)
    lane = iota(shape, 1)
    sub = iota(shape, 0)
    extra_at = 2 * sizes.field
    extra = jnp.zeros(shape, jnp.float32)
    for row in range(sizes.rows):
        for layer in range(sizes.layers):
            spot = (sub == row) & (lane == extra_at + layer * sizes.width)
            extra = jnp.where(spot, gap_ref[layer, 0, row], extra)
        spot = (sub == row) & (lane == extra_at + 1)
        extra = jnp.where(spot, partner_ref[row].astype(jnp.float32), extra)
        spot = (sub == row) & (lane == extra_at + 2)
        extra = jnp.where(spot, order_ref[0, row].astype(jnp.float32), extra)
    for copy in copies[3:]:
        copy.wait()
    blocks = [
        [ref[layer, 0, :, pl.ds(tile * LANES, LANES)] for tile in range(sizes.tiles)]
        for ref in (temp_ref, cond_ref)
        for layer in range(sizes.layers)
    ]
    for device in range(sizes.devices):
        first = device * sizes.chunk - HALO
        packed = extra
        for index, block in enumerate(blocks):
            base = index * sizes.width
            for tile in range(sizes.tiles):
                low = max(first, tile * LANES)
                high = min(first + sizes.width, (tile + 1) * LANES)
                if low >= high:
                    continue
                moved = pltpu.roll(block[tile], (base - first + tile * LANES) % LANES, 1)
                spot = (lane >= base + low - first) & (lane < base + high - first)
                packed = jnp.where(spot, moved, packed)
        out_ref[device] = packed


def sweep_kernel(sizes, dealt_ref, out_ref):
    rows, width, field = sizes.rows, sizes.width, sizes.field
    sections, members = sizes.sections, sizes.members
    shape = (rows, LANES)
    lane = iota(shape, 1)
    sub = iota(shape, 0)
    slabs, per_slab = lax.axis_size("slab"), lax.axis_size("mech")

    def number(section, member):
        return (member % per_slab * slabs + member // per_slab) * sections + section

    place = lax.axis_index("mech") * slabs + lax.axis_index("slab")
    place = place * sections + lax.axis_index("iface")
    first = place * sizes.chunk - HALO
    segment = lane // width
    radius = first + lane % width
    lower_layer = segment % 2 == 0
    at_compact = radius == sizes.gap_row - 1
    at_canister = radius == sizes.gap_row
    in_grid = (radius >= 0) & (radius < sizes.radial)
    weight = jnp.where(at_compact | at_canister, 6.0, 8.0)
    is_temp = lane < field
    at_face = is_temp & (at_compact | at_canister)
    keep_temp = jnp.where(is_temp & in_grid, 1.0, 0.0)
    face_lane = sizes.gap_row - 1 - first

    def turn(value, shift):
        return pltpu.roll(value, shift % LANES, 1)

    dealt = [[dealt_ref[number(s, k)] for k in range(members)] for s in range(sections)]

    strip_lane = (lane < 2 * members) | ((lane >= width) & (lane < width + 2 * members))
    odd = (lane % width) % 2 == 1

    def strip_of(values, start):
        strips = []
        for s in range(sections):
            strip = jnp.zeros(shape, jnp.float32)
            for k in range(members):
                moved = pltpu.roll(values[s][k], (start + 2 * k + LANES) % LANES, 1)
                spot = ((lane % width) // 2 == k) & (lane < 2 * width)
                strip = jnp.where(spot, moved, strip)
            strips.append(strip)
        return jnp.concatenate(strips, axis=0)

    total = sections * rows
    meets = jnp.concatenate(
        [
            jnp.where(
                lane == dealt[s][0][:, 2 * field + 1 : 2 * field + 2].astype(jnp.int32), 1.0, 0.0
            )
            for s in range(sections)
        ]
        + [jnp.zeros((LANES - total, LANES), jnp.float32)],
        axis=0,
    )
    met_by = meets.T[:total, :total]
    meets = meets[:total, :total]
    both = jnp.concatenate([meets, met_by], axis=0)

    def pick(table, strip):
        return jnp.dot(
            table, strip, precision=lax.Precision.HIGHEST, preferred_element_type=jnp.float32
        )

    wide_odd = jnp.concatenate([odd] * sections, axis=0)
    gap = strip_of(dealt, 1 - 2 * field)
    gap = jnp.where(wide_odd, gap, turn(pick(met_by, gap), -1))

    def gains(values):
        strip = strip_of(values, LANES - face_lane)
        met = pick(both, strip)
        met = jnp.where(wide_odd, turn(met[:total], 1), turn(met[total:], -1))
        gain = FLUX_STEP * gap * (met - strip)
        return [gain[s * rows : (s + 1) * rows] for s in range(sections)]

    conds = [[turn(value, -field) for value in line] for line in dealt]

    def with_product(value, cond):
        return jnp.where(lane < 2 * field, value, turn(value * cond, 2 * field))

    def box_sum(values):
        summed = []
        for s in range(sections):
            less = [turn(value, -width) for value in values[s]]
            more = [turn(value, width) for value in values[s]]
            line = []
            for k in range(members):
                low = less[k] + (less[k - 1] if k else 0.0)
                high = more[k] + (more[k + 1] if k < members - 1 else 0.0)
                line.append(values[s][k] + 0.5 * jnp.where(lower_layer, low, high))
            summed.append(line)
        result = []
        up = [[pltpu.roll(value, 1, 0) for value in line] for line in summed]
        down = [[pltpu.roll(value, rows - 1, 0) for value in line] for line in summed]
        for s in range(sections):
            line = []
            for k in range(members):
                before = jnp.where(sub == 0, up[s - 1][k] if s else 0.0, up[s][k])
                after = jnp.where(
                    sub == rows - 1, down[s + 1][k] if s < sections - 1 else 0.0, down[s][k]
                )
                value = summed[s][k] + 0.5 * (before + after)
                inward = jnp.where(at_canister, 0.0, turn(value, 1))
                outward = jnp.where(at_compact, 0.0, turn(value, -1))
                line.append(value + 0.5 * (inward + outward))
            result.append(line)
        return result

    values = dealt
    cond_sums = None
    for sweep in range(SWEEPS):
        gain = gains(values)
        packed = [
            [with_product(value, cond) for value, cond in zip(*lines)]
            for lines in zip(values, conds)
        ]
        sums = box_sum(packed)
        if cond_sums is None:
            cond_sums = [[turn(total_sum, -field) for total_sum in line] for line in sums]
        fresh = []
        for s in range(sections):
            line = []
            for k in range(members):
                value = values[s][k]
                total_sum = sums[s][k]
                change = conds[s][k] * (total_sum - weight * value)
                change = change + turn(total_sum, -2 * field) - value * cond_sums[s][k]
                back = pltpu.roll(gain[s], (face_lane - 2 * k + LANES) % LANES, 1)
                temp = value + FLUX_STEP * change + jnp.where(at_face, back, 0.0)
                line.append(jnp.where(is_temp, keep_temp * temp, value))
            fresh.append(line)
        values = fresh

    per_row = 8 // sizes.layers
    for s in range(sections):
        order = dealt[s][0][:, 2 * field + 2 : 2 * field + 3].astype(jnp.int32)
        order = jnp.broadcast_to(order, shape)
        for half in range(sizes.depth // 8):
            merged = jnp.zeros(shape, jnp.float32)
            for k in range(per_row):
                for layer in range(sizes.layers):
                    spot = (k * sizes.layers + layer) * sizes.chunk
                    moved = turn(values[s][half * per_row + k], spot - layer * width - HALO)
                    merged = jnp.where(lane // sizes.chunk == spot // sizes.chunk, moved, merged)
            chosen = jnp.take_along_axis(merged, order, axis=0)
            halves = sizes.depth // 8
            stride = halves * slabs * sections
            for row in range(0, rows, per_slab):
                start = number(s, row) * halves + half
                out_ref[pl.ds(start, per_slab, stride=stride), :] = chosen[row : row + per_slab]


def swap_blocks(tile, block):
    sub = iota(tile.shape, 0)
    spot = iota(tile.shape, 1) // block
    for bit in (4, 2, 1):
        up = pltpu.roll(pltpu.roll(tile, 8 - bit, 0), bit * block, 1)
        down = pltpu.roll(pltpu.roll(tile, bit, 0), LANES - bit * block, 1)
        moved = jnp.where(sub & bit == 0, up, down)
        tile = jnp.where((sub & bit) == (spot & bit), tile, moved)
    return tile


def creep_kernel(sizes, active_ref, temps_ref, trial_ref, stress_ref, strain_ref):
    tiles = sizes.tiles
    halves = sizes.depth // 8
    active = active_ref[0, 0]
    for tile in range(tiles):
        for element in range(halves):
            source = pl.ds(tile * 8 * halves + element, 8, stride=halves)
            mech_temp = swap_blocks(temps_ref[source, :], sizes.chunk)
            spot = pl.ds(element * 8 * tiles + tile, 8, stride=tiles)
            trial = trial_ref[spot, :]
            rate = CREEP_RATE * jnp.exp(-ACTIVATION / (mech_temp + REFERENCE_TEMP))
            slip = jnp.zeros(trial.shape, jnp.float32)
            for newton_step in range(NEWTON):
                left = trial - slip
                pull = rate * left * left
                slip = slip - (slip - pull * left) / (1.0 + 3.0 * pull)
            creep = jnp.where(element < active, slip, 0.0)
            stress_ref[spot, :] = trial - creep
            strain_ref[pl.ds(element * tiles + tile, 1), :] = 0.125 * jnp.sum(
                creep, axis=0, keepdims=True
            )


def kernel_call(body, sizes, out_shape, memories, scratch, operands):
    out_spec = pl.BlockSpec(memory_space=pltpu.VMEM)
    pinned = [
        pltpu.with_memory_space_constraint(operand, memory) if memory is pltpu.HBM else operand
        for operand, memory in zip(operands, memories)
    ]
    return pl.pallas_call(
        functools.partial(body, sizes),
        out_shape=out_shape,
        in_specs=[pl.BlockSpec(memory_space=memory) for memory in memories],
        out_specs=[out_spec] * len(out_shape),
        scratch_shapes=scratch,
        compiler_params=pltpu.CompilerParams(vmem_limit_bytes=16 * 1024 * 1024),
    )(*pinned)


def on_device(
    temp_start, conductivity, gap_conductance, partner, row_order, active_layers, trial_stress
):
    layers, _, rows, radial = temp_start.shape
    sizes = Sizes(layers, rows, radial)
    if not fits_tiles(sizes):
        return stepwise(
            temp_start,
            conductivity,
            gap_conductance,
            partner,
            row_order,
            active_layers,
            trial_stress,
        )

    def floats(*shape):
        return jax.ShapeDtypeStruct(shape, jnp.float32)

    def near(*shape):
        return pltpu.VMEM(shape, jnp.float32)

    (dealt,) = kernel_call(
        deal_kernel,
        sizes,
        (near(sizes.devices, rows, LANES),),
        [pltpu.HBM] * 5,
        [
            pltpu.SMEM(partner.shape, jnp.int32),
            pltpu.SMEM(row_order.shape, jnp.int32),
            pltpu.SMEM(gap_conductance.shape, jnp.float32),
            pltpu.VMEM(temp_start.shape, jnp.float32),
            pltpu.VMEM(conductivity.shape, jnp.float32),
            pltpu.SemaphoreType.DMA((5,)),
        ],
        (partner, row_order, gap_conductance, temp_start, conductivity),
    )
    dealt = lax.all_to_all(dealt, EVERYONE, split_axis=0, concat_axis=0, tiled=True)
    halves = sizes.depth // 8
    (temps,) = kernel_call(
        sweep_kernel,
        sizes,
        (near(sizes.devices * halves, LANES),),
        [pltpu.VMEM],
        [],
        (dealt,),
    )
    temps = temps.reshape(sizes.devices, halves, LANES)
    temps = lax.all_to_all(temps, EVERYONE, split_axis=0, concat_axis=0, tiled=True)
    stress, strain = kernel_call(
        creep_kernel,
        sizes,
        (floats(sizes.depth * sizes.tiles, LANES), floats(halves * sizes.tiles, LANES)),
        [pltpu.SMEM, pltpu.VMEM, pltpu.VMEM],
        [],
        (
            active_layers,
            temps.reshape(sizes.devices * halves, LANES),
            trial_stress.reshape(sizes.depth * sizes.tiles, LANES),
        ),
    )
    return (
        stress.reshape(sizes.depth, 1, 1, radial),
        strain.reshape(halves, 1, 1, radial),
    )


def solution(mesh):
    placed = (
        P(("slab", "mech"), "iface", None, None),
        P(("slab", "mech"), "iface", None, None),
        P(("slab", "mech"), "iface", None),
        P("iface"),
        P("iface", None),
        P("iface", ("slab", "mech")),
        P(None, "iface", ("slab", "mech"), None),
    )
    return jax.shard_map(
        on_device,
        mesh=mesh,
        in_specs=placed,
        out_specs=(
            P(None, "iface", ("slab", "mech"), None),
            P(None, "iface", ("slab", "mech"), None),
        ),
        check_vma=False,
    )
```

```python
import functools
import jax
import jax.numpy as jnp
from jax import lax
from jax.experimental import pallas as pl
from jax.experimental.pallas import tpu as pltpu
from jax.sharding import PartitionSpec as P

SWEEPS = 2
NEWTON = 4


FLUX_STEP = 0.03
CREEP_RATE = 200.0
ACTIVATION = 12.0
REFERENCE_TEMP = 1.0


def padded(block, sides, width):
    for axis, dim in sides:
        count = lax.axis_size(axis)
        forward = [(i, i + 1) for i in range(count - 1)]
        backward = [(target, source) for source, target in forward]
        low = lax.ppermute(
            lax.slice_in_dim(block, block.shape[dim] - width, None, axis=dim), axis, forward
        )
        high = lax.ppermute(lax.slice_in_dim(block, 0, width, axis=dim), axis, backward)
        block = jnp.concatenate([low, block, high], axis=dim)
    return block


def neighbour_weight(shift_z, shift_a, shift_r):
    reach = abs(shift_z) + abs(shift_a) + abs(shift_r)
    return [0.0, 1.0, 0.5, 0.25][reach]


def conduction(padded_temp, padded_cond):
    center_temp = padded_temp[1:-1, 1:-1, 1:-1]
    center_cond = padded_cond[1:-1, 1:-1, 1:-1]
    depth, across, radial = center_temp.shape
    radial_index = jnp.arange(radial, dtype=jnp.int32)
    gap_row = radial // 2
    outward_open = (radial_index != gap_row - 1).astype(jnp.float32)
    inward_open = (radial_index != gap_row).astype(jnp.float32)
    total = jnp.zeros(center_temp.shape, jnp.float32)
    for shift_z in (-1, 0, 1):
        for shift_a in (-1, 0, 1):
            for shift_r in (-1, 0, 1):
                if shift_z == 0 and shift_a == 0 and (shift_r == 0):
                    continue
                near_temp = padded_temp[
                    1 + shift_z : 1 + shift_z + depth,
                    1 + shift_a : 1 + shift_a + across,
                    1 + shift_r : 1 + shift_r + radial,
                ]
                near_cond = padded_cond[
                    1 + shift_z : 1 + shift_z + depth,
                    1 + shift_a : 1 + shift_a + across,
                    1 + shift_r : 1 + shift_r + radial,
                ]
                face = neighbour_weight(shift_z, shift_a, shift_r) * 0.5 * (center_cond + near_cond)
                if shift_r == 1:
                    face = face * outward_open
                elif shift_r == -1:
                    face = face * inward_open
                total = total + face * (near_temp - center_temp)
    return FLUX_STEP * total


def creep_return(mech_temp, trial, active_layers):
    rate = CREEP_RATE * jnp.exp(-ACTIVATION / (mech_temp + REFERENCE_TEMP))
    slip = jnp.zeros(trial.shape, jnp.float32)
    for newton_step in range(NEWTON):
        left = trial - slip
        residue = slip - rate * left**3
        slope = 1.0 + 3.0 * rate * left**2
        slip = slip - residue / slope
    depth = trial.shape[0]
    layer = jnp.arange(depth, dtype=jnp.int32) // 8
    live = (layer[:, None, None] < active_layers[None, :, :]).astype(jnp.float32)[..., None]
    creep = live * slip
    stress = trial - creep
    strain = jnp.sum(creep.reshape((depth // 8, 8) + trial.shape[1:]), axis=1) * 0.125
    return (stress, strain)


def stepwise(
    temp_start, conductivity, gap_conductance, partner, row_order, active_layers, trial_stress
):
    depth = temp_start.shape[0]
    rows = temp_start.shape[2]
    radial = temp_start.shape[3]
    temp = temp_start.reshape(depth, rows, radial)
    cond = conductivity.reshape(depth, rows, radial)
    gap = gap_conductance.reshape(depth, rows)
    gap_row = radial // 2
    sections = lax.axis_size("iface")
    across = rows * sections
    all_cols = jnp.arange(across, dtype=jnp.int32)
    cond_rim = padded(cond, ((("slab", "mech"), 0), ("iface", 1)), 1)
    padded_cond = jnp.pad(cond_rim, ((0, 0), (0, 0), (1, 1)))
    spread_table = (partner[:, None] == all_cols[None, :]).astype(jnp.float32)
    for sweep in range(SWEEPS):
        temp_rim = padded(temp, ((("slab", "mech"), 0), ("iface", 1)), 1)
        padded_temp = jnp.pad(temp_rim, ((0, 0), (0, 0), (1, 1)))
        compact = temp[:, :, gap_row - 1]
        canister = temp[:, :, gap_row]
        compact_all = lax.all_gather(compact, "iface", axis=1, tiled=True)
        facing = jnp.take(compact_all, partner, axis=1)
        flux = gap * (facing - canister)
        spread = jnp.dot(
            flux, spread_table, precision=lax.Precision.HIGHEST, preferred_element_type=jnp.float32
        )
        returned = lax.psum_scatter(spread, "iface", scatter_dimension=1, tiled=True)
        fresh = temp + conduction(padded_temp, padded_cond)
        temp = (
            fresh.at[:, :, gap_row]
            .add(FLUX_STEP * flux)
            .at[:, :, gap_row - 1]
            .add(-FLUX_STEP * returned)
        )
    permuted = jnp.take(temp, row_order[0], axis=1)
    mech_temp = lax.all_to_all(permuted, ("slab", "mech"), split_axis=1, concat_axis=0, tiled=True)
    mech_temp = mech_temp.reshape(mech_temp.shape[0], 1, mech_temp.shape[1], radial)
    return creep_return(mech_temp, trial_stress, active_layers)


LANES = 128
HALO = 2
EVERYONE = ("iface", "slab", "mech")


def iota(shape, axis):
    return lax.broadcasted_iota(jnp.int32, shape, axis)


class Sizes:
    def __init__(self, layers, rows, radial):
        self.layers = layers
        self.rows = rows
        self.radial = radial
        self.tiles = radial // LANES
        self.sections = lax.axis_size("iface")
        self.members = lax.axis_size("slab") * lax.axis_size("mech")
        self.devices = self.sections * self.members
        self.depth = layers * self.members
        self.chunk = radial // self.devices
        self.width = self.chunk + 2 * HALO
        self.layer_lanes = LANES // layers
        self.extra_at = 3 * self.width
        self.gap_row = radial // 2


def fits_tiles(sizes):
    return (
        sizes.rows == 8
        and sizes.members == sizes.rows
        and sizes.layers == 2
        and sizes.sections * sizes.rows <= LANES
        and sizes.radial % sizes.devices == 0
        and sizes.chunk * 8 == LANES
        and sizes.radial % (2 * LANES) == 0
        and sizes.extra_at + 3 <= sizes.layer_lanes
    )


def deal_kernel(
    sizes,
    partner_hbm,
    order_hbm,
    gap_hbm,
    temp_hbm,
    cond_hbm,
    out_ref,
    partner_ref,
    order_ref,
    gap_ref,
    temp_ref,
    cond_ref,
    sems,
):
    pairs = (
        (gap_hbm, gap_ref),
        (partner_hbm, partner_ref),
        (order_hbm, order_ref),
        (temp_hbm, temp_ref),
        (cond_hbm, cond_ref),
    )
    copies = [
        pltpu.make_async_copy(source, target, sems.at[index])
        for index, (source, target) in enumerate(pairs)
    ]
    for copy in copies:
        copy.start()
    for copy in copies[:3]:
        copy.wait()
    shape = (sizes.rows, LANES)
    lane = iota(shape, 1)
    sub = iota(shape, 0)
    extra_at = sizes.extra_at
    extra = jnp.zeros(shape, jnp.float32)
    for row in range(sizes.rows):
        for layer in range(sizes.layers):
            spot = (sub == row) & (lane == extra_at + layer * sizes.layer_lanes)
            extra = jnp.where(spot, gap_ref[layer, 0, row], extra)
        spot = (sub == row) & (lane == extra_at + 1)
        extra = jnp.where(spot, partner_ref[row].astype(jnp.float32), extra)
        spot = (sub == row) & (lane == extra_at + 2)
        extra = jnp.where(spot, order_ref[0, row].astype(jnp.float32), extra)
    for copy in copies[3:]:
        copy.wait()
    blocks = [
        (
            layer * sizes.layer_lanes + field * sizes.width,
            [ref[layer, 0, :, pl.ds(tile * LANES, LANES)] for tile in range(sizes.tiles)],
        )
        for field, ref in enumerate((temp_ref, cond_ref))
        for layer in range(sizes.layers)
    ]
    for device in range(sizes.devices):
        first = device * sizes.chunk - HALO
        packed = extra
        for base, block in blocks:
            for tile in range(sizes.tiles):
                low = max(first, tile * LANES)
                high = min(first + sizes.width, (tile + 1) * LANES)
                if low >= high:
                    continue
                moved = pltpu.roll(block[tile], (base - first + tile * LANES) % LANES, 1)
                spot = (lane >= base + low - first) & (lane < base + high - first)
                packed = jnp.where(spot, moved, packed)
        out_ref[device] = packed


def sweep_kernel(sizes, dealt_ref, out_ref, line_ref):
    rows, width, half_lanes = sizes.rows, sizes.width, sizes.layer_lanes
    sections, members = sizes.sections, sizes.members
    shape = (rows, LANES)
    lane = iota(shape, 1)
    sub = iota(shape, 0)
    place = lax.axis_index("iface") * members
    place = place + lax.axis_index("slab") * lax.axis_size("mech") + lax.axis_index("mech")
    first = place * sizes.chunk - HALO
    spot_in_layer = lane % half_lanes
    radius = first + spot_in_layer % width
    lower_layer = lane < half_lanes
    at_compact = radius == sizes.gap_row - 1
    at_canister = radius == sizes.gap_row
    in_grid = (radius >= 0) & (radius < sizes.radial)
    weight = jnp.where(at_compact | at_canister, 6.0, 8.0)
    is_temp = spot_in_layer < width
    at_face = is_temp & (at_compact | at_canister)
    keep_temp = jnp.where(is_temp & in_grid, 1.0, 0.0)
    face_lane = sizes.gap_row - 1 - first

    def turn(value, shift):
        return pltpu.roll(value, shift % LANES, 1)

    dealt = [[dealt_ref[s * members + k] for k in range(members)] for s in range(sections)]

    odd = lane % 2 == 1

    def strip_of(values, start):
        strips = []
        for s in range(sections):
            strip = jnp.zeros(shape, jnp.float32)
            for k in range(members):
                moved = pltpu.roll(values[s][k], (start + 2 * k) % LANES, 1)
                spot = spot_in_layer // 2 == k
                strip = jnp.where(spot, moved, strip)
            strips.append(strip)
        return jnp.concatenate(strips, axis=0)

    total = sections * rows
    meets = jnp.concatenate(
        [
            jnp.where(
                lane == dealt[s][0][:, sizes.extra_at + 1 : sizes.extra_at + 2].astype(jnp.int32), 1.0, 0.0
            )
            for s in range(sections)
        ]
        + [jnp.zeros((LANES - total, LANES), jnp.float32)],
        axis=0,
    )
    met_by = meets.T[:total, :total]
    meets = meets[:total, :total]
    both = jnp.concatenate([meets, met_by], axis=0)

    def pick(table, strip):
        return jnp.dot(
            table, strip, precision=lax.Precision.HIGHEST, preferred_element_type=jnp.float32
        )

    wide_odd = jnp.concatenate([odd] * sections, axis=0)
    gap = strip_of(dealt, LANES + 1 - sizes.extra_at)
    gap = jnp.where(wide_odd, gap, turn(pick(met_by, gap), -1))

    def gains(values):
        strip = strip_of(values, LANES - face_lane)
        met = pick(both, strip)
        met = jnp.where(wide_odd, turn(met[:total], 1), turn(met[total:], -1))
        gain = FLUX_STEP * gap * (met - strip)
        return [gain[s * rows : (s + 1) * rows] for s in range(sections)]

    conds = [[turn(value, -width) for value in line] for line in dealt]
    edge = jnp.zeros(shape, jnp.float32)
    for k in range(members):
        line_ref[k, pl.ds(0, rows), :] = edge
        line_ref[k, pl.ds(rows + total, rows), :] = edge

    def with_product(value, cond):
        return jnp.where(spot_in_layer < 2 * width, value, turn(value * cond, 2 * width))

    def box_sum(values):
        for s in range(sections):
            other = [turn(value, half_lanes) for value in values[s]]
            for k in range(members):
                before = other[k - 1] if k else 0.0
                after = other[k + 1] if k < members - 1 else 0.0
                near = other[k] + jnp.where(lower_layer, before, after)
                line_ref[k, pl.ds(rows + s * rows, rows), :] = values[s][k] + 0.5 * near
        result = []
        for s in range(sections):
            line = []
            for k in range(members):
                start = rows + s * rows
                near = line_ref[k, pl.ds(start - 1, rows), :] + line_ref[k, pl.ds(start + 1, rows), :]
                value = line_ref[k, pl.ds(start, rows), :] + 0.5 * near
                inward = jnp.where(at_canister, 0.0, turn(value, 1))
                outward = jnp.where(at_compact, 0.0, turn(value, -1))
                line.append(value + 0.5 * (inward + outward))
            result.append(line)
        return result

    values = dealt
    cond_sums = None
    for sweep in range(SWEEPS):
        gain = gains(values)
        packed = [
            [with_product(value, cond) for value, cond in zip(*lines)]
            for lines in zip(values, conds)
        ]
        sums = box_sum(packed)
        if cond_sums is None:
            cond_sums = [[turn(total_sum, -width) for total_sum in line] for line in sums]
        fresh = []
        for s in range(sections):
            line = []
            for k in range(members):
                value = values[s][k]
                total_sum = sums[s][k]
                change = conds[s][k] * (total_sum - weight * value)
                change = change + turn(total_sum, -2 * width) - value * cond_sums[s][k]
                back = pltpu.roll(gain[s], (face_lane - 2 * k + LANES) % LANES, 1)
                temp = value + FLUX_STEP * change + jnp.where(at_face, back, 0.0)
                line.append(jnp.where(is_temp, keep_temp * temp, value))
            fresh.append(line)
        values = fresh

    per_row = 8 // sizes.layers
    skew = place % 8 * sizes.chunk
    unskewed = (lane - skew + LANES) % half_lanes
    for s in range(sections):
        order = dealt[s][0][:, sizes.extra_at + 2 : sizes.extra_at + 3].astype(jnp.int32)
        order = jnp.broadcast_to(order, shape)
        for half in range(sizes.depth // 8):
            merged = jnp.zeros(shape, jnp.float32)
            for k in range(per_row):
                moved = pltpu.roll(
                    values[s][half * per_row + k], (k * sizes.chunk - HALO + skew) % LANES, 1
                )
                merged = jnp.where(unskewed // sizes.chunk == k, moved, merged)
            chosen = jnp.take_along_axis(merged, order, axis=0)
            start = s * rows * (sizes.depth // 8) + half
            out_ref[pl.ds(start, rows, stride=sizes.depth // 8), :] = chosen


def swap_blocks(tile, block, layers):
    sub = iota(tile.shape, 0)
    spot = iota(tile.shape, 1) // block
    held = sub % layers * (8 // layers) + sub // layers
    gathered = jnp.take_along_axis(tile, (spot - held + 8) % 8, axis=0)
    rolled = [pltpu.roll(gathered, (8 - row) % 8 * block, 1) if row else gathered for row in range(8)]
    result = rolled[0]
    for row in range(1, 8):
        result = jnp.where(held == row, rolled[row], result)
    return result


def creep_kernel(sizes, active_ref, temps_ref, trial_ref, stress_ref, strain_ref):
    tiles = sizes.tiles
    halves = sizes.depth // 8
    active = active_ref[0, 0]
    for tile in range(tiles):
        for element in range(halves):
            source = pl.ds(tile * 8 * halves + element, 8, stride=halves)
            mech_temp = swap_blocks(temps_ref[source, :], sizes.chunk, sizes.layers)
            spot = pl.ds(element * 8 * tiles + tile, 8, stride=tiles)
            trial = trial_ref[spot, :]
            rate = CREEP_RATE * jnp.exp(-ACTIVATION / (mech_temp + REFERENCE_TEMP))
            slip = jnp.zeros(trial.shape, jnp.float32)
            for newton_step in range(NEWTON):
                left = trial - slip
                pull = rate * left * left
                slip = slip - (slip - pull * left) / (1.0 + 3.0 * pull)
            creep = jnp.where(element < active, slip, 0.0)
            stress_ref[spot, :] = trial - creep
            strain_ref[pl.ds(element * tiles + tile, 1), :] = 0.125 * jnp.sum(
                creep, axis=0, keepdims=True
            )


def kernel_call(body, sizes, out_shape, memories, scratch, operands):
    out_spec = pl.BlockSpec(memory_space=pltpu.VMEM)
    pinned = [
        pltpu.with_memory_space_constraint(operand, memory) if memory is pltpu.HBM else operand
        for operand, memory in zip(operands, memories)
    ]
    return pl.pallas_call(
        functools.partial(body, sizes),
        out_shape=out_shape,
        in_specs=[pl.BlockSpec(memory_space=memory) for memory in memories],
        out_specs=[out_spec] * len(out_shape),
        scratch_shapes=scratch,
        compiler_params=pltpu.CompilerParams(vmem_limit_bytes=16 * 1024 * 1024),
    )(*pinned)


def on_device(
    temp_start, conductivity, gap_conductance, partner, row_order, active_layers, trial_stress
):
    layers, _, rows, radial = temp_start.shape
    sizes = Sizes(layers, rows, radial)
    if not fits_tiles(sizes):
        return stepwise(
            temp_start,
            conductivity,
            gap_conductance,
            partner,
            row_order,
            active_layers,
            trial_stress,
        )

    def floats(*shape):
        return jax.ShapeDtypeStruct(shape, jnp.float32)

    def near(*shape):
        return pltpu.VMEM(shape, jnp.float32)

    (dealt,) = kernel_call(
        deal_kernel,
        sizes,
        (near(sizes.devices, rows, LANES),),
        [pltpu.HBM] * 5,
        [
            pltpu.SMEM(partner.shape, jnp.int32),
            pltpu.SMEM(row_order.shape, jnp.int32),
            pltpu.SMEM(gap_conductance.shape, jnp.float32),
            pltpu.VMEM(temp_start.shape, jnp.float32),
            pltpu.VMEM(conductivity.shape, jnp.float32),
            pltpu.SemaphoreType.DMA((5,)),
        ],
        (partner, row_order, gap_conductance, temp_start, conductivity),
    )
    dealt = lax.all_to_all(dealt, EVERYONE, split_axis=0, concat_axis=0, tiled=True)
    halves = sizes.depth // 8
    (temps,) = kernel_call(
        sweep_kernel,
        sizes,
        (near(sizes.devices * halves, LANES),),
        [pltpu.VMEM],
        [pltpu.VMEM((sizes.members, rows * (sizes.sections + 2), LANES), jnp.float32)],
        (dealt,),
    )
    temps = temps.reshape(sizes.devices, halves, LANES)
    temps = lax.all_to_all(temps, EVERYONE, split_axis=0, concat_axis=0, tiled=True)
    stress, strain = kernel_call(
        creep_kernel,
        sizes,
        (floats(sizes.depth * sizes.tiles, LANES), floats(halves * sizes.tiles, LANES)),
        [pltpu.SMEM, pltpu.VMEM, pltpu.VMEM],
        [],
        (
            active_layers,
            temps.reshape(sizes.devices * halves, LANES),
            trial_stress.reshape(sizes.depth * sizes.tiles, LANES),
        ),
    )
    return (
        stress.reshape(sizes.depth, 1, 1, radial),
        strain.reshape(halves, 1, 1, radial),
    )


def solution(mesh):
    placed = (
        P(("slab", "mech"), "iface", None, None),
        P(("slab", "mech"), "iface", None, None),
        P(("slab", "mech"), "iface", None),
        P("iface"),
        P("iface", None),
        P("iface", ("slab", "mech")),
        P(None, "iface", ("slab", "mech"), None),
    )
    return jax.shard_map(
        on_device,
        mesh=mesh,
        in_specs=placed,
        out_specs=(
            P(None, "iface", ("slab", "mech"), None),
            P(None, "iface", ("slab", "mech"), None),
        ),
        check_vma=False,
    )
```

```python
import functools
import jax
import jax.numpy as jnp
from jax import lax
from jax.experimental import pallas as pl
from jax.experimental.pallas import tpu as pltpu
from jax.sharding import PartitionSpec as P

SWEEPS = 2
NEWTON = 4


FLUX_STEP = 0.03
CREEP_RATE = 200.0
ACTIVATION = 12.0
REFERENCE_TEMP = 1.0


def padded(block, sides, width):
    for axis, dim in sides:
        count = lax.axis_size(axis)
        forward = [(i, i + 1) for i in range(count - 1)]
        backward = [(target, source) for source, target in forward]
        low = lax.ppermute(
            lax.slice_in_dim(block, block.shape[dim] - width, None, axis=dim), axis, forward
        )
        high = lax.ppermute(lax.slice_in_dim(block, 0, width, axis=dim), axis, backward)
        block = jnp.concatenate([low, block, high], axis=dim)
    return block


def neighbour_weight(shift_z, shift_a, shift_r):
    reach = abs(shift_z) + abs(shift_a) + abs(shift_r)
    return [0.0, 1.0, 0.5, 0.25][reach]


def conduction(padded_temp, padded_cond):
    center_temp = padded_temp[1:-1, 1:-1, 1:-1]
    center_cond = padded_cond[1:-1, 1:-1, 1:-1]
    depth, across, radial = center_temp.shape
    radial_index = jnp.arange(radial, dtype=jnp.int32)
    gap_row = radial // 2
    outward_open = (radial_index != gap_row - 1).astype(jnp.float32)
    inward_open = (radial_index != gap_row).astype(jnp.float32)
    total = jnp.zeros(center_temp.shape, jnp.float32)
    for shift_z in (-1, 0, 1):
        for shift_a in (-1, 0, 1):
            for shift_r in (-1, 0, 1):
                if shift_z == 0 and shift_a == 0 and (shift_r == 0):
                    continue
                near_temp = padded_temp[
                    1 + shift_z : 1 + shift_z + depth,
                    1 + shift_a : 1 + shift_a + across,
                    1 + shift_r : 1 + shift_r + radial,
                ]
                near_cond = padded_cond[
                    1 + shift_z : 1 + shift_z + depth,
                    1 + shift_a : 1 + shift_a + across,
                    1 + shift_r : 1 + shift_r + radial,
                ]
                face = neighbour_weight(shift_z, shift_a, shift_r) * 0.5 * (center_cond + near_cond)
                if shift_r == 1:
                    face = face * outward_open
                elif shift_r == -1:
                    face = face * inward_open
                total = total + face * (near_temp - center_temp)
    return FLUX_STEP * total


def creep_return(mech_temp, trial, active_layers):
    rate = CREEP_RATE * jnp.exp(-ACTIVATION / (mech_temp + REFERENCE_TEMP))
    slip = jnp.zeros(trial.shape, jnp.float32)
    for newton_step in range(NEWTON):
        left = trial - slip
        residue = slip - rate * left**3
        slope = 1.0 + 3.0 * rate * left**2
        slip = slip - residue / slope
    depth = trial.shape[0]
    layer = jnp.arange(depth, dtype=jnp.int32) // 8
    live = (layer[:, None, None] < active_layers[None, :, :]).astype(jnp.float32)[..., None]
    creep = live * slip
    stress = trial - creep
    strain = jnp.sum(creep.reshape((depth // 8, 8) + trial.shape[1:]), axis=1) * 0.125
    return (stress, strain)


def stepwise(
    temp_start, conductivity, gap_conductance, partner, row_order, active_layers, trial_stress
):
    depth = temp_start.shape[0]
    rows = temp_start.shape[2]
    radial = temp_start.shape[3]
    temp = temp_start.reshape(depth, rows, radial)
    cond = conductivity.reshape(depth, rows, radial)
    gap = gap_conductance.reshape(depth, rows)
    gap_row = radial // 2
    sections = lax.axis_size("iface")
    across = rows * sections
    all_cols = jnp.arange(across, dtype=jnp.int32)
    cond_rim = padded(cond, ((("slab", "mech"), 0), ("iface", 1)), 1)
    padded_cond = jnp.pad(cond_rim, ((0, 0), (0, 0), (1, 1)))
    spread_table = (partner[:, None] == all_cols[None, :]).astype(jnp.float32)
    for sweep in range(SWEEPS):
        temp_rim = padded(temp, ((("slab", "mech"), 0), ("iface", 1)), 1)
        padded_temp = jnp.pad(temp_rim, ((0, 0), (0, 0), (1, 1)))
        compact = temp[:, :, gap_row - 1]
        canister = temp[:, :, gap_row]
        compact_all = lax.all_gather(compact, "iface", axis=1, tiled=True)
        facing = jnp.take(compact_all, partner, axis=1)
        flux = gap * (facing - canister)
        spread = jnp.dot(
            flux, spread_table, precision=lax.Precision.HIGHEST, preferred_element_type=jnp.float32
        )
        returned = lax.psum_scatter(spread, "iface", scatter_dimension=1, tiled=True)
        fresh = temp + conduction(padded_temp, padded_cond)
        temp = (
            fresh.at[:, :, gap_row]
            .add(FLUX_STEP * flux)
            .at[:, :, gap_row - 1]
            .add(-FLUX_STEP * returned)
        )
    permuted = jnp.take(temp, row_order[0], axis=1)
    mech_temp = lax.all_to_all(permuted, ("slab", "mech"), split_axis=1, concat_axis=0, tiled=True)
    mech_temp = mech_temp.reshape(mech_temp.shape[0], 1, mech_temp.shape[1], radial)
    return creep_return(mech_temp, trial_stress, active_layers)


LANES = 128
HALO = 2
EVERYONE = ("iface", "slab", "mech")


def iota(shape, axis):
    return lax.broadcasted_iota(jnp.int32, shape, axis)


class Sizes:
    def __init__(self, layers, rows, radial):
        self.layers = layers
        self.rows = rows
        self.radial = radial
        self.tiles = radial // LANES
        self.sections = lax.axis_size("iface")
        self.members = lax.axis_size("slab") * lax.axis_size("mech")
        self.devices = self.sections * self.members
        self.depth = layers * self.members
        self.chunk = radial // self.devices
        self.width = self.chunk + 2 * HALO
        self.layer_lanes = LANES // layers
        self.extra_at = 3 * self.width
        self.gap_row = radial // 2


def fits_tiles(sizes):
    return (
        sizes.rows == 8
        and sizes.members == sizes.rows
        and sizes.layers == 2
        and sizes.sections * sizes.rows <= LANES
        and sizes.radial % sizes.devices == 0
        and sizes.chunk * 8 == LANES
        and sizes.radial % (2 * LANES) == 0
        and sizes.extra_at + 3 <= sizes.layer_lanes
    )


def deal_kernel(
    sizes,
    partner_hbm,
    order_hbm,
    gap_hbm,
    temp_hbm,
    cond_hbm,
    out_ref,
    partner_ref,
    order_ref,
    gap_ref,
    temp_ref,
    cond_ref,
    sems,
):
    pairs = (
        (gap_hbm, gap_ref),
        (partner_hbm, partner_ref),
        (order_hbm, order_ref),
        (temp_hbm, temp_ref),
        (cond_hbm, cond_ref),
    )
    copies = [
        pltpu.make_async_copy(source, target, sems.at[index])
        for index, (source, target) in enumerate(pairs)
    ]
    for copy in copies:
        copy.start()
    for copy in copies[:3]:
        copy.wait()
    shape = (sizes.rows, LANES)
    lane = iota(shape, 1)
    sub = iota(shape, 0)
    extra_at = sizes.extra_at
    extra = jnp.zeros(shape, jnp.float32)
    for row in range(sizes.rows):
        for layer in range(sizes.layers):
            spot = (sub == row) & (lane == extra_at + layer * sizes.layer_lanes)
            extra = jnp.where(spot, gap_ref[layer, 0, row], extra)
        spot = (sub == row) & (lane == extra_at + 1)
        extra = jnp.where(spot, partner_ref[row].astype(jnp.float32), extra)
        spot = (sub == row) & (lane == extra_at + 2)
        extra = jnp.where(spot, order_ref[0, row].astype(jnp.float32), extra)
    for copy in copies[3:]:
        copy.wait()
    blocks = [
        (
            layer * sizes.layer_lanes + field * sizes.width,
            [scale * ref[layer, 0, :, pl.ds(tile * LANES, LANES)] for tile in range(sizes.tiles)],
        )
        for field, (ref, scale) in enumerate(((temp_ref, 1.0), (cond_ref, FLUX_STEP)))
        for layer in range(sizes.layers)
    ]
    for device in range(sizes.devices):
        first = device * sizes.chunk - HALO
        packed = extra
        for base, block in blocks:
            for tile in range(sizes.tiles):
                low = max(first, tile * LANES)
                high = min(first + sizes.width, (tile + 1) * LANES)
                if low >= high:
                    continue
                moved = pltpu.roll(block[tile], (base - first + tile * LANES) % LANES, 1)
                spot = (lane >= base + low - first) & (lane < base + high - first)
                packed = jnp.where(spot, moved, packed)
        out_ref[device] = packed


def sweep_kernel(sizes, dealt_ref, out_ref, temp_ref, keep_ref):
    rows, width, half_lanes = sizes.rows, sizes.width, sizes.layer_lanes
    sections, members = sizes.sections, sizes.members
    shape = (rows, LANES)
    lane = iota(shape, 1)
    sub = iota(shape, 0)
    place = lax.axis_index("iface") * members
    place = place + lax.axis_index("slab") * lax.axis_size("mech") + lax.axis_index("mech")
    first = place * sizes.chunk - HALO
    spot_in_layer = lane % half_lanes
    radius = first + spot_in_layer % width
    lower_layer = lane < half_lanes
    at_compact = radius == sizes.gap_row - 1
    at_canister = radius == sizes.gap_row
    weight = jnp.where(at_compact | at_canister, 6.0, 8.0)
    is_temp = spot_in_layer < width
    at_face = jnp.where(is_temp & (at_compact | at_canister), 1.0, 0.0)
    from_inward = jnp.where(at_canister | (radius == 0), 0.0, 0.5)
    from_outward = jnp.where(at_compact | (radius == sizes.radial - 1), 0.0, 0.5)
    face_lane = sizes.gap_row - 1 - first
    is_given = spot_in_layer < 2 * width
    top = sub == 0
    bottom = sub == rows - 1
    odd = lane % 2 == 1
    total = sections * rows

    def turn(value, shift):
        return pltpu.roll(value, shift % LANES, 1)

    def dealt(s, k):
        return dealt_ref[s * members + k]

    def add_to_strip(strip, value, start, k):
        moved = pltpu.roll(value, (start + 2 * k) % LANES, 1)
        return jnp.where(spot_in_layer // 2 == k, moved, strip)

    def strips_of_dealt(start):
        strips = [jnp.zeros(shape, jnp.float32)] * sections
        for k in range(members):
            strips = [add_to_strip(strips[s], dealt(s, k), start, k) for s in range(sections)]
        return strips

    meets = [
        jnp.where(
            lane == dealt(s, 0)[:, sizes.extra_at + 1 : sizes.extra_at + 2].astype(jnp.int32),
            1.0,
            0.0,
        )
        for s in range(sections)
    ]
    meets = jnp.concatenate(
        meets + [jnp.zeros((LANES - total, LANES), jnp.float32)], axis=0
    )
    met_by = meets.T[:total, :total]
    both = jnp.concatenate([meets[:total, :total], met_by], axis=0)
    wide_odd = jnp.concatenate([odd] * sections, axis=0)

    def pick(table, strip):
        return jnp.dot(
            table, strip, precision=lax.Precision.HIGHEST, preferred_element_type=jnp.float32
        )

    gap = jnp.concatenate(strips_of_dealt(LANES + 1 - sizes.extra_at), axis=0)
    gap = FLUX_STEP * jnp.where(wide_odd, gap, turn(pick(met_by, gap), -1))

    def gains(strips):
        strip = jnp.concatenate(strips, axis=0)
        met = pick(both, strip)
        met = jnp.where(wide_odd, turn(met[:total], 1), turn(met[total:], -1))
        gain = gap * (met - strip)
        return [gain[s * rows : (s + 1) * rows] for s in range(sections)]

    def sweep(sweep_index, gain, take):
        def prepared(k):
            temps = [dealt(s, k) if sweep_index == 0 else temp_ref[s, k] for s in range(sections)]
            conds = [turn(dealt(s, k), -width) for s in range(sections)]
            packed = [
                jnp.where(is_given, temp, turn(temp * cond, 2 * width))
                for temp, cond in zip(temps, conds)
            ]
            other = [turn(value, half_lanes) for value in packed]
            return temps, conds, packed, other

        nothing = [jnp.zeros(shape, jnp.float32)] * sections
        below = nothing
        current = prepared(0)
        for k in range(members):
            following = prepared(k + 1) if k < members - 1 else None
            above = following[3] if following else nothing
            temps, conds, packed, other = current
            line = []
            for s in range(sections):
                near = other[s] + jnp.where(lower_layer, below[s], above[s])
                line.append(packed[s] + 0.5 * near)
            up = [pltpu.roll(value, 1, 0) for value in line]
            down = [pltpu.roll(value, rows - 1, 0) for value in line]
            fresh = []
            for s in range(sections):
                before = jnp.where(top, up[s - 1] if s else 0.0, up[s])
                after = jnp.where(bottom, down[s + 1] if s < sections - 1 else 0.0, down[s])
                value = line[s] + 0.5 * (before + after)
                value = value + from_inward * turn(value, 1) + from_outward * turn(value, -1)
                if sweep_index == 0:
                    keep = 1.0 - weight * conds[s] - turn(value, -width)
                    keep_ref[s, k] = keep
                else:
                    keep = keep_ref[s, k]
                temp = temps[s] * keep + conds[s] * value + turn(value, -2 * width)
                back = pltpu.roll(gain[s], (face_lane - 2 * k + LANES) % LANES, 1)
                fresh.append(temp + at_face * back)
            take(k, fresh)
            below = other
            current = following

    strips = [jnp.zeros(shape, jnp.float32)] * sections

    def keep_first(k, tiles):
        for s in range(sections):
            temp_ref[s, k] = tiles[s]
            strips[s] = add_to_strip(strips[s], tiles[s], LANES - face_lane, k)

    for sweep_index in range(SWEEPS - 1):
        if sweep_index == 0:
            met_strips = strips_of_dealt(LANES - face_lane)
        else:
            met_strips = list(strips)
        sweep(sweep_index, gains(met_strips), keep_first)

    per_row = 8 // sizes.layers
    halves = sizes.depth // 8
    skew = place % 8 * sizes.chunk
    unskewed = (lane - skew + LANES) % half_lanes
    merged = [jnp.zeros(shape, jnp.float32)] * sections

    def pack_last(k, tiles):
        for s in range(sections):
            shift = (k % per_row * sizes.chunk - HALO + skew) % LANES
            moved = pltpu.roll(tiles[s], shift, 1)
            merged[s] = jnp.where(unskewed // sizes.chunk == k % per_row, moved, merged[s])
            if k % per_row == per_row - 1:
                order = dealt(s, 0)[:, sizes.extra_at + 2 : sizes.extra_at + 3]
                order = jnp.broadcast_to(order.astype(jnp.int32), shape)
                start = s * rows * halves + k // per_row
                out_ref[pl.ds(start, rows, stride=halves), :] = jnp.take_along_axis(
                    merged[s], order, axis=0
                )

    sweep(SWEEPS - 1, gains(list(strips)), pack_last)


def swap_blocks(tile, block, layers):
    sub = iota(tile.shape, 0)
    spot = iota(tile.shape, 1) // block
    held = sub % layers * (8 // layers) + sub // layers
    gathered = jnp.take_along_axis(tile, (spot - held + 8) % 8, axis=0)
    rolled = [pltpu.roll(gathered, (8 - row) % 8 * block, 1) if row else gathered for row in range(8)]
    result = rolled[0]
    for row in range(1, 8):
        result = jnp.where(held == row, rolled[row], result)
    return result


def creep_kernel(sizes, active_ref, temps_ref, trial_ref, stress_ref, strain_ref):
    tiles = sizes.tiles
    halves = sizes.depth // 8
    active = active_ref[0, 0]
    for tile in range(tiles):
        for element in range(halves):
            source = pl.ds(tile * 8 * halves + element, 8, stride=halves)
            mech_temp = swap_blocks(temps_ref[source, :], sizes.chunk, sizes.layers)
            spot = pl.ds(element * 8 * tiles + tile, 8, stride=tiles)
            trial = trial_ref[spot, :]
            rate = CREEP_RATE * jnp.exp(-ACTIVATION / (mech_temp + REFERENCE_TEMP))
            slip = jnp.zeros(trial.shape, jnp.float32)
            for newton_step in range(NEWTON):
                left = trial - slip
                pull = rate * left * left
                slip = slip - (slip - pull * left) / (1.0 + 3.0 * pull)
            creep = jnp.where(element < active, slip, 0.0)
            stress_ref[spot, :] = trial - creep
            strain_ref[pl.ds(element * tiles + tile, 1), :] = 0.125 * jnp.sum(
                creep, axis=0, keepdims=True
            )


def kernel_call(body, sizes, out_shape, memories, scratch, operands):
    out_spec = pl.BlockSpec(memory_space=pltpu.VMEM)
    pinned = [
        pltpu.with_memory_space_constraint(operand, memory) if memory is pltpu.HBM else operand
        for operand, memory in zip(operands, memories)
    ]
    return pl.pallas_call(
        functools.partial(body, sizes),
        out_shape=out_shape,
        in_specs=[pl.BlockSpec(memory_space=memory) for memory in memories],
        out_specs=[out_spec] * len(out_shape),
        scratch_shapes=scratch,
        compiler_params=pltpu.CompilerParams(vmem_limit_bytes=16 * 1024 * 1024),
    )(*pinned)


def on_device(
    temp_start, conductivity, gap_conductance, partner, row_order, active_layers, trial_stress
):
    layers, _, rows, radial = temp_start.shape
    sizes = Sizes(layers, rows, radial)
    if not fits_tiles(sizes):
        return stepwise(
            temp_start,
            conductivity,
            gap_conductance,
            partner,
            row_order,
            active_layers,
            trial_stress,
        )

    def floats(*shape):
        return jax.ShapeDtypeStruct(shape, jnp.float32)

    def near(*shape):
        return pltpu.VMEM(shape, jnp.float32)

    (dealt,) = kernel_call(
        deal_kernel,
        sizes,
        (near(sizes.devices, rows, LANES),),
        [pltpu.HBM] * 5,
        [
            pltpu.SMEM(partner.shape, jnp.int32),
            pltpu.SMEM(row_order.shape, jnp.int32),
            pltpu.SMEM(gap_conductance.shape, jnp.float32),
            pltpu.VMEM(temp_start.shape, jnp.float32),
            pltpu.VMEM(conductivity.shape, jnp.float32),
            pltpu.SemaphoreType.DMA((5,)),
        ],
        (partner, row_order, gap_conductance, temp_start, conductivity),
    )
    dealt = lax.all_to_all(dealt, EVERYONE, split_axis=0, concat_axis=0, tiled=True)
    halves = sizes.depth // 8
    (temps,) = kernel_call(
        sweep_kernel,
        sizes,
        (near(sizes.devices * halves, LANES),),
        [pltpu.VMEM],
        [pltpu.VMEM((sizes.sections, sizes.members, rows, LANES), jnp.float32)] * 2,
        (dealt,),
    )
    temps = temps.reshape(sizes.devices, halves, LANES)
    temps = lax.all_to_all(temps, EVERYONE, split_axis=0, concat_axis=0, tiled=True)
    stress, strain = kernel_call(
        creep_kernel,
        sizes,
        (floats(sizes.depth * sizes.tiles, LANES), floats(halves * sizes.tiles, LANES)),
        [pltpu.SMEM, pltpu.VMEM, pltpu.VMEM],
        [],
        (
            active_layers,
            temps.reshape(sizes.devices * halves, LANES),
            trial_stress.reshape(sizes.depth * sizes.tiles, LANES),
        ),
    )
    return (
        stress.reshape(sizes.depth, 1, 1, radial),
        strain.reshape(halves, 1, 1, radial),
    )


def solution(mesh):
    placed = (
        P(("slab", "mech"), "iface", None, None),
        P(("slab", "mech"), "iface", None, None),
        P(("slab", "mech"), "iface", None),
        P("iface"),
        P("iface", None),
        P("iface", ("slab", "mech")),
        P(None, "iface", ("slab", "mech"), None),
    )
    return jax.shard_map(
        on_device,
        mesh=mesh,
        in_specs=placed,
        out_specs=(
            P(None, "iface", ("slab", "mech"), None),
            P(None, "iface", ("slab", "mech"), None),
        ),
        check_vma=False,
    )
```

```python
import functools
import jax
import jax.numpy as jnp
from jax import lax
from jax.experimental import pallas as pl
from jax.experimental.pallas import tpu as pltpu
from jax.sharding import PartitionSpec as P

SWEEPS = 2
NEWTON = 4


FLUX_STEP = 0.03
CREEP_RATE = 200.0
ACTIVATION = 12.0
REFERENCE_TEMP = 1.0


def padded(block, sides, width):
    for axis, dim in sides:
        count = lax.axis_size(axis)
        forward = [(i, i + 1) for i in range(count - 1)]
        backward = [(target, source) for source, target in forward]
        low = lax.ppermute(
            lax.slice_in_dim(block, block.shape[dim] - width, None, axis=dim), axis, forward
        )
        high = lax.ppermute(lax.slice_in_dim(block, 0, width, axis=dim), axis, backward)
        block = jnp.concatenate([low, block, high], axis=dim)
    return block


def neighbour_weight(shift_z, shift_a, shift_r):
    reach = abs(shift_z) + abs(shift_a) + abs(shift_r)
    return [0.0, 1.0, 0.5, 0.25][reach]


def conduction(padded_temp, padded_cond):
    center_temp = padded_temp[1:-1, 1:-1, 1:-1]
    center_cond = padded_cond[1:-1, 1:-1, 1:-1]
    depth, across, radial = center_temp.shape
    radial_index = jnp.arange(radial, dtype=jnp.int32)
    gap_row = radial // 2
    outward_open = (radial_index != gap_row - 1).astype(jnp.float32)
    inward_open = (radial_index != gap_row).astype(jnp.float32)
    total = jnp.zeros(center_temp.shape, jnp.float32)
    for shift_z in (-1, 0, 1):
        for shift_a in (-1, 0, 1):
            for shift_r in (-1, 0, 1):
                if shift_z == 0 and shift_a == 0 and (shift_r == 0):
                    continue
                near_temp = padded_temp[
                    1 + shift_z : 1 + shift_z + depth,
                    1 + shift_a : 1 + shift_a + across,
                    1 + shift_r : 1 + shift_r + radial,
                ]
                near_cond = padded_cond[
                    1 + shift_z : 1 + shift_z + depth,
                    1 + shift_a : 1 + shift_a + across,
                    1 + shift_r : 1 + shift_r + radial,
                ]
                face = neighbour_weight(shift_z, shift_a, shift_r) * 0.5 * (center_cond + near_cond)
                if shift_r == 1:
                    face = face * outward_open
                elif shift_r == -1:
                    face = face * inward_open
                total = total + face * (near_temp - center_temp)
    return FLUX_STEP * total


def creep_return(mech_temp, trial, active_layers):
    rate = CREEP_RATE * jnp.exp(-ACTIVATION / (mech_temp + REFERENCE_TEMP))
    slip = jnp.zeros(trial.shape, jnp.float32)
    for newton_step in range(NEWTON):
        left = trial - slip
        residue = slip - rate * left**3
        slope = 1.0 + 3.0 * rate * left**2
        slip = slip - residue / slope
    depth = trial.shape[0]
    layer = jnp.arange(depth, dtype=jnp.int32) // 8
    live = (layer[:, None, None] < active_layers[None, :, :]).astype(jnp.float32)[..., None]
    creep = live * slip
    stress = trial - creep
    strain = jnp.sum(creep.reshape((depth // 8, 8) + trial.shape[1:]), axis=1) * 0.125
    return (stress, strain)


def stepwise(
    temp_start, conductivity, gap_conductance, partner, row_order, active_layers, trial_stress
):
    depth = temp_start.shape[0]
    rows = temp_start.shape[2]
    radial = temp_start.shape[3]
    temp = temp_start.reshape(depth, rows, radial)
    cond = conductivity.reshape(depth, rows, radial)
    gap = gap_conductance.reshape(depth, rows)
    gap_row = radial // 2
    sections = lax.axis_size("iface")
    across = rows * sections
    all_cols = jnp.arange(across, dtype=jnp.int32)
    cond_rim = padded(cond, ((("slab", "mech"), 0), ("iface", 1)), 1)
    padded_cond = jnp.pad(cond_rim, ((0, 0), (0, 0), (1, 1)))
    spread_table = (partner[:, None] == all_cols[None, :]).astype(jnp.float32)
    for sweep in range(SWEEPS):
        temp_rim = padded(temp, ((("slab", "mech"), 0), ("iface", 1)), 1)
        padded_temp = jnp.pad(temp_rim, ((0, 0), (0, 0), (1, 1)))
        compact = temp[:, :, gap_row - 1]
        canister = temp[:, :, gap_row]
        compact_all = lax.all_gather(compact, "iface", axis=1, tiled=True)
        facing = jnp.take(compact_all, partner, axis=1)
        flux = gap * (facing - canister)
        spread = jnp.dot(
            flux, spread_table, precision=lax.Precision.HIGHEST, preferred_element_type=jnp.float32
        )
        returned = lax.psum_scatter(spread, "iface", scatter_dimension=1, tiled=True)
        fresh = temp + conduction(padded_temp, padded_cond)
        temp = (
            fresh.at[:, :, gap_row]
            .add(FLUX_STEP * flux)
            .at[:, :, gap_row - 1]
            .add(-FLUX_STEP * returned)
        )
    permuted = jnp.take(temp, row_order[0], axis=1)
    mech_temp = lax.all_to_all(permuted, ("slab", "mech"), split_axis=1, concat_axis=0, tiled=True)
    mech_temp = mech_temp.reshape(mech_temp.shape[0], 1, mech_temp.shape[1], radial)
    return creep_return(mech_temp, trial_stress, active_layers)


LANES = 128
HALO = 2
EVERYONE = ("iface", "slab", "mech")


def iota(shape, axis):
    return lax.broadcasted_iota(jnp.int32, shape, axis)


class Sizes:
    def __init__(self, layers, rows, radial):
        self.layers = layers
        self.rows = rows
        self.radial = radial
        self.tiles = radial // LANES
        self.sections = lax.axis_size("iface")
        self.members = lax.axis_size("slab") * lax.axis_size("mech")
        self.devices = self.sections * self.members
        self.depth = layers * self.members
        self.chunk = radial // self.devices
        self.width = self.chunk + 2 * HALO
        self.layer_lanes = LANES // layers
        self.extra_at = 3 * self.width
        self.gap_row = radial // 2


def fits_tiles(sizes):
    return (
        sizes.rows == 8
        and sizes.members == sizes.rows
        and sizes.layers == 2
        and sizes.sections * sizes.rows <= LANES
        and sizes.radial % sizes.devices == 0
        and sizes.chunk * 8 == LANES
        and sizes.radial % (2 * LANES) == 0
        and sizes.extra_at + 3 <= sizes.layer_lanes
    )


def deal_kernel(
    sizes,
    partner_hbm,
    order_hbm,
    gap_hbm,
    temp_hbm,
    cond_hbm,
    out_ref,
    partner_ref,
    order_ref,
    gap_ref,
    temp_ref,
    cond_ref,
    sems,
):
    pairs = (
        (gap_hbm, gap_ref),
        (partner_hbm, partner_ref),
        (order_hbm, order_ref),
        (temp_hbm, temp_ref),
        (cond_hbm, cond_ref),
    )
    copies = [
        pltpu.make_async_copy(source, target, sems.at[index])
        for index, (source, target) in enumerate(pairs)
    ]
    for copy in copies:
        copy.start()
    for copy in copies[:3]:
        copy.wait()
    shape = (sizes.rows, LANES)
    lane = iota(shape, 1)
    sub = iota(shape, 0)
    extra_at = sizes.extra_at
    extra = jnp.zeros(shape, jnp.float32)
    for row in range(sizes.rows):
        for layer in range(sizes.layers):
            spot = (sub == row) & (lane == extra_at + layer * sizes.layer_lanes)
            extra = jnp.where(spot, gap_ref[layer, 0, row], extra)
        spot = (sub == row) & (lane == extra_at + 1)
        extra = jnp.where(spot, partner_ref[row].astype(jnp.float32), extra)
        spot = (sub == row) & (lane == extra_at + 2)
        extra = jnp.where(spot, order_ref[0, row].astype(jnp.float32), extra)
    for copy in copies[3:]:
        copy.wait()
    blocks = [
        (
            layer * sizes.layer_lanes + field * sizes.width,
            [scale * ref[layer, 0, :, pl.ds(tile * LANES, LANES)] for tile in range(sizes.tiles)],
        )
        for field, (ref, scale) in enumerate(((temp_ref, 1.0), (cond_ref, FLUX_STEP)))
        for layer in range(sizes.layers)
    ]
    for device in range(sizes.devices):
        first = device * sizes.chunk - HALO
        packed = extra
        for base, block in blocks:
            for tile in range(sizes.tiles):
                low = max(first, tile * LANES)
                high = min(first + sizes.width, (tile + 1) * LANES)
                if low >= high:
                    continue
                moved = pltpu.roll(block[tile], (base - first + tile * LANES) % LANES, 1)
                spot = (lane >= base + low - first) & (lane < base + high - first)
                packed = jnp.where(spot, moved, packed)
        out_ref[device] = packed


def sweep_kernel(sizes, dealt_ref, out_ref, line_ref):
    rows, width, half_lanes = sizes.rows, sizes.width, sizes.layer_lanes
    sections, members = sizes.sections, sizes.members
    shape = (rows, LANES)
    lane = iota(shape, 1)
    sub = iota(shape, 0)
    place = lax.axis_index("iface") * members
    place = place + lax.axis_index("slab") * lax.axis_size("mech") + lax.axis_index("mech")
    first = place * sizes.chunk - HALO
    spot_in_layer = lane % half_lanes
    radius = first + spot_in_layer % width
    lower_layer = lane < half_lanes
    at_compact = radius == sizes.gap_row - 1
    at_canister = radius == sizes.gap_row
    weight = jnp.where(at_compact | at_canister, 6.0, 8.0)
    is_temp = spot_in_layer < width
    at_face = jnp.where(is_temp & (at_compact | at_canister), 1.0, 0.0)
    from_inward = jnp.where(at_canister | (radius == 0), 0.0, 0.5)
    from_outward = jnp.where(at_compact | (radius == sizes.radial - 1), 0.0, 0.5)
    face_lane = sizes.gap_row - 1 - first

    def turn(value, shift):
        return pltpu.roll(value, shift % LANES, 1)

    dealt = [[dealt_ref[s * members + k] for k in range(members)] for s in range(sections)]

    odd = lane % 2 == 1

    def strip_of(values, start):
        strips = []
        for s in range(sections):
            strip = jnp.zeros(shape, jnp.float32)
            for k in range(members):
                moved = pltpu.roll(values[s][k], (start + 2 * k) % LANES, 1)
                spot = spot_in_layer // 2 == k
                strip = jnp.where(spot, moved, strip)
            strips.append(strip)
        return jnp.concatenate(strips, axis=0)

    total = sections * rows
    meets = jnp.concatenate(
        [
            jnp.where(
                lane == dealt[s][0][:, sizes.extra_at + 1 : sizes.extra_at + 2].astype(jnp.int32), 1.0, 0.0
            )
            for s in range(sections)
        ]
        + [jnp.zeros((LANES - total, LANES), jnp.float32)],
        axis=0,
    )
    met_by = meets.T[:total, :total]
    meets = meets[:total, :total]
    both = jnp.concatenate([meets, met_by], axis=0)

    def pick(table, strip):
        return jnp.dot(
            table, strip, precision=lax.Precision.HIGHEST, preferred_element_type=jnp.float32
        )

    wide_odd = jnp.concatenate([odd] * sections, axis=0)
    gap = strip_of(dealt, LANES + 1 - sizes.extra_at)
    gap = FLUX_STEP * jnp.where(wide_odd, gap, turn(pick(met_by, gap), -1))

    def gains(values):
        strip = strip_of(values, LANES - face_lane)
        met = pick(both, strip)
        met = jnp.where(wide_odd, turn(met[:total], 1), turn(met[total:], -1))
        gain = gap * (met - strip)
        return [gain[s * rows : (s + 1) * rows] for s in range(sections)]

    conds = [[turn(value, -width) for value in line] for line in dealt]
    edge = jnp.zeros(shape, jnp.float32)
    for k in range(members):
        line_ref[k, pl.ds(0, rows), :] = edge
        line_ref[k, pl.ds(rows + total, rows), :] = edge

    def with_product(value, cond):
        return jnp.where(spot_in_layer < 2 * width, value, turn(value * cond, 2 * width))

    def box_sum(values):
        for s in range(sections):
            other = [turn(value, half_lanes) for value in values[s]]
            for k in range(members):
                before = other[k - 1] if k else 0.0
                after = other[k + 1] if k < members - 1 else 0.0
                near = other[k] + jnp.where(lower_layer, before, after)
                line_ref[k, pl.ds(rows + s * rows, rows), :] = values[s][k] + 0.5 * near
        result = []
        for s in range(sections):
            line = []
            for k in range(members):
                start = rows + s * rows
                near = line_ref[k, pl.ds(start - 1, rows), :] + line_ref[k, pl.ds(start + 1, rows), :]
                value = line_ref[k, pl.ds(start, rows), :] + 0.5 * near
                line.append(value + from_inward * turn(value, 1) + from_outward * turn(value, -1))
            result.append(line)
        return result

    values = dealt
    keeps = None
    for sweep in range(SWEEPS):
        gain = gains(values)
        packed = [
            [with_product(value, cond) for value, cond in zip(*lines)]
            for lines in zip(values, conds)
        ]
        sums = box_sum(packed)
        if keeps is None:
            keeps = [
                [1.0 - weight * cond - turn(total_sum, -width) for cond, total_sum in zip(*lines)]
                for lines in zip(conds, sums)
            ]
        fresh = []
        for s in range(sections):
            line = []
            for k in range(members):
                temp = values[s][k] * keeps[s][k] + conds[s][k] * sums[s][k]
                temp = temp + turn(sums[s][k], -2 * width)
                back = pltpu.roll(gain[s], (face_lane - 2 * k + LANES) % LANES, 1)
                line.append(temp + at_face * back)
            fresh.append(line)
        values = fresh

    per_row = 8 // sizes.layers
    skew = place % 8 * sizes.chunk
    unskewed = (lane - skew + LANES) % half_lanes
    for s in range(sections):
        order = dealt[s][0][:, sizes.extra_at + 2 : sizes.extra_at + 3].astype(jnp.int32)
        order = jnp.broadcast_to(order, shape)
        for half in range(sizes.depth // 8):
            merged = jnp.zeros(shape, jnp.float32)
            for k in range(per_row):
                moved = pltpu.roll(
                    values[s][half * per_row + k], (k * sizes.chunk - HALO + skew) % LANES, 1
                )
                merged = jnp.where(unskewed // sizes.chunk == k, moved, merged)
            chosen = jnp.take_along_axis(merged, order, axis=0)
            start = s * rows * (sizes.depth // 8) + half
            out_ref[pl.ds(start, rows, stride=sizes.depth // 8), :] = chosen


def swap_blocks(tile, block, layers):
    sub = iota(tile.shape, 0)
    spot = iota(tile.shape, 1) // block
    held = sub % layers * (8 // layers) + sub // layers
    gathered = jnp.take_along_axis(tile, (spot - held + 8) % 8, axis=0)
    rolled = [pltpu.roll(gathered, (8 - row) % 8 * block, 1) if row else gathered for row in range(8)]
    result = rolled[0]
    for row in range(1, 8):
        result = jnp.where(held == row, rolled[row], result)
    return result


def creep_kernel(sizes, active_ref, temps_ref, trial_ref, stress_ref, strain_ref):
    tiles = sizes.tiles
    halves = sizes.depth // 8
    active = active_ref[0, 0]
    for tile in range(tiles):
        for element in range(halves):
            source = pl.ds(tile * 8 * halves + element, 8, stride=halves)
            mech_temp = swap_blocks(temps_ref[source, :], sizes.chunk, sizes.layers)
            spot = pl.ds(element * 8 * tiles + tile, 8, stride=tiles)
            trial = trial_ref[spot, :]
            rate = CREEP_RATE * jnp.exp(-ACTIVATION / (mech_temp + REFERENCE_TEMP))
            slip = jnp.zeros(trial.shape, jnp.float32)
            for newton_step in range(NEWTON):
                left = trial - slip
                pull = rate * left * left
                slip = slip - (slip - pull * left) / (1.0 + 3.0 * pull)
            creep = jnp.where(element < active, slip, 0.0)
            stress_ref[spot, :] = trial - creep
            strain_ref[pl.ds(element * tiles + tile, 1), :] = 0.125 * jnp.sum(
                creep, axis=0, keepdims=True
            )


def kernel_call(body, sizes, out_shape, memories, scratch, operands):
    out_spec = pl.BlockSpec(memory_space=pltpu.VMEM)
    pinned = [
        pltpu.with_memory_space_constraint(operand, memory) if memory is pltpu.HBM else operand
        for operand, memory in zip(operands, memories)
    ]
    return pl.pallas_call(
        functools.partial(body, sizes),
        out_shape=out_shape,
        in_specs=[pl.BlockSpec(memory_space=memory) for memory in memories],
        out_specs=[out_spec] * len(out_shape),
        scratch_shapes=scratch,
        compiler_params=pltpu.CompilerParams(vmem_limit_bytes=16 * 1024 * 1024),
    )(*pinned)


def on_device(
    temp_start, conductivity, gap_conductance, partner, row_order, active_layers, trial_stress
):
    layers, _, rows, radial = temp_start.shape
    sizes = Sizes(layers, rows, radial)
    if not fits_tiles(sizes):
        return stepwise(
            temp_start,
            conductivity,
            gap_conductance,
            partner,
            row_order,
            active_layers,
            trial_stress,
        )

    def floats(*shape):
        return jax.ShapeDtypeStruct(shape, jnp.float32)

    def near(*shape):
        return pltpu.VMEM(shape, jnp.float32)

    (dealt,) = kernel_call(
        deal_kernel,
        sizes,
        (near(sizes.devices, rows, LANES),),
        [pltpu.HBM] * 5,
        [
            pltpu.SMEM(partner.shape, jnp.int32),
            pltpu.SMEM(row_order.shape, jnp.int32),
            pltpu.SMEM(gap_conductance.shape, jnp.float32),
            pltpu.VMEM(temp_start.shape, jnp.float32),
            pltpu.VMEM(conductivity.shape, jnp.float32),
            pltpu.SemaphoreType.DMA((5,)),
        ],
        (partner, row_order, gap_conductance, temp_start, conductivity),
    )
    dealt = lax.all_to_all(dealt, EVERYONE, split_axis=0, concat_axis=0, tiled=True)
    halves = sizes.depth // 8
    (temps,) = kernel_call(
        sweep_kernel,
        sizes,
        (near(sizes.devices * halves, LANES),),
        [pltpu.VMEM],
        [pltpu.VMEM((sizes.members, rows * (sizes.sections + 2), LANES), jnp.float32)],
        (dealt,),
    )
    temps = temps.reshape(sizes.devices, halves, LANES)
    temps = lax.all_to_all(temps, EVERYONE, split_axis=0, concat_axis=0, tiled=True)
    stress, strain = kernel_call(
        creep_kernel,
        sizes,
        (floats(sizes.depth * sizes.tiles, LANES), floats(halves * sizes.tiles, LANES)),
        [pltpu.SMEM, pltpu.VMEM, pltpu.VMEM],
        [],
        (
            active_layers,
            temps.reshape(sizes.devices * halves, LANES),
            trial_stress.reshape(sizes.depth * sizes.tiles, LANES),
        ),
    )
    return (
        stress.reshape(sizes.depth, 1, 1, radial),
        strain.reshape(halves, 1, 1, radial),
    )


def solution(mesh):
    placed = (
        P(("slab", "mech"), "iface", None, None),
        P(("slab", "mech"), "iface", None, None),
        P(("slab", "mech"), "iface", None),
        P("iface"),
        P("iface", None),
        P("iface", ("slab", "mech")),
        P(None, "iface", ("slab", "mech"), None),
    )
    return jax.shard_map(
        on_device,
        mesh=mesh,
        in_specs=placed,
        out_specs=(
            P(None, "iface", ("slab", "mech"), None),
            P(None, "iface", ("slab", "mech"), None),
        ),
        check_vma=False,
    )
```

```python
import functools
import jax
import jax.numpy as jnp
from jax import lax
from jax.experimental import pallas as pl
from jax.experimental.pallas import tpu as pltpu
from jax.sharding import PartitionSpec as P

SWEEPS = 2
NEWTON = 4


FLUX_STEP = 0.03
CREEP_RATE = 200.0
ACTIVATION = 12.0
REFERENCE_TEMP = 1.0


def padded(block, sides, width):
    for axis, dim in sides:
        count = lax.axis_size(axis)
        forward = [(i, i + 1) for i in range(count - 1)]
        backward = [(target, source) for source, target in forward]
        low = lax.ppermute(
            lax.slice_in_dim(block, block.shape[dim] - width, None, axis=dim), axis, forward
        )
        high = lax.ppermute(lax.slice_in_dim(block, 0, width, axis=dim), axis, backward)
        block = jnp.concatenate([low, block, high], axis=dim)
    return block


def neighbour_weight(shift_z, shift_a, shift_r):
    reach = abs(shift_z) + abs(shift_a) + abs(shift_r)
    return [0.0, 1.0, 0.5, 0.25][reach]


def conduction(padded_temp, padded_cond):
    center_temp = padded_temp[1:-1, 1:-1, 1:-1]
    center_cond = padded_cond[1:-1, 1:-1, 1:-1]
    depth, across, radial = center_temp.shape
    radial_index = jnp.arange(radial, dtype=jnp.int32)
    gap_row = radial // 2
    outward_open = (radial_index != gap_row - 1).astype(jnp.float32)
    inward_open = (radial_index != gap_row).astype(jnp.float32)
    total = jnp.zeros(center_temp.shape, jnp.float32)
    for shift_z in (-1, 0, 1):
        for shift_a in (-1, 0, 1):
            for shift_r in (-1, 0, 1):
                if shift_z == 0 and shift_a == 0 and (shift_r == 0):
                    continue
                near_temp = padded_temp[
                    1 + shift_z : 1 + shift_z + depth,
                    1 + shift_a : 1 + shift_a + across,
                    1 + shift_r : 1 + shift_r + radial,
                ]
                near_cond = padded_cond[
                    1 + shift_z : 1 + shift_z + depth,
                    1 + shift_a : 1 + shift_a + across,
                    1 + shift_r : 1 + shift_r + radial,
                ]
                face = neighbour_weight(shift_z, shift_a, shift_r) * 0.5 * (center_cond + near_cond)
                if shift_r == 1:
                    face = face * outward_open
                elif shift_r == -1:
                    face = face * inward_open
                total = total + face * (near_temp - center_temp)
    return FLUX_STEP * total


def creep_return(mech_temp, trial, active_layers):
    rate = CREEP_RATE * jnp.exp(-ACTIVATION / (mech_temp + REFERENCE_TEMP))
    slip = jnp.zeros(trial.shape, jnp.float32)
    for newton_step in range(NEWTON):
        left = trial - slip
        residue = slip - rate * left**3
        slope = 1.0 + 3.0 * rate * left**2
        slip = slip - residue / slope
    depth = trial.shape[0]
    layer = jnp.arange(depth, dtype=jnp.int32) // 8
    live = (layer[:, None, None] < active_layers[None, :, :]).astype(jnp.float32)[..., None]
    creep = live * slip
    stress = trial - creep
    strain = jnp.sum(creep.reshape((depth // 8, 8) + trial.shape[1:]), axis=1) * 0.125
    return (stress, strain)


def stepwise(
    temp_start, conductivity, gap_conductance, partner, row_order, active_layers, trial_stress
):
    depth = temp_start.shape[0]
    rows = temp_start.shape[2]
    radial = temp_start.shape[3]
    temp = temp_start.reshape(depth, rows, radial)
    cond = conductivity.reshape(depth, rows, radial)
    gap = gap_conductance.reshape(depth, rows)
    gap_row = radial // 2
    sections = lax.axis_size("iface")
    across = rows * sections
    all_cols = jnp.arange(across, dtype=jnp.int32)
    cond_rim = padded(cond, ((("slab", "mech"), 0), ("iface", 1)), 1)
    padded_cond = jnp.pad(cond_rim, ((0, 0), (0, 0), (1, 1)))
    spread_table = (partner[:, None] == all_cols[None, :]).astype(jnp.float32)
    for sweep in range(SWEEPS):
        temp_rim = padded(temp, ((("slab", "mech"), 0), ("iface", 1)), 1)
        padded_temp = jnp.pad(temp_rim, ((0, 0), (0, 0), (1, 1)))
        compact = temp[:, :, gap_row - 1]
        canister = temp[:, :, gap_row]
        compact_all = lax.all_gather(compact, "iface", axis=1, tiled=True)
        facing = jnp.take(compact_all, partner, axis=1)
        flux = gap * (facing - canister)
        spread = jnp.dot(
            flux, spread_table, precision=lax.Precision.HIGHEST, preferred_element_type=jnp.float32
        )
        returned = lax.psum_scatter(spread, "iface", scatter_dimension=1, tiled=True)
        fresh = temp + conduction(padded_temp, padded_cond)
        temp = (
            fresh.at[:, :, gap_row]
            .add(FLUX_STEP * flux)
            .at[:, :, gap_row - 1]
            .add(-FLUX_STEP * returned)
        )
    permuted = jnp.take(temp, row_order[0], axis=1)
    mech_temp = lax.all_to_all(permuted, ("slab", "mech"), split_axis=1, concat_axis=0, tiled=True)
    mech_temp = mech_temp.reshape(mech_temp.shape[0], 1, mech_temp.shape[1], radial)
    return creep_return(mech_temp, trial_stress, active_layers)


LANES = 128
HALO = 2
EVERYONE = ("iface", "slab", "mech")


def iota(shape, axis):
    return lax.broadcasted_iota(jnp.int32, shape, axis)


class Sizes:
    def __init__(self, layers, rows, radial):
        self.layers = layers
        self.rows = rows
        self.radial = radial
        self.tiles = radial // LANES
        self.sections = lax.axis_size("iface")
        self.members = lax.axis_size("slab") * lax.axis_size("mech")
        self.devices = self.sections * self.members
        self.depth = layers * self.members
        self.chunk = radial // self.devices
        self.width = self.chunk + 2 * HALO
        self.layer_lanes = LANES // layers
        self.extra_at = 3 * self.width
        self.gap_row = radial // 2


def fits_tiles(sizes):
    return (
        sizes.rows == 8
        and sizes.members == sizes.rows
        and sizes.layers == 2
        and sizes.sections * sizes.rows <= LANES
        and sizes.radial % sizes.devices == 0
        and sizes.chunk * 8 == LANES
        and sizes.radial % (2 * LANES) == 0
        and sizes.extra_at + 3 <= sizes.layer_lanes
    )


def deal_kernel(
    sizes,
    partner_hbm,
    order_hbm,
    gap_hbm,
    temp_hbm,
    cond_hbm,
    out_ref,
    partner_ref,
    order_ref,
    gap_ref,
    temp_ref,
    cond_ref,
    sems,
):
    pairs = (
        (gap_hbm, gap_ref),
        (partner_hbm, partner_ref),
        (order_hbm, order_ref),
        (temp_hbm, temp_ref),
        (cond_hbm, cond_ref),
    )
    copies = [
        pltpu.make_async_copy(source, target, sems.at[index])
        for index, (source, target) in enumerate(pairs)
    ]
    for copy in copies:
        copy.start()
    for copy in copies[:3]:
        copy.wait()
    shape = (sizes.rows, LANES)
    lane = iota(shape, 1)
    sub = iota(shape, 0)
    extra_at = sizes.extra_at
    extra = jnp.zeros(shape, jnp.float32)
    for row in range(sizes.rows):
        for layer in range(sizes.layers):
            spot = (sub == row) & (lane == extra_at + layer * sizes.layer_lanes)
            extra = jnp.where(spot, gap_ref[layer, 0, row], extra)
        spot = (sub == row) & (lane == extra_at + 1)
        extra = jnp.where(spot, partner_ref[row].astype(jnp.float32), extra)
        extra = jnp.where(
            lane == 2 * sizes.width + row, partner_ref[row].astype(jnp.float32), extra
        )
        spot = (sub == row) & (lane == extra_at + 2)
        extra = jnp.where(spot, order_ref[0, row].astype(jnp.float32), extra)
    for copy in copies[3:]:
        copy.wait()
    blocks = [
        (
            layer * sizes.layer_lanes + field * sizes.width,
            [scale * ref[layer, 0, :, pl.ds(tile * LANES, LANES)] for tile in range(sizes.tiles)],
        )
        for field, (ref, scale) in enumerate(((temp_ref, 1.0), (cond_ref, FLUX_STEP)))
        for layer in range(sizes.layers)
    ]
    for device in range(sizes.devices):
        first = device * sizes.chunk - HALO
        packed = extra
        for base, block in blocks:
            for tile in range(sizes.tiles):
                low = max(first, tile * LANES)
                high = min(first + sizes.width, (tile + 1) * LANES)
                if low >= high:
                    continue
                moved = pltpu.roll(block[tile], (base - first + tile * LANES) % LANES, 1)
                spot = (lane >= base + low - first) & (lane < base + high - first)
                packed = jnp.where(spot, moved, packed)
        out_ref[device] = packed


def sweep_kernel(sizes, dealt_ref, out_ref, line_ref):
    rows, width, half_lanes = sizes.rows, sizes.width, sizes.layer_lanes
    sections, members = sizes.sections, sizes.members
    shape = (rows, LANES)
    lane = iota(shape, 1)
    sub = iota(shape, 0)
    place = lax.axis_index("iface") * members
    place = place + lax.axis_index("slab") * lax.axis_size("mech") + lax.axis_index("mech")
    first = place * sizes.chunk - HALO
    spot_in_layer = lane % half_lanes
    radius = first + spot_in_layer % width
    lower_layer = lane < half_lanes
    at_compact = radius == sizes.gap_row - 1
    at_canister = radius == sizes.gap_row
    weight = jnp.where(at_compact | at_canister, 6.0, 8.0)
    is_temp = spot_in_layer < width
    at_face = jnp.where(is_temp & (at_compact | at_canister), 1.0, 0.0)
    from_inward = jnp.where(at_canister | (radius == 0), 0.0, 0.5)
    from_outward = jnp.where(at_compact | (radius == sizes.radial - 1), 0.0, 0.5)
    face_lane = sizes.gap_row - 1 - first

    def turn(value, shift):
        return pltpu.roll(value, shift % LANES, 1)

    dealt = [[dealt_ref[s * members + k] for k in range(members)] for s in range(sections)]

    odd = lane % 2 == 1

    def strip_of(values, start):
        strips = []
        for s in range(sections):
            strip = jnp.zeros(shape, jnp.float32)
            for k in range(members):
                moved = pltpu.roll(values[s][k], (start + 2 * k) % LANES, 1)
                spot = spot_in_layer // 2 == k
                strip = jnp.where(spot, moved, strip)
            strips.append(strip)
        return jnp.concatenate(strips, axis=0)

    total = sections * rows
    names = jnp.full(shape, -1.0, jnp.float32)
    for s in range(sections):
        names = jnp.where(lane // rows == s, turn(dealt[s][0], s * rows - 2 * width), names)
    tables = []
    for s in range(sections):
        partner = dealt[s][0][:, sizes.extra_at + 1 : sizes.extra_at + 2].astype(jnp.int32)
        tables.append(jnp.where(lane == partner, 1.0, 0.0))
    for s in range(sections):
        tables.append(jnp.where(names == (s * rows + sub).astype(jnp.float32), 1.0, 0.0))
    both = jnp.concatenate(tables, axis=0)[:, :total].astype(jnp.bfloat16)

    def pick(table, strip):
        rest = strip
        picked = None
        for _ in range(3):
            part = rest.astype(jnp.bfloat16)
            rest = rest - part.astype(jnp.float32)
            share = jnp.dot(table, part, preferred_element_type=jnp.float32)
            picked = share if picked is None else picked + share
        return picked

    wide_odd = jnp.concatenate([odd] * sections, axis=0)
    gap = strip_of(dealt, LANES + 1 - sizes.extra_at)
    gap = FLUX_STEP * jnp.where(wide_odd, gap, turn(pick(both[total:], gap), -1))

    def gains(values):
        strip = strip_of(values, LANES - face_lane)
        met = pick(both, strip)
        met = jnp.where(wide_odd, turn(met[:total], 1), turn(met[total:], -1))
        gain = gap * (met - strip)
        return [gain[s * rows : (s + 1) * rows] for s in range(sections)]

    conds = [[turn(value, -width) for value in line] for line in dealt]
    edge = jnp.zeros(shape, jnp.float32)
    for k in range(members):
        line_ref[k, pl.ds(0, rows), :] = edge
        line_ref[k, pl.ds(rows + total, rows), :] = edge

    def with_product(value, cond):
        return jnp.where(spot_in_layer < 2 * width, value, turn(value * cond, 2 * width))

    def box_sum(values):
        for s in range(sections):
            other = [turn(value, half_lanes) for value in values[s]]
            for k in range(members):
                before = other[k - 1] if k else 0.0
                after = other[k + 1] if k < members - 1 else 0.0
                near = other[k] + jnp.where(lower_layer, before, after)
                line_ref[k, pl.ds(rows + s * rows, rows), :] = values[s][k] + 0.5 * near
        result = []
        for s in range(sections):
            line = []
            for k in range(members):
                start = rows + s * rows
                near = line_ref[k, pl.ds(start - 1, rows), :] + line_ref[k, pl.ds(start + 1, rows), :]
                value = line_ref[k, pl.ds(start, rows), :] + 0.5 * near
                line.append(value + from_inward * turn(value, 1) + from_outward * turn(value, -1))
            result.append(line)
        return result

    values = dealt
    keeps = None
    for sweep in range(SWEEPS):
        gain = gains(values)
        packed = [
            [with_product(value, cond) for value, cond in zip(*lines)]
            for lines in zip(values, conds)
        ]
        sums = box_sum(packed)
        if keeps is None:
            keeps = [
                [1.0 - weight * cond - turn(total_sum, -width) for cond, total_sum in zip(*lines)]
                for lines in zip(conds, sums)
            ]
        fresh = []
        for s in range(sections):
            line = []
            for k in range(members):
                temp = values[s][k] * keeps[s][k] + conds[s][k] * sums[s][k]
                temp = temp + turn(sums[s][k], -2 * width)
                back = pltpu.roll(gain[s], (face_lane - 2 * k + LANES) % LANES, 1)
                line.append(temp + at_face * back)
            fresh.append(line)
        values = fresh

    per_row = 8 // sizes.layers
    skew = place % 8 * sizes.chunk
    unskewed = (lane - skew + LANES) % half_lanes
    for s in range(sections):
        order = dealt[s][0][:, sizes.extra_at + 2 : sizes.extra_at + 3].astype(jnp.int32)
        order = jnp.broadcast_to(order, shape)
        for half in range(sizes.depth // 8):
            merged = jnp.zeros(shape, jnp.float32)
            for k in range(per_row):
                moved = pltpu.roll(
                    values[s][half * per_row + k], (k * sizes.chunk - HALO + skew) % LANES, 1
                )
                merged = jnp.where(unskewed // sizes.chunk == k, moved, merged)
            chosen = jnp.take_along_axis(merged, order, axis=0)
            start = s * rows * (sizes.depth // 8) + half
            out_ref[pl.ds(start, rows, stride=sizes.depth // 8), :] = chosen


def swap_blocks(tile, block, layers):
    sub = iota(tile.shape, 0)
    spot = iota(tile.shape, 1) // block
    held = sub % layers * (8 // layers) + sub // layers
    gathered = jnp.take_along_axis(tile, (spot - held + 8) % 8, axis=0)
    rolled = [pltpu.roll(gathered, (8 - row) % 8 * block, 1) if row else gathered for row in range(8)]
    result = rolled[0]
    for row in range(1, 8):
        result = jnp.where(held == row, rolled[row], result)
    return result


def creep_kernel(sizes, active_ref, temps_ref, trial_ref, stress_ref, strain_ref):
    tiles = sizes.tiles
    halves = sizes.depth // 8
    active = active_ref[0, 0]
    for tile in range(tiles):
        for element in range(halves):
            source = pl.ds(tile * 8 * halves + element, 8, stride=halves)
            mech_temp = swap_blocks(temps_ref[source, :], sizes.chunk, sizes.layers)
            spot = pl.ds(element * 8 * tiles + tile, 8, stride=tiles)
            trial = trial_ref[spot, :]
            rate = CREEP_RATE * jnp.exp(-ACTIVATION / (mech_temp + REFERENCE_TEMP))
            slip = jnp.zeros(trial.shape, jnp.float32)
            for newton_step in range(NEWTON):
                left = trial - slip
                pull = rate * left * left
                slip = slip - (slip - pull * left) / (1.0 + 3.0 * pull)
            creep = jnp.where(element < active, slip, 0.0)
            stress_ref[spot, :] = trial - creep
            strain_ref[pl.ds(element * tiles + tile, 1), :] = 0.125 * jnp.sum(
                creep, axis=0, keepdims=True
            )


def kernel_call(body, sizes, out_shape, memories, scratch, operands):
    out_spec = pl.BlockSpec(memory_space=pltpu.VMEM)
    pinned = [
        pltpu.with_memory_space_constraint(operand, memory) if memory is pltpu.HBM else operand
        for operand, memory in zip(operands, memories)
    ]
    return pl.pallas_call(
        functools.partial(body, sizes),
        out_shape=out_shape,
        in_specs=[pl.BlockSpec(memory_space=memory) for memory in memories],
        out_specs=[out_spec] * len(out_shape),
        scratch_shapes=scratch,
        compiler_params=pltpu.CompilerParams(vmem_limit_bytes=16 * 1024 * 1024),
    )(*pinned)


def on_device(
    temp_start, conductivity, gap_conductance, partner, row_order, active_layers, trial_stress
):
    layers, _, rows, radial = temp_start.shape
    sizes = Sizes(layers, rows, radial)
    if not fits_tiles(sizes):
        return stepwise(
            temp_start,
            conductivity,
            gap_conductance,
            partner,
            row_order,
            active_layers,
            trial_stress,
        )

    def floats(*shape):
        return jax.ShapeDtypeStruct(shape, jnp.float32)

    def near(*shape):
        return pltpu.VMEM(shape, jnp.float32)

    (dealt,) = kernel_call(
        deal_kernel,
        sizes,
        (near(sizes.devices, rows, LANES),),
        [pltpu.HBM] * 5,
        [
            pltpu.SMEM(partner.shape, jnp.int32),
            pltpu.SMEM(row_order.shape, jnp.int32),
            pltpu.SMEM(gap_conductance.shape, jnp.float32),
            pltpu.VMEM(temp_start.shape, jnp.float32),
            pltpu.VMEM(conductivity.shape, jnp.float32),
            pltpu.SemaphoreType.DMA((5,)),
        ],
        (partner, row_order, gap_conductance, temp_start, conductivity),
    )
    dealt = lax.all_to_all(dealt, EVERYONE, split_axis=0, concat_axis=0, tiled=True)
    halves = sizes.depth // 8
    (temps,) = kernel_call(
        sweep_kernel,
        sizes,
        (near(sizes.devices * halves, LANES),),
        [pltpu.VMEM],
        [pltpu.VMEM((sizes.members, rows * (sizes.sections + 2), LANES), jnp.float32)],
        (dealt,),
    )
    temps = temps.reshape(sizes.devices, halves, LANES)
    temps = lax.all_to_all(temps, EVERYONE, split_axis=0, concat_axis=0, tiled=True)
    stress, strain = kernel_call(
        creep_kernel,
        sizes,
        (floats(sizes.depth * sizes.tiles, LANES), floats(halves * sizes.tiles, LANES)),
        [pltpu.SMEM, pltpu.VMEM, pltpu.VMEM],
        [],
        (
            active_layers,
            temps.reshape(sizes.devices * halves, LANES),
            trial_stress.reshape(sizes.depth * sizes.tiles, LANES),
        ),
    )
    return (
        stress.reshape(sizes.depth, 1, 1, radial),
        strain.reshape(halves, 1, 1, radial),
    )


def solution(mesh):
    placed = (
        P(("slab", "mech"), "iface", None, None),
        P(("slab", "mech"), "iface", None, None),
        P(("slab", "mech"), "iface", None),
        P("iface"),
        P("iface", None),
        P("iface", ("slab", "mech")),
        P(None, "iface", ("slab", "mech"), None),
    )
    return jax.shard_map(
        on_device,
        mesh=mesh,
        in_specs=placed,
        out_specs=(
            P(None, "iface", ("slab", "mech"), None),
            P(None, "iface", ("slab", "mech"), None),
        ),
        check_vma=False,
    )
```

```python
import functools
import jax
import jax.numpy as jnp
from jax import lax
from jax.experimental import pallas as pl
from jax.experimental.pallas import tpu as pltpu
from jax.sharding import PartitionSpec as P

SWEEPS = 2
NEWTON = 4


FLUX_STEP = 0.03
CREEP_RATE = 200.0
ACTIVATION = 12.0
REFERENCE_TEMP = 1.0


def padded(block, sides, width):
    for axis, dim in sides:
        count = lax.axis_size(axis)
        forward = [(i, i + 1) for i in range(count - 1)]
        backward = [(target, source) for source, target in forward]
        low = lax.ppermute(
            lax.slice_in_dim(block, block.shape[dim] - width, None, axis=dim), axis, forward
        )
        high = lax.ppermute(lax.slice_in_dim(block, 0, width, axis=dim), axis, backward)
        block = jnp.concatenate([low, block, high], axis=dim)
    return block


def neighbour_weight(shift_z, shift_a, shift_r):
    reach = abs(shift_z) + abs(shift_a) + abs(shift_r)
    return [0.0, 1.0, 0.5, 0.25][reach]


def conduction(padded_temp, padded_cond):
    center_temp = padded_temp[1:-1, 1:-1, 1:-1]
    center_cond = padded_cond[1:-1, 1:-1, 1:-1]
    depth, across, radial = center_temp.shape
    radial_index = jnp.arange(radial, dtype=jnp.int32)
    gap_row = radial // 2
    outward_open = (radial_index != gap_row - 1).astype(jnp.float32)
    inward_open = (radial_index != gap_row).astype(jnp.float32)
    total = jnp.zeros(center_temp.shape, jnp.float32)
    for shift_z in (-1, 0, 1):
        for shift_a in (-1, 0, 1):
            for shift_r in (-1, 0, 1):
                if shift_z == 0 and shift_a == 0 and (shift_r == 0):
                    continue
                near_temp = padded_temp[
                    1 + shift_z : 1 + shift_z + depth,
                    1 + shift_a : 1 + shift_a + across,
                    1 + shift_r : 1 + shift_r + radial,
                ]
                near_cond = padded_cond[
                    1 + shift_z : 1 + shift_z + depth,
                    1 + shift_a : 1 + shift_a + across,
                    1 + shift_r : 1 + shift_r + radial,
                ]
                face = neighbour_weight(shift_z, shift_a, shift_r) * 0.5 * (center_cond + near_cond)
                if shift_r == 1:
                    face = face * outward_open
                elif shift_r == -1:
                    face = face * inward_open
                total = total + face * (near_temp - center_temp)
    return FLUX_STEP * total


def creep_return(mech_temp, trial, active_layers):
    rate = CREEP_RATE * jnp.exp(-ACTIVATION / (mech_temp + REFERENCE_TEMP))
    slip = jnp.zeros(trial.shape, jnp.float32)
    for newton_step in range(NEWTON):
        left = trial - slip
        residue = slip - rate * left**3
        slope = 1.0 + 3.0 * rate * left**2
        slip = slip - residue / slope
    depth = trial.shape[0]
    layer = jnp.arange(depth, dtype=jnp.int32) // 8
    live = (layer[:, None, None] < active_layers[None, :, :]).astype(jnp.float32)[..., None]
    creep = live * slip
    stress = trial - creep
    strain = jnp.sum(creep.reshape((depth // 8, 8) + trial.shape[1:]), axis=1) * 0.125
    return (stress, strain)


def stepwise(
    temp_start, conductivity, gap_conductance, partner, row_order, active_layers, trial_stress
):
    depth = temp_start.shape[0]
    rows = temp_start.shape[2]
    radial = temp_start.shape[3]
    temp = temp_start.reshape(depth, rows, radial)
    cond = conductivity.reshape(depth, rows, radial)
    gap = gap_conductance.reshape(depth, rows)
    gap_row = radial // 2
    sections = lax.axis_size("iface")
    across = rows * sections
    all_cols = jnp.arange(across, dtype=jnp.int32)
    cond_rim = padded(cond, ((("slab", "mech"), 0), ("iface", 1)), 1)
    padded_cond = jnp.pad(cond_rim, ((0, 0), (0, 0), (1, 1)))
    spread_table = (partner[:, None] == all_cols[None, :]).astype(jnp.float32)
    for sweep in range(SWEEPS):
        temp_rim = padded(temp, ((("slab", "mech"), 0), ("iface", 1)), 1)
        padded_temp = jnp.pad(temp_rim, ((0, 0), (0, 0), (1, 1)))
        compact = temp[:, :, gap_row - 1]
        canister = temp[:, :, gap_row]
        compact_all = lax.all_gather(compact, "iface", axis=1, tiled=True)
        facing = jnp.take(compact_all, partner, axis=1)
        flux = gap * (facing - canister)
        spread = jnp.dot(
            flux, spread_table, precision=lax.Precision.HIGHEST, preferred_element_type=jnp.float32
        )
        returned = lax.psum_scatter(spread, "iface", scatter_dimension=1, tiled=True)
        fresh = temp + conduction(padded_temp, padded_cond)
        temp = (
            fresh.at[:, :, gap_row]
            .add(FLUX_STEP * flux)
            .at[:, :, gap_row - 1]
            .add(-FLUX_STEP * returned)
        )
    permuted = jnp.take(temp, row_order[0], axis=1)
    mech_temp = lax.all_to_all(permuted, ("slab", "mech"), split_axis=1, concat_axis=0, tiled=True)
    mech_temp = mech_temp.reshape(mech_temp.shape[0], 1, mech_temp.shape[1], radial)
    return creep_return(mech_temp, trial_stress, active_layers)


LANES = 128
HALO = 2
EVERYONE = ("iface", "slab", "mech")


def iota(shape, axis):
    return lax.broadcasted_iota(jnp.int32, shape, axis)


class Sizes:
    def __init__(self, layers, rows, radial):
        self.layers = layers
        self.rows = rows
        self.radial = radial
        self.tiles = radial // LANES
        self.sections = lax.axis_size("iface")
        self.members = lax.axis_size("slab") * lax.axis_size("mech")
        self.devices = self.sections * self.members
        self.depth = layers * self.members
        self.chunk = radial // self.devices
        self.width = self.chunk + 2 * HALO
        self.layer_lanes = LANES // layers
        self.extra_at = 3 * self.width
        self.gap_row = radial // 2


def fits_tiles(sizes):
    return (
        sizes.rows == 8
        and sizes.members == sizes.rows
        and sizes.layers == 2
        and sizes.sections * sizes.rows <= LANES
        and sizes.radial % sizes.devices == 0
        and sizes.chunk * 8 == LANES
        and sizes.radial % (2 * LANES) == 0
        and sizes.extra_at + 3 <= sizes.layer_lanes
    )


def deal_kernel(
    sizes,
    partner_hbm,
    order_hbm,
    gap_hbm,
    temp_hbm,
    cond_hbm,
    active_ref,
    out_ref,
    live_ref,
    partner_ref,
    order_ref,
    gap_ref,
    temp_ref,
    cond_ref,
    sems,
):
    pairs = (
        (gap_hbm, gap_ref),
        (partner_hbm, partner_ref),
        (order_hbm, order_ref),
        (temp_hbm, temp_ref),
        (cond_hbm, cond_ref),
    )
    copies = [
        pltpu.make_async_copy(source, target, sems.at[index])
        for index, (source, target) in enumerate(pairs)
    ]
    for copy in copies:
        copy.start()
    for copy in copies[:3]:
        copy.wait()
    shape = (sizes.rows, LANES)
    lane = iota(shape, 1)
    sub = iota(shape, 0)
    live_ref[...] = jnp.where(sub < active_ref[0, 0], 1.0, 0.0)
    extra_at = sizes.extra_at
    extra = jnp.zeros(shape, jnp.float32)
    for row in range(sizes.rows):
        for layer in range(sizes.layers):
            spot = (sub == row) & (lane == extra_at + layer * sizes.layer_lanes)
            extra = jnp.where(spot, gap_ref[layer, 0, row], extra)
        spot = (sub == row) & (lane == extra_at + 1)
        extra = jnp.where(spot, partner_ref[row].astype(jnp.float32), extra)
        extra = jnp.where(
            lane == 2 * sizes.width + row, partner_ref[row].astype(jnp.float32), extra
        )
        spot = (sub == row) & (lane == extra_at + 2)
        extra = jnp.where(spot, order_ref[0, row].astype(jnp.float32), extra)
    for copy in copies[3:]:
        copy.wait()
    blocks = [
        (
            layer * sizes.layer_lanes + field * sizes.width,
            [scale * ref[layer, 0, :, pl.ds(tile * LANES, LANES)] for tile in range(sizes.tiles)],
        )
        for field, (ref, scale) in enumerate(((temp_ref, 1.0), (cond_ref, FLUX_STEP)))
        for layer in range(sizes.layers)
    ]
    for device in range(sizes.devices):
        first = device * sizes.chunk - HALO
        packed = extra
        for base, block in blocks:
            for tile in range(sizes.tiles):
                low = max(first, tile * LANES)
                high = min(first + sizes.width, (tile + 1) * LANES)
                if low >= high:
                    continue
                moved = pltpu.roll(block[tile], (base - first + tile * LANES) % LANES, 1)
                spot = (lane >= base + low - first) & (lane < base + high - first)
                packed = jnp.where(spot, moved, packed)
        out_ref[device] = packed


def sweep_kernel(sizes, dealt_ref, out_ref, line_ref):
    rows, width, half_lanes = sizes.rows, sizes.width, sizes.layer_lanes
    sections, members = sizes.sections, sizes.members
    shape = (rows, LANES)
    lane = iota(shape, 1)
    sub = iota(shape, 0)
    place = lax.axis_index("iface") * members
    place = place + lax.axis_index("slab") * lax.axis_size("mech") + lax.axis_index("mech")
    first = place * sizes.chunk - HALO
    spot_in_layer = lane % half_lanes
    radius = first + spot_in_layer % width
    lower_layer = lane < half_lanes
    at_compact = radius == sizes.gap_row - 1
    at_canister = radius == sizes.gap_row
    weight = jnp.where(at_compact | at_canister, 6.0, 8.0)
    is_temp = spot_in_layer < width
    at_face = jnp.where(is_temp & (at_compact | at_canister), 1.0, 0.0)
    from_inward = jnp.where(at_canister | (radius == 0), 0.0, 0.5)
    from_outward = jnp.where(at_compact | (radius == sizes.radial - 1), 0.0, 0.5)
    face_lane = sizes.gap_row - 1 - first

    def turn(value, shift):
        return pltpu.roll(value, shift % LANES, 1)

    dealt = [[dealt_ref[s * members + k] for k in range(members)] for s in range(sections)]

    odd = lane % 2 == 1

    def strip_of(values, start):
        strips = []
        for s in range(sections):
            strip = jnp.zeros(shape, jnp.float32)
            for k in range(members):
                moved = pltpu.roll(values[s][k], (start + 2 * k) % LANES, 1)
                spot = spot_in_layer // 2 == k
                strip = jnp.where(spot, moved, strip)
            strips.append(strip)
        return jnp.concatenate(strips, axis=0)

    total = sections * rows
    names = jnp.full(shape, -1.0, jnp.float32)
    for s in range(sections):
        names = jnp.where(lane // rows == s, turn(dealt[s][0], s * rows - 2 * width), names)
    tables = []
    for s in range(sections):
        partner = dealt[s][0][:, sizes.extra_at + 1 : sizes.extra_at + 2].astype(jnp.int32)
        tables.append(jnp.where(lane == partner, 1.0, 0.0))
    for s in range(sections):
        tables.append(jnp.where(names == (s * rows + sub).astype(jnp.float32), 1.0, 0.0))
    both = jnp.concatenate(tables, axis=0)[:, :total].astype(jnp.bfloat16)

    def pick(table, strip):
        rest = strip
        picked = None
        for _ in range(3):
            part = rest.astype(jnp.bfloat16)
            rest = rest - part.astype(jnp.float32)
            share = jnp.dot(table, part, preferred_element_type=jnp.float32)
            picked = share if picked is None else picked + share
        return picked

    wide_odd = jnp.concatenate([odd] * sections, axis=0)
    gap = strip_of(dealt, LANES + 1 - sizes.extra_at)
    gap = FLUX_STEP * jnp.where(wide_odd, gap, turn(pick(both[total:], gap), -1))

    def gains(values):
        strip = strip_of(values, LANES - face_lane)
        met = pick(both, strip)
        met = jnp.where(wide_odd, turn(met[:total], 1), turn(met[total:], -1))
        gain = gap * (met - strip)
        return [gain[s * rows : (s + 1) * rows] for s in range(sections)]

    conds = [[turn(value, -width) for value in line] for line in dealt]
    edge = jnp.zeros(shape, jnp.float32)
    for k in range(members):
        line_ref[k, pl.ds(0, rows), :] = edge
        line_ref[k, pl.ds(rows + total, rows), :] = edge

    def with_product(value, cond):
        return jnp.where(spot_in_layer < 2 * width, value, turn(value * cond, 2 * width))

    def box_sum(values):
        for s in range(sections):
            other = [turn(value, half_lanes) for value in values[s]]
            for k in range(members):
                before = other[k - 1] if k else 0.0
                after = other[k + 1] if k < members - 1 else 0.0
                near = other[k] + jnp.where(lower_layer, before, after)
                line_ref[k, pl.ds(rows + s * rows, rows), :] = values[s][k] + 0.5 * near
        result = []
        for s in range(sections):
            line = []
            for k in range(members):
                start = rows + s * rows
                near = line_ref[k, pl.ds(start - 1, rows), :] + line_ref[k, pl.ds(start + 1, rows), :]
                value = line_ref[k, pl.ds(start, rows), :] + 0.5 * near
                line.append(value + from_inward * turn(value, 1) + from_outward * turn(value, -1))
            result.append(line)
        return result

    values = dealt
    keeps = None
    for sweep in range(SWEEPS):
        gain = gains(values)
        packed = [
            [with_product(value, cond) for value, cond in zip(*lines)]
            for lines in zip(values, conds)
        ]
        sums = box_sum(packed)
        if keeps is None:
            keeps = [
                [1.0 - weight * cond - turn(total_sum, -width) for cond, total_sum in zip(*lines)]
                for lines in zip(conds, sums)
            ]
        fresh = []
        for s in range(sections):
            line = []
            for k in range(members):
                temp = values[s][k] * keeps[s][k] + conds[s][k] * sums[s][k]
                temp = temp + turn(sums[s][k], -2 * width)
                back = pltpu.roll(gain[s], (face_lane - 2 * k + LANES) % LANES, 1)
                line.append(temp + at_face * back)
            fresh.append(line)
        values = fresh

    per_row = 8 // sizes.layers
    skew = place % 8 * sizes.chunk
    unskewed = (lane - skew + LANES) % half_lanes
    for s in range(sections):
        order = dealt[s][0][:, sizes.extra_at + 2 : sizes.extra_at + 3].astype(jnp.int32)
        order = jnp.broadcast_to(order, shape)
        for half in range(sizes.depth // 8):
            merged = jnp.zeros(shape, jnp.float32)
            for k in range(per_row):
                moved = pltpu.roll(
                    values[s][half * per_row + k], (k * sizes.chunk - HALO + skew) % LANES, 1
                )
                merged = jnp.where(unskewed // sizes.chunk == k, moved, merged)
            chosen = jnp.take_along_axis(merged, order, axis=0)
            start = s * rows * (sizes.depth // 8) + half
            out_ref[pl.ds(start, rows, stride=sizes.depth // 8), :] = chosen


def swap_blocks(tile, block, layers):
    sub = iota(tile.shape, 0)
    spot = iota(tile.shape, 1) // block
    held = sub % layers * (8 // layers) + sub // layers
    gathered = jnp.take_along_axis(tile, (spot - held + 8) % 8, axis=0)
    rolled = [pltpu.roll(gathered, (8 - row) % 8 * block, 1) if row else gathered for row in range(8)]
    result = rolled[0]
    for row in range(1, 8):
        result = jnp.where(held == row, rolled[row], result)
    return result


def creep_kernel(sizes, live_ref, temps_ref, trial_ref, stress_ref, strain_ref):
    tiles = sizes.tiles
    halves = sizes.depth // 8
    for tile in range(tiles):
        for element in range(halves):
            source = pl.ds(tile * 8 * halves + element, 8, stride=halves)
            mech_temp = swap_blocks(temps_ref[source, :], sizes.chunk, sizes.layers)
            spot = pl.ds(element * 8 * tiles + tile, 8, stride=tiles)
            trial = trial_ref[spot, :]
            rate = CREEP_RATE * jnp.exp(-ACTIVATION / (mech_temp + REFERENCE_TEMP))
            slip = jnp.zeros(trial.shape, jnp.float32)
            for newton_step in range(NEWTON):
                left = trial - slip
                pull = rate * left * left
                slip = slip - (slip - pull * left) / (1.0 + 3.0 * pull)
            creep = live_ref[pl.ds(element, 1), :] * slip
            stress_ref[spot, :] = trial - creep
            strain_ref[pl.ds(element * tiles + tile, 1), :] = 0.125 * jnp.sum(
                creep, axis=0, keepdims=True
            )


def kernel_call(body, sizes, out_shape, memories, scratch, operands):
    out_spec = pl.BlockSpec(memory_space=pltpu.VMEM)
    pinned = [
        pltpu.with_memory_space_constraint(operand, memory) if memory is pltpu.HBM else operand
        for operand, memory in zip(operands, memories)
    ]
    return pl.pallas_call(
        functools.partial(body, sizes),
        out_shape=out_shape,
        in_specs=[pl.BlockSpec(memory_space=memory) for memory in memories],
        out_specs=[out_spec] * len(out_shape),
        scratch_shapes=scratch,
        compiler_params=pltpu.CompilerParams(vmem_limit_bytes=16 * 1024 * 1024),
    )(*pinned)


def on_device(
    temp_start, conductivity, gap_conductance, partner, row_order, active_layers, trial_stress
):
    layers, _, rows, radial = temp_start.shape
    sizes = Sizes(layers, rows, radial)
    if not fits_tiles(sizes):
        return stepwise(
            temp_start,
            conductivity,
            gap_conductance,
            partner,
            row_order,
            active_layers,
            trial_stress,
        )

    def floats(*shape):
        return jax.ShapeDtypeStruct(shape, jnp.float32)

    def near(*shape):
        return pltpu.VMEM(shape, jnp.float32)

    dealt, live = kernel_call(
        deal_kernel,
        sizes,
        (near(sizes.devices, rows, LANES), near(8, LANES)),
        [pltpu.HBM] * 5 + [pltpu.SMEM],
        [
            pltpu.SMEM(partner.shape, jnp.int32),
            pltpu.SMEM(row_order.shape, jnp.int32),
            pltpu.SMEM(gap_conductance.shape, jnp.float32),
            pltpu.VMEM(temp_start.shape, jnp.float32),
            pltpu.VMEM(conductivity.shape, jnp.float32),
            pltpu.SemaphoreType.DMA((5,)),
        ],
        (partner, row_order, gap_conductance, temp_start, conductivity, active_layers),
    )
    dealt = lax.all_to_all(dealt, EVERYONE, split_axis=0, concat_axis=0, tiled=True)
    halves = sizes.depth // 8
    (temps,) = kernel_call(
        sweep_kernel,
        sizes,
        (near(sizes.devices * halves, LANES),),
        [pltpu.VMEM],
        [pltpu.VMEM((sizes.members, rows * (sizes.sections + 2), LANES), jnp.float32)],
        (dealt,),
    )
    temps = temps.reshape(sizes.devices, halves, LANES)
    temps = lax.all_to_all(temps, EVERYONE, split_axis=0, concat_axis=0, tiled=True)
    stress, strain = kernel_call(
        creep_kernel,
        sizes,
        (floats(sizes.depth * sizes.tiles, LANES), floats(halves * sizes.tiles, LANES)),
        [pltpu.VMEM, pltpu.VMEM, pltpu.VMEM],
        [],
        (
            live,
            temps.reshape(sizes.devices * halves, LANES),
            trial_stress.reshape(sizes.depth * sizes.tiles, LANES),
        ),
    )
    return (
        stress.reshape(sizes.depth, 1, 1, radial),
        strain.reshape(halves, 1, 1, radial),
    )


def solution(mesh):
    placed = (
        P(("slab", "mech"), "iface", None, None),
        P(("slab", "mech"), "iface", None, None),
        P(("slab", "mech"), "iface", None),
        P("iface"),
        P("iface", None),
        P("iface", ("slab", "mech")),
        P(None, "iface", ("slab", "mech"), None),
    )
    return jax.shard_map(
        on_device,
        mesh=mesh,
        in_specs=placed,
        out_specs=(
            P(None, "iface", ("slab", "mech"), None),
            P(None, "iface", ("slab", "mech"), None),
        ),
        check_vma=False,
    )
```

```python
import functools
import jax
import jax.numpy as jnp
from jax import lax
from jax.experimental import pallas as pl
from jax.experimental.pallas import tpu as pltpu
from jax.sharding import PartitionSpec as P

SWEEPS = 2
NEWTON = 4


FLUX_STEP = 0.03
CREEP_RATE = 200.0
ACTIVATION = 12.0
REFERENCE_TEMP = 1.0


def padded(block, sides, width):
    for axis, dim in sides:
        count = lax.axis_size(axis)
        forward = [(i, i + 1) for i in range(count - 1)]
        backward = [(target, source) for source, target in forward]
        low = lax.ppermute(
            lax.slice_in_dim(block, block.shape[dim] - width, None, axis=dim), axis, forward
        )
        high = lax.ppermute(lax.slice_in_dim(block, 0, width, axis=dim), axis, backward)
        block = jnp.concatenate([low, block, high], axis=dim)
    return block


def neighbour_weight(shift_z, shift_a, shift_r):
    reach = abs(shift_z) + abs(shift_a) + abs(shift_r)
    return [0.0, 1.0, 0.5, 0.25][reach]


def conduction(padded_temp, padded_cond):
    center_temp = padded_temp[1:-1, 1:-1, 1:-1]
    center_cond = padded_cond[1:-1, 1:-1, 1:-1]
    depth, across, radial = center_temp.shape
    radial_index = jnp.arange(radial, dtype=jnp.int32)
    gap_row = radial // 2
    outward_open = (radial_index != gap_row - 1).astype(jnp.float32)
    inward_open = (radial_index != gap_row).astype(jnp.float32)
    total = jnp.zeros(center_temp.shape, jnp.float32)
    for shift_z in (-1, 0, 1):
        for shift_a in (-1, 0, 1):
            for shift_r in (-1, 0, 1):
                if shift_z == 0 and shift_a == 0 and (shift_r == 0):
                    continue
                near_temp = padded_temp[
                    1 + shift_z : 1 + shift_z + depth,
                    1 + shift_a : 1 + shift_a + across,
                    1 + shift_r : 1 + shift_r + radial,
                ]
                near_cond = padded_cond[
                    1 + shift_z : 1 + shift_z + depth,
                    1 + shift_a : 1 + shift_a + across,
                    1 + shift_r : 1 + shift_r + radial,
                ]
                face = neighbour_weight(shift_z, shift_a, shift_r) * 0.5 * (center_cond + near_cond)
                if shift_r == 1:
                    face = face * outward_open
                elif shift_r == -1:
                    face = face * inward_open
                total = total + face * (near_temp - center_temp)
    return FLUX_STEP * total


def creep_return(mech_temp, trial, active_layers):
    rate = CREEP_RATE * jnp.exp(-ACTIVATION / (mech_temp + REFERENCE_TEMP))
    slip = jnp.zeros(trial.shape, jnp.float32)
    for newton_step in range(NEWTON):
        left = trial - slip
        residue = slip - rate * left**3
        slope = 1.0 + 3.0 * rate * left**2
        slip = slip - residue / slope
    depth = trial.shape[0]
    layer = jnp.arange(depth, dtype=jnp.int32) // 8
    live = (layer[:, None, None] < active_layers[None, :, :]).astype(jnp.float32)[..., None]
    creep = live * slip
    stress = trial - creep
    strain = jnp.sum(creep.reshape((depth // 8, 8) + trial.shape[1:]), axis=1) * 0.125
    return (stress, strain)


def stepwise(
    temp_start, conductivity, gap_conductance, partner, row_order, active_layers, trial_stress
):
    depth = temp_start.shape[0]
    rows = temp_start.shape[2]
    radial = temp_start.shape[3]
    temp = temp_start.reshape(depth, rows, radial)
    cond = conductivity.reshape(depth, rows, radial)
    gap = gap_conductance.reshape(depth, rows)
    gap_row = radial // 2
    sections = lax.axis_size("iface")
    across = rows * sections
    all_cols = jnp.arange(across, dtype=jnp.int32)
    cond_rim = padded(cond, ((("slab", "mech"), 0), ("iface", 1)), 1)
    padded_cond = jnp.pad(cond_rim, ((0, 0), (0, 0), (1, 1)))
    spread_table = (partner[:, None] == all_cols[None, :]).astype(jnp.float32)
    for sweep in range(SWEEPS):
        temp_rim = padded(temp, ((("slab", "mech"), 0), ("iface", 1)), 1)
        padded_temp = jnp.pad(temp_rim, ((0, 0), (0, 0), (1, 1)))
        compact = temp[:, :, gap_row - 1]
        canister = temp[:, :, gap_row]
        compact_all = lax.all_gather(compact, "iface", axis=1, tiled=True)
        facing = jnp.take(compact_all, partner, axis=1)
        flux = gap * (facing - canister)
        spread = jnp.dot(
            flux, spread_table, precision=lax.Precision.HIGHEST, preferred_element_type=jnp.float32
        )
        returned = lax.psum_scatter(spread, "iface", scatter_dimension=1, tiled=True)
        fresh = temp + conduction(padded_temp, padded_cond)
        temp = (
            fresh.at[:, :, gap_row]
            .add(FLUX_STEP * flux)
            .at[:, :, gap_row - 1]
            .add(-FLUX_STEP * returned)
        )
    permuted = jnp.take(temp, row_order[0], axis=1)
    mech_temp = lax.all_to_all(permuted, ("slab", "mech"), split_axis=1, concat_axis=0, tiled=True)
    mech_temp = mech_temp.reshape(mech_temp.shape[0], 1, mech_temp.shape[1], radial)
    return creep_return(mech_temp, trial_stress, active_layers)


LANES = 128
HALO = 2
EVERYONE = ("iface", "slab", "mech")


def iota(shape, axis):
    return lax.broadcasted_iota(jnp.int32, shape, axis)


class Sizes:
    def __init__(self, layers, rows, radial):
        self.layers = layers
        self.rows = rows
        self.radial = radial
        self.tiles = radial // LANES
        self.sections = lax.axis_size("iface")
        self.members = lax.axis_size("slab") * lax.axis_size("mech")
        self.devices = self.sections * self.members
        self.depth = layers * self.members
        self.chunk = radial // self.devices
        self.width = self.chunk + 2 * HALO
        self.layer_lanes = LANES // layers
        self.extra_at = 3 * self.width
        self.gap_row = radial // 2


def chunk_of(sizes, section, member):
    mirrored = section < sizes.sections // 2
    if isinstance(section, int):
        place = sizes.members - 1 - member if mirrored else member
    else:
        place = jnp.where(mirrored, sizes.members - 1 - member, member)
    return section * sizes.members + place


def fits_tiles(sizes):
    return (
        sizes.rows == 8
        and sizes.members == sizes.rows
        and sizes.layers == 2
        and sizes.sections * sizes.rows <= LANES
        and sizes.radial % sizes.devices == 0
        and sizes.chunk * 8 == LANES
        and sizes.radial % (2 * LANES) == 0
        and sizes.extra_at + 3 <= sizes.layer_lanes
    )


def deal_kernel(
    sizes,
    partner_hbm,
    order_hbm,
    gap_hbm,
    temp_hbm,
    cond_hbm,
    active_ref,
    out_ref,
    live_ref,
    partner_ref,
    order_ref,
    gap_ref,
    temp_ref,
    cond_ref,
    sems,
):
    pairs = (
        (gap_hbm, gap_ref),
        (partner_hbm, partner_ref),
        (order_hbm, order_ref),
        (temp_hbm, temp_ref),
        (cond_hbm, cond_ref),
    )
    copies = [
        pltpu.make_async_copy(source, target, sems.at[index])
        for index, (source, target) in enumerate(pairs)
    ]
    for copy in copies:
        copy.start()
    for copy in copies[:3]:
        copy.wait()
    shape = (sizes.rows, LANES)
    lane = iota(shape, 1)
    sub = iota(shape, 0)
    live_ref[...] = jnp.where(sub < active_ref[0, 0], 1.0, 0.0)
    extra_at = sizes.extra_at
    extra = jnp.zeros(shape, jnp.float32)
    for row in range(sizes.rows):
        for layer in range(sizes.layers):
            spot = (sub == row) & (lane == extra_at + layer * sizes.layer_lanes)
            extra = jnp.where(spot, gap_ref[layer, 0, row], extra)
        spot = (sub == row) & (lane == extra_at + 1)
        extra = jnp.where(spot, partner_ref[row].astype(jnp.float32), extra)
        extra = jnp.where(
            lane == 2 * sizes.width + row, partner_ref[row].astype(jnp.float32), extra
        )
        spot = (sub == row) & (lane == extra_at + 2)
        extra = jnp.where(spot, order_ref[0, row].astype(jnp.float32), extra)
    for copy in copies[3:]:
        copy.wait()
    blocks = [
        (
            layer * sizes.layer_lanes + field * sizes.width,
            [scale * ref[layer, 0, :, pl.ds(tile * LANES, LANES)] for tile in range(sizes.tiles)],
        )
        for field, (ref, scale) in enumerate(((temp_ref, 1.0), (cond_ref, FLUX_STEP)))
        for layer in range(sizes.layers)
    ]
    for device in range(sizes.devices):
        chunk = chunk_of(sizes, device // sizes.members, device % sizes.members)
        first = chunk * sizes.chunk - HALO
        packed = extra
        for base, block in blocks:
            for tile in range(sizes.tiles):
                low = max(first, tile * LANES)
                high = min(first + sizes.width, (tile + 1) * LANES)
                if low >= high:
                    continue
                moved = pltpu.roll(block[tile], (base - first + tile * LANES) % LANES, 1)
                spot = (lane >= base + low - first) & (lane < base + high - first)
                packed = jnp.where(spot, moved, packed)
        out_ref[device] = packed


def sweep_kernel(sizes, dealt_ref, out_ref, line_ref, temp_ref, table_ref, gap_ref):
    rows, width, half_lanes = sizes.rows, sizes.width, sizes.layer_lanes
    sections, members = sizes.sections, sizes.members
    shape = (rows, LANES)
    lane = iota(shape, 1)
    sub = iota(shape, 0)
    member = lax.axis_index("slab") * lax.axis_size("mech") + lax.axis_index("mech")
    place = chunk_of(sizes, lax.axis_index("iface"), member)
    first = place * sizes.chunk - HALO
    spot_in_layer = lane % half_lanes
    radius = first + spot_in_layer % width
    lower_layer = lane < half_lanes
    at_compact = radius == sizes.gap_row - 1
    at_canister = radius == sizes.gap_row
    weight = jnp.where(at_compact | at_canister, 6.0, 8.0)
    is_temp = spot_in_layer < width
    at_face = jnp.where(is_temp & (at_compact | at_canister), 1.0, 0.0)
    from_inward = jnp.where(at_canister | (radius == 0), 0.0, 0.5)
    from_outward = jnp.where(at_compact | (radius == sizes.radial - 1), 0.0, 0.5)
    face_lane = sizes.gap_row - 1 - first

    def turn(value, shift):
        return pltpu.roll(value, shift % LANES, 1)

    dealt = [[dealt_ref[s * members + k] for k in range(members)] for s in range(sections)]

    odd = lane % 2 == 1

    def strip_of(values, start):
        strips = []
        for s in range(sections):
            strip = jnp.zeros(shape, jnp.float32)
            for k in range(members):
                moved = pltpu.roll(values[s][k], (start + 2 * k) % LANES, 1)
                spot = spot_in_layer // 2 == k
                strip = jnp.where(spot, moved, strip)
            strips.append(strip)
        return jnp.concatenate(strips, axis=0)

    total = sections * rows
    has_face = (first < sizes.gap_row) & (first + width > sizes.gap_row)
    wide_odd = jnp.concatenate([odd] * sections, axis=0)

    def pick(table, strip):
        rest = strip
        picked = None
        for _ in range(3):
            part = rest.astype(jnp.bfloat16)
            rest = rest - part.astype(jnp.float32)
            share = jnp.dot(table, part, preferred_element_type=jnp.float32)
            picked = share if picked is None else picked + share
        return picked

    @pl.when(has_face)
    def prepare_exchange():
        names = jnp.full(shape, -1.0, jnp.float32)
        for s in range(sections):
            names = jnp.where(lane // rows == s, turn(dealt[s][0], s * rows - 2 * width), names)
        for s in range(sections):
            partner = dealt[s][0][:, sizes.extra_at + 1 : sizes.extra_at + 2].astype(jnp.int32)
            table_ref[pl.ds(s * rows, rows), :] = jnp.where(lane == partner, 1.0, 0.0)
        for s in range(sections):
            target = (s * rows + sub).astype(jnp.float32)
            table_ref[pl.ds(total + s * rows, rows), :] = jnp.where(names == target, 1.0, 0.0)
        table = table_ref[pl.ds(total, total), :][:, :total].astype(jnp.bfloat16)
        gap = strip_of(dealt, LANES + 1 - sizes.extra_at)
        gap_ref[...] = FLUX_STEP * jnp.where(wide_odd, gap, turn(pick(table, gap), -1))

    def exchange(values):
        strip = strip_of(values, LANES - face_lane)
        met = pick(table_ref[...][:, :total].astype(jnp.bfloat16), strip)
        met = jnp.where(wide_odd, turn(met[:total], 1), turn(met[total:], -1))
        gain = gap_ref[...] * (met - strip)
        for s in range(sections):
            own = gain[s * rows : (s + 1) * rows]
            for k in range(members):
                back = pltpu.roll(own, (face_lane - 2 * k + LANES) % LANES, 1)
                temp_ref[s, k] = temp_ref[s, k] + at_face * back

    conds = [[turn(value, -width) for value in line] for line in dealt]
    edge = jnp.zeros(shape, jnp.float32)
    for k in range(members):
        line_ref[k, pl.ds(0, rows), :] = edge
        line_ref[k, pl.ds(rows + total, rows), :] = edge

    def with_product(value, cond):
        return jnp.where(spot_in_layer < 2 * width, value, turn(value * cond, 2 * width))

    def box_sum(values):
        for s in range(sections):
            other = [turn(value, half_lanes) for value in values[s]]
            for k in range(members):
                before = other[k - 1] if k else 0.0
                after = other[k + 1] if k < members - 1 else 0.0
                near = other[k] + jnp.where(lower_layer, before, after)
                line_ref[k, pl.ds(rows + s * rows, rows), :] = values[s][k] + 0.5 * near
        result = []
        for s in range(sections):
            line = []
            for k in range(members):
                start = rows + s * rows
                near = line_ref[k, pl.ds(start - 1, rows), :] + line_ref[k, pl.ds(start + 1, rows), :]
                value = line_ref[k, pl.ds(start, rows), :] + 0.5 * near
                line.append(value + from_inward * turn(value, 1) + from_outward * turn(value, -1))
            result.append(line)
        return result

    values = dealt
    keeps = None
    for sweep in range(SWEEPS):
        packed = [
            [with_product(value, cond) for value, cond in zip(*lines)]
            for lines in zip(values, conds)
        ]
        sums = box_sum(packed)
        if keeps is None:
            keeps = [
                [1.0 - weight * cond - turn(total_sum, -width) for cond, total_sum in zip(*lines)]
                for lines in zip(conds, sums)
            ]
        for s in range(sections):
            for k in range(members):
                temp = values[s][k] * keeps[s][k] + conds[s][k] * sums[s][k]
                temp_ref[s, k] = temp + turn(sums[s][k], -2 * width)
        pl.when(has_face)(functools.partial(exchange, values))
        values = [[temp_ref[s, k] for k in range(members)] for s in range(sections)]

    per_row = 8 // sizes.layers
    skew = place % 8 * sizes.chunk
    unskewed = (lane - skew + LANES) % half_lanes
    for s in range(sections):
        order = dealt[s][0][:, sizes.extra_at + 2 : sizes.extra_at + 3].astype(jnp.int32)
        order = jnp.broadcast_to(order, shape)
        for half in range(sizes.depth // 8):
            merged = jnp.zeros(shape, jnp.float32)
            for k in range(per_row):
                moved = pltpu.roll(
                    values[s][half * per_row + k], (k * sizes.chunk - HALO + skew) % LANES, 1
                )
                merged = jnp.where(unskewed // sizes.chunk == k, moved, merged)
            chosen = jnp.take_along_axis(merged, order, axis=0)
            start = s * rows * (sizes.depth // 8) + half
            out_ref[pl.ds(start, rows, stride=sizes.depth // 8), :] = chosen


def swap_blocks(tile, block, layers, mirrored):
    sub = iota(tile.shape, 0)
    spot = iota(tile.shape, 1) // block
    held = sub % layers * (8 // layers) + sub // layers
    source = (spot - held + 8) % 8
    gathered = jnp.take_along_axis(tile, 7 - source if mirrored else source, axis=0)
    rolled = [pltpu.roll(gathered, (8 - row) % 8 * block, 1) if row else gathered for row in range(8)]
    result = rolled[0]
    for row in range(1, 8):
        result = jnp.where(held == row, rolled[row], result)
    return result


def creep_kernel(sizes, live_ref, temps_ref, trial_ref, stress_ref, strain_ref):
    tiles = sizes.tiles
    halves = sizes.depth // 8
    for tile in range(tiles):
        for element in range(halves):
            source = pl.ds(tile * 8 * halves + element, 8, stride=halves)
            mech_temp = swap_blocks(
                temps_ref[source, :], sizes.chunk, sizes.layers, tile < sizes.sections // 2
            )
            spot = pl.ds(element * 8 * tiles + tile, 8, stride=tiles)
            trial = trial_ref[spot, :]
            rate = CREEP_RATE * jnp.exp(-ACTIVATION / (mech_temp + REFERENCE_TEMP))
            slip = jnp.zeros(trial.shape, jnp.float32)
            for newton_step in range(NEWTON):
                left = trial - slip
                pull = rate * left * left
                slip = slip - (slip - pull * left) / (1.0 + 3.0 * pull)
            creep = live_ref[pl.ds(element, 1), :] * slip
            stress_ref[spot, :] = trial - creep
            strain_ref[pl.ds(element * tiles + tile, 1), :] = 0.125 * jnp.sum(
                creep, axis=0, keepdims=True
            )


def kernel_call(body, sizes, out_shape, memories, scratch, operands):
    out_spec = pl.BlockSpec(memory_space=pltpu.VMEM)
    pinned = [
        pltpu.with_memory_space_constraint(operand, memory) if memory is pltpu.HBM else operand
        for operand, memory in zip(operands, memories)
    ]
    return pl.pallas_call(
        functools.partial(body, sizes),
        out_shape=out_shape,
        in_specs=[pl.BlockSpec(memory_space=memory) for memory in memories],
        out_specs=[out_spec] * len(out_shape),
        scratch_shapes=scratch,
        compiler_params=pltpu.CompilerParams(vmem_limit_bytes=16 * 1024 * 1024),
    )(*pinned)


def on_device(
    temp_start, conductivity, gap_conductance, partner, row_order, active_layers, trial_stress
):
    layers, _, rows, radial = temp_start.shape
    sizes = Sizes(layers, rows, radial)
    if not fits_tiles(sizes):
        return stepwise(
            temp_start,
            conductivity,
            gap_conductance,
            partner,
            row_order,
            active_layers,
            trial_stress,
        )

    def floats(*shape):
        return jax.ShapeDtypeStruct(shape, jnp.float32)

    def near(*shape):
        return pltpu.VMEM(shape, jnp.float32)

    dealt, live = kernel_call(
        deal_kernel,
        sizes,
        (near(sizes.devices, rows, LANES), near(8, LANES)),
        [pltpu.HBM] * 5 + [pltpu.SMEM],
        [
            pltpu.SMEM(partner.shape, jnp.int32),
            pltpu.SMEM(row_order.shape, jnp.int32),
            pltpu.SMEM(gap_conductance.shape, jnp.float32),
            pltpu.VMEM(temp_start.shape, jnp.float32),
            pltpu.VMEM(conductivity.shape, jnp.float32),
            pltpu.SemaphoreType.DMA((5,)),
        ],
        (partner, row_order, gap_conductance, temp_start, conductivity, active_layers),
    )
    dealt = lax.all_to_all(dealt, EVERYONE, split_axis=0, concat_axis=0, tiled=True)
    halves = sizes.depth // 8
    (temps,) = kernel_call(
        sweep_kernel,
        sizes,
        (near(sizes.devices * halves, LANES),),
        [pltpu.VMEM],
        [
            pltpu.VMEM((sizes.members, rows * (sizes.sections + 2), LANES), jnp.float32),
            pltpu.VMEM((sizes.sections, sizes.members, rows, LANES), jnp.float32),
            pltpu.VMEM((2 * sizes.sections * rows, LANES), jnp.float32),
            pltpu.VMEM((sizes.sections * rows, LANES), jnp.float32),
        ],
        (dealt,),
    )
    temps = temps.reshape(sizes.devices, halves, LANES)
    temps = lax.all_to_all(temps, EVERYONE, split_axis=0, concat_axis=0, tiled=True)
    stress, strain = kernel_call(
        creep_kernel,
        sizes,
        (floats(sizes.depth * sizes.tiles, LANES), floats(halves * sizes.tiles, LANES)),
        [pltpu.VMEM, pltpu.VMEM, pltpu.VMEM],
        [],
        (
            live,
            temps.reshape(sizes.devices * halves, LANES),
            trial_stress.reshape(sizes.depth * sizes.tiles, LANES),
        ),
    )
    return (
        stress.reshape(sizes.depth, 1, 1, radial),
        strain.reshape(halves, 1, 1, radial),
    )


def solution(mesh):
    placed = (
        P(("slab", "mech"), "iface", None, None),
        P(("slab", "mech"), "iface", None, None),
        P(("slab", "mech"), "iface", None),
        P("iface"),
        P("iface", None),
        P("iface", ("slab", "mech")),
        P(None, "iface", ("slab", "mech"), None),
    )
    return jax.shard_map(
        on_device,
        mesh=mesh,
        in_specs=placed,
        out_specs=(
            P(None, "iface", ("slab", "mech"), None),
            P(None, "iface", ("slab", "mech"), None),
        ),
        check_vma=False,
    )
```

```python
import functools
import jax
import jax.numpy as jnp
from jax import lax
from jax.experimental import pallas as pl
from jax.experimental.pallas import tpu as pltpu
from jax.sharding import PartitionSpec as P

SWEEPS = 2
NEWTON = 4


FLUX_STEP = 0.03
CREEP_RATE = 200.0
ACTIVATION = 12.0
REFERENCE_TEMP = 1.0


def padded(block, sides, width):
    for axis, dim in sides:
        count = lax.axis_size(axis)
        forward = [(i, i + 1) for i in range(count - 1)]
        backward = [(target, source) for source, target in forward]
        low = lax.ppermute(
            lax.slice_in_dim(block, block.shape[dim] - width, None, axis=dim), axis, forward
        )
        high = lax.ppermute(lax.slice_in_dim(block, 0, width, axis=dim), axis, backward)
        block = jnp.concatenate([low, block, high], axis=dim)
    return block


def neighbour_weight(shift_z, shift_a, shift_r):
    reach = abs(shift_z) + abs(shift_a) + abs(shift_r)
    return [0.0, 1.0, 0.5, 0.25][reach]


def conduction(padded_temp, padded_cond):
    center_temp = padded_temp[1:-1, 1:-1, 1:-1]
    center_cond = padded_cond[1:-1, 1:-1, 1:-1]
    depth, across, radial = center_temp.shape
    radial_index = jnp.arange(radial, dtype=jnp.int32)
    gap_row = radial // 2
    outward_open = (radial_index != gap_row - 1).astype(jnp.float32)
    inward_open = (radial_index != gap_row).astype(jnp.float32)
    total = jnp.zeros(center_temp.shape, jnp.float32)
    for shift_z in (-1, 0, 1):
        for shift_a in (-1, 0, 1):
            for shift_r in (-1, 0, 1):
                if shift_z == 0 and shift_a == 0 and (shift_r == 0):
                    continue
                near_temp = padded_temp[
                    1 + shift_z : 1 + shift_z + depth,
                    1 + shift_a : 1 + shift_a + across,
                    1 + shift_r : 1 + shift_r + radial,
                ]
                near_cond = padded_cond[
                    1 + shift_z : 1 + shift_z + depth,
                    1 + shift_a : 1 + shift_a + across,
                    1 + shift_r : 1 + shift_r + radial,
                ]
                face = neighbour_weight(shift_z, shift_a, shift_r) * 0.5 * (center_cond + near_cond)
                if shift_r == 1:
                    face = face * outward_open
                elif shift_r == -1:
                    face = face * inward_open
                total = total + face * (near_temp - center_temp)
    return FLUX_STEP * total


def creep_return(mech_temp, trial, active_layers):
    rate = CREEP_RATE * jnp.exp(-ACTIVATION / (mech_temp + REFERENCE_TEMP))
    slip = jnp.zeros(trial.shape, jnp.float32)
    for newton_step in range(NEWTON):
        left = trial - slip
        residue = slip - rate * left**3
        slope = 1.0 + 3.0 * rate * left**2
        slip = slip - residue / slope
    depth = trial.shape[0]
    layer = jnp.arange(depth, dtype=jnp.int32) // 8
    live = (layer[:, None, None] < active_layers[None, :, :]).astype(jnp.float32)[..., None]
    creep = live * slip
    stress = trial - creep
    strain = jnp.sum(creep.reshape((depth // 8, 8) + trial.shape[1:]), axis=1) * 0.125
    return (stress, strain)


def stepwise(
    temp_start, conductivity, gap_conductance, partner, row_order, active_layers, trial_stress
):
    depth = temp_start.shape[0]
    rows = temp_start.shape[2]
    radial = temp_start.shape[3]
    temp = temp_start.reshape(depth, rows, radial)
    cond = conductivity.reshape(depth, rows, radial)
    gap = gap_conductance.reshape(depth, rows)
    gap_row = radial // 2
    sections = lax.axis_size("iface")
    across = rows * sections
    all_cols = jnp.arange(across, dtype=jnp.int32)
    cond_rim = padded(cond, ((("slab", "mech"), 0), ("iface", 1)), 1)
    padded_cond = jnp.pad(cond_rim, ((0, 0), (0, 0), (1, 1)))
    spread_table = (partner[:, None] == all_cols[None, :]).astype(jnp.float32)
    for sweep in range(SWEEPS):
        temp_rim = padded(temp, ((("slab", "mech"), 0), ("iface", 1)), 1)
        padded_temp = jnp.pad(temp_rim, ((0, 0), (0, 0), (1, 1)))
        compact = temp[:, :, gap_row - 1]
        canister = temp[:, :, gap_row]
        compact_all = lax.all_gather(compact, "iface", axis=1, tiled=True)
        facing = jnp.take(compact_all, partner, axis=1)
        flux = gap * (facing - canister)
        spread = jnp.dot(
            flux, spread_table, precision=lax.Precision.HIGHEST, preferred_element_type=jnp.float32
        )
        returned = lax.psum_scatter(spread, "iface", scatter_dimension=1, tiled=True)
        fresh = temp + conduction(padded_temp, padded_cond)
        temp = (
            fresh.at[:, :, gap_row]
            .add(FLUX_STEP * flux)
            .at[:, :, gap_row - 1]
            .add(-FLUX_STEP * returned)
        )
    permuted = jnp.take(temp, row_order[0], axis=1)
    mech_temp = lax.all_to_all(permuted, ("slab", "mech"), split_axis=1, concat_axis=0, tiled=True)
    mech_temp = mech_temp.reshape(mech_temp.shape[0], 1, mech_temp.shape[1], radial)
    return creep_return(mech_temp, trial_stress, active_layers)


LANES = 128
HALO = 2
EVERYONE = ("iface", "slab", "mech")


def iota(shape, axis):
    return lax.broadcasted_iota(jnp.int32, shape, axis)


class Sizes:
    def __init__(self, layers, rows, radial):
        self.layers = layers
        self.rows = rows
        self.radial = radial
        self.tiles = radial // LANES
        self.sections = lax.axis_size("iface")
        self.members = lax.axis_size("slab") * lax.axis_size("mech")
        self.devices = self.sections * self.members
        self.depth = layers * self.members
        self.chunk = radial // self.devices
        self.width = self.chunk + 2 * HALO
        self.layer_lanes = LANES // layers
        self.extra_at = 3 * self.width
        self.gap_row = radial // 2


def chunk_of(sizes, section, member):
    mirrored = section < sizes.sections // 2
    if isinstance(section, int):
        place = sizes.members - 1 - member if mirrored else member
    else:
        place = jnp.where(mirrored, sizes.members - 1 - member, member)
    return section * sizes.members + place


def fits_tiles(sizes):
    return (
        sizes.rows == 8
        and sizes.members == sizes.rows
        and sizes.layers == 2
        and sizes.sections * sizes.rows <= LANES
        and sizes.radial % sizes.devices == 0
        and sizes.chunk * 8 == LANES
        and sizes.radial % (2 * LANES) == 0
        and sizes.extra_at + 3 <= sizes.layer_lanes
    )


def deal_kernel(
    sizes,
    partner_hbm,
    order_hbm,
    gap_hbm,
    temp_hbm,
    cond_hbm,
    active_ref,
    out_ref,
    live_ref,
    partner_ref,
    order_ref,
    gap_ref,
    temp_ref,
    cond_ref,
    sems,
):
    pairs = (
        (gap_hbm, gap_ref),
        (partner_hbm, partner_ref),
        (order_hbm, order_ref),
        (temp_hbm, temp_ref),
        (cond_hbm, cond_ref),
    )
    copies = [
        pltpu.make_async_copy(source, target, sems.at[index])
        for index, (source, target) in enumerate(pairs)
    ]
    for copy in copies:
        copy.start()
    for copy in copies[:3]:
        copy.wait()
    shape = (sizes.rows, LANES)
    lane = iota(shape, 1)
    sub = iota(shape, 0)
    live_ref[...] = jnp.where(sub < active_ref[0, 0], 1.0, 0.0)
    width, half_lanes = sizes.width, sizes.layer_lanes
    spot = lane % half_lanes
    extra = jnp.zeros(shape, jnp.float32)
    for row in range(sizes.rows):
        name = partner_ref[row].astype(jnp.float32)
        values = jnp.where(spot == sizes.extra_at + 1, name, 0.0)
        values = jnp.where(
            spot == sizes.extra_at + 2, order_ref[0, row].astype(jnp.float32), values
        )
        for layer in range(sizes.layers):
            values = jnp.where(
                lane == sizes.extra_at + layer * half_lanes, gap_ref[layer, 0, row], values
            )
        extra = jnp.where(sub == row, values, extra)
    for row in range(sizes.rows):
        name = partner_ref[row].astype(jnp.float32)
        extra = jnp.where(lane == 2 * width + row, name, extra)
    for copy in copies[3:]:
        copy.wait()
    bases = []
    blocks = []
    for layer in range(sizes.layers):
        for field, (ref, scale) in enumerate(((temp_ref, 1.0), (cond_ref, FLUX_STEP))):
            base = layer * half_lanes + field * width
            bases.append(base)
            blocks.append(
                [
                    pltpu.roll(scale * ref[layer, 0, :, pl.ds(tile * LANES, LANES)], base, 1)
                    for tile in range(sizes.tiles)
                ]
            )
    for device in range(sizes.devices):
        chunk = chunk_of(sizes, device // sizes.members, device % sizes.members)
        first = chunk * sizes.chunk - HALO
        tile = chunk * sizes.chunk // LANES
        start = first - tile * LANES
        place = (lane - start + LANES) % LANES
        merged = None
        for base, block in zip(bases, blocks):
            value = block[tile]
            if start < 0 and tile > 0:
                value = jnp.where((place >= base) & (place < base - start), block[tile - 1], value)
            over = start + width - LANES
            if over > 0 and tile < sizes.tiles - 1:
                inside = (place < base + width) & (place >= base + width - over)
                value = jnp.where(inside, block[tile + 1], value)
            merged = value if merged is None else jnp.where(place >= base, value, merged)
        moved = pltpu.roll(merged, -start % LANES, 1)
        out_ref[device] = jnp.where(spot < 2 * width, moved, extra)


def sweep_kernel(sizes, dealt_ref, out_ref, line_ref, temp_ref, table_ref, gap_ref):
    rows, width, half_lanes = sizes.rows, sizes.width, sizes.layer_lanes
    sections, members = sizes.sections, sizes.members
    shape = (rows, LANES)
    lane = iota(shape, 1)
    sub = iota(shape, 0)
    member = lax.axis_index("slab") * lax.axis_size("mech") + lax.axis_index("mech")
    place = chunk_of(sizes, lax.axis_index("iface"), member)
    first = place * sizes.chunk - HALO
    spot_in_layer = lane % half_lanes
    radius = first + spot_in_layer % width
    lower_layer = lane < half_lanes
    at_compact = radius == sizes.gap_row - 1
    at_canister = radius == sizes.gap_row
    weight = jnp.where(at_compact | at_canister, 6.0, 8.0)
    is_temp = spot_in_layer < width
    at_face = jnp.where(is_temp & (at_compact | at_canister), 1.0, 0.0)
    from_inward = jnp.where(at_canister | (radius == 0), 0.0, 0.5)
    from_outward = jnp.where(at_compact | (radius == sizes.radial - 1), 0.0, 0.5)
    face_lane = sizes.gap_row - 1 - first

    def turn(value, shift):
        return pltpu.roll(value, shift % LANES, 1)

    dealt = [[dealt_ref[s * members + k] for k in range(members)] for s in range(sections)]

    odd = lane % 2 == 1

    def strip_of(values, start):
        strips = []
        for s in range(sections):
            strip = jnp.zeros(shape, jnp.float32)
            for k in range(members):
                moved = pltpu.roll(values[s][k], (start + 2 * k) % LANES, 1)
                spot = spot_in_layer // 2 == k
                strip = jnp.where(spot, moved, strip)
            strips.append(strip)
        return jnp.concatenate(strips, axis=0)

    total = sections * rows
    has_face = (first < sizes.gap_row) & (first + width > sizes.gap_row)
    wide_odd = jnp.concatenate([odd] * sections, axis=0)

    def pick(table, strip):
        rest = strip
        picked = None
        for _ in range(3):
            part = rest.astype(jnp.bfloat16)
            rest = rest - part.astype(jnp.float32)
            share = jnp.dot(table, part, preferred_element_type=jnp.float32)
            picked = share if picked is None else picked + share
        return picked

    @pl.when(has_face)
    def prepare_exchange():
        names = jnp.full(shape, -1.0, jnp.float32)
        for s in range(sections):
            names = jnp.where(lane // rows == s, turn(dealt[s][0], s * rows - 2 * width), names)
        for s in range(sections):
            partner = dealt[s][0][:, sizes.extra_at + 1 : sizes.extra_at + 2].astype(jnp.int32)
            table_ref[pl.ds(s * rows, rows), :] = jnp.where(lane == partner, 1.0, 0.0)
        for s in range(sections):
            target = (s * rows + sub).astype(jnp.float32)
            table_ref[pl.ds(total + s * rows, rows), :] = jnp.where(names == target, 1.0, 0.0)
        table = table_ref[pl.ds(total, total), :][:, :total].astype(jnp.bfloat16)
        gap = strip_of(dealt, LANES + 1 - sizes.extra_at)
        gap_ref[...] = FLUX_STEP * jnp.where(wide_odd, gap, turn(pick(table, gap), -1))

    def exchange(values):
        strip = strip_of(values, LANES - face_lane)
        met = pick(table_ref[...][:, :total].astype(jnp.bfloat16), strip)
        met = jnp.where(wide_odd, turn(met[:total], 1), turn(met[total:], -1))
        gain = gap_ref[...] * (met - strip)
        for s in range(sections):
            own = gain[s * rows : (s + 1) * rows]
            for k in range(members):
                back = pltpu.roll(own, (face_lane - 2 * k + LANES) % LANES, 1)
                temp_ref[s, k] = temp_ref[s, k] + at_face * back

    conds = [[turn(value, -width) for value in line] for line in dealt]
    edge = jnp.zeros(shape, jnp.float32)
    for k in range(members):
        line_ref[k, pl.ds(0, rows), :] = edge
        line_ref[k, pl.ds(rows + total, rows), :] = edge

    def with_product(value, cond):
        return jnp.where(spot_in_layer < 2 * width, value, turn(value * cond, 2 * width))

    def box_sum(values):
        for s in range(sections):
            other = [turn(value, half_lanes) for value in values[s]]
            for k in range(members):
                before = other[k - 1] if k else 0.0
                after = other[k + 1] if k < members - 1 else 0.0
                near = other[k] + jnp.where(lower_layer, before, after)
                line_ref[k, pl.ds(rows + s * rows, rows), :] = values[s][k] + 0.5 * near
        result = []
        for s in range(sections):
            line = []
            for k in range(members):
                start = rows + s * rows
                near = line_ref[k, pl.ds(start - 1, rows), :] + line_ref[k, pl.ds(start + 1, rows), :]
                value = line_ref[k, pl.ds(start, rows), :] + 0.5 * near
                line.append(value + from_inward * turn(value, 1) + from_outward * turn(value, -1))
            result.append(line)
        return result

    values = dealt
    keeps = None
    for sweep in range(SWEEPS):
        packed = [
            [with_product(value, cond) for value, cond in zip(*lines)]
            for lines in zip(values, conds)
        ]
        sums = box_sum(packed)
        if keeps is None:
            keeps = [
                [1.0 - weight * cond - turn(total_sum, -width) for cond, total_sum in zip(*lines)]
                for lines in zip(conds, sums)
            ]
        for s in range(sections):
            for k in range(members):
                temp = values[s][k] * keeps[s][k] + conds[s][k] * sums[s][k]
                temp_ref[s, k] = temp + turn(sums[s][k], -2 * width)
        pl.when(has_face)(functools.partial(exchange, values))
        values = [[temp_ref[s, k] for k in range(members)] for s in range(sections)]

    per_row = 8 // sizes.layers
    skew = place % 8 * sizes.chunk
    unskewed = (lane - skew + LANES) % half_lanes
    for s in range(sections):
        order = dealt[s][0][:, sizes.extra_at + 2 : sizes.extra_at + 3].astype(jnp.int32)
        order = jnp.broadcast_to(order, shape)
        for half in range(sizes.depth // 8):
            merged = jnp.zeros(shape, jnp.float32)
            for k in range(per_row):
                moved = pltpu.roll(
                    values[s][half * per_row + k], (k * sizes.chunk - HALO + skew) % LANES, 1
                )
                merged = jnp.where(unskewed // sizes.chunk == k, moved, merged)
            chosen = jnp.take_along_axis(merged, order, axis=0)
            start = s * rows * (sizes.depth // 8) + half
            out_ref[pl.ds(start, rows, stride=sizes.depth // 8), :] = chosen


def swap_blocks(tile, block, layers, mirrored):
    sub = iota(tile.shape, 0)
    spot = iota(tile.shape, 1) // block
    held = sub % layers * (8 // layers) + sub // layers
    source = (spot - held + 8) % 8
    gathered = jnp.take_along_axis(tile, 7 - source if mirrored else source, axis=0)
    rolled = [pltpu.roll(gathered, (8 - row) % 8 * block, 1) if row else gathered for row in range(8)]
    result = rolled[0]
    for row in range(1, 8):
        result = jnp.where(held == row, rolled[row], result)
    return result


def creep_kernel(sizes, live_ref, temps_ref, trial_ref, stress_ref, strain_ref):
    tiles = sizes.tiles
    halves = sizes.depth // 8
    for tile in range(tiles):
        for element in range(halves):
            source = pl.ds(tile * 8 * halves + element, 8, stride=halves)
            mech_temp = swap_blocks(
                temps_ref[source, :], sizes.chunk, sizes.layers, tile < sizes.sections // 2
            )
            spot = pl.ds(element * 8 * tiles + tile, 8, stride=tiles)
            trial = trial_ref[spot, :]
            rate = CREEP_RATE * jnp.exp(-ACTIVATION / (mech_temp + REFERENCE_TEMP))
            slip = jnp.zeros(trial.shape, jnp.float32)
            for newton_step in range(NEWTON):
                left = trial - slip
                pull = rate * left * left
                slip = slip - (slip - pull * left) / (1.0 + 3.0 * pull)
            creep = live_ref[pl.ds(element, 1), :] * slip
            stress_ref[spot, :] = trial - creep
            strain_ref[pl.ds(element * tiles + tile, 1), :] = 0.125 * jnp.sum(
                creep, axis=0, keepdims=True
            )


def kernel_call(body, sizes, out_shape, memories, scratch, operands):
    out_spec = pl.BlockSpec(memory_space=pltpu.VMEM)
    pinned = [
        pltpu.with_memory_space_constraint(operand, memory) if memory is pltpu.HBM else operand
        for operand, memory in zip(operands, memories)
    ]
    return pl.pallas_call(
        functools.partial(body, sizes),
        out_shape=out_shape,
        in_specs=[pl.BlockSpec(memory_space=memory) for memory in memories],
        out_specs=[out_spec] * len(out_shape),
        scratch_shapes=scratch,
        compiler_params=pltpu.CompilerParams(vmem_limit_bytes=16 * 1024 * 1024),
    )(*pinned)


def on_device(
    temp_start, conductivity, gap_conductance, partner, row_order, active_layers, trial_stress
):
    layers, _, rows, radial = temp_start.shape
    sizes = Sizes(layers, rows, radial)
    if not fits_tiles(sizes):
        return stepwise(
            temp_start,
            conductivity,
            gap_conductance,
            partner,
            row_order,
            active_layers,
            trial_stress,
        )

    def floats(*shape):
        return jax.ShapeDtypeStruct(shape, jnp.float32)

    def near(*shape):
        return pltpu.VMEM(shape, jnp.float32)

    dealt, live = kernel_call(
        deal_kernel,
        sizes,
        (near(sizes.devices, rows, LANES), near(8, LANES)),
        [pltpu.HBM] * 5 + [pltpu.SMEM],
        [
            pltpu.SMEM(partner.shape, jnp.int32),
            pltpu.SMEM(row_order.shape, jnp.int32),
            pltpu.SMEM(gap_conductance.shape, jnp.float32),
            pltpu.VMEM(temp_start.shape, jnp.float32),
            pltpu.VMEM(conductivity.shape, jnp.float32),
            pltpu.SemaphoreType.DMA((5,)),
        ],
        (partner, row_order, gap_conductance, temp_start, conductivity, active_layers),
    )
    dealt = lax.all_to_all(dealt, EVERYONE, split_axis=0, concat_axis=0, tiled=True)
    halves = sizes.depth // 8
    (temps,) = kernel_call(
        sweep_kernel,
        sizes,
        (near(sizes.devices * halves, LANES),),
        [pltpu.VMEM],
        [
            pltpu.VMEM((sizes.members, rows * (sizes.sections + 2), LANES), jnp.float32),
            pltpu.VMEM((sizes.sections, sizes.members, rows, LANES), jnp.float32),
            pltpu.VMEM((2 * sizes.sections * rows, LANES), jnp.float32),
            pltpu.VMEM((sizes.sections * rows, LANES), jnp.float32),
        ],
        (dealt,),
    )
    temps = temps.reshape(sizes.devices, halves, LANES)
    temps = lax.all_to_all(temps, EVERYONE, split_axis=0, concat_axis=0, tiled=True)
    stress, strain = kernel_call(
        creep_kernel,
        sizes,
        (floats(sizes.depth * sizes.tiles, LANES), floats(halves * sizes.tiles, LANES)),
        [pltpu.VMEM, pltpu.VMEM, pltpu.VMEM],
        [],
        (
            live,
            temps.reshape(sizes.devices * halves, LANES),
            trial_stress.reshape(sizes.depth * sizes.tiles, LANES),
        ),
    )
    return (
        stress.reshape(sizes.depth, 1, 1, radial),
        strain.reshape(halves, 1, 1, radial),
    )


def solution(mesh):
    placed = (
        P(("slab", "mech"), "iface", None, None),
        P(("slab", "mech"), "iface", None, None),
        P(("slab", "mech"), "iface", None),
        P("iface"),
        P("iface", None),
        P("iface", ("slab", "mech")),
        P(None, "iface", ("slab", "mech"), None),
    )
    return jax.shard_map(
        on_device,
        mesh=mesh,
        in_specs=placed,
        out_specs=(
            P(None, "iface", ("slab", "mech"), None),
            P(None, "iface", ("slab", "mech"), None),
        ),
        check_vma=False,
    )
```

```python
import functools
import jax
import jax.numpy as jnp
from jax import lax
from jax.experimental import pallas as pl
from jax.experimental.pallas import tpu as pltpu
from jax.sharding import PartitionSpec as P

SWEEPS = 2
NEWTON = 4


FLUX_STEP = 0.03
CREEP_RATE = 200.0
ACTIVATION = 12.0
REFERENCE_TEMP = 1.0


def padded(block, sides, width):
    for axis, dim in sides:
        count = lax.axis_size(axis)
        forward = [(i, i + 1) for i in range(count - 1)]
        backward = [(target, source) for source, target in forward]
        low = lax.ppermute(
            lax.slice_in_dim(block, block.shape[dim] - width, None, axis=dim), axis, forward
        )
        high = lax.ppermute(lax.slice_in_dim(block, 0, width, axis=dim), axis, backward)
        block = jnp.concatenate([low, block, high], axis=dim)
    return block


def neighbour_weight(shift_z, shift_a, shift_r):
    reach = abs(shift_z) + abs(shift_a) + abs(shift_r)
    return [0.0, 1.0, 0.5, 0.25][reach]


def conduction(padded_temp, padded_cond):
    center_temp = padded_temp[1:-1, 1:-1, 1:-1]
    center_cond = padded_cond[1:-1, 1:-1, 1:-1]
    depth, across, radial = center_temp.shape
    radial_index = jnp.arange(radial, dtype=jnp.int32)
    gap_row = radial // 2
    outward_open = (radial_index != gap_row - 1).astype(jnp.float32)
    inward_open = (radial_index != gap_row).astype(jnp.float32)
    total = jnp.zeros(center_temp.shape, jnp.float32)
    for shift_z in (-1, 0, 1):
        for shift_a in (-1, 0, 1):
            for shift_r in (-1, 0, 1):
                if shift_z == 0 and shift_a == 0 and (shift_r == 0):
                    continue
                near_temp = padded_temp[
                    1 + shift_z : 1 + shift_z + depth,
                    1 + shift_a : 1 + shift_a + across,
                    1 + shift_r : 1 + shift_r + radial,
                ]
                near_cond = padded_cond[
                    1 + shift_z : 1 + shift_z + depth,
                    1 + shift_a : 1 + shift_a + across,
                    1 + shift_r : 1 + shift_r + radial,
                ]
                face = neighbour_weight(shift_z, shift_a, shift_r) * 0.5 * (center_cond + near_cond)
                if shift_r == 1:
                    face = face * outward_open
                elif shift_r == -1:
                    face = face * inward_open
                total = total + face * (near_temp - center_temp)
    return FLUX_STEP * total


def creep_return(mech_temp, trial, active_layers):
    rate = CREEP_RATE * jnp.exp(-ACTIVATION / (mech_temp + REFERENCE_TEMP))
    slip = jnp.zeros(trial.shape, jnp.float32)
    for newton_step in range(NEWTON):
        left = trial - slip
        residue = slip - rate * left**3
        slope = 1.0 + 3.0 * rate * left**2
        slip = slip - residue / slope
    depth = trial.shape[0]
    layer = jnp.arange(depth, dtype=jnp.int32) // 8
    live = (layer[:, None, None] < active_layers[None, :, :]).astype(jnp.float32)[..., None]
    creep = live * slip
    stress = trial - creep
    strain = jnp.sum(creep.reshape((depth // 8, 8) + trial.shape[1:]), axis=1) * 0.125
    return (stress, strain)


def stepwise(
    temp_start, conductivity, gap_conductance, partner, row_order, active_layers, trial_stress
):
    depth = temp_start.shape[0]
    rows = temp_start.shape[2]
    radial = temp_start.shape[3]
    temp = temp_start.reshape(depth, rows, radial)
    cond = conductivity.reshape(depth, rows, radial)
    gap = gap_conductance.reshape(depth, rows)
    gap_row = radial // 2
    sections = lax.axis_size("iface")
    across = rows * sections
    all_cols = jnp.arange(across, dtype=jnp.int32)
    cond_rim = padded(cond, ((("slab", "mech"), 0), ("iface", 1)), 1)
    padded_cond = jnp.pad(cond_rim, ((0, 0), (0, 0), (1, 1)))
    spread_table = (partner[:, None] == all_cols[None, :]).astype(jnp.float32)
    for sweep in range(SWEEPS):
        temp_rim = padded(temp, ((("slab", "mech"), 0), ("iface", 1)), 1)
        padded_temp = jnp.pad(temp_rim, ((0, 0), (0, 0), (1, 1)))
        compact = temp[:, :, gap_row - 1]
        canister = temp[:, :, gap_row]
        compact_all = lax.all_gather(compact, "iface", axis=1, tiled=True)
        facing = jnp.take(compact_all, partner, axis=1)
        flux = gap * (facing - canister)
        spread = jnp.dot(
            flux, spread_table, precision=lax.Precision.HIGHEST, preferred_element_type=jnp.float32
        )
        returned = lax.psum_scatter(spread, "iface", scatter_dimension=1, tiled=True)
        fresh = temp + conduction(padded_temp, padded_cond)
        temp = (
            fresh.at[:, :, gap_row]
            .add(FLUX_STEP * flux)
            .at[:, :, gap_row - 1]
            .add(-FLUX_STEP * returned)
        )
    permuted = jnp.take(temp, row_order[0], axis=1)
    mech_temp = lax.all_to_all(permuted, ("slab", "mech"), split_axis=1, concat_axis=0, tiled=True)
    mech_temp = mech_temp.reshape(mech_temp.shape[0], 1, mech_temp.shape[1], radial)
    return creep_return(mech_temp, trial_stress, active_layers)


LANES = 128
HALO = 2
EVERYONE = ("iface", "mech", "slab")


def iota(shape, axis):
    return lax.broadcasted_iota(jnp.int32, shape, axis)


class Sizes:
    def __init__(self, layers, rows, radial):
        self.layers = layers
        self.rows = rows
        self.radial = radial
        self.tiles = radial // LANES
        self.sections = lax.axis_size("iface")
        self.members = lax.axis_size("slab") * lax.axis_size("mech")
        self.devices = self.sections * self.members
        self.depth = layers * self.members
        self.chunk = radial // self.devices
        self.width = self.chunk + 2 * HALO
        self.layer_lanes = LANES // layers
        self.extra_at = 3 * self.width
        self.gap_row = radial // 2


def chunk_of(sizes, section, member):
    mirrored = section < sizes.sections // 2
    if isinstance(section, int):
        place = sizes.members - 1 - member if mirrored else member
    else:
        place = jnp.where(mirrored, sizes.members - 1 - member, member)
    return section * sizes.members + place


def fits_tiles(sizes):
    return (
        sizes.rows == 8
        and sizes.members == sizes.rows
        and sizes.layers == 2
        and sizes.sections * sizes.rows <= LANES
        and sizes.radial % sizes.devices == 0
        and sizes.chunk * 8 == LANES
        and sizes.radial % (2 * LANES) == 0
        and sizes.extra_at + 3 <= sizes.layer_lanes
    )


def deal_kernel(
    sizes,
    partner_hbm,
    order_hbm,
    gap_hbm,
    temp_hbm,
    cond_hbm,
    active_ref,
    out_ref,
    live_ref,
    partner_ref,
    order_ref,
    gap_ref,
    temp_ref,
    cond_ref,
    sems,
):
    pairs = (
        (gap_hbm, gap_ref),
        (partner_hbm, partner_ref),
        (order_hbm, order_ref),
        (temp_hbm, temp_ref),
        (cond_hbm, cond_ref),
    )
    copies = [
        pltpu.make_async_copy(source, target, sems.at[index])
        for index, (source, target) in enumerate(pairs)
    ]
    for copy in copies:
        copy.start()
    for copy in copies[:3]:
        copy.wait()
    shape = (sizes.rows, LANES)
    lane = iota(shape, 1)
    sub = iota(shape, 0)
    live_ref[...] = jnp.where(sub < active_ref[0, 0], 1.0, 0.0)
    extra_at = sizes.extra_at
    extra = jnp.zeros(shape, jnp.float32)
    for row in range(sizes.rows):
        for layer in range(sizes.layers):
            spot = (sub == row) & (lane == extra_at + layer * sizes.layer_lanes)
            extra = jnp.where(spot, gap_ref[layer, 0, row], extra)
        spot = (sub == row) & (lane == extra_at + 1)
        extra = jnp.where(spot, partner_ref[row].astype(jnp.float32), extra)
        extra = jnp.where(
            lane == 2 * sizes.width + row, partner_ref[row].astype(jnp.float32), extra
        )
        spot = (sub == row) & (lane == extra_at + 2)
        extra = jnp.where(spot, order_ref[0, row].astype(jnp.float32), extra)
    for copy in copies[3:]:
        copy.wait()
    blocks = [
        (
            layer * sizes.layer_lanes + field * sizes.width,
            [scale * ref[layer, 0, :, pl.ds(tile * LANES, LANES)] for tile in range(sizes.tiles)],
        )
        for field, (ref, scale) in enumerate(((temp_ref, 1.0), (cond_ref, FLUX_STEP)))
        for layer in range(sizes.layers)
    ]
    for device in range(sizes.devices):
        chunk = chunk_of(sizes, device // sizes.members, device % sizes.members)
        first = chunk * sizes.chunk - HALO
        packed = extra
        for base, block in blocks:
            for tile in range(sizes.tiles):
                low = max(first, tile * LANES)
                high = min(first + sizes.width, (tile + 1) * LANES)
                if low >= high:
                    continue
                moved = pltpu.roll(block[tile], (base - first + tile * LANES) % LANES, 1)
                spot = (lane >= base + low - first) & (lane < base + high - first)
                packed = jnp.where(spot, moved, packed)
        out_ref[device] = packed


def sweep_kernel(sizes, dealt_ref, out_ref, line_ref, temp_ref, table_ref, gap_ref):
    rows, width, half_lanes = sizes.rows, sizes.width, sizes.layer_lanes
    sections, members = sizes.sections, sizes.members
    shape = (rows, LANES)
    lane = iota(shape, 1)
    sub = iota(shape, 0)
    slabs, per_slab = lax.axis_size("slab"), lax.axis_size("mech")
    member = lax.axis_index("mech") * slabs + lax.axis_index("slab")
    place = chunk_of(sizes, lax.axis_index("iface"), member)
    first = place * sizes.chunk - HALO
    spot_in_layer = lane % half_lanes
    radius = first + spot_in_layer % width
    lower_layer = lane < half_lanes
    at_compact = radius == sizes.gap_row - 1
    at_canister = radius == sizes.gap_row
    weight = jnp.where(at_compact | at_canister, 6.0, 8.0)
    is_temp = spot_in_layer < width
    at_face = jnp.where(is_temp & (at_compact | at_canister), 1.0, 0.0)
    from_inward = jnp.where(at_canister | (radius == 0), 0.0, 0.5)
    from_outward = jnp.where(at_compact | (radius == sizes.radial - 1), 0.0, 0.5)
    face_lane = sizes.gap_row - 1 - first

    def turn(value, shift):
        return pltpu.roll(value, shift % LANES, 1)

    dealt = [[dealt_ref[s * members + k % per_slab * slabs + k // per_slab] for k in range(members)] for s in range(sections)]

    odd = lane % 2 == 1

    def strip_of(values, start):
        strips = []
        for s in range(sections):
            strip = jnp.zeros(shape, jnp.float32)
            for k in range(members):
                moved = pltpu.roll(values[s][k], (start + 2 * k) % LANES, 1)
                spot = spot_in_layer // 2 == k
                strip = jnp.where(spot, moved, strip)
            strips.append(strip)
        return jnp.concatenate(strips, axis=0)

    total = sections * rows
    has_face = (first < sizes.gap_row) & (first + width > sizes.gap_row)
    wide_odd = jnp.concatenate([odd] * sections, axis=0)

    def pick(table, strip):
        rest = strip
        picked = None
        for _ in range(3):
            part = rest.astype(jnp.bfloat16)
            rest = rest - part.astype(jnp.float32)
            share = jnp.dot(table, part, preferred_element_type=jnp.float32)
            picked = share if picked is None else picked + share
        return picked

    @pl.when(has_face)
    def prepare_exchange():
        names = jnp.full(shape, -1.0, jnp.float32)
        for s in range(sections):
            names = jnp.where(lane // rows == s, turn(dealt[s][0], s * rows - 2 * width), names)
        for s in range(sections):
            partner = dealt[s][0][:, sizes.extra_at + 1 : sizes.extra_at + 2].astype(jnp.int32)
            table_ref[pl.ds(s * rows, rows), :] = jnp.where(lane == partner, 1.0, 0.0)
        for s in range(sections):
            target = (s * rows + sub).astype(jnp.float32)
            table_ref[pl.ds(total + s * rows, rows), :] = jnp.where(names == target, 1.0, 0.0)
        table = table_ref[pl.ds(total, total), :][:, :total].astype(jnp.bfloat16)
        gap = strip_of(dealt, LANES + 1 - sizes.extra_at)
        gap_ref[...] = FLUX_STEP * jnp.where(wide_odd, gap, turn(pick(table, gap), -1))

    def exchange(values):
        strip = strip_of(values, LANES - face_lane)
        met = pick(table_ref[...][:, :total].astype(jnp.bfloat16), strip)
        met = jnp.where(wide_odd, turn(met[:total], 1), turn(met[total:], -1))
        gain = gap_ref[...] * (met - strip)
        for s in range(sections):
            own = gain[s * rows : (s + 1) * rows]
            for k in range(members):
                back = pltpu.roll(own, (face_lane - 2 * k + LANES) % LANES, 1)
                temp_ref[s, k] = temp_ref[s, k] + at_face * back

    conds = [[turn(value, -width) for value in line] for line in dealt]
    edge = jnp.zeros(shape, jnp.float32)
    for k in range(members):
        line_ref[k, pl.ds(0, rows), :] = edge
        line_ref[k, pl.ds(rows + total, rows), :] = edge

    def with_product(value, cond):
        return jnp.where(spot_in_layer < 2 * width, value, turn(value * cond, 2 * width))

    def box_sum(values):
        for s in range(sections):
            other = [turn(value, half_lanes) for value in values[s]]
            for k in range(members):
                before = other[k - 1] if k else 0.0
                after = other[k + 1] if k < members - 1 else 0.0
                near = other[k] + jnp.where(lower_layer, before, after)
                line_ref[k, pl.ds(rows + s * rows, rows), :] = values[s][k] + 0.5 * near
        result = []
        for s in range(sections):
            line = []
            for k in range(members):
                start = rows + s * rows
                near = line_ref[k, pl.ds(start - 1, rows), :] + line_ref[k, pl.ds(start + 1, rows), :]
                value = line_ref[k, pl.ds(start, rows), :] + 0.5 * near
                line.append(value + from_inward * turn(value, 1) + from_outward * turn(value, -1))
            result.append(line)
        return result

    values = dealt
    keeps = None
    for sweep in range(SWEEPS):
        packed = [
            [with_product(value, cond) for value, cond in zip(*lines)]
            for lines in zip(values, conds)
        ]
        sums = box_sum(packed)
        if keeps is None:
            keeps = [
                [1.0 - weight * cond - turn(total_sum, -width) for cond, total_sum in zip(*lines)]
                for lines in zip(conds, sums)
            ]
        for s in range(sections):
            for k in range(members):
                temp = values[s][k] * keeps[s][k] + conds[s][k] * sums[s][k]
                temp_ref[s, k] = temp + turn(sums[s][k], -2 * width)
        pl.when(has_face)(functools.partial(exchange, values))
        values = [[temp_ref[s, k] for k in range(members)] for s in range(sections)]

    per_row = 8 // sizes.layers
    skew = place % 8 * sizes.chunk
    unskewed = (lane - skew + LANES) % half_lanes
    for s in range(sections):
        order = dealt[s][0][:, sizes.extra_at + 2 : sizes.extra_at + 3].astype(jnp.int32)
        order = jnp.broadcast_to(order, shape)
        for half in range(sizes.depth // 8):
            merged = jnp.zeros(shape, jnp.float32)
            for k in range(per_row):
                moved = pltpu.roll(
                    values[s][half * per_row + k], (k * sizes.chunk - HALO + skew) % LANES, 1
                )
                merged = jnp.where(unskewed // sizes.chunk == k, moved, merged)
            chosen = jnp.take_along_axis(merged, order, axis=0)
            halves = sizes.depth // 8
            for slab in range(slabs):
                start = (s * members + slab) * halves + half
                out_ref[pl.ds(start, per_slab, stride=slabs * halves), :] = chosen[
                    slab * per_slab : (slab + 1) * per_slab
                ]


def swap_blocks(tile, block, layers, mirrored):
    sub = iota(tile.shape, 0)
    spot = iota(tile.shape, 1) // block
    held = sub % layers * (8 // layers) + sub // layers
    source = (spot - held + 8) % 8
    gathered = jnp.take_along_axis(tile, 7 - source if mirrored else source, axis=0)
    rolled = [pltpu.roll(gathered, (8 - row) % 8 * block, 1) if row else gathered for row in range(8)]
    result = rolled[0]
    for row in range(1, 8):
        result = jnp.where(held == row, rolled[row], result)
    return result


def creep_kernel(sizes, live_ref, temps_ref, trial_ref, stress_ref, strain_ref):
    tiles = sizes.tiles
    halves = sizes.depth // 8
    for tile in range(tiles):
        for element in range(halves):
            source = pl.ds(tile * 8 * halves + element, 8, stride=halves)
            mech_temp = swap_blocks(
                temps_ref[source, :], sizes.chunk, sizes.layers, tile < sizes.sections // 2
            )
            spot = pl.ds(element * 8 * tiles + tile, 8, stride=tiles)
            trial = trial_ref[spot, :]
            rate = CREEP_RATE * jnp.exp(-ACTIVATION / (mech_temp + REFERENCE_TEMP))
            slip = jnp.zeros(trial.shape, jnp.float32)
            for newton_step in range(NEWTON):
                left = trial - slip
                pull = rate * left * left
                slip = slip - (slip - pull * left) / (1.0 + 3.0 * pull)
            creep = live_ref[pl.ds(element, 1), :] * slip
            stress_ref[spot, :] = trial - creep
            strain_ref[pl.ds(element * tiles + tile, 1), :] = 0.125 * jnp.sum(
                creep, axis=0, keepdims=True
            )


def kernel_call(body, sizes, out_shape, memories, scratch, operands):
    out_spec = pl.BlockSpec(memory_space=pltpu.VMEM)
    pinned = [
        pltpu.with_memory_space_constraint(operand, memory) if memory is pltpu.HBM else operand
        for operand, memory in zip(operands, memories)
    ]
    return pl.pallas_call(
        functools.partial(body, sizes),
        out_shape=out_shape,
        in_specs=[pl.BlockSpec(memory_space=memory) for memory in memories],
        out_specs=[out_spec] * len(out_shape),
        scratch_shapes=scratch,
        compiler_params=pltpu.CompilerParams(vmem_limit_bytes=16 * 1024 * 1024),
    )(*pinned)


def on_device(
    temp_start, conductivity, gap_conductance, partner, row_order, active_layers, trial_stress
):
    layers, _, rows, radial = temp_start.shape
    sizes = Sizes(layers, rows, radial)
    if not fits_tiles(sizes):
        return stepwise(
            temp_start,
            conductivity,
            gap_conductance,
            partner,
            row_order,
            active_layers,
            trial_stress,
        )

    def floats(*shape):
        return jax.ShapeDtypeStruct(shape, jnp.float32)

    def near(*shape):
        return pltpu.VMEM(shape, jnp.float32)

    dealt, live = kernel_call(
        deal_kernel,
        sizes,
        (near(sizes.devices, rows, LANES), near(8, LANES)),
        [pltpu.HBM] * 5 + [pltpu.SMEM],
        [
            pltpu.SMEM(partner.shape, jnp.int32),
            pltpu.SMEM(row_order.shape, jnp.int32),
            pltpu.SMEM(gap_conductance.shape, jnp.float32),
            pltpu.VMEM(temp_start.shape, jnp.float32),
            pltpu.VMEM(conductivity.shape, jnp.float32),
            pltpu.SemaphoreType.DMA((5,)),
        ],
        (partner, row_order, gap_conductance, temp_start, conductivity, active_layers),
    )
    dealt = lax.all_to_all(dealt, EVERYONE, split_axis=0, concat_axis=0, tiled=True)
    halves = sizes.depth // 8
    (temps,) = kernel_call(
        sweep_kernel,
        sizes,
        (near(sizes.devices * halves, LANES),),
        [pltpu.VMEM],
        [
            pltpu.VMEM((sizes.members, rows * (sizes.sections + 2), LANES), jnp.float32),
            pltpu.VMEM((sizes.sections, sizes.members, rows, LANES), jnp.float32),
            pltpu.VMEM((2 * sizes.sections * rows, LANES), jnp.float32),
            pltpu.VMEM((sizes.sections * rows, LANES), jnp.float32),
        ],
        (dealt,),
    )
    temps = temps.reshape(sizes.devices, halves, LANES)
    temps = lax.all_to_all(temps, EVERYONE, split_axis=0, concat_axis=0, tiled=True)
    stress, strain = kernel_call(
        creep_kernel,
        sizes,
        (floats(sizes.depth * sizes.tiles, LANES), floats(halves * sizes.tiles, LANES)),
        [pltpu.VMEM, pltpu.VMEM, pltpu.VMEM],
        [],
        (
            live,
            temps.reshape(sizes.devices * halves, LANES),
            trial_stress.reshape(sizes.depth * sizes.tiles, LANES),
        ),
    )
    return (
        stress.reshape(sizes.depth, 1, 1, radial),
        strain.reshape(halves, 1, 1, radial),
    )


def solution(mesh):
    placed = (
        P(("slab", "mech"), "iface", None, None),
        P(("slab", "mech"), "iface", None, None),
        P(("slab", "mech"), "iface", None),
        P("iface"),
        P("iface", None),
        P("iface", ("slab", "mech")),
        P(None, "iface", ("slab", "mech"), None),
    )
    return jax.shard_map(
        on_device,
        mesh=mesh,
        in_specs=placed,
        out_specs=(
            P(None, "iface", ("slab", "mech"), None),
            P(None, "iface", ("slab", "mech"), None),
        ),
        check_vma=False,
    )
```

```python
import functools
import jax
import jax.numpy as jnp
from jax import lax
from jax.experimental import pallas as pl
from jax.experimental.pallas import tpu as pltpu
from jax.sharding import PartitionSpec as P

SWEEPS = 2
NEWTON = 4


FLUX_STEP = 0.03
CREEP_RATE = 200.0
ACTIVATION = 12.0
REFERENCE_TEMP = 1.0


def padded(block, sides, width):
    for axis, dim in sides:
        count = lax.axis_size(axis)
        forward = [(i, i + 1) for i in range(count - 1)]
        backward = [(target, source) for source, target in forward]
        low = lax.ppermute(
            lax.slice_in_dim(block, block.shape[dim] - width, None, axis=dim), axis, forward
        )
        high = lax.ppermute(lax.slice_in_dim(block, 0, width, axis=dim), axis, backward)
        block = jnp.concatenate([low, block, high], axis=dim)
    return block


def neighbour_weight(shift_z, shift_a, shift_r):
    reach = abs(shift_z) + abs(shift_a) + abs(shift_r)
    return [0.0, 1.0, 0.5, 0.25][reach]


def conduction(padded_temp, padded_cond):
    center_temp = padded_temp[1:-1, 1:-1, 1:-1]
    center_cond = padded_cond[1:-1, 1:-1, 1:-1]
    depth, across, radial = center_temp.shape
    radial_index = jnp.arange(radial, dtype=jnp.int32)
    gap_row = radial // 2
    outward_open = (radial_index != gap_row - 1).astype(jnp.float32)
    inward_open = (radial_index != gap_row).astype(jnp.float32)
    total = jnp.zeros(center_temp.shape, jnp.float32)
    for shift_z in (-1, 0, 1):
        for shift_a in (-1, 0, 1):
            for shift_r in (-1, 0, 1):
                if shift_z == 0 and shift_a == 0 and (shift_r == 0):
                    continue
                near_temp = padded_temp[
                    1 + shift_z : 1 + shift_z + depth,
                    1 + shift_a : 1 + shift_a + across,
                    1 + shift_r : 1 + shift_r + radial,
                ]
                near_cond = padded_cond[
                    1 + shift_z : 1 + shift_z + depth,
                    1 + shift_a : 1 + shift_a + across,
                    1 + shift_r : 1 + shift_r + radial,
                ]
                face = neighbour_weight(shift_z, shift_a, shift_r) * 0.5 * (center_cond + near_cond)
                if shift_r == 1:
                    face = face * outward_open
                elif shift_r == -1:
                    face = face * inward_open
                total = total + face * (near_temp - center_temp)
    return FLUX_STEP * total


def creep_return(mech_temp, trial, active_layers):
    rate = CREEP_RATE * jnp.exp(-ACTIVATION / (mech_temp + REFERENCE_TEMP))
    slip = jnp.zeros(trial.shape, jnp.float32)
    for newton_step in range(NEWTON):
        left = trial - slip
        residue = slip - rate * left**3
        slope = 1.0 + 3.0 * rate * left**2
        slip = slip - residue / slope
    depth = trial.shape[0]
    layer = jnp.arange(depth, dtype=jnp.int32) // 8
    live = (layer[:, None, None] < active_layers[None, :, :]).astype(jnp.float32)[..., None]
    creep = live * slip
    stress = trial - creep
    strain = jnp.sum(creep.reshape((depth // 8, 8) + trial.shape[1:]), axis=1) * 0.125
    return (stress, strain)


def stepwise(
    temp_start, conductivity, gap_conductance, partner, row_order, active_layers, trial_stress
):
    depth = temp_start.shape[0]
    rows = temp_start.shape[2]
    radial = temp_start.shape[3]
    temp = temp_start.reshape(depth, rows, radial)
    cond = conductivity.reshape(depth, rows, radial)
    gap = gap_conductance.reshape(depth, rows)
    gap_row = radial // 2
    sections = lax.axis_size("iface")
    across = rows * sections
    all_cols = jnp.arange(across, dtype=jnp.int32)
    cond_rim = padded(cond, ((("slab", "mech"), 0), ("iface", 1)), 1)
    padded_cond = jnp.pad(cond_rim, ((0, 0), (0, 0), (1, 1)))
    spread_table = (partner[:, None] == all_cols[None, :]).astype(jnp.float32)
    for sweep in range(SWEEPS):
        temp_rim = padded(temp, ((("slab", "mech"), 0), ("iface", 1)), 1)
        padded_temp = jnp.pad(temp_rim, ((0, 0), (0, 0), (1, 1)))
        compact = temp[:, :, gap_row - 1]
        canister = temp[:, :, gap_row]
        compact_all = lax.all_gather(compact, "iface", axis=1, tiled=True)
        facing = jnp.take(compact_all, partner, axis=1)
        flux = gap * (facing - canister)
        spread = jnp.dot(
            flux, spread_table, precision=lax.Precision.HIGHEST, preferred_element_type=jnp.float32
        )
        returned = lax.psum_scatter(spread, "iface", scatter_dimension=1, tiled=True)
        fresh = temp + conduction(padded_temp, padded_cond)
        temp = (
            fresh.at[:, :, gap_row]
            .add(FLUX_STEP * flux)
            .at[:, :, gap_row - 1]
            .add(-FLUX_STEP * returned)
        )
    permuted = jnp.take(temp, row_order[0], axis=1)
    mech_temp = lax.all_to_all(permuted, ("slab", "mech"), split_axis=1, concat_axis=0, tiled=True)
    mech_temp = mech_temp.reshape(mech_temp.shape[0], 1, mech_temp.shape[1], radial)
    return creep_return(mech_temp, trial_stress, active_layers)


LANES = 128
HALO = 2
EVERYONE = ("iface", "slab", "mech")


def iota(shape, axis):
    return lax.broadcasted_iota(jnp.int32, shape, axis)


class Sizes:
    def __init__(self, layers, rows, radial):
        self.layers = layers
        self.rows = rows
        self.radial = radial
        self.tiles = radial // LANES
        self.sections = lax.axis_size("iface")
        self.members = lax.axis_size("slab") * lax.axis_size("mech")
        self.devices = self.sections * self.members
        self.depth = layers * self.members
        self.chunk = radial // self.devices
        self.width = self.chunk + 2 * HALO
        self.layer_lanes = LANES // layers
        self.extra_at = 3 * self.width
        self.gap_row = radial // 2


def chunk_of(sizes, section, member):
    mirrored = section < sizes.sections // 2
    if isinstance(section, int):
        place = sizes.members - 1 - member if mirrored else member
    else:
        place = jnp.where(mirrored, sizes.members - 1 - member, member)
    return section * sizes.members + place


def fits_tiles(sizes):
    return (
        sizes.rows == 8
        and sizes.members == sizes.rows
        and sizes.layers == 2
        and sizes.sections * sizes.rows <= LANES
        and sizes.radial % sizes.devices == 0
        and sizes.chunk * 8 == LANES
        and sizes.radial % (2 * LANES) == 0
        and sizes.extra_at + 3 <= sizes.layer_lanes
    )


def deal_kernel(
    sizes,
    partner_hbm,
    order_hbm,
    gap_hbm,
    temp_hbm,
    cond_hbm,
    active_ref,
    out_ref,
    live_ref,
    partner_ref,
    order_ref,
    gap_ref,
    temp_ref,
    cond_ref,
    sems,
):
    pairs = (
        (gap_hbm, gap_ref),
        (partner_hbm, partner_ref),
        (order_hbm, order_ref),
        (temp_hbm, temp_ref),
        (cond_hbm, cond_ref),
    )
    copies = [
        pltpu.make_async_copy(source, target, sems.at[index])
        for index, (source, target) in enumerate(pairs)
    ]
    for copy in copies:
        copy.start()
    for copy in copies[:3]:
        copy.wait()
    shape = (sizes.rows, LANES)
    lane = iota(shape, 1)
    sub = iota(shape, 0)
    live_ref[...] = jnp.where(sub < active_ref[0, 0], 1.0, 0.0)
    extra_at = sizes.extra_at
    extra = jnp.zeros(shape, jnp.float32)
    for row in range(sizes.rows):
        for layer in range(sizes.layers):
            spot = (sub == row) & (lane == extra_at + layer * sizes.layer_lanes)
            extra = jnp.where(spot, gap_ref[layer, 0, row], extra)
        spot = (sub == row) & (lane == extra_at + 1)
        extra = jnp.where(spot, partner_ref[row].astype(jnp.float32), extra)
        extra = jnp.where(
            lane == 2 * sizes.width + row, partner_ref[row].astype(jnp.float32), extra
        )
        spot = (sub == row) & (lane == extra_at + 2)
        extra = jnp.where(spot, order_ref[0, row].astype(jnp.float32), extra)
    for copy in copies[3:]:
        copy.wait()
    blocks = [
        (
            layer * sizes.layer_lanes + field * sizes.width,
            [scale * ref[layer, 0, :, pl.ds(tile * LANES, LANES)] for tile in range(sizes.tiles)],
        )
        for field, (ref, scale) in enumerate(((temp_ref, 1.0), (cond_ref, FLUX_STEP)))
        for layer in range(sizes.layers)
    ]
    for device in range(sizes.devices):
        chunk = chunk_of(sizes, device // sizes.members, device % sizes.members)
        first = chunk * sizes.chunk - HALO
        packed = extra
        for base, block in blocks:
            for tile in range(sizes.tiles):
                low = max(first, tile * LANES)
                high = min(first + sizes.width, (tile + 1) * LANES)
                if low >= high:
                    continue
                moved = pltpu.roll(block[tile], (base - first + tile * LANES) % LANES, 1)
                spot = (lane >= base + low - first) & (lane < base + high - first)
                packed = jnp.where(spot, moved, packed)
        out_ref[device] = packed


def sweep_kernel(sizes, dealt_ref, out_ref, line_ref, temp_ref, table_ref, gap_ref):
    rows, width, half_lanes = sizes.rows, sizes.width, sizes.layer_lanes
    sections, members = sizes.sections, sizes.members
    shape = (rows, LANES)
    lane = iota(shape, 1)
    sub = iota(shape, 0)
    member = lax.axis_index("slab") * lax.axis_size("mech") + lax.axis_index("mech")
    place = chunk_of(sizes, lax.axis_index("iface"), member)
    first = place * sizes.chunk - HALO
    spot_in_layer = lane % half_lanes
    radius = first + spot_in_layer % width
    lower_layer = lane < half_lanes
    at_compact = radius == sizes.gap_row - 1
    at_canister = radius == sizes.gap_row
    weight = jnp.where(at_compact | at_canister, 6.0, 8.0)
    is_temp = spot_in_layer < width
    at_face = jnp.where(is_temp & (at_compact | at_canister), 1.0, 0.0)
    from_inward = jnp.where(at_canister | (radius == 0), 0.0, 0.5)
    from_outward = jnp.where(at_compact | (radius == sizes.radial - 1), 0.0, 0.5)
    face_lane = sizes.gap_row - 1 - first

    def turn(value, shift):
        return pltpu.roll(value, shift % LANES, 1)

    dealt = [[dealt_ref[s * members + k] for k in range(members)] for s in range(sections)]

    odd = lane % 2 == 1

    def strip_of(values, start):
        strips = []
        for s in range(sections):
            strip = jnp.zeros(shape, jnp.float32)
            for k in range(members):
                moved = pltpu.roll(values[s][k], (start + 2 * k) % LANES, 1)
                spot = spot_in_layer // 2 == k
                strip = jnp.where(spot, moved, strip)
            strips.append(strip)
        return jnp.concatenate(strips, axis=0)

    total = sections * rows
    has_face = (first < sizes.gap_row) & (first + width > sizes.gap_row)
    wide_odd = jnp.concatenate([odd] * sections, axis=0)

    def pick(table, strip):
        rest = strip
        picked = None
        for _ in range(3):
            part = rest.astype(jnp.bfloat16)
            rest = rest - part.astype(jnp.float32)
            share = jnp.dot(table, part, preferred_element_type=jnp.float32)
            picked = share if picked is None else picked + share
        return picked

    @pl.when(has_face)
    def prepare_exchange():
        names = jnp.full(shape, -1.0, jnp.float32)
        for s in range(sections):
            names = jnp.where(lane // rows == s, turn(dealt[s][0], s * rows - 2 * width), names)
        for s in range(sections):
            partner = dealt[s][0][:, sizes.extra_at + 1 : sizes.extra_at + 2].astype(jnp.int32)
            table_ref[pl.ds(s * rows, rows), :] = jnp.where(lane == partner, 1.0, 0.0)
        for s in range(sections):
            target = (s * rows + sub).astype(jnp.float32)
            table_ref[pl.ds(total + s * rows, rows), :] = jnp.where(names == target, 1.0, 0.0)
        table = table_ref[pl.ds(total, total), :][:, :total].astype(jnp.bfloat16)
        gap = strip_of(dealt, LANES + 1 - sizes.extra_at)
        gap_ref[...] = FLUX_STEP * jnp.where(wide_odd, gap, turn(pick(table, gap), -1))

    def exchange(values):
        strip = strip_of(values, LANES - face_lane)
        met = pick(table_ref[...][:, :total].astype(jnp.bfloat16), strip)
        met = jnp.where(wide_odd, turn(met[:total], 1), turn(met[total:], -1))
        gain = gap_ref[...] * (met - strip)
        for s in range(sections):
            own = gain[s * rows : (s + 1) * rows]
            for k in range(members):
                back = pltpu.roll(own, (face_lane - 2 * k + LANES) % LANES, 1)
                temp_ref[s, k] = temp_ref[s, k] + at_face * back

    conds = [[turn(value, -width) for value in line] for line in dealt]
    edge = jnp.zeros(shape, jnp.float32)
    for k in range(members):
        line_ref[k, pl.ds(0, rows), :] = edge
        line_ref[k, pl.ds(rows + total, rows), :] = edge

    def with_product(value, cond):
        return jnp.where(spot_in_layer < 2 * width, value, turn(value * cond, 2 * width))

    def box_sum(values):
        for s in range(sections):
            other = [turn(value, half_lanes) for value in values[s]]
            for k in range(members):
                before = other[k - 1] if k else 0.0
                after = other[k + 1] if k < members - 1 else 0.0
                near = other[k] + jnp.where(lower_layer, before, after)
                line_ref[k, pl.ds(rows + s * rows, rows), :] = values[s][k] + 0.5 * near
        result = []
        for s in range(sections):
            line = []
            for k in range(members):
                start = rows + s * rows
                near = line_ref[k, pl.ds(start - 1, rows), :] + line_ref[k, pl.ds(start + 1, rows), :]
                value = line_ref[k, pl.ds(start, rows), :] + 0.5 * near
                line.append(value + from_inward * turn(value, 1) + from_outward * turn(value, -1))
            result.append(line)
        return result

    values = dealt
    keeps = None
    for sweep in range(SWEEPS):
        packed = [
            [with_product(value, cond) for value, cond in zip(*lines)]
            for lines in zip(values, conds)
        ]
        sums = box_sum(packed)
        if keeps is None:
            keeps = [
                [1.0 - weight * cond - turn(total_sum, -width) for cond, total_sum in zip(*lines)]
                for lines in zip(conds, sums)
            ]
        for s in range(sections):
            for k in range(members):
                temp = values[s][k] * keeps[s][k] + conds[s][k] * sums[s][k]
                temp_ref[s, k] = temp + turn(sums[s][k], -2 * width)
        pl.when(has_face)(functools.partial(exchange, values))
        values = [[temp_ref[s, k] for k in range(members)] for s in range(sections)]

    per_row = 8 // sizes.layers
    skew = place % 8 * sizes.chunk
    unskewed = (lane - skew + LANES) % half_lanes
    for s in range(sections):
        order = dealt[s][0][:, sizes.extra_at + 2 : sizes.extra_at + 3].astype(jnp.int32)
        order = jnp.broadcast_to(order, shape)
        for half in range(sizes.depth // 8):
            merged = jnp.zeros(shape, jnp.float32)
            for k in range(per_row):
                moved = pltpu.roll(
                    values[s][half * per_row + k], (k * sizes.chunk - HALO + skew) % LANES, 1
                )
                merged = jnp.where(unskewed // sizes.chunk == k, moved, merged)
            chosen = jnp.take_along_axis(merged, order, axis=0)
            start = s * rows * (sizes.depth // 8) + half
            out_ref[pl.ds(start, rows, stride=sizes.depth // 8), :] = chosen


def swap_blocks(tile, block, layers, mirrored):
    sub = iota(tile.shape, 0)
    spot = iota(tile.shape, 1) // block
    held = sub % layers * (8 // layers) + sub // layers
    source = (spot - held + 8) % 8
    gathered = jnp.take_along_axis(tile, 7 - source if mirrored else source, axis=0)
    rolled = [pltpu.roll(gathered, (8 - row) % 8 * block, 1) if row else gathered for row in range(8)]
    result = rolled[0]
    for row in range(1, 8):
        result = jnp.where(held == row, rolled[row], result)
    return result


def creep_kernel(
    sizes, live_ref, temps_ref, trial_ref, stress_hbm, strain_hbm, stress_ref, strain_ref, sems
):
    tiles = sizes.tiles
    halves = sizes.depth // 8
    copies = []
    for element in range(halves):
        for tile in range(tiles):
            source = pl.ds(tile * 8 * halves + element, 8, stride=halves)
            mech_temp = swap_blocks(
                temps_ref[source, :], sizes.chunk, sizes.layers, tile < sizes.sections // 2
            )
            trial = trial_ref[pl.ds(element * 8 * tiles + tile, 8, stride=tiles), :]
            rate = CREEP_RATE * jnp.exp(-ACTIVATION / (mech_temp + REFERENCE_TEMP))
            slip = jnp.zeros(trial.shape, jnp.float32)
            for newton_step in range(NEWTON):
                left = trial - slip
                pull = rate * left * left
                slip = slip - (slip - pull * left) / (1.0 + 3.0 * pull)
            creep = live_ref[pl.ds(element, 1), :] * slip
            stress_ref[element, pl.ds(tile, 8, stride=tiles), :] = trial - creep
            strain_ref[pl.ds(element * tiles + tile, 1), :] = 0.125 * jnp.sum(
                creep, axis=0, keepdims=True
            )
        rows = pl.ds(element * 8 * tiles, 8 * tiles)
        copies.append(
            pltpu.make_async_copy(stress_ref.at[element], stress_hbm.at[rows], sems.at[element])
        )
        copies[-1].start()
    copies.append(pltpu.make_async_copy(strain_ref, strain_hbm, sems.at[halves]))
    copies[-1].start()
    for copy in copies:
        copy.wait()


def kernel_call(body, sizes, out_shape, memories, scratch, operands, space=pltpu.VMEM):
    out_spec = pl.BlockSpec(memory_space=space)
    pinned = [
        pltpu.with_memory_space_constraint(operand, memory) if memory is pltpu.HBM else operand
        for operand, memory in zip(operands, memories)
    ]
    return pl.pallas_call(
        functools.partial(body, sizes),
        out_shape=out_shape,
        in_specs=[pl.BlockSpec(memory_space=memory) for memory in memories],
        out_specs=[out_spec] * len(out_shape),
        scratch_shapes=scratch,
        compiler_params=pltpu.CompilerParams(vmem_limit_bytes=16 * 1024 * 1024),
    )(*pinned)


def on_device(
    temp_start, conductivity, gap_conductance, partner, row_order, active_layers, trial_stress
):
    layers, _, rows, radial = temp_start.shape
    sizes = Sizes(layers, rows, radial)
    if not fits_tiles(sizes):
        return stepwise(
            temp_start,
            conductivity,
            gap_conductance,
            partner,
            row_order,
            active_layers,
            trial_stress,
        )

    def floats(*shape):
        return jax.ShapeDtypeStruct(shape, jnp.float32)

    def near(*shape):
        return pltpu.VMEM(shape, jnp.float32)

    dealt, live = kernel_call(
        deal_kernel,
        sizes,
        (near(sizes.devices, rows, LANES), near(8, LANES)),
        [pltpu.HBM] * 5 + [pltpu.SMEM],
        [
            pltpu.SMEM(partner.shape, jnp.int32),
            pltpu.SMEM(row_order.shape, jnp.int32),
            pltpu.SMEM(gap_conductance.shape, jnp.float32),
            pltpu.VMEM(temp_start.shape, jnp.float32),
            pltpu.VMEM(conductivity.shape, jnp.float32),
            pltpu.SemaphoreType.DMA((5,)),
        ],
        (partner, row_order, gap_conductance, temp_start, conductivity, active_layers),
    )
    dealt = lax.all_to_all(dealt, EVERYONE, split_axis=0, concat_axis=0, tiled=True)
    halves = sizes.depth // 8
    (temps,) = kernel_call(
        sweep_kernel,
        sizes,
        (near(sizes.devices * halves, LANES),),
        [pltpu.VMEM],
        [
            pltpu.VMEM((sizes.members, rows * (sizes.sections + 2), LANES), jnp.float32),
            pltpu.VMEM((sizes.sections, sizes.members, rows, LANES), jnp.float32),
            pltpu.VMEM((2 * sizes.sections * rows, LANES), jnp.float32),
            pltpu.VMEM((sizes.sections * rows, LANES), jnp.float32),
        ],
        (dealt,),
    )
    temps = temps.reshape(sizes.devices, halves, LANES)
    temps = lax.all_to_all(temps, EVERYONE, split_axis=0, concat_axis=0, tiled=True)
    stress, strain = kernel_call(
        creep_kernel,
        sizes,
        (floats(sizes.depth * sizes.tiles, LANES), floats(halves * sizes.tiles, LANES)),
        [pltpu.VMEM, pltpu.VMEM, pltpu.VMEM],
        [
            pltpu.VMEM((halves, 8 * sizes.tiles, LANES), jnp.float32),
            pltpu.VMEM((halves * sizes.tiles, LANES), jnp.float32),
            pltpu.SemaphoreType.DMA((halves + 1,)),
        ],
        (
            live,
            temps.reshape(sizes.devices * halves, LANES),
            trial_stress.reshape(sizes.depth * sizes.tiles, LANES),
        ),
        space=pltpu.HBM,
    )
    return (
        stress.reshape(sizes.depth, 1, 1, radial),
        strain.reshape(halves, 1, 1, radial),
    )


def solution(mesh):
    placed = (
        P(("slab", "mech"), "iface", None, None),
        P(("slab", "mech"), "iface", None, None),
        P(("slab", "mech"), "iface", None),
        P("iface"),
        P("iface", None),
        P("iface", ("slab", "mech")),
        P(None, "iface", ("slab", "mech"), None),
    )
    return jax.shard_map(
        on_device,
        mesh=mesh,
        in_specs=placed,
        out_specs=(
            P(None, "iface", ("slab", "mech"), None),
            P(None, "iface", ("slab", "mech"), None),
        ),
        check_vma=False,
    )
```

```python
import functools
import jax
import jax.numpy as jnp
from jax import lax
from jax.experimental import pallas as pl
from jax.experimental.pallas import tpu as pltpu
from jax.sharding import PartitionSpec as P

SWEEPS = 2
NEWTON = 4


FLUX_STEP = 0.03
CREEP_RATE = 200.0
ACTIVATION = 12.0
REFERENCE_TEMP = 1.0


def padded(block, sides, width):
    for axis, dim in sides:
        count = lax.axis_size(axis)
        forward = [(i, i + 1) for i in range(count - 1)]
        backward = [(target, source) for source, target in forward]
        low = lax.ppermute(
            lax.slice_in_dim(block, block.shape[dim] - width, None, axis=dim), axis, forward
        )
        high = lax.ppermute(lax.slice_in_dim(block, 0, width, axis=dim), axis, backward)
        block = jnp.concatenate([low, block, high], axis=dim)
    return block


def neighbour_weight(shift_z, shift_a, shift_r):
    reach = abs(shift_z) + abs(shift_a) + abs(shift_r)
    return [0.0, 1.0, 0.5, 0.25][reach]


def conduction(padded_temp, padded_cond):
    center_temp = padded_temp[1:-1, 1:-1, 1:-1]
    center_cond = padded_cond[1:-1, 1:-1, 1:-1]
    depth, across, radial = center_temp.shape
    radial_index = jnp.arange(radial, dtype=jnp.int32)
    gap_row = radial // 2
    outward_open = (radial_index != gap_row - 1).astype(jnp.float32)
    inward_open = (radial_index != gap_row).astype(jnp.float32)
    total = jnp.zeros(center_temp.shape, jnp.float32)
    for shift_z in (-1, 0, 1):
        for shift_a in (-1, 0, 1):
            for shift_r in (-1, 0, 1):
                if shift_z == 0 and shift_a == 0 and (shift_r == 0):
                    continue
                near_temp = padded_temp[
                    1 + shift_z : 1 + shift_z + depth,
                    1 + shift_a : 1 + shift_a + across,
                    1 + shift_r : 1 + shift_r + radial,
                ]
                near_cond = padded_cond[
                    1 + shift_z : 1 + shift_z + depth,
                    1 + shift_a : 1 + shift_a + across,
                    1 + shift_r : 1 + shift_r + radial,
                ]
                face = neighbour_weight(shift_z, shift_a, shift_r) * 0.5 * (center_cond + near_cond)
                if shift_r == 1:
                    face = face * outward_open
                elif shift_r == -1:
                    face = face * inward_open
                total = total + face * (near_temp - center_temp)
    return FLUX_STEP * total


def creep_return(mech_temp, trial, active_layers):
    rate = CREEP_RATE * jnp.exp(-ACTIVATION / (mech_temp + REFERENCE_TEMP))
    slip = jnp.zeros(trial.shape, jnp.float32)
    for newton_step in range(NEWTON):
        left = trial - slip
        residue = slip - rate * left**3
        slope = 1.0 + 3.0 * rate * left**2
        slip = slip - residue / slope
    depth = trial.shape[0]
    layer = jnp.arange(depth, dtype=jnp.int32) // 8
    live = (layer[:, None, None] < active_layers[None, :, :]).astype(jnp.float32)[..., None]
    creep = live * slip
    stress = trial - creep
    strain = jnp.sum(creep.reshape((depth // 8, 8) + trial.shape[1:]), axis=1) * 0.125
    return (stress, strain)


def stepwise(
    temp_start, conductivity, gap_conductance, partner, row_order, active_layers, trial_stress
):
    depth = temp_start.shape[0]
    rows = temp_start.shape[2]
    radial = temp_start.shape[3]
    temp = temp_start.reshape(depth, rows, radial)
    cond = conductivity.reshape(depth, rows, radial)
    gap = gap_conductance.reshape(depth, rows)
    gap_row = radial // 2
    sections = lax.axis_size("iface")
    across = rows * sections
    all_cols = jnp.arange(across, dtype=jnp.int32)
    cond_rim = padded(cond, ((("slab", "mech"), 0), ("iface", 1)), 1)
    padded_cond = jnp.pad(cond_rim, ((0, 0), (0, 0), (1, 1)))
    spread_table = (partner[:, None] == all_cols[None, :]).astype(jnp.float32)
    for sweep in range(SWEEPS):
        temp_rim = padded(temp, ((("slab", "mech"), 0), ("iface", 1)), 1)
        padded_temp = jnp.pad(temp_rim, ((0, 0), (0, 0), (1, 1)))
        compact = temp[:, :, gap_row - 1]
        canister = temp[:, :, gap_row]
        compact_all = lax.all_gather(compact, "iface", axis=1, tiled=True)
        facing = jnp.take(compact_all, partner, axis=1)
        flux = gap * (facing - canister)
        spread = jnp.dot(
            flux, spread_table, precision=lax.Precision.HIGHEST, preferred_element_type=jnp.float32
        )
        returned = lax.psum_scatter(spread, "iface", scatter_dimension=1, tiled=True)
        fresh = temp + conduction(padded_temp, padded_cond)
        temp = (
            fresh.at[:, :, gap_row]
            .add(FLUX_STEP * flux)
            .at[:, :, gap_row - 1]
            .add(-FLUX_STEP * returned)
        )
    permuted = jnp.take(temp, row_order[0], axis=1)
    mech_temp = lax.all_to_all(permuted, ("slab", "mech"), split_axis=1, concat_axis=0, tiled=True)
    mech_temp = mech_temp.reshape(mech_temp.shape[0], 1, mech_temp.shape[1], radial)
    return creep_return(mech_temp, trial_stress, active_layers)


LANES = 128
HALO = 2
EVERYONE = ("iface", "slab", "mech")


def iota(shape, axis):
    return lax.broadcasted_iota(jnp.int32, shape, axis)


class Sizes:
    def __init__(self, layers, rows, radial):
        self.layers = layers
        self.rows = rows
        self.radial = radial
        self.tiles = radial // LANES
        self.sections = lax.axis_size("iface")
        self.members = lax.axis_size("slab") * lax.axis_size("mech")
        self.devices = self.sections * self.members
        self.depth = layers * self.members
        self.chunk = radial // self.devices
        self.width = self.chunk + 2 * HALO
        self.layer_lanes = LANES // layers
        self.extra_at = 3 * self.width
        self.gap_row = radial // 2


def chunk_of(sizes, section, member):
    mirrored = section < sizes.sections // 2
    if isinstance(section, int):
        place = sizes.members - 1 - member if mirrored else member
    else:
        place = jnp.where(mirrored, sizes.members - 1 - member, member)
    return section * sizes.members + place


def fits_tiles(sizes):
    return (
        sizes.rows == 8
        and sizes.members == sizes.rows
        and sizes.layers == 2
        and sizes.sections * sizes.rows <= LANES
        and sizes.radial % sizes.devices == 0
        and sizes.chunk * 8 == LANES
        and sizes.radial % (2 * LANES) == 0
        and sizes.extra_at + 3 <= sizes.layer_lanes
    )


def deal_kernel(
    sizes,
    partner_hbm,
    order_hbm,
    gap_hbm,
    temp_hbm,
    cond_hbm,
    active_ref,
    out_ref,
    live_ref,
    partner_ref,
    order_ref,
    gap_ref,
    temp_ref,
    cond_ref,
    sems,
):
    pairs = (
        (gap_hbm, gap_ref),
        (partner_hbm, partner_ref),
        (order_hbm, order_ref),
        (temp_hbm, temp_ref),
        (cond_hbm, cond_ref),
    )
    copies = [
        pltpu.make_async_copy(source, target, sems.at[index])
        for index, (source, target) in enumerate(pairs)
    ]
    for copy in copies[3:] + copies[:3]:
        copy.start()
    for copy in copies[:3]:
        copy.wait()
    shape = (sizes.rows, LANES)
    lane = iota(shape, 1)
    sub = iota(shape, 0)
    live_ref[...] = jnp.where(sub < active_ref[0, 0], 1.0, 0.0)
    extra_at = sizes.extra_at
    extra = jnp.zeros(shape, jnp.float32)
    for row in range(sizes.rows):
        for layer in range(sizes.layers):
            spot = (sub == row) & (lane == extra_at + layer * sizes.layer_lanes)
            extra = jnp.where(spot, gap_ref[layer, 0, row], extra)
        spot = (sub == row) & (lane == extra_at + 1)
        extra = jnp.where(spot, partner_ref[row].astype(jnp.float32), extra)
        extra = jnp.where(
            lane == 2 * sizes.width + row, partner_ref[row].astype(jnp.float32), extra
        )
        spot = (sub == row) & (lane == extra_at + 2)
        extra = jnp.where(spot, order_ref[0, row].astype(jnp.float32), extra)
    for copy in copies[3:]:
        copy.wait()
    blocks = [
        (
            layer * sizes.layer_lanes + field * sizes.width,
            [scale * ref[layer, 0, :, pl.ds(tile * LANES, LANES)] for tile in range(sizes.tiles)],
        )
        for field, (ref, scale) in enumerate(((temp_ref, 1.0), (cond_ref, FLUX_STEP)))
        for layer in range(sizes.layers)
    ]
    for device in range(sizes.devices):
        chunk = chunk_of(sizes, device // sizes.members, device % sizes.members)
        first = chunk * sizes.chunk - HALO
        packed = extra
        for base, block in blocks:
            for tile in range(sizes.tiles):
                low = max(first, tile * LANES)
                high = min(first + sizes.width, (tile + 1) * LANES)
                if low >= high:
                    continue
                moved = pltpu.roll(block[tile], (base - first + tile * LANES) % LANES, 1)
                spot = (lane >= base + low - first) & (lane < base + high - first)
                packed = jnp.where(spot, moved, packed)
        out_ref[device] = packed


def sweep_kernel(sizes, dealt_ref, out_ref, line_ref, temp_ref, table_ref, gap_ref):
    rows, width, half_lanes = sizes.rows, sizes.width, sizes.layer_lanes
    sections, members = sizes.sections, sizes.members
    shape = (rows, LANES)
    lane = iota(shape, 1)
    sub = iota(shape, 0)
    member = lax.axis_index("slab") * lax.axis_size("mech") + lax.axis_index("mech")
    place = chunk_of(sizes, lax.axis_index("iface"), member)
    first = place * sizes.chunk - HALO
    spot_in_layer = lane % half_lanes
    radius = first + spot_in_layer % width
    lower_layer = lane < half_lanes
    at_compact = radius == sizes.gap_row - 1
    at_canister = radius == sizes.gap_row
    weight = jnp.where(at_compact | at_canister, 6.0, 8.0)
    is_temp = spot_in_layer < width
    at_face = jnp.where(is_temp & (at_compact | at_canister), 1.0, 0.0)
    from_inward = jnp.where(at_canister | (radius == 0), 0.0, 0.5)
    from_outward = jnp.where(at_compact | (radius == sizes.radial - 1), 0.0, 0.5)
    face_lane = sizes.gap_row - 1 - first

    def turn(value, shift):
        return pltpu.roll(value, shift % LANES, 1)

    dealt = [[dealt_ref[s * members + k] for k in range(members)] for s in range(sections)]

    odd = lane % 2 == 1

    def strip_of(values, start):
        strips = []
        for s in range(sections):
            strip = jnp.zeros(shape, jnp.float32)
            for k in range(members):
                moved = pltpu.roll(values[s][k], (start + 2 * k) % LANES, 1)
                spot = spot_in_layer // 2 == k
                strip = jnp.where(spot, moved, strip)
            strips.append(strip)
        return jnp.concatenate(strips, axis=0)

    total = sections * rows
    has_face = (first < sizes.gap_row) & (first + width > sizes.gap_row)
    wide_odd = jnp.concatenate([odd] * sections, axis=0)

    def pick(table, strip):
        rest = strip
        picked = None
        for _ in range(3):
            part = rest.astype(jnp.bfloat16)
            rest = rest - part.astype(jnp.float32)
            share = jnp.dot(table, part, preferred_element_type=jnp.float32)
            picked = share if picked is None else picked + share
        return picked

    @pl.when(has_face)
    def prepare_exchange():
        names = jnp.full(shape, -1.0, jnp.float32)
        for s in range(sections):
            names = jnp.where(lane // rows == s, turn(dealt[s][0], s * rows - 2 * width), names)
        for s in range(sections):
            partner = dealt[s][0][:, sizes.extra_at + 1 : sizes.extra_at + 2].astype(jnp.int32)
            table_ref[pl.ds(s * rows, rows), :] = jnp.where(lane == partner, 1.0, 0.0)
        for s in range(sections):
            target = (s * rows + sub).astype(jnp.float32)
            table_ref[pl.ds(total + s * rows, rows), :] = jnp.where(names == target, 1.0, 0.0)
        table = table_ref[pl.ds(total, total), :][:, :total].astype(jnp.bfloat16)
        gap = strip_of(dealt, LANES + 1 - sizes.extra_at)
        gap_ref[...] = FLUX_STEP * jnp.where(wide_odd, gap, turn(pick(table, gap), -1))

    def exchange(values):
        strip = strip_of(values, LANES - face_lane)
        met = pick(table_ref[...][:, :total].astype(jnp.bfloat16), strip)
        met = jnp.where(wide_odd, turn(met[:total], 1), turn(met[total:], -1))
        gain = gap_ref[...] * (met - strip)
        for s in range(sections):
            own = gain[s * rows : (s + 1) * rows]
            for k in range(members):
                back = pltpu.roll(own, (face_lane - 2 * k + LANES) % LANES, 1)
                temp_ref[s, k] = temp_ref[s, k] + at_face * back

    conds = [[turn(value, -width) for value in line] for line in dealt]
    edge = jnp.zeros(shape, jnp.float32)
    for k in range(members):
        line_ref[k, pl.ds(0, rows), :] = edge
        line_ref[k, pl.ds(rows + total, rows), :] = edge

    def with_product(value, cond):
        return jnp.where(spot_in_layer < 2 * width, value, turn(value * cond, 2 * width))

    def box_sum(values):
        for s in range(sections):
            other = [turn(value, half_lanes) for value in values[s]]
            for k in range(members):
                before = other[k - 1] if k else 0.0
                after = other[k + 1] if k < members - 1 else 0.0
                near = other[k] + jnp.where(lower_layer, before, after)
                line_ref[k, pl.ds(rows + s * rows, rows), :] = values[s][k] + 0.5 * near
        result = []
        for s in range(sections):
            line = []
            for k in range(members):
                start = rows + s * rows
                near = line_ref[k, pl.ds(start - 1, rows), :] + line_ref[k, pl.ds(start + 1, rows), :]
                value = line_ref[k, pl.ds(start, rows), :] + 0.5 * near
                line.append(value + from_inward * turn(value, 1) + from_outward * turn(value, -1))
            result.append(line)
        return result

    values = dealt
    keeps = None
    for sweep in range(SWEEPS):
        packed = [
            [with_product(value, cond) for value, cond in zip(*lines)]
            for lines in zip(values, conds)
        ]
        sums = box_sum(packed)
        if keeps is None:
            keeps = [
                [1.0 - weight * cond - turn(total_sum, -width) for cond, total_sum in zip(*lines)]
                for lines in zip(conds, sums)
            ]
        for s in range(sections):
            for k in range(members):
                temp = values[s][k] * keeps[s][k] + conds[s][k] * sums[s][k]
                temp_ref[s, k] = temp + turn(sums[s][k], -2 * width)
        pl.when(has_face)(functools.partial(exchange, values))
        values = [[temp_ref[s, k] for k in range(members)] for s in range(sections)]

    per_row = 8 // sizes.layers
    skew = place % 8 * sizes.chunk
    unskewed = (lane - skew + LANES) % half_lanes
    for s in range(sections):
        order = dealt[s][0][:, sizes.extra_at + 2 : sizes.extra_at + 3].astype(jnp.int32)
        order = jnp.broadcast_to(order, shape)
        for half in range(sizes.depth // 8):
            merged = jnp.zeros(shape, jnp.float32)
            for k in range(per_row):
                moved = pltpu.roll(
                    values[s][half * per_row + k], (k * sizes.chunk - HALO + skew) % LANES, 1
                )
                merged = jnp.where(unskewed // sizes.chunk == k, moved, merged)
            chosen = jnp.take_along_axis(merged, order, axis=0)
            start = s * rows * (sizes.depth // 8) + half
            out_ref[pl.ds(start, rows, stride=sizes.depth // 8), :] = chosen


def swap_blocks(tile, block, layers, mirrored):
    sub = iota(tile.shape, 0)
    spot = iota(tile.shape, 1) // block
    held = sub % layers * (8 // layers) + sub // layers
    source = (spot - held + 8) % 8
    gathered = jnp.take_along_axis(tile, 7 - source if mirrored else source, axis=0)
    rolled = [pltpu.roll(gathered, (8 - row) % 8 * block, 1) if row else gathered for row in range(8)]
    result = rolled[0]
    for row in range(1, 8):
        result = jnp.where(held == row, rolled[row], result)
    return result


def creep_kernel(sizes, live_ref, temps_ref, trial_ref, stress_ref, strain_ref):
    tiles = sizes.tiles
    halves = sizes.depth // 8
    for tile in range(tiles):
        for element in range(halves):
            source = pl.ds(tile * 8 * halves + element, 8, stride=halves)
            mech_temp = swap_blocks(
                temps_ref[source, :], sizes.chunk, sizes.layers, tile < sizes.sections // 2
            )
            spot = pl.ds(element * 8 * tiles + tile, 8, stride=tiles)
            trial = trial_ref[spot, :]
            rate = CREEP_RATE * jnp.exp(-ACTIVATION / (mech_temp + REFERENCE_TEMP))
            slip = jnp.zeros(trial.shape, jnp.float32)
            for newton_step in range(NEWTON):
                left = trial - slip
                pull = rate * left * left
                slip = slip - (slip - pull * left) / (1.0 + 3.0 * pull)
            creep = live_ref[pl.ds(element, 1), :] * slip
            stress_ref[spot, :] = trial - creep
            strain_ref[pl.ds(element * tiles + tile, 1), :] = 0.125 * jnp.sum(
                creep, axis=0, keepdims=True
            )


def kernel_call(body, sizes, out_shape, memories, scratch, operands):
    out_spec = pl.BlockSpec(memory_space=pltpu.VMEM)
    pinned = [
        pltpu.with_memory_space_constraint(operand, memory) if memory is pltpu.HBM else operand
        for operand, memory in zip(operands, memories)
    ]
    return pl.pallas_call(
        functools.partial(body, sizes),
        out_shape=out_shape,
        in_specs=[pl.BlockSpec(memory_space=memory) for memory in memories],
        out_specs=[out_spec] * len(out_shape),
        scratch_shapes=scratch,
        compiler_params=pltpu.CompilerParams(vmem_limit_bytes=16 * 1024 * 1024),
    )(*pinned)


def on_device(
    temp_start, conductivity, gap_conductance, partner, row_order, active_layers, trial_stress
):
    layers, _, rows, radial = temp_start.shape
    sizes = Sizes(layers, rows, radial)
    if not fits_tiles(sizes):
        return stepwise(
            temp_start,
            conductivity,
            gap_conductance,
            partner,
            row_order,
            active_layers,
            trial_stress,
        )

    def floats(*shape):
        return jax.ShapeDtypeStruct(shape, jnp.float32)

    def near(*shape):
        return pltpu.VMEM(shape, jnp.float32)

    dealt, live = kernel_call(
        deal_kernel,
        sizes,
        (near(sizes.devices, rows, LANES), near(8, LANES)),
        [pltpu.HBM] * 5 + [pltpu.SMEM],
        [
            pltpu.SMEM(partner.shape, jnp.int32),
            pltpu.SMEM(row_order.shape, jnp.int32),
            pltpu.SMEM(gap_conductance.shape, jnp.float32),
            pltpu.VMEM(temp_start.shape, jnp.float32),
            pltpu.VMEM(conductivity.shape, jnp.float32),
            pltpu.SemaphoreType.DMA((5,)),
        ],
        (partner, row_order, gap_conductance, temp_start, conductivity, active_layers),
    )
    dealt = lax.all_to_all(dealt, EVERYONE, split_axis=0, concat_axis=0, tiled=True)
    halves = sizes.depth // 8
    (temps,) = kernel_call(
        sweep_kernel,
        sizes,
        (near(sizes.devices * halves, LANES),),
        [pltpu.VMEM],
        [
            pltpu.VMEM((sizes.members, rows * (sizes.sections + 2), LANES), jnp.float32),
            pltpu.VMEM((sizes.sections, sizes.members, rows, LANES), jnp.float32),
            pltpu.VMEM((2 * sizes.sections * rows, LANES), jnp.float32),
            pltpu.VMEM((sizes.sections * rows, LANES), jnp.float32),
        ],
        (dealt,),
    )
    temps = temps.reshape(sizes.devices, halves, LANES)
    temps = lax.all_to_all(temps, EVERYONE, split_axis=0, concat_axis=0, tiled=True)
    stress, strain = kernel_call(
        creep_kernel,
        sizes,
        (floats(sizes.depth * sizes.tiles, LANES), floats(halves * sizes.tiles, LANES)),
        [pltpu.VMEM, pltpu.VMEM, pltpu.VMEM],
        [],
        (
            live,
            temps.reshape(sizes.devices * halves, LANES),
            trial_stress.reshape(sizes.depth * sizes.tiles, LANES),
        ),
    )
    return (
        stress.reshape(sizes.depth, 1, 1, radial),
        strain.reshape(halves, 1, 1, radial),
    )


def solution(mesh):
    placed = (
        P(("slab", "mech"), "iface", None, None),
        P(("slab", "mech"), "iface", None, None),
        P(("slab", "mech"), "iface", None),
        P("iface"),
        P("iface", None),
        P("iface", ("slab", "mech")),
        P(None, "iface", ("slab", "mech"), None),
    )
    return jax.shard_map(
        on_device,
        mesh=mesh,
        in_specs=placed,
        out_specs=(
            P(None, "iface", ("slab", "mech"), None),
            P(None, "iface", ("slab", "mech"), None),
        ),
        check_vma=False,
    )
```

```python
import functools
import jax
import jax.numpy as jnp
from jax import lax
from jax.experimental import pallas as pl
from jax.experimental.pallas import tpu as pltpu
from jax.sharding import PartitionSpec as P

SWEEPS = 2
NEWTON = 4


FLUX_STEP = 0.03
CREEP_RATE = 200.0
ACTIVATION = 12.0
REFERENCE_TEMP = 1.0


def padded(block, sides, width):
    for axis, dim in sides:
        count = lax.axis_size(axis)
        forward = [(i, i + 1) for i in range(count - 1)]
        backward = [(target, source) for source, target in forward]
        low = lax.ppermute(
            lax.slice_in_dim(block, block.shape[dim] - width, None, axis=dim), axis, forward
        )
        high = lax.ppermute(lax.slice_in_dim(block, 0, width, axis=dim), axis, backward)
        block = jnp.concatenate([low, block, high], axis=dim)
    return block


def neighbour_weight(shift_z, shift_a, shift_r):
    reach = abs(shift_z) + abs(shift_a) + abs(shift_r)
    return [0.0, 1.0, 0.5, 0.25][reach]


def conduction(padded_temp, padded_cond):
    center_temp = padded_temp[1:-1, 1:-1, 1:-1]
    center_cond = padded_cond[1:-1, 1:-1, 1:-1]
    depth, across, radial = center_temp.shape
    radial_index = jnp.arange(radial, dtype=jnp.int32)
    gap_row = radial // 2
    outward_open = (radial_index != gap_row - 1).astype(jnp.float32)
    inward_open = (radial_index != gap_row).astype(jnp.float32)
    total = jnp.zeros(center_temp.shape, jnp.float32)
    for shift_z in (-1, 0, 1):
        for shift_a in (-1, 0, 1):
            for shift_r in (-1, 0, 1):
                if shift_z == 0 and shift_a == 0 and (shift_r == 0):
                    continue
                near_temp = padded_temp[
                    1 + shift_z : 1 + shift_z + depth,
                    1 + shift_a : 1 + shift_a + across,
                    1 + shift_r : 1 + shift_r + radial,
                ]
                near_cond = padded_cond[
                    1 + shift_z : 1 + shift_z + depth,
                    1 + shift_a : 1 + shift_a + across,
                    1 + shift_r : 1 + shift_r + radial,
                ]
                face = neighbour_weight(shift_z, shift_a, shift_r) * 0.5 * (center_cond + near_cond)
                if shift_r == 1:
                    face = face * outward_open
                elif shift_r == -1:
                    face = face * inward_open
                total = total + face * (near_temp - center_temp)
    return FLUX_STEP * total


def creep_return(mech_temp, trial, active_layers):
    rate = CREEP_RATE * jnp.exp(-ACTIVATION / (mech_temp + REFERENCE_TEMP))
    slip = jnp.zeros(trial.shape, jnp.float32)
    for newton_step in range(NEWTON):
        left = trial - slip
        residue = slip - rate * left**3
        slope = 1.0 + 3.0 * rate * left**2
        slip = slip - residue / slope
    depth = trial.shape[0]
    layer = jnp.arange(depth, dtype=jnp.int32) // 8
    live = (layer[:, None, None] < active_layers[None, :, :]).astype(jnp.float32)[..., None]
    creep = live * slip
    stress = trial - creep
    strain = jnp.sum(creep.reshape((depth // 8, 8) + trial.shape[1:]), axis=1) * 0.125
    return (stress, strain)


def stepwise(
    temp_start, conductivity, gap_conductance, partner, row_order, active_layers, trial_stress
):
    depth = temp_start.shape[0]
    rows = temp_start.shape[2]
    radial = temp_start.shape[3]
    temp = temp_start.reshape(depth, rows, radial)
    cond = conductivity.reshape(depth, rows, radial)
    gap = gap_conductance.reshape(depth, rows)
    gap_row = radial // 2
    sections = lax.axis_size("iface")
    across = rows * sections
    all_cols = jnp.arange(across, dtype=jnp.int32)
    cond_rim = padded(cond, ((("slab", "mech"), 0), ("iface", 1)), 1)
    padded_cond = jnp.pad(cond_rim, ((0, 0), (0, 0), (1, 1)))
    spread_table = (partner[:, None] == all_cols[None, :]).astype(jnp.float32)
    for sweep in range(SWEEPS):
        temp_rim = padded(temp, ((("slab", "mech"), 0), ("iface", 1)), 1)
        padded_temp = jnp.pad(temp_rim, ((0, 0), (0, 0), (1, 1)))
        compact = temp[:, :, gap_row - 1]
        canister = temp[:, :, gap_row]
        compact_all = lax.all_gather(compact, "iface", axis=1, tiled=True)
        facing = jnp.take(compact_all, partner, axis=1)
        flux = gap * (facing - canister)
        spread = jnp.dot(
            flux, spread_table, precision=lax.Precision.HIGHEST, preferred_element_type=jnp.float32
        )
        returned = lax.psum_scatter(spread, "iface", scatter_dimension=1, tiled=True)
        fresh = temp + conduction(padded_temp, padded_cond)
        temp = (
            fresh.at[:, :, gap_row]
            .add(FLUX_STEP * flux)
            .at[:, :, gap_row - 1]
            .add(-FLUX_STEP * returned)
        )
    permuted = jnp.take(temp, row_order[0], axis=1)
    mech_temp = lax.all_to_all(permuted, ("slab", "mech"), split_axis=1, concat_axis=0, tiled=True)
    mech_temp = mech_temp.reshape(mech_temp.shape[0], 1, mech_temp.shape[1], radial)
    return creep_return(mech_temp, trial_stress, active_layers)


LANES = 128
HALO = 2
EVERYONE = ("iface", "slab", "mech")


def iota(shape, axis):
    return lax.broadcasted_iota(jnp.int32, shape, axis)


class Sizes:
    def __init__(self, layers, rows, radial):
        self.layers = layers
        self.rows = rows
        self.radial = radial
        self.tiles = radial // LANES
        self.sections = lax.axis_size("iface")
        self.members = lax.axis_size("slab") * lax.axis_size("mech")
        self.devices = self.sections * self.members
        self.depth = layers * self.members
        self.chunk = radial // self.devices
        self.width = self.chunk + 2 * HALO
        self.layer_lanes = LANES // layers
        self.extra_at = 3 * self.width
        self.gap_row = radial // 2


def chunk_of(sizes, section, member):
    mirrored = section < sizes.sections // 2
    if isinstance(section, int):
        place = sizes.members - 1 - member if mirrored else member
    else:
        place = jnp.where(mirrored, sizes.members - 1 - member, member)
    return section * sizes.members + place


def fits_tiles(sizes):
    return (
        sizes.rows == 8
        and sizes.members == sizes.rows
        and sizes.layers == 2
        and sizes.sections * sizes.rows <= LANES
        and sizes.radial % sizes.devices == 0
        and sizes.chunk * 8 == LANES
        and sizes.radial % (2 * LANES) == 0
        and sizes.extra_at + 3 <= sizes.layer_lanes
    )


def deal_kernel(
    sizes,
    partner_hbm,
    order_hbm,
    gap_hbm,
    temp_hbm,
    cond_hbm,
    active_ref,
    out_ref,
    live_ref,
    partner_ref,
    order_ref,
    gap_ref,
    temp_ref,
    cond_ref,
    sems,
):
    pairs = (
        (gap_hbm, gap_ref),
        (partner_hbm, partner_ref),
        (order_hbm, order_ref),
        (temp_hbm, temp_ref),
        (cond_hbm, cond_ref),
    )
    copies = [
        pltpu.make_async_copy(source, target, sems.at[index])
        for index, (source, target) in enumerate(pairs)
    ]
    for index, copy in enumerate(copies):
        copy.start(priority=0 if index < 3 else 1)
    for copy in copies[:3]:
        copy.wait()
    shape = (sizes.rows, LANES)
    lane = iota(shape, 1)
    sub = iota(shape, 0)
    live_ref[...] = jnp.where(sub < active_ref[0, 0], 1.0, 0.0)
    extra_at = sizes.extra_at
    extra = jnp.zeros(shape, jnp.float32)
    for row in range(sizes.rows):
        for layer in range(sizes.layers):
            spot = (sub == row) & (lane == extra_at + layer * sizes.layer_lanes)
            extra = jnp.where(spot, gap_ref[layer, 0, row], extra)
        spot = (sub == row) & (lane == extra_at + 1)
        extra = jnp.where(spot, partner_ref[row].astype(jnp.float32), extra)
        extra = jnp.where(
            lane == 2 * sizes.width + row, partner_ref[row].astype(jnp.float32), extra
        )
        spot = (sub == row) & (lane == extra_at + 2)
        extra = jnp.where(spot, order_ref[0, row].astype(jnp.float32), extra)
    for copy in copies[3:]:
        copy.wait()
    blocks = [
        (
            layer * sizes.layer_lanes + field * sizes.width,
            [scale * ref[layer, 0, :, pl.ds(tile * LANES, LANES)] for tile in range(sizes.tiles)],
        )
        for field, (ref, scale) in enumerate(((temp_ref, 1.0), (cond_ref, FLUX_STEP)))
        for layer in range(sizes.layers)
    ]
    for device in range(sizes.devices):
        chunk = chunk_of(sizes, device // sizes.members, device % sizes.members)
        first = chunk * sizes.chunk - HALO
        packed = extra
        for base, block in blocks:
            for tile in range(sizes.tiles):
                low = max(first, tile * LANES)
                high = min(first + sizes.width, (tile + 1) * LANES)
                if low >= high:
                    continue
                moved = pltpu.roll(block[tile], (base - first + tile * LANES) % LANES, 1)
                spot = (lane >= base + low - first) & (lane < base + high - first)
                packed = jnp.where(spot, moved, packed)
        out_ref[device] = packed


def sweep_kernel(sizes, dealt_ref, out_ref, line_ref, temp_ref, table_ref, gap_ref):
    rows, width, half_lanes = sizes.rows, sizes.width, sizes.layer_lanes
    sections, members = sizes.sections, sizes.members
    shape = (rows, LANES)
    lane = iota(shape, 1)
    sub = iota(shape, 0)
    member = lax.axis_index("slab") * lax.axis_size("mech") + lax.axis_index("mech")
    place = chunk_of(sizes, lax.axis_index("iface"), member)
    first = place * sizes.chunk - HALO
    spot_in_layer = lane % half_lanes
    radius = first + spot_in_layer % width
    lower_layer = lane < half_lanes
    at_compact = radius == sizes.gap_row - 1
    at_canister = radius == sizes.gap_row
    weight = jnp.where(at_compact | at_canister, 6.0, 8.0)
    is_temp = spot_in_layer < width
    at_face = jnp.where(is_temp & (at_compact | at_canister), 1.0, 0.0)
    from_inward = jnp.where(at_canister | (radius == 0), 0.0, 0.5)
    from_outward = jnp.where(at_compact | (radius == sizes.radial - 1), 0.0, 0.5)
    face_lane = sizes.gap_row - 1 - first

    def turn(value, shift):
        return pltpu.roll(value, shift % LANES, 1)

    dealt = [[dealt_ref[s * members + k] for k in range(members)] for s in range(sections)]

    odd = lane % 2 == 1

    def strip_of(values, start):
        strips = []
        for s in range(sections):
            strip = jnp.zeros(shape, jnp.float32)
            for k in range(members):
                moved = pltpu.roll(values[s][k], (start + 2 * k) % LANES, 1)
                spot = spot_in_layer // 2 == k
                strip = jnp.where(spot, moved, strip)
            strips.append(strip)
        return jnp.concatenate(strips, axis=0)

    total = sections * rows
    has_face = (first < sizes.gap_row) & (first + width > sizes.gap_row)
    wide_odd = jnp.concatenate([odd] * sections, axis=0)

    def pick(table, strip):
        rest = strip
        picked = None
        for _ in range(3):
            part = rest.astype(jnp.bfloat16)
            rest = rest - part.astype(jnp.float32)
            share = jnp.dot(table, part, preferred_element_type=jnp.float32)
            picked = share if picked is None else picked + share
        return picked

    @pl.when(has_face)
    def prepare_exchange():
        names = jnp.full(shape, -1.0, jnp.float32)
        for s in range(sections):
            names = jnp.where(lane // rows == s, turn(dealt[s][0], s * rows - 2 * width), names)
        for s in range(sections):
            partner = dealt[s][0][:, sizes.extra_at + 1 : sizes.extra_at + 2].astype(jnp.int32)
            table_ref[pl.ds(s * rows, rows), :] = jnp.where(lane == partner, 1.0, 0.0)
        for s in range(sections):
            target = (s * rows + sub).astype(jnp.float32)
            table_ref[pl.ds(total + s * rows, rows), :] = jnp.where(names == target, 1.0, 0.0)
        table = table_ref[pl.ds(total, total), :][:, :total].astype(jnp.bfloat16)
        gap = strip_of(dealt, LANES + 1 - sizes.extra_at)
        gap_ref[...] = FLUX_STEP * jnp.where(wide_odd, gap, turn(pick(table, gap), -1))

    def exchange(values):
        strip = strip_of(values, LANES - face_lane)
        met = pick(table_ref[...][:, :total].astype(jnp.bfloat16), strip)
        met = jnp.where(wide_odd, turn(met[:total], 1), turn(met[total:], -1))
        gain = gap_ref[...] * (met - strip)
        for s in range(sections):
            own = gain[s * rows : (s + 1) * rows]
            for k in range(members):
                back = pltpu.roll(own, (face_lane - 2 * k + LANES) % LANES, 1)
                temp_ref[s, k] = temp_ref[s, k] + at_face * back

    conds = [[turn(value, -width) for value in line] for line in dealt]
    edge = jnp.zeros(shape, jnp.float32)
    for k in range(members):
        line_ref[k, pl.ds(0, rows), :] = edge
        line_ref[k, pl.ds(rows + total, rows), :] = edge

    def with_product(value, cond):
        return jnp.where(spot_in_layer < 2 * width, value, turn(value * cond, 2 * width))

    def box_sum(values):
        for s in range(sections):
            other = [turn(value, half_lanes) for value in values[s]]
            for k in range(members):
                before = other[k - 1] if k else 0.0
                after = other[k + 1] if k < members - 1 else 0.0
                near = other[k] + jnp.where(lower_layer, before, after)
                line_ref[k, pl.ds(rows + s * rows, rows), :] = values[s][k] + 0.5 * near
        result = []
        for s in range(sections):
            line = []
            for k in range(members):
                start = rows + s * rows
                near = line_ref[k, pl.ds(start - 1, rows), :] + line_ref[k, pl.ds(start + 1, rows), :]
                value = line_ref[k, pl.ds(start, rows), :] + 0.5 * near
                line.append(value + from_inward * turn(value, 1) + from_outward * turn(value, -1))
            result.append(line)
        return result

    values = dealt
    keeps = None
    for sweep in range(SWEEPS):
        packed = [
            [with_product(value, cond) for value, cond in zip(*lines)]
            for lines in zip(values, conds)
        ]
        sums = box_sum(packed)
        if keeps is None:
            keeps = [
                [1.0 - weight * cond - turn(total_sum, -width) for cond, total_sum in zip(*lines)]
                for lines in zip(conds, sums)
            ]
        for s in range(sections):
            for k in range(members):
                temp = values[s][k] * keeps[s][k] + conds[s][k] * sums[s][k]
                temp_ref[s, k] = temp + turn(sums[s][k], -2 * width)
        pl.when(has_face)(functools.partial(exchange, values))
        values = [[temp_ref[s, k] for k in range(members)] for s in range(sections)]

    per_row = 8 // sizes.layers
    skew = place % 8 * sizes.chunk
    unskewed = (lane - skew + LANES) % half_lanes
    for s in range(sections):
        order = dealt[s][0][:, sizes.extra_at + 2 : sizes.extra_at + 3].astype(jnp.int32)
        order = jnp.broadcast_to(order, shape)
        for half in range(sizes.depth // 8):
            merged = jnp.zeros(shape, jnp.float32)
            for k in range(per_row):
                moved = pltpu.roll(
                    values[s][half * per_row + k], (k * sizes.chunk - HALO + skew) % LANES, 1
                )
                merged = jnp.where(unskewed // sizes.chunk == k, moved, merged)
            chosen = jnp.take_along_axis(merged, order, axis=0)
            start = s * rows * (sizes.depth // 8) + half
            out_ref[pl.ds(start, rows, stride=sizes.depth // 8), :] = chosen


def swap_blocks(tile, block, layers, mirrored):
    sub = iota(tile.shape, 0)
    spot = iota(tile.shape, 1) // block
    held = sub % layers * (8 // layers) + sub // layers
    source = (spot - held + 8) % 8
    gathered = jnp.take_along_axis(tile, 7 - source if mirrored else source, axis=0)
    rolled = [pltpu.roll(gathered, (8 - row) % 8 * block, 1) if row else gathered for row in range(8)]
    result = rolled[0]
    for row in range(1, 8):
        result = jnp.where(held == row, rolled[row], result)
    return result


def creep_kernel(sizes, live_ref, temps_ref, trial_ref, stress_ref, strain_ref):
    tiles = sizes.tiles
    halves = sizes.depth // 8
    for tile in range(tiles):
        for element in range(halves):
            source = pl.ds(tile * 8 * halves + element, 8, stride=halves)
            mech_temp = swap_blocks(
                temps_ref[source, :], sizes.chunk, sizes.layers, tile < sizes.sections // 2
            )
            spot = pl.ds(element * 8 * tiles + tile, 8, stride=tiles)
            trial = trial_ref[spot, :]
            rate = CREEP_RATE * jnp.exp(-ACTIVATION / (mech_temp + REFERENCE_TEMP))
            slip = jnp.zeros(trial.shape, jnp.float32)
            for newton_step in range(NEWTON):
                left = trial - slip
                pull = rate * left * left
                slip = slip - (slip - pull * left) / (1.0 + 3.0 * pull)
            creep = live_ref[pl.ds(element, 1), :] * slip
            stress_ref[spot, :] = trial - creep
            strain_ref[pl.ds(element * tiles + tile, 1), :] = 0.125 * jnp.sum(
                creep, axis=0, keepdims=True
            )


def kernel_call(body, sizes, out_shape, memories, scratch, operands):
    out_spec = pl.BlockSpec(memory_space=pltpu.VMEM)
    pinned = [
        pltpu.with_memory_space_constraint(operand, memory) if memory is pltpu.HBM else operand
        for operand, memory in zip(operands, memories)
    ]
    return pl.pallas_call(
        functools.partial(body, sizes),
        out_shape=out_shape,
        in_specs=[pl.BlockSpec(memory_space=memory) for memory in memories],
        out_specs=[out_spec] * len(out_shape),
        scratch_shapes=scratch,
        compiler_params=pltpu.CompilerParams(vmem_limit_bytes=16 * 1024 * 1024),
    )(*pinned)


def on_device(
    temp_start, conductivity, gap_conductance, partner, row_order, active_layers, trial_stress
):
    layers, _, rows, radial = temp_start.shape
    sizes = Sizes(layers, rows, radial)
    if not fits_tiles(sizes):
        return stepwise(
            temp_start,
            conductivity,
            gap_conductance,
            partner,
            row_order,
            active_layers,
            trial_stress,
        )

    def floats(*shape):
        return jax.ShapeDtypeStruct(shape, jnp.float32)

    def near(*shape):
        return pltpu.VMEM(shape, jnp.float32)

    dealt, live = kernel_call(
        deal_kernel,
        sizes,
        (near(sizes.devices, rows, LANES), near(8, LANES)),
        [pltpu.HBM] * 5 + [pltpu.SMEM],
        [
            pltpu.SMEM(partner.shape, jnp.int32),
            pltpu.SMEM(row_order.shape, jnp.int32),
            pltpu.SMEM(gap_conductance.shape, jnp.float32),
            pltpu.VMEM(temp_start.shape, jnp.float32),
            pltpu.VMEM(conductivity.shape, jnp.float32),
            pltpu.SemaphoreType.DMA((5,)),
        ],
        (partner, row_order, gap_conductance, temp_start, conductivity, active_layers),
    )
    dealt = lax.all_to_all(dealt, EVERYONE, split_axis=0, concat_axis=0, tiled=True)
    halves = sizes.depth // 8
    (temps,) = kernel_call(
        sweep_kernel,
        sizes,
        (near(sizes.devices * halves, LANES),),
        [pltpu.VMEM],
        [
            pltpu.VMEM((sizes.members, rows * (sizes.sections + 2), LANES), jnp.float32),
            pltpu.VMEM((sizes.sections, sizes.members, rows, LANES), jnp.float32),
            pltpu.VMEM((2 * sizes.sections * rows, LANES), jnp.float32),
            pltpu.VMEM((sizes.sections * rows, LANES), jnp.float32),
        ],
        (dealt,),
    )
    temps = temps.reshape(sizes.devices, halves, LANES)
    temps = lax.all_to_all(temps, EVERYONE, split_axis=0, concat_axis=0, tiled=True)
    stress, strain = kernel_call(
        creep_kernel,
        sizes,
        (floats(sizes.depth * sizes.tiles, LANES), floats(halves * sizes.tiles, LANES)),
        [pltpu.VMEM, pltpu.VMEM, pltpu.VMEM],
        [],
        (
            live,
            temps.reshape(sizes.devices * halves, LANES),
            trial_stress.reshape(sizes.depth * sizes.tiles, LANES),
        ),
    )
    return (
        stress.reshape(sizes.depth, 1, 1, radial),
        strain.reshape(halves, 1, 1, radial),
    )


def solution(mesh):
    placed = (
        P(("slab", "mech"), "iface", None, None),
        P(("slab", "mech"), "iface", None, None),
        P(("slab", "mech"), "iface", None),
        P("iface"),
        P("iface", None),
        P("iface", ("slab", "mech")),
        P(None, "iface", ("slab", "mech"), None),
    )
    return jax.shard_map(
        on_device,
        mesh=mesh,
        in_specs=placed,
        out_specs=(
            P(None, "iface", ("slab", "mech"), None),
            P(None, "iface", ("slab", "mech"), None),
        ),
        check_vma=False,
    )
```
